32 devices in a mesh: wide: 16 (over z, x, core), narrow: 2 (over y).
Axes of the slice: x: 2, y: 2, z: 4, core: 2. Of those that a mesh axis runs over, the one named last changes fastest.
Arguments:
- tokens: bfloat16 [8192, 1536], P(('wide', 'narrow')), may hold values from -6 to 6
- cotangent: bfloat16 [8192, 1536], P(('wide', 'narrow')), may hold values from -6 to 6
- segments: int32 [16, 512], replicated, may hold values from 0 to 3, never falling along the last dimension, each value on 1 to 256 neighbouring positions
- owner_list: int32 [1440], replicated, may hold values from 0 to 1428, as said below
- masters: float32 [2880, 128, 128], P(('wide', 'narrow'))
- first_moment: float32 [2880, 128, 128], P(('wide', 'narrow'))
- second_moment: float32 [2880, 128, 128], P(('wide', 'narrow')), as said below
- left_basis: float32 [2880, 128, 128], P(('wide', 'narrow')), may hold values from -1 to 1, as said below
- right_basis: float32 [2880, 128, 128], P(('wide', 'narrow')), may hold values from -1 to 1, as said below
- gains: float32 [3072], P(('wide', 'narrow')), may hold values from 0.5 to 1.5
- gain_first: float32 [3072], P(('wide', 'narrow'))
- gain_second: float32 [3072], P(('wide', 'narrow')), as said below
- biases: float32 [2, 1024], P('narrow', 'wide'), may hold values from -1.5 to 1.5
- bias_first: float32 [2, 1024], P('narrow', 'wide')
- bias_second: float32 [2, 1024], P('narrow', 'wide'), as said below
Outputs:
- output: bfloat16 [8192, 1536], P(('wide', 'narrow'))
- input_grad: float32 [8192, 1536], P(('wide', 'narrow'))
- block_grad: float32 [2880, 128, 128], P(('wide', 'narrow'))
- new_masters: float32 [2880, 128, 128], P(('wide', 'narrow'))
- new_first: float32 [2880, 128, 128], P(('wide', 'narrow'))
- new_second: float32 [2880, 128, 128], P(('wide', 'narrow'))
- gain_grad: float32 [3072], P(('wide', 'narrow'))
- new_gains: float32 [3072], P(('wide', 'narrow'))
- new_gain_first: float32 [3072], P(('wide', 'narrow'))
- new_gain_second: float32 [3072], P(('wide', 'narrow'))
- bias_grad: float32 [2, 1024], P('narrow', 'wide')
- new_biases: float32 [2, 1024], P('narrow', 'wide')
- new_bias_first: float32 [2, 1024], P('narrow', 'wide')
- new_bias_second: float32 [2, 1024], P('narrow', 'wide')
The draws below stay inside these ranges and needn't reach their ends.
Inputs may be any that keep to these rules, and one draw needn't show every extreme that they name: `owner_list`: each block number 0 to 1427 stands exactly once; the other entries equal 1428 and mark empty slots. `left_basis`: every 128 x 128 block is orthogonal. `right_basis`: every 128 x 128 block is orthogonal. `second_moment`: every entry is positive. `gain_second`: every entry is positive. `bias_second`: every entry is positive.
All inputs are finite; a program needn't handle non-finite values.
Results may differ from the reference program's by a relative error of at most 0.012.
Values may be sent and summed in bfloat16 or wider, within the bound.
A program may use at most 384 MiB of HBM per device.

```python
import math
import jax
import jax.numpy as jnp
import numpy as np
from jax import lax

D = 1536
FF = 8960
HEADS = 12
KV_HEADS = 2
HEAD_DIM = 128
BLK = 128
STEP_COUNT = 5
ROW = 512
ROWS = 16
TOKENS = 8192
QW = 768
KW = 128
FH = 4480
BIAS_H = 1024
NBH = 1428
SLOT_DEV = 90
SLOTS_H = 1440
SLOTS = 2880
N_WIDE = 16
N_NARROW = 2


decay_ratio = 0.05 / 0.95


grad_levels = [0.8, 2.0, 3.2, 0.22, 0.2, 0.25, 0.6]


def owner_table(key):
    order = jax.random.permutation(jax.random.fold_in(key, 11), SLOTS_H)
    return jnp.minimum(order, NBH).astype(jnp.int32)


def kind_counts():
    row_blocks = D // BLK
    query_cols = QW // BLK
    pair_cols = KW // BLK
    hidden_cols = FH // BLK
    return [row_blocks * query_cols, row_blocks * pair_cols, row_blocks * pair_cols, query_cols * row_blocks, row_blocks * hidden_cols, row_blocks * hidden_cols, hidden_cols * row_blocks]


def per_kind(block_ids, levels, empty_level):
    result = jnp.full(block_ids.shape, empty_level, jnp.float32)
    begin_at = 0
    for count_here, level_here in zip(kind_counts(), levels):
        inside = (block_ids >= begin_at) & (block_ids < begin_at + count_here)
        result = jnp.where(inside, level_here, result)
        begin_at += count_here
    return result


def slot_blocks(key):
    owners = owner_table(key)
    slot_index = jnp.arange(SLOTS, dtype=jnp.int32)
    device_slot = slot_index // SLOT_DEV
    wide_index = device_slot // N_NARROW
    within = slot_index % SLOT_DEV
    return owners[wide_index * SLOT_DEV + within]


def grad_scale(key):
    return per_kind(slot_blocks(key), grad_levels, 0.5) * math.sqrt(TOKENS)


def draw_owner_list(key, part):
    return owner_table(key)


def draw_masters(key, part):
    spreads = per_kind(slot_blocks(key), [D ** (-0.5), D ** (-0.5), D ** (-0.5), (D // 16) ** (-0.5), D ** (-0.5), D ** (-0.5), FF ** (-0.5)], D ** (-0.5))
    random_part = jax.random.normal(jax.random.fold_in(key, 21), (SLOTS, BLK, BLK), jnp.float32)
    return random_part * spreads[:, None, None]


def draw_first_moment(key, part):
    random_part = jax.random.normal(jax.random.fold_in(key, 31), (SLOTS, BLK, BLK), jnp.float32)
    return random_part * (decay_ratio * grad_scale(key))[:, None, None]


def draw_second_moment(key, part):
    factor = jax.random.uniform(jax.random.fold_in(key, 33), (SLOTS, BLK, BLK), jnp.float32, 1.0, 4.0)
    level = grad_scale(key)
    return factor * (decay_ratio * level * level)[:, None, None]


def orthogonal_blocks(key):
    random_part = jax.random.normal(key, (SLOTS, BLK, BLK), jnp.float32)
    basis, _ = jnp.linalg.qr(random_part)
    return basis


def draw_left_basis(key, part):
    return orthogonal_blocks(jax.random.fold_in(key, 41))


def draw_right_basis(key, part):
    return orthogonal_blocks(jax.random.fold_in(key, 43))


def gain_level():
    return jnp.concatenate([jnp.full((D,), 1.7, jnp.float32), jnp.full((D,), 0.5, jnp.float32)]) * math.sqrt(TOKENS)


def draw_gain_first(key, part):
    random_part = jax.random.normal(jax.random.fold_in(key, 51), (2 * D,), jnp.float32)
    return random_part * decay_ratio * gain_level()


def draw_gain_second(key, part):
    factor = jax.random.uniform(jax.random.fold_in(key, 53), (2 * D,), jnp.float32, 1.0, 4.0)
    level = gain_level()
    return factor * decay_ratio * level * level


def bias_level():
    row_level = jnp.concatenate([jnp.full((QW,), 0.8, jnp.float32), jnp.full((KW,), 2.0, jnp.float32), jnp.full((KW,), 3.2, jnp.float32)]) * math.sqrt(TOKENS)
    return jnp.broadcast_to(row_level[None, :], (N_NARROW, BIAS_H))


def draw_bias_first(key, part):
    random_part = jax.random.normal(jax.random.fold_in(key, 61), (N_NARROW, BIAS_H), jnp.float32)
    return random_part * decay_ratio * bias_level()


def draw_bias_second(key, part):
    factor = jax.random.uniform(jax.random.fold_in(key, 63), (N_NARROW, BIAS_H), jnp.float32, 1.0, 4.0)
    level = bias_level()
    return factor * decay_ratio * level * level


def block_scale(stream_key, dims, cuts, low, high):
    def one(axis_at, parts):
        steps = jax.random.uniform(jax.random.fold_in(jax.random.fold_in(stream_key, 6), axis_at), (parts,), jnp.float32, low / len(cuts), high / len(cuts))
        return jnp.repeat(jnp.exp(steps), dims[axis_at] // parts).reshape((-1,) + (1,) * (len(dims) - axis_at - 1))

    loudness = one(*cuts[0])
    for cut in cuts[1:]:
        loudness = loudness * one(*cut)
    return loudness


def split_up(number_of, total, reach, slope):
    loads = [(1 << 20) // math.isqrt(grade ** slope) + 1 for grade in range(2, number_of + 1)]
    rest, given = total - reach - (number_of - 1), [1] * (number_of - 1)
    while rest > 0:
        movable = [i for i in range(number_of - 1) if given[i] < reach]
        mass, left = sum([loads[i] for i in movable]), rest
        for i in movable:
            addition = min(reach - given[i], max(1, left * loads[i] // mass), rest)
            given[i] = given[i] + addition
            rest = rest - addition
    return np.array([reach] + given)


def ragged(own_key, amount, total, reach, lean):
    if amount == 2:
        one = jax.random.randint(own_key, (), max(1, total - reach), min(reach, total - 1) + 1)
        return jnp.stack([one, total - one])
    tallies = jnp.asarray(split_up(amount, total, reach, lean), jnp.int32)
    twos = (amount - 1) // 2
    giver, sink = tallies[1:1 + 2 * twos:2], tallies[2:2 + 2 * twos:2]
    slack = jnp.minimum(giver - 1, reach - sink)
    moved = jax.random.randint(jax.random.fold_in(own_key, 1), (twos,), 0, 1 << 20) % (slack + 1)
    tallies = tallies.at[1:1 + 2 * twos:2].set(giver - moved).at[2:2 + 2 * twos:2].set(sink + moved)
    return tallies[jax.random.permutation(jax.random.fold_in(own_key, 2), amount)]


def centred(own_key, dims, width, most, cuts=(), kind=jnp.bfloat16):
    values = jax.random.normal(own_key, dims, jnp.float32) * width
    if len(cuts) > 0:
        values = block_scale(own_key, dims, cuts, -0.22, 0.18) * values
    return jnp.clip(values, min=-most, max=most).astype(kind)


def setup_inputs(seed: int = 0) -> dict:
    streams_of = jax.random.split(jax.random.key(seed), 16)
    tokens = centred(streams_of[0], (TOKENS, D), 1.0, 6.0, ((0, 32),))
    cotangent = centred(streams_of[1], (TOKENS, D), 1.0, 6.0, ((0, 32),))
    segments = jax.vmap(lambda own: jnp.searchsorted(jnp.cumsum(ragged(own, 4, ROW, ROW // 2, 2)), jnp.arange(ROW), side="right"))(jax.random.split(streams_of[2], ROWS)).reshape((ROWS, ROW)).astype(jnp.int32)
    owner_list = draw_owner_list(jax.random.fold_in(streams_of[15], 71), 0)
    masters = draw_masters(jax.random.fold_in(streams_of[15], 71), 0)
    first_moment = draw_first_moment(jax.random.fold_in(streams_of[15], 71), 0)
    second_moment = draw_second_moment(jax.random.fold_in(streams_of[15], 71), 0)
    left_basis = draw_left_basis(jax.random.fold_in(streams_of[15], 71), 0)
    right_basis = draw_right_basis(jax.random.fold_in(streams_of[15], 71), 0)
    gains = jnp.clip(1.0 + 0.1 * jax.random.normal(streams_of[9], (2 * D,), jnp.float32), 0.5, 1.5)
    gain_first = draw_gain_first(jax.random.fold_in(streams_of[15], 71), 0)
    gain_second = draw_gain_second(jax.random.fold_in(streams_of[15], 71), 0)
    biases = centred(streams_of[12], (N_NARROW, BIAS_H), 0.25, 1.5, ((0, 2), (1, 16)), jnp.float32)
    bias_first = draw_bias_first(jax.random.fold_in(streams_of[15], 71), 0)
    bias_second = draw_bias_second(jax.random.fold_in(streams_of[15], 71), 0)
    return {"tokens": tokens, "cotangent": cotangent, "segments": segments, "owner_list": owner_list, "masters": masters, "first_moment": first_moment, "second_moment": second_moment, "left_basis": left_basis, "right_basis": right_basis, "gains": gains, "gain_first": gain_first, "gain_second": gain_second, "biases": biases, "bias_first": bias_first, "bias_second": bias_second}


beta_first = 0.95
beta_second = 0.95
adam_eps = 1e-08
rate_blocks = 0.03
rate_small = 0.4
rate_gains = 0.6
norm_eps = 1e-06
rope_base = 10000.0
masked_score = -1e+30

@jax.custom_vjp
def low(v):
    return lax.optimization_barrier(v.astype(jnp.bfloat16)).astype(jnp.float32)

@jax.custom_vjp
def low_back(v):
    return v

def low_keep(v):
    return (low(v), None)

def low_pass(kept, grad):
    return (grad,)

def back_keep(v):
    return (v, None)

def back_low(kept, grad):
    return (low(grad),)
low.defvjp(low_keep, low_pass)
low_back.defvjp(back_keep, back_low)

def product(left_side, right_side):
    return jnp.dot(left_side.astype(jnp.float32), right_side.astype(jnp.float32), precision=lax.Precision.HIGHEST, preferred_element_type=jnp.float32)

def rms_scale(values):
    return values * lax.rsqrt(lax.optimization_barrier(jnp.mean(values * values, axis=-1, keepdims=True)) + norm_eps)

def rotate_half(vector):
    middle = vector.shape[-1] // 2
    return jnp.concatenate([-vector[..., middle:], vector[..., :middle]], axis=-1)

def rope_tables(segment_row):
    token_index = jnp.arange(segment_row.shape[0], dtype=jnp.int32)
    changed = jnp.concatenate([jnp.ones((1,), dtype=bool), segment_row[1:] != segment_row[:-1]])
    begins = lax.cummax(jnp.where(changed, token_index, jnp.zeros_like(token_index)), axis=0)
    places = (token_index - begins).astype(jnp.float32)
    frequency = rope_base ** (-(jnp.arange(HEAD_DIM // 2, dtype=jnp.float32) * 2.0) / HEAD_DIM)
    angles = places[:, None] * frequency[None, :]
    cosine = jnp.concatenate([jnp.cos(angles), jnp.cos(angles)], axis=-1)[:, None, :]
    sine_table = jnp.concatenate([jnp.sin(angles), jnp.sin(angles)], axis=-1)[:, None, :]
    return (cosine, sine_table)

def layer_row(params, hidden_in, segment_row):
    w_query, w_key, w_value, w_out, w_gate, w_up, w_down, b_query, b_key, b_value, gain_one, gain_two = params
    row_length = hidden_in.shape[0]
    group_size = HEADS // KV_HEADS
    cosine, sine_table = rope_tables(segment_row)
    token_index = jnp.arange(row_length, dtype=jnp.int32)
    allowed = (segment_row[:, None] == segment_row[None, :]) & (token_index[:, None] >= token_index[None, :])
    norm_one = low(rms_scale(hidden_in) * gain_one)
    queries = low_back(product(norm_one, w_query) + b_query).reshape(row_length, HEADS, HEAD_DIM)
    keys_pre = low_back(product(norm_one, w_key) + b_key).reshape(row_length, KV_HEADS, HEAD_DIM)
    values = low(low_back(product(norm_one, w_value) + b_value)).reshape(row_length, KV_HEADS, HEAD_DIM)
    queries = low(queries * cosine + rotate_half(queries) * sine_table)
    keys_rot = low(keys_pre * cosine + rotate_half(keys_pre) * sine_table)
    grouped = queries.reshape(row_length, KV_HEADS, group_size, HEAD_DIM)
    scores = jnp.einsum('ikgd,jkd->kgij', grouped, keys_rot, precision=lax.Precision.HIGHEST) * HEAD_DIM ** (-0.5)
    scores = jnp.where(allowed, low_back(scores), masked_score)
    weights_soft = low(jax.nn.softmax(scores, axis=-1))
    mixed_heads = jnp.einsum('kgij,jkd->ikgd', weights_soft, values, precision=lax.Precision.HIGHEST)
    mixed_heads = low(low_back(mixed_heads.reshape(row_length, HEADS * HEAD_DIM)))
    residual = hidden_in + low_back(product(mixed_heads, w_out))
    norm_two = low(rms_scale(residual) * gain_two)
    gate_pre = low_back(product(norm_two, w_gate))
    upper_pre = low_back(product(norm_two, w_up))
    active = low(jax.nn.silu(gate_pre) * upper_pre)
    return residual + low_back(product(active, w_down))

def piece_shapes():
    row_blocks = D // BLK
    query_cols = QW // BLK
    pair_cols = KW // BLK
    hidden_cols = FH // BLK
    return [(row_blocks, query_cols), (row_blocks, pair_cols), (row_blocks, pair_cols), (query_cols, row_blocks), (row_blocks, hidden_cols), (row_blocks, hidden_cols), (hidden_cols, row_blocks)]

def to_halves(stacked):
    trailing = stacked.shape[1:]
    return jnp.swapaxes(stacked.reshape((N_WIDE, N_NARROW, SLOT_DEV) + trailing), 0, 1).reshape((N_NARROW, SLOTS_H) + trailing)

def from_halves(stacked):
    trailing = stacked.shape[2:]
    return jnp.swapaxes(stacked.reshape((N_NARROW, N_WIDE, SLOT_DEV) + trailing), 0, 1).reshape((SLOTS,) + trailing)

def blocks_to_matrix(blocks, row_blocks, col_blocks):
    return blocks.reshape(row_blocks, col_blocks, BLK, BLK).transpose(0, 2, 1, 3).reshape(row_blocks * BLK, col_blocks * BLK)

def matrix_to_blocks(matrix, row_blocks, col_blocks):
    return matrix.reshape(row_blocks, BLK, col_blocks, BLK).transpose(0, 2, 1, 3).reshape(row_blocks * col_blocks, BLK, BLK)

def adam_small(param_now, gradient, first_now, second_now, rate_here):
    first_new = beta_first * first_now + (1.0 - beta_first) * gradient
    second_new = beta_second * second_now + (1.0 - beta_second) * gradient * gradient
    first_fix = 1.0 - beta_first ** STEP_COUNT
    second_fix = 1.0 - beta_second ** STEP_COUNT
    param_new = param_now - rate_here * (first_new / first_fix) / (jnp.sqrt(second_new / second_fix) + adam_eps)
    return (param_new, first_new, second_new)

def reference(tokens, cotangent, segments, owner_list, masters, first_moment, second_moment, left_basis, right_basis, gains, gain_first, gain_second, biases, bias_first, bias_second):
    shapes = piece_shapes()
    joined_axes = [1, 1, 1, 0, 1, 1, 0]
    halves = to_halves(low(masters))
    pieces_by_half = []
    for half_index in range(N_NARROW):
        stacked = jnp.zeros((NBH + 1, BLK, BLK), jnp.float32).at[owner_list].set(halves[half_index])
        pieces = []
        running = 0
        for row_blocks, col_blocks in shapes:
            pieces.append(blocks_to_matrix(stacked[running:running + row_blocks * col_blocks], row_blocks, col_blocks))
            running += row_blocks * col_blocks
        pieces_by_half.append(pieces)
    matrices = [jnp.concatenate([pieces_by_half[half_index][kind_index] for half_index in range(N_NARROW)], axis=joined_axes[kind_index]) for kind_index in range(7)]
    bias_low = low(biases)
    b_query = jnp.concatenate([bias_low[half_index, :QW] for half_index in range(N_NARROW)])
    b_key = jnp.concatenate([bias_low[half_index, QW:QW + KW] for half_index in range(N_NARROW)])
    b_value = jnp.concatenate([bias_low[half_index, QW + KW:] for half_index in range(N_NARROW)])
    params = tuple(matrices) + (b_query, b_key, b_value, gains[:D], gains[D:])
    hidden_rows = tokens.astype(jnp.float32).reshape(ROWS, ROW, D)
    cotangent_rows = cotangent.astype(jnp.float32).reshape(ROWS, ROW, D)

    def row_step(totals, row_inputs):
        hidden_row, segment_row, cotangent_row = row_inputs

        def forward(params_in, hidden_in):
            return layer_row(params_in, hidden_in, segment_row)
        out_row, pullback = jax.vjp(forward, params, hidden_row)
        grad_params, grad_hidden = pullback(cotangent_row)
        return (jax.tree.map(jnp.add, totals, grad_params), (out_row.astype(jnp.bfloat16), grad_hidden))
    start_totals = jax.tree.map(jnp.zeros_like, params)
    totals, (out_rows, grad_rows) = lax.scan(row_step, start_totals, (hidden_rows, segments, cotangent_rows))
    output = out_rows.reshape(TOKENS, D)
    input_grad = grad_rows.reshape(TOKENS, D)
    slot_grads = []
    for half_index in range(N_NARROW):
        pieces = []
        for kind_index in range(7):
            row_blocks, col_blocks = shapes[kind_index]
            whole = totals[kind_index]
            if joined_axes[kind_index] == 1:
                width_here = col_blocks * BLK
                part_here = whole[:, half_index * width_here:(half_index + 1) * width_here]
            else:
                width_here = row_blocks * BLK
                part_here = whole[half_index * width_here:(half_index + 1) * width_here]
            pieces.append(matrix_to_blocks(part_here, row_blocks, col_blocks))
        pieces.append(jnp.zeros((1, BLK, BLK), jnp.float32))
        slot_grads.append(jnp.concatenate(pieces, axis=0)[owner_list])
    block_grad = from_halves(jnp.stack(slot_grads))
    highest = lax.Precision.HIGHEST
    rotated = jnp.matmul(jnp.swapaxes(left_basis, 1, 2), jnp.matmul(block_grad, right_basis, precision=highest), precision=highest)
    new_first = beta_first * first_moment + (1.0 - beta_first) * rotated
    new_second = beta_second * second_moment + (1.0 - beta_second) * rotated * rotated
    first_fix = 1.0 - beta_first ** STEP_COUNT
    second_fix = 1.0 - beta_second ** STEP_COUNT
    normalized = new_first / first_fix / (jnp.sqrt(new_second / second_fix) + adam_eps)
    update = jnp.matmul(left_basis, jnp.matmul(normalized, jnp.swapaxes(right_basis, 1, 2), precision=highest), precision=highest)
    new_masters = masters - rate_blocks * update
    gain_grad = jnp.concatenate([totals[10], totals[11]])
    new_gains, new_gain_first, new_gain_second = adam_small(gains, gain_grad, gain_first, gain_second, rate_gains)
    bias_grad = jnp.stack([jnp.concatenate([totals[7][half_index * QW:(half_index + 1) * QW], totals[8][half_index * KW:(half_index + 1) * KW], totals[9][half_index * KW:(half_index + 1) * KW]]) for half_index in range(N_NARROW)])
    new_biases, new_bias_first, new_bias_second = adam_small(biases, bias_grad, bias_first, bias_second, rate_small)
    return (output, input_grad, block_grad, new_masters, new_first, new_second, gain_grad, new_gains, new_gain_first, new_gain_second, bias_grad, new_biases, new_bias_first, new_bias_second)
```

```python
import functools

import jax
import jax.numpy as jnp
from jax import lax
from jax.experimental import pallas as pl
from jax.experimental.pallas import tpu as pltpu
from jax.sharding import PartitionSpec as P

D = 1536
FF = 8960
HEADS = 12
KV_HEADS = 2
HEAD_DIM = 128
BLK = 128
STEP_COUNT = 5


beta_first = 0.95
beta_second = 0.95
adam_eps = 1e-08
rate_blocks = 0.03
rate_small = 0.4
rate_gains = 0.6
norm_eps = 1e-06
rope_base = 10000.0
masked_score = -1e30
first_fix = 1.0 - beta_first**STEP_COUNT
second_fix = 1.0 - beta_second**STEP_COUNT
scaling = HEAD_DIM ** (-0.5)

bf16 = jnp.bfloat16
f32 = jnp.float32

NARROW = 2
ROW_BLOCKS = D // BLK
QUERY_COLS = HEADS * HEAD_DIM // NARROW // BLK
PAIR_COLS = KV_HEADS * HEAD_DIM // NARROW // BLK
HIDDEN_COLS = FF // NARROW // BLK
QKV_COLS = QUERY_COLS + 2 * PAIR_COLS
QUERY_WIDTH = QUERY_COLS * BLK
QKV_WIDTH = QKV_COLS * BLK
KEY_BASE = ROW_BLOCKS * QUERY_COLS
VALUE_BASE = KEY_BASE + ROW_BLOCKS * PAIR_COLS
OUT_BASE = VALUE_BASE + ROW_BLOCKS * PAIR_COLS
GATE_BASE = OUT_BASE + QUERY_COLS * ROW_BLOCKS
UP_BASE = GATE_BASE + ROW_BLOCKS * HIDDEN_COLS
DOWN_BASE = UP_BASE + ROW_BLOCKS * HIDDEN_COLS
BLOCK_TOTAL = DOWN_BASE + HIDDEN_COLS * ROW_BLOCKS

TILE_BLOCKS = 5
TILES = HIDDEN_COLS // TILE_BLOCKS
TILE = TILE_BLOCKS * BLK
COLS = 256
ROWS = 64
SMALL_ROWS = 16
VMEM_LIMIT = 60 * 2**20

EARLY = 4
DEPTH = 3
CROSS_LAG = 2
HOP_LAG = 1

VMEM_SPEC = pl.BlockSpec(memory_space=pltpu.VMEM)
SMEM_SPEC = pl.BlockSpec(memory_space=pltpu.SMEM)
ANY_SPEC = pl.BlockSpec(memory_space=pl.ANY)


def spans(total, step):
    return [(begin, min(step, total - begin)) for begin in range(0, total, step)]


def dot_nn(left, right):
    return jnp.dot(left, right, preferred_element_type=f32)


def dot_nt(left, right):
    return lax.dot_general(left, right, (((1,), (1,)), ((), ())), preferred_element_type=f32)


def block_ref(ref, row_block, col_block):
    return ref.at[pl.ds(row_block * BLK, BLK), pl.ds(col_block * BLK, BLK)]


def fetch_piece(rows_ref, weights, target, base, pitch, row_blocks, col_blocks, first_col, sem):
    @pl.loop(0, row_blocks)
    def _(i):
        for j in range(col_blocks):
            pltpu.make_async_copy(
                weights.at[rows_ref[base + i * pitch + j]],
                block_ref(target, i, first_col + j),
                sem,
            ).start()


def store_piece(rows_ref, source, grads, base, pitch, row_blocks, col_blocks, first_col, sem):
    @pl.loop(0, row_blocks)
    def _(i):
        for j in range(col_blocks):
            pltpu.make_async_copy(
                block_ref(source, i, first_col + j),
                grads.at[rows_ref[base + i * pitch + j]],
                sem,
            ).start()


def wait_bytes(ref, sem):
    pltpu.make_async_copy(ref, ref, sem).wait()


def fetch_attention(rows_ref, weights, w_qkv, w_out, sems):
    fetch_piece(rows_ref, weights, w_qkv, 0, QUERY_COLS, ROW_BLOCKS, QUERY_COLS, 0, sems.at[0])
    fetch_piece(rows_ref, weights, w_qkv, KEY_BASE, PAIR_COLS, ROW_BLOCKS, PAIR_COLS, QUERY_COLS, sems.at[0])
    fetch_piece(
        rows_ref, weights, w_qkv, VALUE_BASE, PAIR_COLS, ROW_BLOCKS, PAIR_COLS, QUERY_COLS + PAIR_COLS, sems.at[0]
    )
    fetch_piece(rows_ref, weights, w_out, OUT_BASE, ROW_BLOCKS, QUERY_COLS, ROW_BLOCKS, 0, sems.at[1])


def rms_inverse(values):
    return lax.rsqrt(jnp.mean(values * values, axis=-1, keepdims=True) + norm_eps)


def row_chunks(total, step, run):
    @pl.loop(0, total // step)
    def _(chunk):
        run(pl.ds(pl.multiple_of(chunk * step, step), step))


def small_places(owner, wide_count):
    gain_first = owner * (2 * D // wide_count)
    bias_first = owner * (QKV_WIDTH // wide_count)
    gain_row = min(gain_first // BLK, 2 * D // BLK - 2)
    return (gain_row, gain_first - gain_row * BLK, bias_first // BLK, bias_first % BLK)


def scores_turned(keys, queries, allowed):
    return jnp.where(allowed, dot_nt(keys, queries) * scaling, masked_score)


def attention_forward(
    rows_ref,
    x_ref,
    gain_ref,
    bias_ref,
    cos_ref,
    sin_ref,
    allowed_ref,
    weights,
    part_ref,
    normed_turned_ref,
    qkv_ref,
    mixed_turned_ref,
    log_ref,
    w_qkv,
    w_out,
    normed,
    mixed,
    sems,
):
    fetch_attention(rows_ref, weights, w_qkv, w_out, sems)
    length = x_ref.shape[0]

    def norm_rows(rows):
        values = x_ref[rows, :].astype(f32)
        normed[rows, :] = (values * rms_inverse(values) * gain_ref[...]).astype(bf16)

    row_chunks(length, ROWS, norm_rows)
    for begin, size in spans(D, COLS):
        normed_turned_ref[pl.ds(begin, size), :] = normed[:, pl.ds(begin, size)].T
    wait_bytes(w_qkv, sems.at[0])
    for begin, size in spans(QKV_WIDTH, COLS):
        products = dot_nn(normed[...], w_qkv[:, pl.ds(begin, size)]) + bias_ref[:, pl.ds(begin, size)]
        for offset, width in spans(size, HEAD_DIM):
            head = products[:, offset : offset + width]
            if begin + offset < QUERY_WIDTH + PAIR_COLS * BLK:
                head = head * cos_ref[...] + pltpu.roll(head, HEAD_DIM // 2, 1) * sin_ref[...]
            qkv_ref[:, pl.ds(begin + offset, width)] = head.astype(bf16)
    keys = qkv_ref[:, pl.ds(QUERY_WIDTH, HEAD_DIM)]
    values_turned = qkv_ref[:, pl.ds(QUERY_WIDTH + HEAD_DIM, HEAD_DIM)].T
    for head in range(QUERY_COLS):
        columns = pl.ds(head * HEAD_DIM, HEAD_DIM)
        scores = scores_turned(keys, qkv_ref[:, columns], allowed_ref[...] > 0)
        peak = jnp.max(scores, axis=0, keepdims=True)
        expo = jnp.exp(scores - peak)
        total = jnp.sum(expo, axis=0, keepdims=True)
        log_ref[pl.ds(head, 1), :] = peak + jnp.log(total)
        probs = (expo / total).astype(bf16)
        mixed_head = dot_nn(values_turned, probs).astype(bf16)
        mixed_turned_ref[columns, :] = mixed_head
        mixed[:, columns] = mixed_head.T
    wait_bytes(w_out, sems.at[1])
    for begin, size in spans(D, COLS):
        part_ref[:, pl.ds(begin, size)] = dot_nn(mixed[...], w_out[:, pl.ds(begin, size)]).astype(bf16)


def hidden_grads(
    rows_ref,
    x_ref,
    own_ref,
    other_ref,
    gain_ref,
    cot_ref,
    weights,
    branch_ref,
    grad_ref,
    resid_ref,
    normed_turned_ref,
    gain_part_ref,
    pair_grads,
    active_turned,
    w_pair,
    w_down,
    pair,
    grad_active,
    active,
    turned,
    grads,
    normed,
    branch_sum,
    grad_sum,
    load_sems,
    store_sems,
):
    length = x_ref.shape[0]

    def fetch(tile, slot):
        first = tile * TILE_BLOCKS
        fetch_piece(
            rows_ref, weights, w_down.at[slot], DOWN_BASE + first * ROW_BLOCKS, ROW_BLOCKS, TILE_BLOCKS, ROW_BLOCKS, 0,
            load_sems.at[slot, 1],
        )
        fetch_piece(
            rows_ref, weights, w_pair.at[slot], GATE_BASE + first, HIDDEN_COLS, ROW_BLOCKS, TILE_BLOCKS, 0,
            load_sems.at[slot, 0],
        )
        fetch_piece(
            rows_ref, weights, w_pair.at[slot], UP_BASE + first, HIDDEN_COLS, ROW_BLOCKS, TILE_BLOCKS, TILE_BLOCKS,
            load_sems.at[slot, 0],
        )

    fetch(0, 0)

    def norm_rows(rows):
        values = x_ref[rows, :].astype(f32) + own_ref[rows, :].astype(f32) + other_ref[rows, :].astype(f32)
        resid_ref[rows, :] = values
        normed[rows, :] = (values * rms_inverse(values) * gain_ref[...]).astype(bf16)

    row_chunks(length, ROWS, norm_rows)
    for begin, size in spans(D, COLS):
        normed_turned_ref[pl.ds(begin, size), :] = normed[:, pl.ds(begin, size)].T
    branch_sum[...] = jnp.zeros_like(branch_sum)
    grad_sum[...] = jnp.zeros_like(grad_sum)

    @pl.loop(0, TILES)
    def _(tile):
        slot = lax.rem(tile, 2)

        @pl.when(tile + 1 < TILES)
        def _():
            fetch(tile + 1, 1 - slot)

        wait_bytes(w_down.at[slot], load_sems.at[slot, 1])
        for begin, size in spans(TILE, COLS):
            grad_active[:, pl.ds(begin, size)] = dot_nt(cot_ref[...], w_down[slot, pl.ds(begin, size), :])
        wait_bytes(w_pair.at[slot], load_sems.at[slot, 0])
        for begin, size in spans(2 * TILE, COLS):
            pair[:, pl.ds(begin, size)] = dot_nn(normed[...], w_pair[slot, :, pl.ds(begin, size)])

        @pl.when(tile >= 2)
        def _():
            wait_bytes(turned.at[slot], store_sems.at[slot, 0])
            wait_bytes(grads.at[slot], store_sems.at[slot, 1])

        for begin, size in spans(TILE, BLK):
            gate = pair[:, pl.ds(begin, size)]
            upper = pair[:, pl.ds(TILE + begin, size)]
            grad = grad_active[:, pl.ds(begin, size)]
            sigmoid = jax.nn.sigmoid(gate)
            silu = gate * sigmoid
            active_here = (silu * upper).astype(bf16)
            active[:, pl.ds(begin, size)] = active_here
            turned[slot, pl.ds(begin, size), :] = active_here.T
            grads[slot, :, pl.ds(begin, size)] = (
                grad * upper * sigmoid * (1.0 + gate * (1.0 - sigmoid))
            ).astype(bf16)
            grads[slot, :, pl.ds(TILE + begin, size)] = (grad * silu).astype(bf16)
        pltpu.make_async_copy(turned.at[slot], active_turned.at[tile], store_sems.at[slot, 0]).start()
        pltpu.make_async_copy(grads.at[slot], pair_grads.at[tile], store_sems.at[slot, 1]).start()
        for begin, size in spans(D, COLS):
            columns = pl.ds(begin, size)
            branch_sum[:, columns] += dot_nn(active[...], w_down[slot, :, columns])
            grad_sum[:, columns] += dot_nt(grads[slot], w_pair[slot, columns, :])

    branch_ref[...] = branch_sum[...].astype(bf16)
    grad_ref[...] = grad_sum[...].astype(bf16)
    gain_part_ref[...] = jnp.zeros_like(gain_part_ref)

    def gain_rows(rows):
        values = resid_ref[rows, :]
        gain_part_ref[...] += jnp.sum(grad_sum[rows, :] * values * rms_inverse(values), axis=0, keepdims=True)

    row_chunks(length, ROWS, gain_rows)
    for tile in range(max(TILES - 2, 0), TILES):
        slot = tile % 2
        wait_bytes(turned.at[slot], store_sems.at[slot, 0])
        wait_bytes(grads.at[slot], store_sems.at[slot, 1])


def hidden_weight_grads(
    rows_ref, normed_turned_ref, cot_ref, pair_ref, turned_ref, grads, pair_stage, down_stage, sems
):
    tile = pl.program_id(0)
    slot = lax.rem(tile, 2)

    def drain(which):
        wait_bytes(pair_stage.at[which], sems.at[which, 0])
        wait_bytes(down_stage.at[which], sems.at[which, 1])

    @pl.when(tile >= 2)
    def _():
        drain(slot)

    first = tile * TILE_BLOCKS
    for row_begin, row_size in spans(D, 512):
        for begin, size in spans(2 * TILE, COLS):
            pair_stage[slot, pl.ds(row_begin, row_size), pl.ds(begin, size)] = dot_nn(
                normed_turned_ref[pl.ds(row_begin, row_size), :], pair_ref[0, :, pl.ds(begin, size)]
            ).astype(bf16)
    store_piece(
        rows_ref, pair_stage.at[slot], grads, GATE_BASE + first, HIDDEN_COLS, ROW_BLOCKS, TILE_BLOCKS, 0, sems.at[slot, 0]
    )
    store_piece(
        rows_ref, pair_stage.at[slot], grads, UP_BASE + first, HIDDEN_COLS, ROW_BLOCKS, TILE_BLOCKS, TILE_BLOCKS,
        sems.at[slot, 0],
    )
    for begin, size in spans(D, COLS):
        down_stage[slot, :, pl.ds(begin, size)] = dot_nn(turned_ref[0], cot_ref[:, pl.ds(begin, size)]).astype(bf16)
    store_piece(
        rows_ref, down_stage.at[slot], grads, DOWN_BASE + first * ROW_BLOCKS, ROW_BLOCKS, TILE_BLOCKS, ROW_BLOCKS, 0,
        sems.at[slot, 1],
    )

    @pl.when(tile == TILES - 1)
    def _():
        for which in range(2 if TILES > 1 else 1):
            drain(which)


def attention_backward(
    rows_ref,
    x_ref,
    resid_ref,
    own_ref,
    other_ref,
    cot_ref,
    gain_ref,
    cos_ref,
    sin_ref,
    allowed_ref,
    normed_turned_ref,
    qkv_ref,
    mixed_turned_ref,
    log_ref,
    gain_two_ref,
    weights,
    grads_in,
    grad_resid_ref,
    grad_ref,
    grads,
    w_qkv,
    w_out,
    grad_attention,
    grad_mixed,
    grad_qkv,
    grad_sum,
    gain_part,
    bias_part,
    qkv_stage,
    out_stage,
    small_stage,
    blank,
    load_sems,
    store_sems,
):
    del grads_in
    wide_count = small_stage.shape[0]
    owner_rows = grads.shape[0] // wide_count
    small_stage[...] = jnp.zeros_like(small_stage)
    fetch_attention(rows_ref, weights, w_qkv, w_out, load_sems)
    length = x_ref.shape[0]
    empty_count = rows_ref.shape[0] - BLOCK_TOTAL
    blank[...] = jnp.zeros_like(blank)
    for index in range(empty_count):
        pltpu.make_async_copy(blank.at[index], grads.at[rows_ref[BLOCK_TOTAL + index]], store_sems.at[2]).start()

    def resid_rows(rows):
        values = resid_ref[rows, :]
        inverse = rms_inverse(values)
        normed = values * inverse
        scaled = (own_ref[rows, :].astype(f32) + other_ref[rows, :].astype(f32)) * gain_ref[1:2, :]
        total = cot_ref[rows, :].astype(f32) + inverse * (
            scaled - normed * jnp.mean(scaled * normed, axis=-1, keepdims=True)
        )
        grad_resid_ref[rows, :] = total
        grad_attention[rows, :] = total.astype(bf16)

    row_chunks(length, ROWS, resid_rows)
    wait_bytes(w_out, load_sems.at[1])
    for begin, size in spans(QUERY_WIDTH, COLS):
        grad_mixed[:, pl.ds(begin, size)] = dot_nt(grad_attention[...], w_out[pl.ds(begin, size), :]).astype(bf16)
    keys = qkv_ref[:, pl.ds(QUERY_WIDTH, HEAD_DIM)]
    keys_turned = keys.T
    values = qkv_ref[:, pl.ds(QUERY_WIDTH + HEAD_DIM, HEAD_DIM)]

    def rope_back(vector):
        return vector * cos_ref[...] - pltpu.roll(vector, HEAD_DIM // 2, 1) * sin_ref[...]

    grad_keys = jnp.zeros((length, HEAD_DIM), f32)
    grad_values = jnp.zeros((length, HEAD_DIM), f32)
    for head in range(QUERY_COLS):
        columns = pl.ds(head * HEAD_DIM, HEAD_DIM)
        queries = qkv_ref[:, columns]
        scores = scores_turned(keys, queries, allowed_ref[...] > 0)
        probs = jnp.exp(scores - log_ref[pl.ds(head, 1), :])
        grad_values += dot_nn(probs.astype(bf16), grad_mixed[:, columns])
        grad_probs = dot_nt(values, grad_mixed[:, columns])
        row_dot = jnp.sum(probs * grad_probs, axis=0, keepdims=True)
        grad_scores = (probs * (grad_probs - row_dot)).astype(bf16)
        grad_keys += dot_nn(grad_scores, queries)
        grad_queries = dot_nn(keys_turned, grad_scores).T * scaling
        grad_qkv[:, columns] = rope_back(grad_queries).astype(bf16)
    grad_qkv[:, pl.ds(QUERY_WIDTH, HEAD_DIM)] = rope_back(grad_keys * scaling).astype(bf16)
    grad_qkv[:, pl.ds(QUERY_WIDTH + HEAD_DIM, HEAD_DIM)] = grad_values.astype(bf16)

    for begin, size in spans(D, COLS):
        out_stage[:, pl.ds(begin, size)] = dot_nn(
            mixed_turned_ref[...], grad_attention[:, pl.ds(begin, size)]
        ).astype(bf16)
    store_piece(rows_ref, out_stage, grads, OUT_BASE, ROW_BLOCKS, QUERY_COLS, ROW_BLOCKS, 0, store_sems.at[1])
    for begin, size in spans(QKV_WIDTH, COLS):
        qkv_stage[:, pl.ds(begin, size)] = dot_nn(
            normed_turned_ref[...], grad_qkv[:, pl.ds(begin, size)]
        ).astype(bf16)
    store_piece(rows_ref, qkv_stage, grads, 0, QUERY_COLS, ROW_BLOCKS, QUERY_COLS, 0, store_sems.at[0])
    store_piece(rows_ref, qkv_stage, grads, KEY_BASE, PAIR_COLS, ROW_BLOCKS, PAIR_COLS, QUERY_COLS, store_sems.at[0])
    store_piece(
        rows_ref, qkv_stage, grads, VALUE_BASE, PAIR_COLS, ROW_BLOCKS, PAIR_COLS, QUERY_COLS + PAIR_COLS, store_sems.at[0]
    )
    wait_bytes(w_qkv, load_sems.at[0])
    for begin, size in spans(D, COLS):
        products = dot_nt(grad_qkv[...], w_qkv[pl.ds(begin, size), :])
        grad_sum[:, pl.ds(begin, size)] = products
        grad_ref[:, pl.ds(begin, size)] = products.astype(bf16)
    gain_part[...] = jnp.zeros_like(gain_part)
    bias_part[...] = jnp.zeros_like(bias_part)

    def gain_rows(rows):
        tokens = x_ref[rows, :].astype(f32)
        gain_part[...] += jnp.sum(grad_sum[rows, :] * tokens * rms_inverse(tokens), axis=0, keepdims=True)
        bias_part[...] += jnp.sum(grad_qkv[rows, :].astype(f32), axis=0, keepdims=True)

    row_chunks(length, ROWS, gain_rows)
    for owner in range(wide_count):
        gain_row, bias_row = small_places(owner, wide_count)[::2]
        small_rows = []
        for row in (gain_row, gain_row + 1):
            source = gain_part if row < D // BLK else gain_two_ref
            small_rows.append(source[:, pl.ds(row % (D // BLK) * BLK, BLK)])
        small_rows.append(bias_part[:, pl.ds(bias_row * BLK, BLK)])
        small_rows.append(jnp.zeros((SMALL_ROWS - len(small_rows), BLK), f32))
        small_stage[owner, pl.ds(0, SMALL_ROWS), :] = jnp.concatenate(small_rows, axis=0).astype(bf16)
        pltpu.make_async_copy(
            small_stage.at[owner], grads.at[owner * owner_rows + owner_rows - 1], store_sems.at[3]
        ).start()
    wait_bytes(small_stage, store_sems.at[3])
    wait_bytes(qkv_stage, store_sems.at[0])
    wait_bytes(out_stage, store_sems.at[1])
    if empty_count > 0:
        wait_bytes(blank.at[pl.ds(0, empty_count)], store_sems.at[2])


def soap_update(
    grad_in,
    masters_ref,
    first_ref,
    second_ref,
    left_ref,
    right_ref,
    grad_ref,
    new_masters_ref,
    new_first_ref,
    new_second_ref,
):
    for index in range(masters_ref.shape[0]):
        left = left_ref[index].astype(bf16)
        left_turned = left_ref[index].T.astype(bf16)
        right = right_ref[index].astype(bf16)
        grad_ref[index] = grad_in[index].astype(f32)
        rotated = dot_nn(left_turned, dot_nn(grad_in[index].astype(bf16), right).astype(bf16))
        new_first = beta_first * first_ref[index] + (1.0 - beta_first) * rotated
        new_second = beta_second * second_ref[index] + (1.0 - beta_second) * rotated * rotated
        new_first_ref[index] = new_first
        new_second_ref[index] = new_second
        normalized = new_first / first_fix / (jnp.sqrt(new_second / second_fix) + adam_eps)
        update = dot_nn(left, dot_nt(normalized.astype(bf16), right).astype(bf16))
        new_masters_ref[index] = masters_ref[index] - rate_blocks * update


def params(**options):
    return pltpu.CompilerParams(vmem_limit_bytes=VMEM_LIMIT, **options)


def run_attention_forward(rows, x, gain, bias, cosine, sine, allowed, weights):
    length = x.shape[0]
    shape = jax.ShapeDtypeStruct
    return pl.pallas_call(
        attention_forward,
        out_shape=[
            shape((length, D), bf16),
            shape((D, length), bf16),
            shape((length, QKV_WIDTH), bf16),
            shape((QUERY_WIDTH, length), bf16),
            shape((8, length), f32),
        ],
        in_specs=[SMEM_SPEC] + [VMEM_SPEC] * 6 + [ANY_SPEC],
        out_specs=[VMEM_SPEC] * 5,
        scratch_shapes=[
            pltpu.VMEM((D, QKV_WIDTH), bf16),
            pltpu.VMEM((QUERY_WIDTH, D), bf16),
            pltpu.VMEM((length, D), bf16),
            pltpu.VMEM((length, QUERY_WIDTH), bf16),
            pltpu.SemaphoreType.DMA((2,)),
        ],
        compiler_params=params(),
        name="attention_forward",
    )(rows, x, gain, bias, cosine, sine, allowed, weights)


def run_hidden_grads(rows, x, own, other, gain, cotangent, weights):
    length = x.shape[0]
    shape = jax.ShapeDtypeStruct
    return pl.pallas_call(
        hidden_grads,
        out_shape=[
            shape((length, D), bf16),
            shape((length, D), bf16),
            shape((length, D), f32),
            shape((D, length), bf16),
            shape((1, D), f32),
            shape((TILES, length, 2 * TILE), bf16),
            shape((TILES, TILE, length), bf16),
        ],
        in_specs=[SMEM_SPEC] + [VMEM_SPEC] * 5 + [ANY_SPEC],
        out_specs=[VMEM_SPEC] * 5 + [ANY_SPEC] * 2,
        scratch_shapes=[
            pltpu.VMEM((2, D, 2 * TILE), bf16),
            pltpu.VMEM((2, TILE, D), bf16),
            pltpu.VMEM((length, 2 * TILE), f32),
            pltpu.VMEM((length, TILE), f32),
            pltpu.VMEM((length, TILE), bf16),
            pltpu.VMEM((2, TILE, length), bf16),
            pltpu.VMEM((2, length, 2 * TILE), bf16),
            pltpu.VMEM((length, D), bf16),
            pltpu.VMEM((length, D), f32),
            pltpu.VMEM((length, D), f32),
            pltpu.SemaphoreType.DMA((2, 2)),
            pltpu.SemaphoreType.DMA((2, 2)),
        ],
        compiler_params=params(),
        name="hidden_grads",
    )(rows, x, own, other, gain, cotangent, weights)


def run_hidden_weight_grads(rows, normed_turned, cotangent, pair_grads, active_turned, slots):
    length = cotangent.shape[0]
    flops = 2 * length * 3 * D * TILE * TILES
    bytes_moved = 2 * (3 * D * TILE * TILES + 3 * TILE * TILES * length)
    return pl.pallas_call(
        hidden_weight_grads,
        grid=(TILES,),
        out_shape=jax.ShapeDtypeStruct((slots, BLK, BLK), bf16),
        in_specs=[
            SMEM_SPEC,
            VMEM_SPEC,
            VMEM_SPEC,
            pl.BlockSpec((1, length, 2 * TILE), lambda tile: (tile, 0, 0)),
            pl.BlockSpec((1, TILE, length), lambda tile: (tile, 0, 0)),
        ],
        out_specs=ANY_SPEC,
        scratch_shapes=[
            pltpu.VMEM((2, D, 2 * TILE), bf16),
            pltpu.VMEM((2, TILE, D), bf16),
            pltpu.SemaphoreType.DMA((2, 2)),
        ],
        compiler_params=params(),
        cost_estimate=pl.CostEstimate(flops=flops, bytes_accessed=bytes_moved, transcendentals=0),
        name="hidden_weight_grads",
    )(rows, normed_turned, cotangent, pair_grads, active_turned)


def run_attention_backward(
    rows, x, resid, own, other, cotangent, gains, cosine, sine, allowed, normed_turned, qkv, mixed_turned, log_total,
    gain_two_part, weights, grads, wide_count,
):
    length = x.shape[0]
    shape = jax.ShapeDtypeStruct
    empty_count = max(rows.shape[0] - BLOCK_TOTAL, 1)
    return pl.pallas_call(
        attention_backward,
        out_shape=[
            shape((length, D), f32),
            shape((length, D), bf16),
            shape(grads.shape, bf16),
        ],
        in_specs=[SMEM_SPEC] + [VMEM_SPEC] * 14 + [ANY_SPEC] * 2,
        out_specs=[VMEM_SPEC] * 2 + [ANY_SPEC],
        input_output_aliases={16: 2},
        scratch_shapes=[
            pltpu.VMEM((D, QKV_WIDTH), bf16),
            pltpu.VMEM((QUERY_WIDTH, D), bf16),
            pltpu.VMEM((length, D), bf16),
            pltpu.VMEM((length, QUERY_WIDTH), bf16),
            pltpu.VMEM((length, QKV_WIDTH), bf16),
            pltpu.VMEM((length, D), f32),
            pltpu.VMEM((1, D), f32),
            pltpu.VMEM((1, QKV_WIDTH), f32),
            pltpu.VMEM((D, QKV_WIDTH), bf16),
            pltpu.VMEM((QUERY_WIDTH, D), bf16),
            pltpu.VMEM((wide_count, BLK, BLK), bf16),
            pltpu.VMEM((empty_count, BLK, BLK), bf16),
            pltpu.SemaphoreType.DMA((2,)),
            pltpu.SemaphoreType.DMA((4,)),
        ],
        compiler_params=params(),
        name="attention_backward",
    )(
        rows, x, resid, own, other, cotangent, gains, cosine, sine, allowed, normed_turned, qkv, mixed_turned, log_total,
        gain_two_part, weights, grads,
    )


def run_soap(reduced, masters, first_moment, second_moment, left_basis, right_basis):
    slots = masters.shape[0]
    group = max(size for size in range(1, 11) if slots % size == 0)
    spec = pl.BlockSpec((group, BLK, BLK), lambda step: (step, 0, 0))
    shape = jax.ShapeDtypeStruct(masters.shape, f32)
    return pl.pallas_call(
        soap_update,
        grid=(slots // group,),
        out_shape=[shape] * 4,
        in_specs=[spec] * 6,
        out_specs=[spec] * 4,
        compiler_params=params(),
        name="soap_update",
    )(reduced, masters, first_moment, second_moment, left_basis, right_basis)


def sum_for_owners(
    line, steps, late_steps, grads, out,
    a_in, a_own, a_sum, a_send, a_cross, a_up, a_down,
    b_in, b_own, b_sum, b_keep, b_send, b_cross, b_up, b_down,
    result,
    core_send, core_recv, own_sems, cross_send, cross_recv, up_send, up_recv, down_send, down_recv,
    b_core_send, b_core_recv, b_own_sems, b_cross_send, b_cross_recv, b_up_send, b_up_recv, b_down_send, b_down_recv,
    out_sem, credits,
):
    wide = lax.axis_index("wide")
    narrow = lax.axis_index("narrow")
    z = wide // 4
    x = lax.rem(wide // 2, 2)
    core = lax.rem(wide, 2)
    mesh_id = pl.DeviceIdType.MESH
    core_peer = (wide + 1 - 2 * core, narrow)
    cross_peer = (wide + 2 - 4 * x, narrow)
    upper = (lax.rem(wide + 4, 4 * line), narrow)
    lower = (lax.rem(wide + 4 * line - 4, 4 * line), narrow)
    has_upper = z < line - 1
    has_lower = z > 0
    sum_depth = a_sum.shape[0]
    hop_depth = a_up.shape[0]
    b_sum_depth = b_sum.shape[0]

    barrier = pltpu.get_barrier_semaphore()
    pl.semaphore_signal(barrier, inc=1, device_id=core_peer, device_id_type=mesh_id)
    pl.semaphore_signal(barrier, inc=1, device_id=cross_peer, device_id_type=mesh_id)

    @pl.when(has_upper)
    def _():
        pl.semaphore_signal(barrier, inc=1, device_id=upper, device_id_type=mesh_id)

    @pl.when(has_lower)
    def _():
        pl.semaphore_signal(barrier, inc=1, device_id=lower, device_id_type=mesh_id)

    pl.semaphore_wait(barrier, 2 + has_upper.astype(jnp.int32) + has_lower.astype(jnp.int32))

    def remote(source, target, send_sem, recv_sem, peer):
        return pltpu.make_async_remote_copy(
            src_ref=source, dst_ref=target, send_sem=send_sem, recv_sem=recv_sem, device_id=peer, device_id_type=mesh_id
        )

    def core_copy(step):
        slot = lax.rem(step, DEPTH)
        source = grads.at[:, :, 1 - core, pl.ds(step * EARLY, EARLY)]
        return remote(source, a_in.at[slot], core_send.at[slot], core_recv.at[slot], core_peer)

    def own_copy(step):
        slot = lax.rem(step, DEPTH)
        return pltpu.make_async_copy(
            grads.at[:, :, core, pl.ds(step * EARLY, EARLY)], a_own.at[slot], own_sems.at[slot]
        )

    def b_core_copy(step):
        slot = lax.rem(step, DEPTH)
        source = grads.at[:, :, 1 - core, steps * EARLY + step]
        return remote(source, b_in.at[slot], b_core_send.at[slot], b_core_recv.at[slot], core_peer)

    def b_own_copy(step):
        slot = lax.rem(step, DEPTH)
        return pltpu.make_async_copy(
            grads.at[:, :, core, steps * EARLY + step], b_own.at[slot], b_own_sems.at[slot]
        )

    def cross_copy(step):
        slot = lax.rem(step, DEPTH)
        return remote(a_send.at[slot], a_cross.at[slot], cross_send.at[slot], cross_recv.at[slot], cross_peer)

    def b_cross_copy(step):
        slot = lax.rem(step, DEPTH)
        return remote(b_send.at[slot], b_cross.at[slot], b_cross_send.at[slot], b_cross_recv.at[slot], cross_peer)

    def up_copy(step, target):
        slot = lax.rem(step, hop_depth)
        return remote(
            a_sum.at[lax.rem(step, sum_depth), target], a_up.at[slot, target],
            up_send.at[slot, target], up_recv.at[slot, target], upper,
        )

    def down_copy(step, target):
        slot = lax.rem(step, hop_depth)
        return remote(
            a_sum.at[lax.rem(step, sum_depth), target], a_down.at[slot, target],
            down_send.at[slot, target], down_recv.at[slot, target], lower,
        )

    def b_up_copy(step, target):
        slot = lax.rem(step, hop_depth)
        return remote(
            b_sum.at[lax.rem(step, b_sum_depth), target], b_up.at[slot, target],
            b_up_send.at[slot, target], b_up_recv.at[slot, target], upper,
        )

    def b_down_copy(step, target):
        slot = lax.rem(step, hop_depth)
        return remote(
            b_sum.at[lax.rem(step, b_sum_depth), target], b_down.at[slot, target],
            b_down_send.at[slot, target], b_down_recv.at[slot, target], lower,
        )

    def give(channel, peer):
        pl.semaphore_signal(credits.at[channel], inc=1, device_id=peer, device_id_type=mesh_id)

    def take(channel, step, depth):
        @pl.when(step >= depth)
        def _():
            pl.semaphore_wait(credits.at[channel], 1)

    def feed(step, count, channel, remote_copy, local_copy):
        @pl.when(step < count)
        def _():
            take(channel, step, DEPTH)
            remote_copy(step).start()
            local_copy(step).start()

    for early in range(DEPTH - 1):
        feed(early, steps, 0, core_copy, own_copy)
        feed(early, late_steps, 1, b_core_copy, b_own_copy)

    def active(step, count):
        return (step >= 0) & (step < count)

    far = jnp.maximum(z, line - 1 - z)

    def hops(step_up, step_down, count, sums, depth, ups, downs, up, down, channel):
        @pl.when(active(step_up, count) & has_upper)
        def _():
            take(channel, step_up, hop_depth)
            slot = lax.rem(step_up, hop_depth)
            place = lax.rem(step_up, depth)

            def one(target, _):
                @pl.when(has_lower)
                def _():
                    up(step_up, target).wait_recv()
                    sums[place, target] += ups[slot, target]

                up(step_up, target).start()
                return 0

            lax.fori_loop(z + 1, line, one, 0)

        @pl.when(active(step_down, count) & has_lower)
        def _():
            take(channel + 1, step_down, hop_depth)
            slot = lax.rem(step_down, hop_depth)
            place = lax.rem(step_down, depth)

            def one(target, _):
                @pl.when(has_upper)
                def _():
                    down(step_down, target).wait_recv()
                    sums[place, target] += downs[slot, target]

                down(step_down, target).start()
                return 0

            lax.fori_loop(0, z, one, 0)

    def gather_hops(step, count, sums, depth, ups, downs, up, down, channel, total):
        slot = lax.rem(step, hop_depth)
        total[...] = sums[lax.rem(step, depth), z].astype(f32)

        @pl.when(has_lower)
        def _():
            up(step, z).wait_recv()
            total[...] += ups[slot, z].astype(f32)

            @pl.when(step < count - hop_depth)
            def _():
                give(channel, lower)

        @pl.when(has_upper)
        def _():
            down(step, z).wait_recv()
            total[...] += downs[slot, z].astype(f32)

            @pl.when(step < count - hop_depth)
            def _():
                give(channel + 1, upper)

    def retire(step, count, up, down):
        @pl.when(active(step, count))
        def _():
            def sent_up(target, _):
                up(step, target).wait_send()
                return 0

            def sent_down(target, _):
                down(step, target).wait_send()
                return 0

            lax.fori_loop(z + 1, line, sent_up, 0)
            lax.fori_loop(0, z, sent_down, 0)

    def iteration(step, _):
        feed(step + DEPTH - 1, steps, 0, core_copy, own_copy)
        feed(step + DEPTH - 1, late_steps, 1, b_core_copy, b_own_copy)

        retire(step - CROSS_LAG - HOP_LAG * far - 1, steps, up_copy, down_copy)
        retire(step - HOP_LAG * far - 1, late_steps, b_up_copy, b_down_copy)

        @pl.when(step < steps)
        def _():
            slot = lax.rem(step, DEPTH)
            place = lax.rem(step, sum_depth)
            core_copy(step).wait()
            own_copy(step).wait()

            @pl.when(step >= DEPTH)
            def _():
                cross_copy(step - DEPTH).wait_send()

            for target in range(line):
                a_send[slot, target] = a_own[slot, target, 1 - x] + a_in[slot, target, 1 - x]
            take(2, step, DEPTH)
            cross_copy(step).start()
            for target in range(line):
                a_sum[place, target] = a_own[slot, target, x] + a_in[slot, target, x]

            @pl.when(step < steps - DEPTH)
            def _():
                give(0, core_peer)

        @pl.when(step < late_steps)
        def _():
            slot = lax.rem(step, DEPTH)
            b_core_copy(step).wait()
            b_own_copy(step).wait()
            b_sum[lax.rem(step, b_sum_depth)] = b_own[slot] + b_in[slot]

            @pl.when(step < late_steps - DEPTH)
            def _():
                give(1, core_peer)

        crossed = step - CROSS_LAG

        @pl.when(active(crossed, steps))
        def _():
            slot = lax.rem(crossed, DEPTH)
            place = lax.rem(crossed, sum_depth)
            cross_copy(crossed).wait_recv()
            for target in range(line):
                a_sum[place, target] += a_cross[slot, target]

            @pl.when(crossed < steps - DEPTH)
            def _():
                give(2, cross_peer)

        hops(
            step - HOP_LAG * z, step - HOP_LAG * (line - 1 - z), late_steps, b_sum, b_sum_depth, b_up, b_down,
            b_up_copy, b_down_copy, 6,
        )
        hops(
            crossed - HOP_LAG * z, crossed - HOP_LAG * (line - 1 - z), steps, a_sum, sum_depth, a_up, a_down,
            up_copy, down_copy, 4,
        )

        last = crossed - HOP_LAG * far

        @pl.when(active(last, steps))
        def _():
            total = result.at[pl.ds(last * EARLY, EARLY)]
            gather_hops(last, steps, a_sum, sum_depth, a_up, a_down, up_copy, down_copy, 4, total)
            pltpu.make_async_copy(total, out.at[pl.ds(last * EARLY, EARLY)], out_sem).start()

        arrived = step - HOP_LAG * far

        @pl.when(active(arrived, late_steps))
        def _():
            slot = lax.rem(arrived, DEPTH)

            @pl.when(arrived >= DEPTH)
            def _():
                b_cross_copy(arrived - DEPTH).wait_send()

            gather_hops(
                arrived, late_steps, b_sum, b_sum_depth, b_up, b_down, b_up_copy, b_down_copy, 6, b_keep.at[slot]
            )
            b_send[slot] = b_keep[slot, 1 - x].astype(bf16)
            take(3, arrived, DEPTH)
            b_cross_copy(arrived).start()

        paired = arrived - CROSS_LAG

        @pl.when(active(paired, late_steps))
        def _():
            slot = lax.rem(paired, DEPTH)
            b_cross_copy(paired).wait_recv()
            place = steps * EARLY + paired
            result[place] = b_keep[slot, x] + b_cross[slot].astype(f32)

            @pl.when(paired < late_steps - DEPTH)
            def _():
                give(3, cross_peer)

            pltpu.make_async_copy(result.at[place], out.at[place], out_sem).start()

        return 0

    lag = HOP_LAG * (line - 1) + CROSS_LAG
    lax.fori_loop(0, max(steps, late_steps) + lag + 2, iteration, 0)
    for step in range(max(steps - DEPTH, 0), steps):
        cross_copy(step).wait_send()
    for step in range(max(late_steps - DEPTH, 0), late_steps):
        b_cross_copy(step).wait_send()
    pltpu.make_async_copy(result, out, out_sem).wait()


def run_sum_for_owners(grads, wide_count):
    line = wide_count // 4
    slots, block = grads.shape[0] // wide_count, grads.shape[1:]
    steps = (slots - 1) // (EARLY + 1)
    late_steps = slots - EARLY * steps
    sum_depth = CROSS_LAG + HOP_LAG * (line - 1) + 2
    b_sum_depth = HOP_LAG * (line - 1) + 2
    hop_depth = 2 * HOP_LAG + 2
    dma = pltpu.SemaphoreType.DMA

    def vmem(*shape):
        return pltpu.VMEM(shape + block, bf16)

    def wide_vmem(*shape):
        return pltpu.VMEM(shape + block, f32)

    return pl.pallas_call(
        functools.partial(sum_for_owners, line, steps, late_steps),
        out_shape=jax.ShapeDtypeStruct((slots,) + block, f32),
        in_specs=[ANY_SPEC],
        out_specs=ANY_SPEC,
        scratch_shapes=[
            vmem(DEPTH, line, 2, EARLY),
            vmem(DEPTH, line, 2, EARLY),
            vmem(sum_depth, line, EARLY),
            vmem(DEPTH, line, EARLY),
            vmem(DEPTH, line, EARLY),
            vmem(hop_depth, line, EARLY),
            vmem(hop_depth, line, EARLY),
            vmem(DEPTH, line, 2),
            vmem(DEPTH, line, 2),
            vmem(b_sum_depth, line, 2),
            wide_vmem(DEPTH, 2),
            vmem(DEPTH),
            vmem(DEPTH),
            vmem(hop_depth, line, 2),
            vmem(hop_depth, line, 2),
            wide_vmem(slots),
        ]
        + ([dma((DEPTH,))] * 5 + [dma((hop_depth, line))] * 4) * 2
        + [dma, pltpu.SemaphoreType.REGULAR((8,))],
        compiler_params=params(collective_id=0, has_side_effects=True),
        cost_estimate=pl.CostEstimate(flops=0, bytes_accessed=2 * grads.size * 8, transcendentals=0),
        name="sum_for_owners",
    )(grads.reshape((line, 2, 2, slots) + block))


def rope_tables(segment_row):
    token_index = jnp.arange(segment_row.shape[0], dtype=jnp.int32)
    changed = jnp.concatenate([jnp.ones((1,), dtype=bool), segment_row[1:] != segment_row[:-1]])
    begins = lax.cummax(jnp.where(changed, token_index, jnp.zeros_like(token_index)), axis=0)
    places = (token_index - begins).astype(f32)
    frequency = rope_base ** (-(jnp.arange(HEAD_DIM // 2, dtype=f32) * 2.0) / HEAD_DIM)
    angles = places[:, None] * frequency[None, :]
    cosine = jnp.concatenate([jnp.cos(angles), jnp.cos(angles)], axis=-1)
    sine_signed = jnp.concatenate([-jnp.sin(angles), jnp.sin(angles)], axis=-1)
    return (cosine, sine_signed)


def rms_parts(values):
    inverse = rms_inverse(values)
    return (inverse, values * inverse)


def norm_back(grad_scaled, normed, inverse):
    return inverse * (grad_scaled - normed * jnp.mean(grad_scaled * normed, axis=-1, keepdims=True))


def adam_small(param_now, gradient, first_now, second_now, rate_here):
    first_new = beta_first * first_now + (1.0 - beta_first) * gradient
    second_new = beta_second * second_now + (1.0 - beta_second) * gradient * gradient
    param_new = param_now - rate_here * (first_new / first_fix) / (
        jnp.sqrt(second_new / second_fix) + adam_eps
    )
    return (param_new, first_new, second_new)


def swap_halves(values):
    return lax.ppermute(values, "narrow", [(0, 1), (1, 0)])


def body(
    tokens,
    cotangent,
    segments,
    owner_list,
    masters,
    first_moment,
    second_moment,
    left_basis,
    right_basis,
    gains,
    gain_first,
    gain_second,
    biases,
    bias_first,
    bias_second,
):
    half = lax.axis_index("narrow")
    wide_index = lax.axis_index("wide")
    wide_count = lax.axis_size("wide")
    tokens_here = tokens.shape[0]
    slots_here = masters.shape[0]
    slots_half = owner_list.shape[0]
    own_start = half * tokens_here
    gains_here = gains.shape[0]
    biases_here = biases.shape[1]

    def join_halves(own, other, axis=0):
        return jnp.where(
            half == 0, jnp.concatenate([own, other], axis=axis), jnp.concatenate([other, own], axis=axis)
        )

    gain_pair = join_halves(gains, swap_halves(gains))
    gain_high = lax.reduce_precision(gain_pair, 8, 7)
    small_values = jnp.concatenate([gain_high, gain_pair - gain_high, biases.reshape(-1)]).astype(bf16)
    pair_gains = 2 * gains_here
    small_block = jnp.pad(small_values, (0, BLK * BLK - small_values.shape[0])).reshape(1, BLK, BLK)
    weights = lax.all_gather(
        jnp.concatenate([masters.astype(bf16), small_block], axis=0), "wide", axis=0, tiled=True
    )
    position = jnp.arange(slots_half, dtype=jnp.int32)
    empty = owner_list == BLOCK_TOTAL
    number = jnp.where(empty, BLOCK_TOTAL - 1 + jnp.cumsum(empty.astype(jnp.int32)), owner_list)
    slot_rows = position + position // slots_here
    rows = jnp.zeros((slots_half,), jnp.int32).at[number].set(slot_rows, unique_indices=True)

    segment_row = lax.dynamic_index_in_dim(segments, wide_index, 0, keepdims=False)
    cosine, sine = rope_tables(segment_row)
    token_index = jnp.arange(segment_row.shape[0], dtype=jnp.int32)
    allowed_turned = (
        (segment_row[None, :] == segment_row[:, None]) & (token_index[None, :] >= token_index[:, None])
    ).astype(f32)
    tokens_row = join_halves(tokens, swap_halves(tokens))
    cotangent_row = join_halves(cotangent, swap_halves(cotangent))
    weights, tokens_row, cotangent_row = lax.optimization_barrier((weights, tokens_row, cotangent_row))
    small_all = weights[slots_here :: slots_here + 1].reshape(wide_count, BLK * BLK)[:, : small_values.shape[0]]
    small_all = small_all.astype(f32)
    gain_full = (small_all[:, :pair_gains] + small_all[:, pair_gains : 2 * pair_gains]).reshape(2, D)
    bias_full = small_all[:, 2 * pair_gains :].reshape(1, QKV_WIDTH)

    attention_part, normed_one_turned, qkv, mixed_turned, log_total = run_attention_forward(
        rows, tokens_row, gain_full[0:1], bias_full, cosine, sine, allowed_turned, weights
    )
    attention_other = swap_halves(attention_part)
    branch_part, grad_two_part, resid, normed_two_turned, gain_two_part, pair_grads, active_turned = run_hidden_grads(
        rows, tokens_row, attention_part, attention_other, gain_full[1:2], cotangent_row, weights
    )
    grad_two_other = swap_halves(grad_two_part)
    grads = run_hidden_weight_grads(
        rows, normed_two_turned, cotangent_row, pair_grads, active_turned, wide_count * (slots_here + 1)
    )
    grad_resid, grad_one_part, grads = run_attention_backward(
        rows, tokens_row, resid, grad_two_part, grad_two_other, cotangent_row, gain_full, cosine, sine, allowed_turned,
        normed_one_turned, qkv, mixed_turned, log_total, gain_two_part, weights, grads, wide_count,
    )

    def own_rows(values):
        return lax.dynamic_slice_in_dim(values, own_start, tokens_here, 0)

    def other_rows(values):
        return lax.dynamic_slice_in_dim(values, tokens_here - own_start, tokens_here, 0)

    branch_send, grad_resid = lax.optimization_barrier((other_rows(branch_part), grad_resid))
    branch_other = swap_halves(branch_send)
    output = (
        own_rows(resid) + own_rows(branch_part).astype(f32) + branch_other.astype(f32)
    ).astype(bf16)
    grad_one_other = swap_halves(other_rows(grad_one_part))

    if wide_count == 16:
        reduced = run_sum_for_owners(grads, wide_count)
    else:
        reduced = lax.psum_scatter(grads, "wide", scatter_dimension=0, tiled=True)

    block_grad, new_masters, new_first, new_second = run_soap(
        reduced, masters, first_moment, second_moment, left_basis, right_basis
    )
    places = [small_places(owner, wide_count) for owner in range(wide_count)]
    gain_offset = jnp.asarray([place[1] for place in places], jnp.int32)[wide_index]
    bias_offset = jnp.asarray([place[3] for place in places], jnp.int32)[wide_index]
    small_sums = reduced[slots_here, :8].astype(f32)
    gain_sums = lax.dynamic_slice_in_dim(small_sums[:2].reshape(-1), gain_offset, pair_gains, 0)
    gain_sums = gain_sums.reshape(2, gains_here)
    gain_sums = gain_sums + swap_halves(gain_sums)
    gain_grad = lax.dynamic_index_in_dim(gain_sums, half, 0, keepdims=False)
    bias_grad = lax.dynamic_slice_in_dim(small_sums[2], bias_offset, biases_here, 0).reshape(biases.shape)
    new_gains, new_gain_first, new_gain_second = adam_small(gains, gain_grad, gain_first, gain_second, rate_gains)
    new_biases, new_bias_first, new_bias_second = adam_small(biases, bias_grad, bias_first, bias_second, rate_small)

    inverse_one, normed_one = rms_parts(tokens.astype(f32))
    grad_one = own_rows(grad_one_part).astype(f32) + grad_one_other.astype(f32)
    input_grad = own_rows(grad_resid) + norm_back(grad_one * gain_full[0:1], normed_one, inverse_one)
    return (
        output,
        input_grad,
        block_grad,
        new_masters,
        new_first,
        new_second,
        gain_grad,
        new_gains,
        new_gain_first,
        new_gain_second,
        bias_grad,
        new_biases,
        new_bias_first,
        new_bias_second,
    )


def solution(mesh):
    tokens_spec = P(("wide", "narrow"), None)
    blocks_spec = P(("wide", "narrow"), None, None)
    gains_spec = P(("wide", "narrow"))
    bias_spec = P("narrow", "wide")
    in_specs = (
        (tokens_spec, tokens_spec, P(), P()) + (blocks_spec,) * 5 + (gains_spec,) * 3 + (bias_spec,) * 3
    )
    out_specs = (tokens_spec, tokens_spec) + (blocks_spec,) * 4 + (gains_spec,) * 4 + (bias_spec,) * 4
    return jax.shard_map(body, mesh=mesh, in_specs=in_specs, out_specs=out_specs, check_vma=False)
```

```python
import functools

import jax
import jax.numpy as jnp
from jax import lax
from jax.experimental import pallas as pl
from jax.experimental.pallas import tpu as pltpu
from jax.sharding import PartitionSpec as P

D = 1536
FF = 8960
HEADS = 12
KV_HEADS = 2
HEAD_DIM = 128
BLK = 128
STEP_COUNT = 5


beta_first = 0.95
beta_second = 0.95
adam_eps = 1e-08
rate_blocks = 0.03
rate_small = 0.4
rate_gains = 0.6
norm_eps = 1e-06
rope_base = 10000.0
masked_score = -1e30
first_fix = 1.0 - beta_first**STEP_COUNT
second_fix = 1.0 - beta_second**STEP_COUNT
scaling = HEAD_DIM ** (-0.5)

bf16 = jnp.bfloat16
f32 = jnp.float32

NARROW = 2
ROW_BLOCKS = D // BLK
QUERY_COLS = HEADS * HEAD_DIM // NARROW // BLK
PAIR_COLS = KV_HEADS * HEAD_DIM // NARROW // BLK
HIDDEN_COLS = FF // NARROW // BLK
QKV_COLS = QUERY_COLS + 2 * PAIR_COLS
QUERY_WIDTH = QUERY_COLS * BLK
QKV_WIDTH = QKV_COLS * BLK
KEY_BASE = ROW_BLOCKS * QUERY_COLS
VALUE_BASE = KEY_BASE + ROW_BLOCKS * PAIR_COLS
OUT_BASE = VALUE_BASE + ROW_BLOCKS * PAIR_COLS
GATE_BASE = OUT_BASE + QUERY_COLS * ROW_BLOCKS
UP_BASE = GATE_BASE + ROW_BLOCKS * HIDDEN_COLS
DOWN_BASE = UP_BASE + ROW_BLOCKS * HIDDEN_COLS
BLOCK_TOTAL = DOWN_BASE + HIDDEN_COLS * ROW_BLOCKS

TILE_BLOCKS = 6
TILES = -(-HIDDEN_COLS // TILE_BLOCKS)
LAST_BLOCKS = HIDDEN_COLS - (TILES - 1) * TILE_BLOCKS
TILE = TILE_BLOCKS * BLK
COLS = 256
ROWS = 64
SMALL_ROWS = 16
VMEM_LIMIT = 60 * 2**20

EARLY = 4
DEPTH = 3
CROSS_LAG = 2
HOP_LAG = 1

VMEM_SPEC = pl.BlockSpec(memory_space=pltpu.VMEM)
SMEM_SPEC = pl.BlockSpec(memory_space=pltpu.SMEM)
ANY_SPEC = pl.BlockSpec(memory_space=pl.ANY)


def spans(total, step):
    return [(begin, min(step, total - begin)) for begin in range(0, total, step)]


def dot_nn(left, right):
    return jnp.dot(left, right, preferred_element_type=f32)


def dot_nt(left, right):
    return lax.dot_general(left, right, (((1,), (1,)), ((), ())), preferred_element_type=f32)


def block_ref(ref, row_block, col_block):
    return ref.at[pl.ds(row_block * BLK, BLK), pl.ds(col_block * BLK, BLK)]


def fetch_piece(rows_ref, weights, target, base, pitch, row_blocks, col_blocks, first_col, sem):
    @pl.loop(0, row_blocks)
    def _(i):
        for j in range(col_blocks):
            pltpu.make_async_copy(
                weights.at[rows_ref[base + i * pitch + j]],
                block_ref(target, i, first_col + j),
                sem,
            ).start()


def store_piece(rows_ref, source, grads, base, pitch, row_blocks, col_blocks, first_col, sem):
    @pl.loop(0, row_blocks)
    def _(i):
        for j in range(col_blocks):
            pltpu.make_async_copy(
                block_ref(source, i, first_col + j),
                grads.at[rows_ref[base + i * pitch + j]],
                sem,
            ).start()


def wait_bytes(ref, sem):
    pltpu.make_async_copy(ref, ref, sem).wait()


def fetch_attention(rows_ref, weights, w_qkv, w_out, sems):
    fetch_piece(rows_ref, weights, w_qkv, 0, QUERY_COLS, ROW_BLOCKS, QUERY_COLS, 0, sems.at[0])
    fetch_piece(rows_ref, weights, w_qkv, KEY_BASE, PAIR_COLS, ROW_BLOCKS, PAIR_COLS, QUERY_COLS, sems.at[0])
    fetch_piece(
        rows_ref, weights, w_qkv, VALUE_BASE, PAIR_COLS, ROW_BLOCKS, PAIR_COLS, QUERY_COLS + PAIR_COLS, sems.at[0]
    )
    fetch_piece(rows_ref, weights, w_out, OUT_BASE, ROW_BLOCKS, QUERY_COLS, ROW_BLOCKS, 0, sems.at[1])


def rms_inverse(values):
    return lax.rsqrt(jnp.mean(values * values, axis=-1, keepdims=True) + norm_eps)


def row_chunks(total, step, run):
    @pl.loop(0, total // step)
    def _(chunk):
        run(pl.ds(pl.multiple_of(chunk * step, step), step))


def small_places(owner, wide_count):
    gain_first = owner * (2 * D // wide_count)
    bias_first = owner * (QKV_WIDTH // wide_count)
    gain_row = min(gain_first // BLK, 2 * D // BLK - 2)
    return (gain_row, gain_first - gain_row * BLK, bias_first // BLK, bias_first % BLK)


def scores_turned(keys, queries, allowed):
    return jnp.where(allowed, dot_nt(keys, queries) * scaling, masked_score)


def attention_forward(
    rows_ref,
    x_ref,
    gain_ref,
    bias_ref,
    cos_ref,
    sin_ref,
    allowed_ref,
    weights,
    part_ref,
    normed_turned_ref,
    qkv_ref,
    mixed_turned_ref,
    log_ref,
    w_qkv,
    w_out,
    normed,
    mixed,
    sems,
):
    fetch_attention(rows_ref, weights, w_qkv, w_out, sems)
    length = x_ref.shape[0]

    def norm_rows(rows):
        values = x_ref[rows, :].astype(f32)
        normed[rows, :] = (values * rms_inverse(values) * gain_ref[...]).astype(bf16)

    row_chunks(length, ROWS, norm_rows)
    for begin, size in spans(D, COLS):
        normed_turned_ref[pl.ds(begin, size), :] = normed[:, pl.ds(begin, size)].T
    wait_bytes(w_qkv, sems.at[0])
    for begin, size in spans(QKV_WIDTH, COLS):
        products = dot_nn(normed[...], w_qkv[:, pl.ds(begin, size)]) + bias_ref[:, pl.ds(begin, size)]
        for offset, width in spans(size, HEAD_DIM):
            head = products[:, offset : offset + width]
            if begin + offset < QUERY_WIDTH + PAIR_COLS * BLK:
                head = head * cos_ref[...] + pltpu.roll(head, HEAD_DIM // 2, 1) * sin_ref[...]
            qkv_ref[:, pl.ds(begin + offset, width)] = head.astype(bf16)
    keys = qkv_ref[:, pl.ds(QUERY_WIDTH, HEAD_DIM)]
    values_turned = qkv_ref[:, pl.ds(QUERY_WIDTH + HEAD_DIM, HEAD_DIM)].T
    for head in range(QUERY_COLS):
        columns = pl.ds(head * HEAD_DIM, HEAD_DIM)
        scores = scores_turned(keys, qkv_ref[:, columns], allowed_ref[...] > 0)
        peak = jnp.max(scores, axis=0, keepdims=True)
        expo = jnp.exp(scores - peak)
        total = jnp.sum(expo, axis=0, keepdims=True)
        log_ref[pl.ds(head, 1), :] = peak + jnp.log(total)
        probs = (expo / total).astype(bf16)
        mixed_head = dot_nn(values_turned, probs).astype(bf16)
        mixed_turned_ref[columns, :] = mixed_head
        mixed[:, columns] = mixed_head.T
    wait_bytes(w_out, sems.at[1])
    for begin, size in spans(D, COLS):
        part_ref[:, pl.ds(begin, size)] = dot_nn(mixed[...], w_out[:, pl.ds(begin, size)]).astype(bf16)


def pair_copies(rows_ref, blocks_hbm, pair, sem, column, place, outward=False):
    return [
        block_copy(blocks_hbm.at[rows_ref[base + i * HIDDEN_COLS + column]], block_ref(pair, i, which), sem, outward)
        for i in range(ROW_BLOCKS)
        for base, which in ((GATE_BASE, 2 * place), (UP_BASE, 2 * place + 1))
    ]


def down_copies(rows_ref, blocks_hbm, down, sem, column, place, outward=False):
    return [
        block_copy(blocks_hbm.at[rows_ref[DOWN_BASE + column * ROW_BLOCKS + i]], block_ref(down, place, i), sem, outward)
        for i in range(ROW_BLOCKS)
    ]


def block_copy(in_hbm, in_vmem, sem, outward):
    return pltpu.make_async_copy(*((in_vmem, in_hbm) if outward else (in_hbm, in_vmem)), sem)


def start_all(copies):
    for copy in copies:
        copy.start()


def hidden_column(tile, place):
    return jnp.minimum(tile * TILE_BLOCKS + place, HIDDEN_COLS - 1)


def hidden_tiles(run):
    @pl.loop(0, TILES - 1)
    def _(tile):
        run(tile, lax.rem(tile, 2), TILE_BLOCKS, True)

    run(TILES - 1, (TILES - 1) % 2, LAST_BLOCKS, False)


def active_grads(rows_ref, cot_ref, weights, out, w_down, stage, load_sems, store_sems):
    def fetch(tile, slot, place):
        start_all(
            down_copies(rows_ref, weights, w_down.at[slot], load_sems.at[slot], hidden_column(tile, place), place)
        )

    for place in range(TILE_BLOCKS):
        fetch(0, 0, place)

    def run(tile, slot, blocks, more):
        wait_bytes(w_down.at[slot], load_sems.at[slot])

        @pl.when(tile >= 2)
        def _():
            wait_bytes(stage.at[slot], store_sems.at[slot])

        if more:
            for place in range(TILE_BLOCKS):
                fetch(tile + 1, 1 - slot, place)
        for begin, size in spans(blocks * BLK, COLS):
            stage[slot, :, pl.ds(begin, size)] = dot_nt(cot_ref[...], w_down[slot, pl.ds(begin, size), :])
        pltpu.make_async_copy(stage.at[slot], out.at[tile], store_sems.at[slot]).start()

    hidden_tiles(run)
    for tile in range(max(TILES - 2, 0), TILES):
        wait_bytes(stage.at[tile % 2], store_sems.at[tile % 2])


def hidden_grads(
    rows_ref,
    x_ref,
    own_ref,
    other_ref,
    gain_ref,
    active_grad,
    weights,
    grad_ref,
    resid_ref,
    normed_turned_ref,
    gain_part_ref,
    pair_grads,
    active,
    active_turned,
    w_pair,
    grad_active,
    straight,
    turned,
    grads,
    normed,
    grad_sum,
    load_sems,
    store_sems,
):
    length = x_ref.shape[0]

    def fetch(tile, slot, place):
        start_all(
            pair_copies(rows_ref, weights, w_pair.at[slot], load_sems.at[slot, 0], hidden_column(tile, place), place)
        )

    def load_grad(tile, slot):
        return pltpu.make_async_copy(active_grad.at[tile], grad_active.at[slot], load_sems.at[slot, 1])

    def stores(tile, slot):
        return (
            pltpu.make_async_copy(turned.at[slot], active_turned.at[tile], store_sems.at[slot, 0]),
            pltpu.make_async_copy(grads.at[slot], pair_grads.at[tile], store_sems.at[slot, 1]),
            pltpu.make_async_copy(straight.at[slot], active.at[tile], store_sems.at[slot, 2]),
        )

    for place in range(TILE_BLOCKS):
        fetch(0, 0, place)
    load_grad(0, 0).start()

    def norm_rows(rows):
        values = x_ref[rows, :].astype(f32) + own_ref[rows, :].astype(f32) + other_ref[rows, :].astype(f32)
        resid_ref[rows, :] = values
        normed[rows, :] = (values * rms_inverse(values) * gain_ref[...]).astype(bf16)

    row_chunks(length, ROWS, norm_rows)
    grad_sum[...] = jnp.zeros_like(grad_sum)

    def run(tile, slot, blocks, more):
        wait_bytes(w_pair.at[slot], load_sems.at[slot, 0])
        load_grad(tile, slot).wait()
        if more:
            load_grad(tile + 1, 1 - slot).start()

        @pl.when(tile >= 2)
        def _():
            for copy in stores(tile - 2, slot):
                copy.wait()

        for place in range(blocks):
            columns = pl.ds(place * BLK, BLK)
            pair = dot_nn(normed[...], w_pair[slot, :, pl.ds(2 * place * BLK, 2 * BLK)])
            gate = pair[:, :BLK]
            upper = pair[:, BLK:]
            grad = grad_active[slot, :, columns]
            sigmoid = jax.nn.sigmoid(gate)
            silu = gate * sigmoid
            active_here = (silu * upper).astype(bf16)
            straight[slot, :, columns] = active_here
            turned[slot, columns, :] = active_here.T
            grads[slot, :, pl.ds(2 * place * BLK, BLK)] = (
                grad * upper * sigmoid * (1.0 + gate * (1.0 - sigmoid))
            ).astype(bf16)
            grads[slot, :, pl.ds((2 * place + 1) * BLK, BLK)] = (grad * silu).astype(bf16)
            if more:
                fetch(tile + 1, 1 - slot, place)
        if more:
            for place in range(blocks, TILE_BLOCKS):
                fetch(tile + 1, 1 - slot, place)
        turn = pl.ds(pl.multiple_of(tile * COLS, COLS), COLS)
        normed_turned_ref[turn, :] = normed[:, turn].T
        width = 2 * blocks * BLK
        for begin, size in spans(D, COLS):
            columns = pl.ds(begin, size)
            grad_sum[:, columns] += dot_nt(grads[slot, :, :width], w_pair[slot, columns, :width])
        start_all(stores(tile, slot))

    hidden_tiles(run)
    grad_ref[...] = grad_sum[...].astype(bf16)
    gain_part_ref[...] = jnp.zeros_like(gain_part_ref)

    def gain_rows(rows):
        values = resid_ref[rows, :]
        gain_part_ref[...] += jnp.sum(grad_sum[rows, :] * values * rms_inverse(values), axis=0, keepdims=True)

    row_chunks(length, ROWS, gain_rows)
    for tile in range(max(TILES - 2, 0), TILES):
        for copy in stores(tile, tile % 2):
            copy.wait()


def hidden_weight_grads(
    rows_ref, normed_turned_ref, cot_ref, pair_grads, active, active_turned, weights, branch_ref, grads,
    pair, straight, turned, w_down, branch_sum, pair_stage, down_stage, load_sems, store_sems,
):
    def loads(tile, slot):
        return (
            pltpu.make_async_copy(pair_grads.at[tile], pair.at[slot], load_sems.at[slot, 0]),
            pltpu.make_async_copy(active_turned.at[tile], turned.at[slot], load_sems.at[slot, 1]),
            pltpu.make_async_copy(active.at[tile], straight.at[slot], load_sems.at[slot, 2]),
        )

    def fetch(tile, slot, place):
        start_all(
            down_copies(rows_ref, weights, w_down.at[slot], load_sems.at[slot, 3], hidden_column(tile, place), place)
        )

    def drain(slot, blocks):
        wait_bytes(pair_stage.at[slot, :, pl.ds(0, 2 * blocks * BLK)], store_sems.at[slot, 0])
        wait_bytes(down_stage.at[slot, pl.ds(0, blocks * BLK)], store_sems.at[slot, 1])

    start_all(loads(0, 0))
    for place in range(TILE_BLOCKS):
        fetch(0, 0, place)
    branch_sum[...] = jnp.zeros_like(branch_sum)

    def run(tile, slot, blocks, more):
        for copy in loads(tile, slot):
            copy.wait()
        wait_bytes(w_down.at[slot], load_sems.at[slot, 3])
        if more:
            start_all(loads(tile + 1, 1 - slot))

        @pl.when(tile >= 2)
        def _():
            drain(slot, TILE_BLOCKS)

        width = blocks * BLK
        down = turned[slot, pl.ds(0, width), :]
        for begin, size in spans(D, COLS):
            columns = pl.ds(begin, size)
            down_stage[slot, pl.ds(0, width), columns] = dot_nn(down, cot_ref[:, columns]).astype(bf16)
        for place in range(blocks):
            column = tile * TILE_BLOCKS + place
            start_all(
                down_copies(rows_ref, grads, down_stage.at[slot], store_sems.at[slot, 1], column, place, outward=True)
            )
            columns = pl.ds(2 * place * BLK, 2 * BLK)
            for begin, size in spans(D, 512):
                pair_stage[slot, pl.ds(begin, size), columns] = dot_nn(
                    normed_turned_ref[pl.ds(begin, size), :], pair[slot, :, columns]
                ).astype(bf16)
            start_all(
                pair_copies(rows_ref, grads, pair_stage.at[slot], store_sems.at[slot, 0], column, place, outward=True)
            )
            if more:
                fetch(tile + 1, 1 - slot, place)
        if more:
            for place in range(blocks, TILE_BLOCKS):
                fetch(tile + 1, 1 - slot, place)
        for begin, size in spans(D, COLS):
            columns = pl.ds(begin, size)
            branch_sum[:, columns] += dot_nn(straight[slot, :, :width], w_down[slot, :width, columns])

    hidden_tiles(run)
    branch_ref[...] = branch_sum[...].astype(bf16)
    if TILES > 1:
        drain((TILES - 2) % 2, TILE_BLOCKS)
    drain((TILES - 1) % 2, LAST_BLOCKS)


def attention_backward(
    rows_ref,
    x_ref,
    resid_ref,
    own_ref,
    other_ref,
    cot_ref,
    gain_ref,
    cos_ref,
    sin_ref,
    allowed_ref,
    normed_turned_ref,
    qkv_ref,
    mixed_turned_ref,
    log_ref,
    gain_two_ref,
    weights,
    grads_in,
    grad_resid_ref,
    grad_ref,
    grads,
    w_qkv,
    w_out,
    grad_attention,
    grad_mixed,
    grad_qkv,
    grad_sum,
    gain_part,
    bias_part,
    qkv_stage,
    out_stage,
    small_stage,
    blank,
    load_sems,
    store_sems,
):
    del grads_in
    wide_count = small_stage.shape[0]
    owner_rows = grads.shape[0] // wide_count
    small_stage[...] = jnp.zeros_like(small_stage)
    fetch_attention(rows_ref, weights, w_qkv, w_out, load_sems)
    length = x_ref.shape[0]
    empty_count = rows_ref.shape[0] - BLOCK_TOTAL
    blank[...] = jnp.zeros_like(blank)
    for index in range(empty_count):
        pltpu.make_async_copy(blank.at[index], grads.at[rows_ref[BLOCK_TOTAL + index]], store_sems.at[2]).start()

    def resid_rows(rows):
        values = resid_ref[rows, :]
        inverse = rms_inverse(values)
        normed = values * inverse
        scaled = (own_ref[rows, :].astype(f32) + other_ref[rows, :].astype(f32)) * gain_ref[1:2, :]
        total = cot_ref[rows, :].astype(f32) + inverse * (
            scaled - normed * jnp.mean(scaled * normed, axis=-1, keepdims=True)
        )
        grad_resid_ref[rows, :] = total
        grad_attention[rows, :] = total.astype(bf16)

    row_chunks(length, ROWS, resid_rows)
    wait_bytes(w_out, load_sems.at[1])
    for begin, size in spans(QUERY_WIDTH, COLS):
        grad_mixed[:, pl.ds(begin, size)] = dot_nt(grad_attention[...], w_out[pl.ds(begin, size), :]).astype(bf16)
    keys = qkv_ref[:, pl.ds(QUERY_WIDTH, HEAD_DIM)]
    keys_turned = keys.T
    values = qkv_ref[:, pl.ds(QUERY_WIDTH + HEAD_DIM, HEAD_DIM)]

    def rope_back(vector):
        return vector * cos_ref[...] - pltpu.roll(vector, HEAD_DIM // 2, 1) * sin_ref[...]

    grad_keys = jnp.zeros((length, HEAD_DIM), f32)
    grad_values = jnp.zeros((length, HEAD_DIM), f32)
    for head in range(QUERY_COLS):
        columns = pl.ds(head * HEAD_DIM, HEAD_DIM)
        queries = qkv_ref[:, columns]
        scores = scores_turned(keys, queries, allowed_ref[...] > 0)
        probs = jnp.exp(scores - log_ref[pl.ds(head, 1), :])
        grad_values += dot_nn(probs.astype(bf16), grad_mixed[:, columns])
        grad_probs = dot_nt(values, grad_mixed[:, columns])
        row_dot = jnp.sum(probs * grad_probs, axis=0, keepdims=True)
        grad_scores = (probs * (grad_probs - row_dot)).astype(bf16)
        grad_keys += dot_nn(grad_scores, queries)
        grad_queries = dot_nn(keys_turned, grad_scores).T * scaling
        grad_qkv[:, columns] = rope_back(grad_queries).astype(bf16)
    grad_qkv[:, pl.ds(QUERY_WIDTH, HEAD_DIM)] = rope_back(grad_keys * scaling).astype(bf16)
    grad_qkv[:, pl.ds(QUERY_WIDTH + HEAD_DIM, HEAD_DIM)] = grad_values.astype(bf16)

    for begin, size in spans(D, COLS):
        out_stage[:, pl.ds(begin, size)] = dot_nn(
            mixed_turned_ref[...], grad_attention[:, pl.ds(begin, size)]
        ).astype(bf16)
    store_piece(rows_ref, out_stage, grads, OUT_BASE, ROW_BLOCKS, QUERY_COLS, ROW_BLOCKS, 0, store_sems.at[1])
    for begin, size in spans(QKV_WIDTH, COLS):
        qkv_stage[:, pl.ds(begin, size)] = dot_nn(
            normed_turned_ref[...], grad_qkv[:, pl.ds(begin, size)]
        ).astype(bf16)
    store_piece(rows_ref, qkv_stage, grads, 0, QUERY_COLS, ROW_BLOCKS, QUERY_COLS, 0, store_sems.at[0])
    store_piece(rows_ref, qkv_stage, grads, KEY_BASE, PAIR_COLS, ROW_BLOCKS, PAIR_COLS, QUERY_COLS, store_sems.at[0])
    store_piece(
        rows_ref, qkv_stage, grads, VALUE_BASE, PAIR_COLS, ROW_BLOCKS, PAIR_COLS, QUERY_COLS + PAIR_COLS, store_sems.at[0]
    )
    wait_bytes(w_qkv, load_sems.at[0])
    for begin, size in spans(D, COLS):
        products = dot_nt(grad_qkv[...], w_qkv[pl.ds(begin, size), :])
        grad_sum[:, pl.ds(begin, size)] = products
        grad_ref[:, pl.ds(begin, size)] = products.astype(bf16)
    gain_part[...] = jnp.zeros_like(gain_part)
    bias_part[...] = jnp.zeros_like(bias_part)

    def gain_rows(rows):
        tokens = x_ref[rows, :].astype(f32)
        gain_part[...] += jnp.sum(grad_sum[rows, :] * tokens * rms_inverse(tokens), axis=0, keepdims=True)
        bias_part[...] += jnp.sum(grad_qkv[rows, :].astype(f32), axis=0, keepdims=True)

    row_chunks(length, ROWS, gain_rows)
    for owner in range(wide_count):
        gain_row, bias_row = small_places(owner, wide_count)[::2]
        small_rows = []
        for row in (gain_row, gain_row + 1):
            source = gain_part if row < D // BLK else gain_two_ref
            small_rows.append(source[:, pl.ds(row % (D // BLK) * BLK, BLK)])
        small_rows.append(bias_part[:, pl.ds(bias_row * BLK, BLK)])
        small_rows.append(jnp.zeros((SMALL_ROWS - len(small_rows), BLK), f32))
        small_stage[owner, pl.ds(0, SMALL_ROWS), :] = jnp.concatenate(small_rows, axis=0).astype(bf16)
        pltpu.make_async_copy(
            small_stage.at[owner], grads.at[owner * owner_rows + owner_rows - 1], store_sems.at[3]
        ).start()
    wait_bytes(small_stage, store_sems.at[3])
    wait_bytes(qkv_stage, store_sems.at[0])
    wait_bytes(out_stage, store_sems.at[1])
    if empty_count > 0:
        wait_bytes(blank.at[pl.ds(0, empty_count)], store_sems.at[2])


def soap_update(
    grad_in,
    masters_ref,
    first_ref,
    second_ref,
    left_ref,
    right_ref,
    grad_ref,
    new_masters_ref,
    new_first_ref,
    new_second_ref,
):
    blocks = range(masters_ref.shape[0])
    rights = [right_ref[index].astype(bf16) for index in blocks]
    products = [dot_nn(grad_in[index].astype(bf16), rights[index]).astype(bf16) for index in blocks]
    lefts = [left_ref[index].astype(bf16) for index in blocks]
    rotated_blocks = [dot_nn(lefts[index].T, products[index]) for index in blocks]
    normalized = []
    for index in blocks:
        rotated = rotated_blocks[index]
        grad_ref[index] = grad_in[index]
        new_first = beta_first * first_ref[index] + (1.0 - beta_first) * rotated
        new_second = beta_second * second_ref[index] + (1.0 - beta_second) * rotated * rotated
        new_first_ref[index] = new_first
        new_second_ref[index] = new_second
        normalized.append(
            (new_first / first_fix / (jnp.sqrt(new_second / second_fix) + adam_eps)).astype(bf16)
        )
    products = [dot_nt(normalized[index], rights[index]).astype(bf16) for index in blocks]
    for index in blocks:
        new_masters_ref[index] = masters_ref[index] - rate_blocks * dot_nn(lefts[index], products[index])


def params(**options):
    return pltpu.CompilerParams(vmem_limit_bytes=VMEM_LIMIT, **options)


def run_attention_forward(rows, x, gain, bias, cosine, sine, allowed, weights):
    length = x.shape[0]
    shape = jax.ShapeDtypeStruct
    return pl.pallas_call(
        attention_forward,
        out_shape=[
            shape((length, D), bf16),
            shape((D, length), bf16),
            shape((length, QKV_WIDTH), bf16),
            shape((QUERY_WIDTH, length), bf16),
            shape((8, length), f32),
        ],
        in_specs=[SMEM_SPEC] + [VMEM_SPEC] * 6 + [ANY_SPEC],
        out_specs=[VMEM_SPEC] * 5,
        scratch_shapes=[
            pltpu.VMEM((D, QKV_WIDTH), bf16),
            pltpu.VMEM((QUERY_WIDTH, D), bf16),
            pltpu.VMEM((length, D), bf16),
            pltpu.VMEM((length, QUERY_WIDTH), bf16),
            pltpu.SemaphoreType.DMA((2,)),
        ],
        compiler_params=params(),
        name="attention_forward",
    )(rows, x, gain, bias, cosine, sine, allowed, weights)


def hidden_cost(length, products, bytes_moved):
    return pl.CostEstimate(
        flops=2 * products * length * D * TILE * TILES, bytes_accessed=bytes_moved, transcendentals=0
    )


def run_active_grads(rows, cotangent, weights):
    length = cotangent.shape[0]
    return pl.pallas_call(
        active_grads,
        out_shape=jax.ShapeDtypeStruct((TILES, length, TILE), f32),
        in_specs=[SMEM_SPEC, VMEM_SPEC, ANY_SPEC],
        out_specs=ANY_SPEC,
        scratch_shapes=[
            pltpu.VMEM((2, TILE, D), bf16),
            pltpu.VMEM((2, length, TILE), f32),
            pltpu.SemaphoreType.DMA((2,)),
            pltpu.SemaphoreType.DMA((2,)),
        ],
        compiler_params=params(),
        cost_estimate=hidden_cost(length, 1, TILES * TILE * (2 * D + 4 * length)),
        name="active_grads",
    )(rows, cotangent, weights)


def run_hidden_grads(rows, x, own, other, gain, active_grad, weights):
    length = x.shape[0]
    shape = jax.ShapeDtypeStruct
    return pl.pallas_call(
        hidden_grads,
        out_shape=[
            shape((length, D), bf16),
            shape((length, D), f32),
            shape((D, length), bf16),
            shape((1, D), f32),
            shape((TILES, length, 2 * TILE), bf16),
            shape((TILES, length, TILE), bf16),
            shape((TILES, TILE, length), bf16),
        ],
        in_specs=[SMEM_SPEC] + [VMEM_SPEC] * 4 + [ANY_SPEC] * 2,
        out_specs=[VMEM_SPEC] * 4 + [ANY_SPEC] * 3,
        scratch_shapes=[
            pltpu.VMEM((2, D, 2 * TILE), bf16),
            pltpu.VMEM((2, length, TILE), f32),
            pltpu.VMEM((2, length, TILE), bf16),
            pltpu.VMEM((2, TILE, length), bf16),
            pltpu.VMEM((2, length, 2 * TILE), bf16),
            pltpu.VMEM((length, D), bf16),
            pltpu.VMEM((length, D), f32),
            pltpu.SemaphoreType.DMA((2, 2)),
            pltpu.SemaphoreType.DMA((2, 3)),
        ],
        compiler_params=params(),
        cost_estimate=hidden_cost(length, 4, 2 * TILES * TILE * (2 * D + 6 * length)),
        name="hidden_grads",
    )(rows, x, own, other, gain, active_grad, weights)


def run_hidden_weight_grads(
    rows, normed_turned, cotangent, pair_grads, active, active_turned, weights, slots
):
    length = cotangent.shape[0]
    shape = jax.ShapeDtypeStruct
    return pl.pallas_call(
        hidden_weight_grads,
        out_shape=[shape((length, D), bf16), shape((slots, BLK, BLK), bf16)],
        in_specs=[SMEM_SPEC] + [VMEM_SPEC] * 2 + [ANY_SPEC] * 4,
        out_specs=[VMEM_SPEC, ANY_SPEC],
        scratch_shapes=[
            pltpu.VMEM((2, length, 2 * TILE), bf16),
            pltpu.VMEM((2, length, TILE), bf16),
            pltpu.VMEM((2, TILE, length), bf16),
            pltpu.VMEM((2, TILE, D), bf16),
            pltpu.VMEM((length, D), f32),
            pltpu.VMEM((2, D, 2 * TILE), bf16),
            pltpu.VMEM((2, TILE, D), bf16),
            pltpu.SemaphoreType.DMA((2, 4)),
            pltpu.SemaphoreType.DMA((2, 2)),
        ],
        compiler_params=params(),
        cost_estimate=hidden_cost(length, 4, 2 * TILES * TILE * (4 * D + 4 * length)),
        name="hidden_weight_grads",
    )(rows, normed_turned, cotangent, pair_grads, active, active_turned, weights)


def run_attention_backward(
    rows, x, resid, own, other, cotangent, gains, cosine, sine, allowed, normed_turned, qkv, mixed_turned, log_total,
    gain_two_part, weights, grads, wide_count,
):
    length = x.shape[0]
    shape = jax.ShapeDtypeStruct
    empty_count = max(rows.shape[0] - BLOCK_TOTAL, 1)
    return pl.pallas_call(
        attention_backward,
        out_shape=[
            shape((length, D), f32),
            shape((length, D), bf16),
            shape(grads.shape, bf16),
        ],
        in_specs=[SMEM_SPEC] + [VMEM_SPEC] * 14 + [ANY_SPEC] * 2,
        out_specs=[VMEM_SPEC] * 2 + [ANY_SPEC],
        input_output_aliases={16: 2},
        scratch_shapes=[
            pltpu.VMEM((D, QKV_WIDTH), bf16),
            pltpu.VMEM((QUERY_WIDTH, D), bf16),
            pltpu.VMEM((length, D), bf16),
            pltpu.VMEM((length, QUERY_WIDTH), bf16),
            pltpu.VMEM((length, QKV_WIDTH), bf16),
            pltpu.VMEM((length, D), f32),
            pltpu.VMEM((1, D), f32),
            pltpu.VMEM((1, QKV_WIDTH), f32),
            pltpu.VMEM((D, QKV_WIDTH), bf16),
            pltpu.VMEM((QUERY_WIDTH, D), bf16),
            pltpu.VMEM((wide_count, BLK, BLK), bf16),
            pltpu.VMEM((empty_count, BLK, BLK), bf16),
            pltpu.SemaphoreType.DMA((2,)),
            pltpu.SemaphoreType.DMA((4,)),
        ],
        compiler_params=params(),
        name="attention_backward",
    )(
        rows, x, resid, own, other, cotangent, gains, cosine, sine, allowed, normed_turned, qkv, mixed_turned, log_total,
        gain_two_part, weights, grads,
    )


def run_soap(reduced, masters, first_moment, second_moment, left_basis, right_basis):
    slots = masters.shape[0]
    group = max(size for size in range(1, 11) if slots % size == 0)
    spec = pl.BlockSpec((group, BLK, BLK), lambda step: (step, 0, 0))
    shape = jax.ShapeDtypeStruct(masters.shape, f32)
    return pl.pallas_call(
        soap_update,
        grid=(slots // group,),
        out_shape=[shape] * 4,
        in_specs=[spec] * 6,
        out_specs=[spec] * 4,
        compiler_params=params(),
        name="soap_update",
    )(reduced, masters, first_moment, second_moment, left_basis, right_basis)


def sum_for_owners(
    line, steps, late_steps, grads, out,
    a_in, a_own, a_sum, a_send, a_cross, a_up, a_down,
    b_in, b_own, b_sum, b_keep, b_send, b_cross, b_up, b_down,
    result,
    core_send, core_recv, own_sems, cross_send, cross_recv, up_send, up_recv, down_send, down_recv,
    b_core_send, b_core_recv, b_own_sems, b_cross_send, b_cross_recv, b_up_send, b_up_recv, b_down_send, b_down_recv,
    out_sem, credits,
):
    wide = lax.axis_index("wide")
    narrow = lax.axis_index("narrow")
    z = wide // 4
    x = lax.rem(wide // 2, 2)
    core = lax.rem(wide, 2)
    mesh_id = pl.DeviceIdType.MESH
    core_peer = (wide + 1 - 2 * core, narrow)
    cross_peer = (wide + 2 - 4 * x, narrow)
    upper = (lax.rem(wide + 4, 4 * line), narrow)
    lower = (lax.rem(wide + 4 * line - 4, 4 * line), narrow)
    has_upper = z < line - 1
    has_lower = z > 0
    sum_depth = a_sum.shape[0]
    hop_depth = a_up.shape[0]
    b_sum_depth = b_sum.shape[0]

    barrier = pltpu.get_barrier_semaphore()
    pl.semaphore_signal(barrier, inc=1, device_id=core_peer, device_id_type=mesh_id)
    pl.semaphore_signal(barrier, inc=1, device_id=cross_peer, device_id_type=mesh_id)

    @pl.when(has_upper)
    def _():
        pl.semaphore_signal(barrier, inc=1, device_id=upper, device_id_type=mesh_id)

    @pl.when(has_lower)
    def _():
        pl.semaphore_signal(barrier, inc=1, device_id=lower, device_id_type=mesh_id)

    pl.semaphore_wait(barrier, 2 + has_upper.astype(jnp.int32) + has_lower.astype(jnp.int32))

    def remote(source, target, send_sem, recv_sem, peer):
        return pltpu.make_async_remote_copy(
            src_ref=source, dst_ref=target, send_sem=send_sem, recv_sem=recv_sem, device_id=peer, device_id_type=mesh_id
        )

    def core_copy(step):
        slot = lax.rem(step, DEPTH)
        source = grads.at[:, :, 1 - core, pl.ds(step * EARLY, EARLY)]
        return remote(source, a_in.at[slot], core_send.at[slot], core_recv.at[slot], core_peer)

    def own_copy(step):
        slot = lax.rem(step, DEPTH)
        return pltpu.make_async_copy(
            grads.at[:, :, core, pl.ds(step * EARLY, EARLY)], a_own.at[slot], own_sems.at[slot]
        )

    def b_core_copy(step):
        slot = lax.rem(step, DEPTH)
        source = grads.at[:, :, 1 - core, steps * EARLY + step]
        return remote(source, b_in.at[slot], b_core_send.at[slot], b_core_recv.at[slot], core_peer)

    def b_own_copy(step):
        slot = lax.rem(step, DEPTH)
        return pltpu.make_async_copy(
            grads.at[:, :, core, steps * EARLY + step], b_own.at[slot], b_own_sems.at[slot]
        )

    def cross_copy(step):
        slot = lax.rem(step, DEPTH)
        return remote(a_send.at[slot], a_cross.at[slot], cross_send.at[slot], cross_recv.at[slot], cross_peer)

    def b_cross_copy(step):
        slot = lax.rem(step, DEPTH)
        return remote(b_send.at[slot], b_cross.at[slot], b_cross_send.at[slot], b_cross_recv.at[slot], cross_peer)

    def up_copy(step, target):
        slot = lax.rem(step, hop_depth)
        return remote(
            a_sum.at[lax.rem(step, sum_depth), target], a_up.at[slot, target],
            up_send.at[slot, target], up_recv.at[slot, target], upper,
        )

    def down_copy(step, target):
        slot = lax.rem(step, hop_depth)
        return remote(
            a_sum.at[lax.rem(step, sum_depth), target], a_down.at[slot, target],
            down_send.at[slot, target], down_recv.at[slot, target], lower,
        )

    def b_up_copy(step, target):
        slot = lax.rem(step, hop_depth)
        return remote(
            b_sum.at[lax.rem(step, b_sum_depth), target], b_up.at[slot, target],
            b_up_send.at[slot, target], b_up_recv.at[slot, target], upper,
        )

    def b_down_copy(step, target):
        slot = lax.rem(step, hop_depth)
        return remote(
            b_sum.at[lax.rem(step, b_sum_depth), target], b_down.at[slot, target],
            b_down_send.at[slot, target], b_down_recv.at[slot, target], lower,
        )

    def give(channel, peer):
        pl.semaphore_signal(credits.at[channel], inc=1, device_id=peer, device_id_type=mesh_id)

    def take(channel, step, depth):
        @pl.when(step >= depth)
        def _():
            pl.semaphore_wait(credits.at[channel], 1)

    def feed(step, count, channel, remote_copy, local_copy):
        @pl.when(step < count)
        def _():
            take(channel, step, DEPTH)
            remote_copy(step).start()
            local_copy(step).start()

    for early in range(DEPTH - 1):
        feed(early, steps, 0, core_copy, own_copy)
        feed(early, late_steps, 1, b_core_copy, b_own_copy)

    def active(step, count):
        return (step >= 0) & (step < count)

    far = jnp.maximum(z, line - 1 - z)

    def hops(step_up, step_down, count, sums, depth, ups, downs, up, down, channel):
        @pl.when(active(step_up, count) & has_upper)
        def _():
            take(channel, step_up, hop_depth)
            slot = lax.rem(step_up, hop_depth)
            place = lax.rem(step_up, depth)

            def one(target, _):
                @pl.when(has_lower)
                def _():
                    up(step_up, target).wait_recv()
                    sums[place, target] += ups[slot, target]

                up(step_up, target).start()
                return 0

            lax.fori_loop(z + 1, line, one, 0)

        @pl.when(active(step_down, count) & has_lower)
        def _():
            take(channel + 1, step_down, hop_depth)
            slot = lax.rem(step_down, hop_depth)
            place = lax.rem(step_down, depth)

            def one(target, _):
                @pl.when(has_upper)
                def _():
                    down(step_down, target).wait_recv()
                    sums[place, target] += downs[slot, target]

                down(step_down, target).start()
                return 0

            lax.fori_loop(0, z, one, 0)

    def gather_hops(step, count, sums, depth, ups, downs, up, down, channel, total):
        slot = lax.rem(step, hop_depth)
        total[...] = sums[lax.rem(step, depth), z].astype(f32)

        @pl.when(has_lower)
        def _():
            up(step, z).wait_recv()
            total[...] += ups[slot, z].astype(f32)

            @pl.when(step < count - hop_depth)
            def _():
                give(channel, lower)

        @pl.when(has_upper)
        def _():
            down(step, z).wait_recv()
            total[...] += downs[slot, z].astype(f32)

            @pl.when(step < count - hop_depth)
            def _():
                give(channel + 1, upper)

    def retire(step, count, up, down):
        @pl.when(active(step, count))
        def _():
            def sent_up(target, _):
                up(step, target).wait_send()
                return 0

            def sent_down(target, _):
                down(step, target).wait_send()
                return 0

            lax.fori_loop(z + 1, line, sent_up, 0)
            lax.fori_loop(0, z, sent_down, 0)

    def iteration(step, _):
        feed(step + DEPTH - 1, steps, 0, core_copy, own_copy)
        feed(step + DEPTH - 1, late_steps, 1, b_core_copy, b_own_copy)

        retire(step - CROSS_LAG - HOP_LAG * far - 1, steps, up_copy, down_copy)
        retire(step - HOP_LAG * far - 1, late_steps, b_up_copy, b_down_copy)

        @pl.when(step < steps)
        def _():
            slot = lax.rem(step, DEPTH)
            place = lax.rem(step, sum_depth)
            core_copy(step).wait()
            own_copy(step).wait()

            @pl.when(step >= DEPTH)
            def _():
                cross_copy(step - DEPTH).wait_send()

            for target in range(line):
                a_send[slot, target] = a_own[slot, target, 1 - x] + a_in[slot, target, 1 - x]
            take(2, step, DEPTH)
            cross_copy(step).start()
            for target in range(line):
                a_sum[place, target] = a_own[slot, target, x] + a_in[slot, target, x]

            @pl.when(step < steps - DEPTH)
            def _():
                give(0, core_peer)

        @pl.when(step < late_steps)
        def _():
            slot = lax.rem(step, DEPTH)
            b_core_copy(step).wait()
            b_own_copy(step).wait()
            b_sum[lax.rem(step, b_sum_depth)] = b_own[slot] + b_in[slot]

            @pl.when(step < late_steps - DEPTH)
            def _():
                give(1, core_peer)

        crossed = step - CROSS_LAG

        @pl.when(active(crossed, steps))
        def _():
            slot = lax.rem(crossed, DEPTH)
            place = lax.rem(crossed, sum_depth)
            cross_copy(crossed).wait_recv()
            for target in range(line):
                a_sum[place, target] += a_cross[slot, target]

            @pl.when(crossed < steps - DEPTH)
            def _():
                give(2, cross_peer)

        hops(
            step - HOP_LAG * z, step - HOP_LAG * (line - 1 - z), late_steps, b_sum, b_sum_depth, b_up, b_down,
            b_up_copy, b_down_copy, 6,
        )
        hops(
            crossed - HOP_LAG * z, crossed - HOP_LAG * (line - 1 - z), steps, a_sum, sum_depth, a_up, a_down,
            up_copy, down_copy, 4,
        )

        last = crossed - HOP_LAG * far

        @pl.when(active(last, steps))
        def _():
            total = result.at[pl.ds(last * EARLY, EARLY)]
            gather_hops(last, steps, a_sum, sum_depth, a_up, a_down, up_copy, down_copy, 4, total)
            pltpu.make_async_copy(total, out.at[pl.ds(last * EARLY, EARLY)], out_sem).start()

        arrived = step - HOP_LAG * far

        @pl.when(active(arrived, late_steps))
        def _():
            slot = lax.rem(arrived, DEPTH)

            @pl.when(arrived >= DEPTH)
            def _():
                b_cross_copy(arrived - DEPTH).wait_send()

            gather_hops(
                arrived, late_steps, b_sum, b_sum_depth, b_up, b_down, b_up_copy, b_down_copy, 6, b_keep.at[slot]
            )
            b_send[slot] = b_keep[slot, 1 - x].astype(bf16)
            take(3, arrived, DEPTH)
            b_cross_copy(arrived).start()

        paired = arrived - CROSS_LAG

        @pl.when(active(paired, late_steps))
        def _():
            slot = lax.rem(paired, DEPTH)
            b_cross_copy(paired).wait_recv()
            place = steps * EARLY + paired
            result[place] = b_keep[slot, x] + b_cross[slot].astype(f32)

            @pl.when(paired < late_steps - DEPTH)
            def _():
                give(3, cross_peer)

            pltpu.make_async_copy(result.at[place], out.at[place], out_sem).start()

        return 0

    lag = HOP_LAG * (line - 1) + CROSS_LAG
    lax.fori_loop(0, max(steps, late_steps) + lag + 2, iteration, 0)
    for step in range(max(steps - DEPTH, 0), steps):
        cross_copy(step).wait_send()
    for step in range(max(late_steps - DEPTH, 0), late_steps):
        b_cross_copy(step).wait_send()
    pltpu.make_async_copy(result, out, out_sem).wait()


def run_sum_for_owners(grads, wide_count):
    line = wide_count // 4
    slots, block = grads.shape[0] // wide_count, grads.shape[1:]
    steps = (slots - 1) // (EARLY + 1)
    late_steps = slots - EARLY * steps
    sum_depth = CROSS_LAG + HOP_LAG * (line - 1) + 2
    b_sum_depth = HOP_LAG * (line - 1) + 2
    hop_depth = 2 * HOP_LAG + 2
    dma = pltpu.SemaphoreType.DMA

    def vmem(*shape):
        return pltpu.VMEM(shape + block, bf16)

    def wide_vmem(*shape):
        return pltpu.VMEM(shape + block, f32)

    return pl.pallas_call(
        functools.partial(sum_for_owners, line, steps, late_steps),
        out_shape=jax.ShapeDtypeStruct((slots,) + block, f32),
        in_specs=[ANY_SPEC],
        out_specs=ANY_SPEC,
        scratch_shapes=[
            vmem(DEPTH, line, 2, EARLY),
            vmem(DEPTH, line, 2, EARLY),
            vmem(sum_depth, line, EARLY),
            vmem(DEPTH, line, EARLY),
            vmem(DEPTH, line, EARLY),
            vmem(hop_depth, line, EARLY),
            vmem(hop_depth, line, EARLY),
            vmem(DEPTH, line, 2),
            vmem(DEPTH, line, 2),
            vmem(b_sum_depth, line, 2),
            wide_vmem(DEPTH, 2),
            vmem(DEPTH),
            vmem(DEPTH),
            vmem(hop_depth, line, 2),
            vmem(hop_depth, line, 2),
            wide_vmem(slots),
        ]
        + ([dma((DEPTH,))] * 5 + [dma((hop_depth, line))] * 4) * 2
        + [dma, pltpu.SemaphoreType.REGULAR((8,))],
        compiler_params=params(collective_id=0, has_side_effects=True),
        cost_estimate=pl.CostEstimate(flops=0, bytes_accessed=2 * grads.size * 8, transcendentals=0),
        name="sum_for_owners",
    )(grads.reshape((line, 2, 2, slots) + block))


def rope_tables(segment_row):
    token_index = jnp.arange(segment_row.shape[0], dtype=jnp.int32)
    changed = jnp.concatenate([jnp.ones((1,), dtype=bool), segment_row[1:] != segment_row[:-1]])
    begins = lax.cummax(jnp.where(changed, token_index, jnp.zeros_like(token_index)), axis=0)
    places = (token_index - begins).astype(f32)
    frequency = rope_base ** (-(jnp.arange(HEAD_DIM // 2, dtype=f32) * 2.0) / HEAD_DIM)
    angles = places[:, None] * frequency[None, :]
    cosine = jnp.concatenate([jnp.cos(angles), jnp.cos(angles)], axis=-1)
    sine_signed = jnp.concatenate([-jnp.sin(angles), jnp.sin(angles)], axis=-1)
    return (cosine, sine_signed)


def rms_parts(values):
    inverse = rms_inverse(values)
    return (inverse, values * inverse)


def norm_back(grad_scaled, normed, inverse):
    return inverse * (grad_scaled - normed * jnp.mean(grad_scaled * normed, axis=-1, keepdims=True))


def adam_small(param_now, gradient, first_now, second_now, rate_here):
    first_new = beta_first * first_now + (1.0 - beta_first) * gradient
    second_new = beta_second * second_now + (1.0 - beta_second) * gradient * gradient
    param_new = param_now - rate_here * (first_new / first_fix) / (
        jnp.sqrt(second_new / second_fix) + adam_eps
    )
    return (param_new, first_new, second_new)


def swap_halves(values):
    return lax.ppermute(values, "narrow", [(0, 1), (1, 0)])


def body(
    tokens,
    cotangent,
    segments,
    owner_list,
    masters,
    first_moment,
    second_moment,
    left_basis,
    right_basis,
    gains,
    gain_first,
    gain_second,
    biases,
    bias_first,
    bias_second,
):
    half = lax.axis_index("narrow")
    wide_index = lax.axis_index("wide")
    wide_count = lax.axis_size("wide")
    tokens_here = tokens.shape[0]
    slots_here = masters.shape[0]
    slots_half = owner_list.shape[0]
    own_start = half * tokens_here
    gains_here = gains.shape[0]
    biases_here = biases.shape[1]

    def join_halves(own, other, axis=0):
        return jnp.where(
            half == 0, jnp.concatenate([own, other], axis=axis), jnp.concatenate([other, own], axis=axis)
        )

    gain_pair = join_halves(gains, swap_halves(gains))
    gain_high = lax.reduce_precision(gain_pair, 8, 7)
    small_values = jnp.concatenate([gain_high, gain_pair - gain_high, biases.reshape(-1)]).astype(bf16)
    pair_gains = 2 * gains_here
    small_block = jnp.pad(small_values, (0, BLK * BLK - small_values.shape[0])).reshape(1, BLK, BLK)
    weights = lax.all_gather(
        jnp.concatenate([masters.astype(bf16), small_block], axis=0), "wide", axis=0, tiled=True
    )
    position = jnp.arange(slots_half, dtype=jnp.int32)
    empty = owner_list == BLOCK_TOTAL
    number = jnp.where(empty, BLOCK_TOTAL - 1 + jnp.cumsum(empty.astype(jnp.int32)), owner_list)
    slot_rows = position + position // slots_here
    rows = jnp.zeros((slots_half,), jnp.int32).at[number].set(slot_rows, unique_indices=True)

    segment_row = lax.dynamic_index_in_dim(segments, wide_index, 0, keepdims=False)
    cosine, sine = rope_tables(segment_row)
    token_index = jnp.arange(segment_row.shape[0], dtype=jnp.int32)
    allowed_turned = (
        (segment_row[None, :] == segment_row[:, None]) & (token_index[None, :] >= token_index[:, None])
    ).astype(f32)
    tokens_row = join_halves(tokens, swap_halves(tokens))
    cotangent_row = join_halves(cotangent, swap_halves(cotangent))
    weights, tokens_row, cotangent_row = lax.optimization_barrier((weights, tokens_row, cotangent_row))
    small_all = weights[slots_here :: slots_here + 1].reshape(wide_count, BLK * BLK)[:, : small_values.shape[0]]
    small_all = small_all.astype(f32)
    gain_full = (small_all[:, :pair_gains] + small_all[:, pair_gains : 2 * pair_gains]).reshape(2, D)
    bias_full = small_all[:, 2 * pair_gains :].reshape(1, QKV_WIDTH)

    attention_part, normed_one_turned, qkv, mixed_turned, log_total = run_attention_forward(
        rows, tokens_row, gain_full[0:1], bias_full, cosine, sine, allowed_turned, weights
    )
    attention_other = swap_halves(attention_part)
    active_grad = run_active_grads(rows, cotangent_row, weights)
    grad_two_part, resid, normed_two_turned, gain_two_part, pair_grads, active, active_turned = run_hidden_grads(
        rows, tokens_row, attention_part, attention_other, gain_full[1:2], active_grad, weights
    )
    grad_two_other = swap_halves(grad_two_part)
    branch_part, grads = run_hidden_weight_grads(
        rows, normed_two_turned, cotangent_row, pair_grads, active, active_turned, weights,
        wide_count * (slots_here + 1),
    )
    grad_resid, grad_one_part, grads = run_attention_backward(
        rows, tokens_row, resid, grad_two_part, grad_two_other, cotangent_row, gain_full, cosine, sine, allowed_turned,
        normed_one_turned, qkv, mixed_turned, log_total, gain_two_part, weights, grads, wide_count,
    )

    def own_rows(values):
        return lax.dynamic_slice_in_dim(values, own_start, tokens_here, 0)

    def other_rows(values):
        return lax.dynamic_slice_in_dim(values, tokens_here - own_start, tokens_here, 0)

    branch_other = swap_halves(other_rows(branch_part))
    output = (
        own_rows(resid) + own_rows(branch_part).astype(f32) + branch_other.astype(f32)
    ).astype(bf16)
    grad_one_other = swap_halves(other_rows(grad_one_part))

    if wide_count == 16:
        reduced = run_sum_for_owners(grads, wide_count)
    else:
        reduced = lax.psum_scatter(grads, "wide", scatter_dimension=0, tiled=True)

    block_grad, new_masters, new_first, new_second = run_soap(
        reduced.astype(f32), masters, first_moment, second_moment, left_basis, right_basis
    )
    places = [small_places(owner, wide_count) for owner in range(wide_count)]
    gain_offset = jnp.asarray([place[1] for place in places], jnp.int32)[wide_index]
    bias_offset = jnp.asarray([place[3] for place in places], jnp.int32)[wide_index]
    small_sums = reduced[slots_here, :8].astype(f32)
    gain_sums = lax.dynamic_slice_in_dim(small_sums[:2].reshape(-1), gain_offset, pair_gains, 0)
    gain_sums = gain_sums.reshape(2, gains_here)
    gain_sums = gain_sums + swap_halves(gain_sums)
    gain_grad = lax.dynamic_index_in_dim(gain_sums, half, 0, keepdims=False)
    bias_grad = lax.dynamic_slice_in_dim(small_sums[2], bias_offset, biases_here, 0).reshape(biases.shape)
    new_gains, new_gain_first, new_gain_second = adam_small(gains, gain_grad, gain_first, gain_second, rate_gains)
    new_biases, new_bias_first, new_bias_second = adam_small(biases, bias_grad, bias_first, bias_second, rate_small)

    inverse_one, normed_one = rms_parts(tokens.astype(f32))
    grad_one = own_rows(grad_one_part).astype(f32) + grad_one_other.astype(f32)
    input_grad = own_rows(grad_resid) + norm_back(grad_one * gain_full[0:1], normed_one, inverse_one)
    return (
        output,
        input_grad,
        block_grad,
        new_masters,
        new_first,
        new_second,
        gain_grad,
        new_gains,
        new_gain_first,
        new_gain_second,
        bias_grad,
        new_biases,
        new_bias_first,
        new_bias_second,
    )


def solution(mesh):
    tokens_spec = P(("wide", "narrow"), None)
    blocks_spec = P(("wide", "narrow"), None, None)
    gains_spec = P(("wide", "narrow"))
    bias_spec = P("narrow", "wide")
    in_specs = (
        (tokens_spec, tokens_spec, P(), P()) + (blocks_spec,) * 5 + (gains_spec,) * 3 + (bias_spec,) * 3
    )
    out_specs = (tokens_spec, tokens_spec) + (blocks_spec,) * 4 + (gains_spec,) * 4 + (bias_spec,) * 4
    return jax.shard_map(body, mesh=mesh, in_specs=in_specs, out_specs=out_specs, check_vma=False)
```

```python
import functools

import jax
import jax.numpy as jnp
from jax import lax
from jax.experimental import pallas as pl
from jax.experimental.pallas import tpu as pltpu
from jax.sharding import PartitionSpec as P

D = 1536
FF = 8960
HEADS = 12
KV_HEADS = 2
HEAD_DIM = 128
BLK = 128
STEP_COUNT = 5


beta_first = 0.95
beta_second = 0.95
adam_eps = 1e-08
rate_blocks = 0.03
rate_small = 0.4
rate_gains = 0.6
norm_eps = 1e-06
rope_base = 10000.0
masked_score = -1e30
first_fix = 1.0 - beta_first**STEP_COUNT
second_fix = 1.0 - beta_second**STEP_COUNT
scaling = HEAD_DIM ** (-0.5)

bf16 = jnp.bfloat16
f32 = jnp.float32

NARROW = 2
ROW_BLOCKS = D // BLK
QUERY_COLS = HEADS * HEAD_DIM // NARROW // BLK
PAIR_COLS = KV_HEADS * HEAD_DIM // NARROW // BLK
HIDDEN_COLS = FF // NARROW // BLK
QKV_COLS = QUERY_COLS + 2 * PAIR_COLS
QUERY_WIDTH = QUERY_COLS * BLK
QKV_WIDTH = QKV_COLS * BLK
KEY_BASE = ROW_BLOCKS * QUERY_COLS
VALUE_BASE = KEY_BASE + ROW_BLOCKS * PAIR_COLS
OUT_BASE = VALUE_BASE + ROW_BLOCKS * PAIR_COLS
GATE_BASE = OUT_BASE + QUERY_COLS * ROW_BLOCKS
UP_BASE = GATE_BASE + ROW_BLOCKS * HIDDEN_COLS
DOWN_BASE = UP_BASE + ROW_BLOCKS * HIDDEN_COLS
BLOCK_TOTAL = DOWN_BASE + HIDDEN_COLS * ROW_BLOCKS

TILE_BLOCKS = 6
TILES = -(-HIDDEN_COLS // TILE_BLOCKS)
LAST_BLOCKS = HIDDEN_COLS - (TILES - 1) * TILE_BLOCKS
TILE = TILE_BLOCKS * BLK
COLS = 256
ROWS = 64
SMALL_ROWS = 16
VMEM_LIMIT = 60 * 2**20

EARLY = 4
DEPTH = 3
CROSS_LAG = 2
HOP_LAG = 1

VMEM_SPEC = pl.BlockSpec(memory_space=pltpu.VMEM)
SMEM_SPEC = pl.BlockSpec(memory_space=pltpu.SMEM)
ANY_SPEC = pl.BlockSpec(memory_space=pl.ANY)


def spans(total, step):
    return [(begin, min(step, total - begin)) for begin in range(0, total, step)]


def dot_nn(left, right):
    return jnp.dot(left, right, preferred_element_type=f32)


def dot_nt(left, right):
    return lax.dot_general(left, right, (((1,), (1,)), ((), ())), preferred_element_type=f32)


def block_ref(ref, row_block, col_block):
    return ref.at[pl.ds(row_block * BLK, BLK), pl.ds(col_block * BLK, BLK)]


def fetch_piece(rows_ref, weights, target, base, pitch, row_blocks, col_blocks, first_col, sem):
    @pl.loop(0, row_blocks)
    def _(i):
        for j in range(col_blocks):
            pltpu.make_async_copy(
                weights.at[rows_ref[base + i * pitch + j]],
                block_ref(target, i, first_col + j),
                sem,
            ).start()


def store_piece(rows_ref, source, grads, base, pitch, row_blocks, col_blocks, first_col, sem):
    @pl.loop(0, row_blocks)
    def _(i):
        for j in range(col_blocks):
            pltpu.make_async_copy(
                block_ref(source, i, first_col + j),
                grads.at[rows_ref[base + i * pitch + j]],
                sem,
            ).start()


def wait_bytes(ref, sem):
    pltpu.make_async_copy(ref, ref, sem).wait()


def fetch_attention(rows_ref, weights, w_qkv, w_out, sems):
    fetch_piece(rows_ref, weights, w_qkv, 0, QUERY_COLS, ROW_BLOCKS, QUERY_COLS, 0, sems.at[0])
    fetch_piece(rows_ref, weights, w_qkv, KEY_BASE, PAIR_COLS, ROW_BLOCKS, PAIR_COLS, QUERY_COLS, sems.at[0])
    fetch_piece(
        rows_ref, weights, w_qkv, VALUE_BASE, PAIR_COLS, ROW_BLOCKS, PAIR_COLS, QUERY_COLS + PAIR_COLS, sems.at[0]
    )
    fetch_piece(rows_ref, weights, w_out, OUT_BASE, ROW_BLOCKS, QUERY_COLS, ROW_BLOCKS, 0, sems.at[1])


def rms_inverse(values):
    return lax.rsqrt(jnp.mean(values * values, axis=-1, keepdims=True) + norm_eps)


def row_chunks(total, step, run):
    @pl.loop(0, total // step)
    def _(chunk):
        run(pl.ds(pl.multiple_of(chunk * step, step), step))


def small_places(owner, wide_count):
    gain_first = owner * (2 * D // wide_count)
    bias_first = owner * (QKV_WIDTH // wide_count)
    gain_row = min(gain_first // BLK, 2 * D // BLK - 2)
    return (gain_row, gain_first - gain_row * BLK, bias_first // BLK, bias_first % BLK)


def scores_turned(keys, queries, allowed):
    return jnp.where(allowed, dot_nt(keys, queries) * scaling, masked_score)


def attention_forward(
    rows_ref,
    x_ref,
    gain_ref,
    bias_ref,
    cos_ref,
    sin_ref,
    allowed_ref,
    weights,
    part_low_ref,
    part_high_ref,
    normed_turned_ref,
    qkv_ref,
    mixed_turned_ref,
    log_ref,
    w_qkv,
    w_out,
    normed,
    mixed,
    sems,
):
    fetch_attention(rows_ref, weights, w_qkv, w_out, sems)
    length = x_ref.shape[0]

    def norm_rows(rows):
        values = x_ref[rows, :].astype(f32)
        normed[rows, :] = (values * rms_inverse(values) * gain_ref[...]).astype(bf16)

    row_chunks(length, ROWS, norm_rows)
    for begin, size in spans(D, COLS):
        normed_turned_ref[pl.ds(begin, size), :] = normed[:, pl.ds(begin, size)].T
    wait_bytes(w_qkv, sems.at[0])
    for begin, size in spans(QKV_WIDTH, COLS):
        products = dot_nn(normed[...], w_qkv[:, pl.ds(begin, size)]) + bias_ref[:, pl.ds(begin, size)]
        for offset, width in spans(size, HEAD_DIM):
            head = products[:, offset : offset + width]
            if begin + offset < QUERY_WIDTH + PAIR_COLS * BLK:
                head = head * cos_ref[...] + pltpu.roll(head, HEAD_DIM // 2, 1) * sin_ref[...]
            qkv_ref[:, pl.ds(begin + offset, width)] = head.astype(bf16)
    keys = qkv_ref[:, pl.ds(QUERY_WIDTH, HEAD_DIM)]
    values_turned = qkv_ref[:, pl.ds(QUERY_WIDTH + HEAD_DIM, HEAD_DIM)].T
    for head in range(QUERY_COLS):
        columns = pl.ds(head * HEAD_DIM, HEAD_DIM)
        scores = scores_turned(keys, qkv_ref[:, columns], allowed_ref[...] > 0)
        peak = jnp.max(scores, axis=0, keepdims=True)
        expo = jnp.exp(scores - peak)
        total = jnp.sum(expo, axis=0, keepdims=True)
        log_ref[pl.ds(head, 1), :] = peak + jnp.log(total)
        probs = (expo / total).astype(bf16)
        mixed_head = dot_nn(values_turned, probs).astype(bf16)
        mixed_turned_ref[columns, :] = mixed_head
        mixed[:, columns] = mixed_head.T
    wait_bytes(w_out, sems.at[1])
    for part_ref, first in ((part_low_ref, 0), (part_high_ref, length // NARROW)):
        for begin, size in spans(D, COLS):
            part_ref[:, pl.ds(begin, size)] = dot_nn(
                mixed[pl.ds(first, length // NARROW), :], w_out[:, pl.ds(begin, size)]
            ).astype(bf16)


def pair_copies(rows_ref, blocks_hbm, pair, sem, column, place, outward=False):
    return [
        block_copy(blocks_hbm.at[rows_ref[base + i * HIDDEN_COLS + column]], block_ref(pair, i, which), sem, outward)
        for i in range(ROW_BLOCKS)
        for base, which in ((GATE_BASE, 2 * place), (UP_BASE, 2 * place + 1))
    ]


def down_copies(rows_ref, blocks_hbm, down, sem, column, place, outward=False):
    return [
        block_copy(blocks_hbm.at[rows_ref[DOWN_BASE + column * ROW_BLOCKS + i]], block_ref(down, place, i), sem, outward)
        for i in range(ROW_BLOCKS)
    ]


def block_copy(in_hbm, in_vmem, sem, outward):
    return pltpu.make_async_copy(*((in_vmem, in_hbm) if outward else (in_hbm, in_vmem)), sem)


def start_all(copies):
    for copy in copies:
        copy.start()


def half_rows(half_ref, length):
    begin = pl.multiple_of(half_ref[0] * length, length)
    return (pl.ds(begin, length), pl.ds(pl.multiple_of(length - begin, length), length))


def hidden_column(tile, place):
    return jnp.minimum(tile * TILE_BLOCKS + place, HIDDEN_COLS - 1)


def hidden_tiles(run):
    @pl.loop(0, TILES - 1)
    def _(tile):
        run(tile, lax.rem(tile, 2), TILE_BLOCKS, True)

    run(TILES - 1, (TILES - 1) % 2, LAST_BLOCKS, False)


def active_grads(rows_ref, cot_ref, weights, out, w_down, stage, load_sems, store_sems):
    def fetch(tile, slot, place):
        start_all(
            down_copies(rows_ref, weights, w_down.at[slot], load_sems.at[slot], hidden_column(tile, place), place)
        )

    for place in range(TILE_BLOCKS):
        fetch(0, 0, place)

    def run(tile, slot, blocks, more):
        wait_bytes(w_down.at[slot], load_sems.at[slot])

        @pl.when(tile >= 2)
        def _():
            wait_bytes(stage.at[slot], store_sems.at[slot])

        if more:
            for place in range(TILE_BLOCKS):
                fetch(tile + 1, 1 - slot, place)
        for begin, size in spans(blocks * BLK, COLS):
            stage[slot, :, pl.ds(begin, size)] = dot_nt(cot_ref[...], w_down[slot, pl.ds(begin, size), :])
        pltpu.make_async_copy(stage.at[slot], out.at[tile], store_sems.at[slot]).start()

    hidden_tiles(run)
    for tile in range(max(TILES - 2, 0), TILES):
        wait_bytes(stage.at[tile % 2], store_sems.at[tile % 2])


def hidden_grads(
    first_row,
    rows_ref,
    x_ref,
    own_ref,
    other_ref,
    gain_ref,
    active_grad,
    weights,
    grad_ref,
    resid_ref,
    normed_turned_ref,
    gain_part_ref,
    pair_grads,
    active,
    active_turned,
    w_pair,
    grad_active,
    straight,
    turned,
    grads,
    normed,
    grad_sum,
    load_sems,
    store_sems,
):
    length = own_ref.shape[0]

    def fetch(tile, slot, place):
        start_all(
            pair_copies(rows_ref, weights, w_pair.at[slot], load_sems.at[slot, 0], hidden_column(tile, place), place)
        )

    def load_grad(tile, slot):
        return pltpu.make_async_copy(active_grad.at[tile, pl.ds(first_row, length)], grad_active.at[slot], load_sems.at[slot, 1])

    def stores(tile, slot):
        return (
            pltpu.make_async_copy(turned.at[slot], active_turned.at[tile], store_sems.at[slot, 0]),
            pltpu.make_async_copy(grads.at[slot], pair_grads.at[tile], store_sems.at[slot, 1]),
            pltpu.make_async_copy(straight.at[slot], active.at[tile], store_sems.at[slot, 2]),
        )

    for place in range(TILE_BLOCKS):
        fetch(0, 0, place)
    load_grad(0, 0).start()

    def norm_rows(rows):
        tokens = x_ref[pl.ds(rows.start + first_row, rows.size), :]
        values = tokens.astype(f32) + own_ref[rows, :].astype(f32) + other_ref[rows, :].astype(f32)
        resid_ref[rows, :] = values
        normed[rows, :] = (values * rms_inverse(values) * gain_ref[...]).astype(bf16)

    row_chunks(length, ROWS, norm_rows)
    grad_sum[...] = jnp.zeros_like(grad_sum)

    def run(tile, slot, blocks, more):
        wait_bytes(w_pair.at[slot], load_sems.at[slot, 0])
        load_grad(tile, slot).wait()
        if more:
            load_grad(tile + 1, 1 - slot).start()

        @pl.when(tile >= 2)
        def _():
            for copy in stores(tile - 2, slot):
                copy.wait()

        for place in range(blocks):
            columns = pl.ds(place * BLK, BLK)
            pair = dot_nn(normed[...], w_pair[slot, :, pl.ds(2 * place * BLK, 2 * BLK)])
            gate = pair[:, :BLK]
            upper = pair[:, BLK:]
            grad = grad_active[slot, :, columns]
            sigmoid = jax.nn.sigmoid(gate)
            silu = gate * sigmoid
            active_here = (silu * upper).astype(bf16)
            straight[slot, :, columns] = active_here
            turned[slot, columns, :] = active_here.T
            grads[slot, :, pl.ds(2 * place * BLK, BLK)] = (
                grad * upper * sigmoid * (1.0 + gate * (1.0 - sigmoid))
            ).astype(bf16)
            grads[slot, :, pl.ds((2 * place + 1) * BLK, BLK)] = (grad * silu).astype(bf16)
            if more:
                fetch(tile + 1, 1 - slot, place)
        if more:
            for place in range(blocks, TILE_BLOCKS):
                fetch(tile + 1, 1 - slot, place)
        turn = pl.ds(pl.multiple_of(tile * COLS, COLS), COLS)
        normed_turned_ref[turn, :] = normed[:, turn].T
        width = 2 * blocks * BLK
        for begin, size in spans(D, COLS):
            columns = pl.ds(begin, size)
            grad_sum[:, columns] += dot_nt(grads[slot, :, :width], w_pair[slot, columns, :width])
        start_all(stores(tile, slot))

    hidden_tiles(run)
    grad_ref[...] = grad_sum[...].astype(bf16)
    gain_part_ref[...] = jnp.zeros_like(gain_part_ref)

    def gain_rows(rows):
        values = resid_ref[rows, :]
        gain_part_ref[...] += jnp.sum(grad_sum[rows, :] * values * rms_inverse(values), axis=0, keepdims=True)

    row_chunks(length, ROWS, gain_rows)
    for tile in range(max(TILES - 2, 0), TILES):
        for copy in stores(tile, tile % 2):
            copy.wait()


def hidden_weight_grads(
    weight_rows_ref, rows_ref, half_ref, cot_ref, *refs
):
    parts, (weights, branch_own_ref, branch_other_ref, grads), scratch = refs[: 4 * NARROW], refs[8:12], refs[12:]
    normed_turned, pair, straight, turned, w_down, branch_sum, pair_stage, down_stage, load_sems, store_sems, sems = scratch
    length = cot_ref.shape[0] // NARROW

    def loads(tile, slot):
        copies = []
        for part in range(NARROW):
            pair_grads, active, active_turned = parts[part * 4 + 1 : part * 4 + 4]
            tokens = pl.ds(part * length, length)
            copies += [
                pltpu.make_async_copy(pair_grads.at[tile], pair.at[slot, tokens], load_sems.at[slot, part * 3]),
                pltpu.make_async_copy(active.at[tile], straight.at[slot, tokens], load_sems.at[slot, part * 3 + 1]),
                pltpu.make_async_copy(
                    active_turned.at[tile], turned.at[slot, :, tokens], load_sems.at[slot, part * 3 + 2]
                ),
            ]
        return copies

    def fetch(tile, slot, place):
        start_all(
            down_copies(
                weight_rows_ref, weights, w_down.at[slot], load_sems.at[slot, 3 * NARROW], hidden_column(tile, place), place
            )
        )

    def drain(slot, blocks):
        wait_bytes(pair_stage.at[slot, :, pl.ds(0, 2 * blocks * BLK)], store_sems.at[slot, 0])
        wait_bytes(down_stage.at[slot, pl.ds(0, blocks * BLK)], store_sems.at[slot, 1])

    turned_loads = [
        pltpu.make_async_copy(parts[part * 4], normed_turned.at[:, pl.ds(part * length, length)], sems.at[part])
        for part in range(NARROW)
    ]
    start_all(loads(0, 0) + turned_loads)
    for place in range(TILE_BLOCKS):
        fetch(0, 0, place)
    branch_sum[...] = jnp.zeros_like(branch_sum)
    for copy in turned_loads:
        copy.wait()

    def run(tile, slot, blocks, more):
        for copy in loads(tile, slot):
            copy.wait()
        wait_bytes(w_down.at[slot], load_sems.at[slot, 3 * NARROW])
        if more:
            start_all(loads(tile + 1, 1 - slot))

        @pl.when(tile >= 2)
        def _():
            drain(slot, TILE_BLOCKS)

        width = blocks * BLK
        down = turned[slot, pl.ds(0, width), :]
        for begin, size in spans(D, COLS):
            columns = pl.ds(begin, size)
            down_stage[slot, pl.ds(0, width), columns] = dot_nn(down, cot_ref[:, columns]).astype(bf16)
        for place in range(blocks):
            column = tile * TILE_BLOCKS + place
            start_all(
                down_copies(rows_ref, grads, down_stage.at[slot], store_sems.at[slot, 1], column, place, outward=True)
            )
            columns = pl.ds(2 * place * BLK, 2 * BLK)
            for begin, size in spans(D, 512):
                pair_stage[slot, pl.ds(begin, size), columns] = dot_nn(
                    normed_turned[pl.ds(begin, size), :], pair[slot, :, columns]
                ).astype(bf16)
            start_all(
                pair_copies(rows_ref, grads, pair_stage.at[slot], store_sems.at[slot, 0], column, place, outward=True)
            )
            if more:
                fetch(tile + 1, 1 - slot, place)
        if more:
            for place in range(blocks, TILE_BLOCKS):
                fetch(tile + 1, 1 - slot, place)
        for begin, size in spans(D, COLS):
            columns = pl.ds(begin, size)
            branch_sum[:, columns] += dot_nn(straight[slot, :, :width], w_down[slot, :width, columns])

    hidden_tiles(run)
    own, other = half_rows(half_ref, length)
    branch_own_ref[...] = branch_sum[own, :].astype(bf16)
    branch_other_ref[...] = branch_sum[other, :].astype(bf16)
    if TILES > 1:
        drain((TILES - 2) % 2, TILE_BLOCKS)
    drain((TILES - 1) % 2, LAST_BLOCKS)


def attention_backward(
    weight_rows_ref,
    rows_ref,
    half_ref,
    x_ref,
    resid_low_ref,
    own_low_ref,
    other_low_ref,
    resid_high_ref,
    own_high_ref,
    other_high_ref,
    cot_ref,
    gain_ref,
    cos_ref,
    sin_ref,
    allowed_ref,
    normed_turned_ref,
    qkv_ref,
    mixed_turned_ref,
    log_ref,
    gain_two_low_ref,
    gain_two_high_ref,
    weights,
    grads_in,
    grad_resid_ref,
    grad_own_ref,
    grad_other_ref,
    grads,
    w_qkv,
    w_out,
    grad_resid,
    grad_attention,
    grad_mixed,
    grad_qkv,
    grad_sum,
    gain_part,
    bias_part,
    qkv_stage,
    out_stage,
    small_stage,
    blank,
    load_sems,
    store_sems,
):
    del grads_in
    wide_count = small_stage.shape[0]
    owner_rows = grads.shape[0] // wide_count
    small_stage[...] = jnp.zeros_like(small_stage)
    fetch_attention(weight_rows_ref, weights, w_qkv, w_out, load_sems)
    length = x_ref.shape[0]
    empty_count = rows_ref.shape[0] - BLOCK_TOTAL
    blank[...] = jnp.zeros_like(blank)
    for index in range(empty_count):
        pltpu.make_async_copy(blank.at[index], grads.at[rows_ref[BLOCK_TOTAL + index]], store_sems.at[2]).start()

    part = length // NARROW
    own_rows, other_rows = half_rows(half_ref, part)
    for first, resid_ref, own_ref, other_ref in (
        (0, resid_low_ref, own_low_ref, other_low_ref),
        (part, resid_high_ref, own_high_ref, other_high_ref),
    ):

        def resid_rows(rows, first=first, resid_ref=resid_ref, own_ref=own_ref, other_ref=other_ref):
            values = resid_ref[rows, :]
            inverse = rms_inverse(values)
            normed = values * inverse
            scaled = (own_ref[rows, :].astype(f32) + other_ref[rows, :].astype(f32)) * gain_ref[1:2, :]
            place = pl.ds(rows.start + first, rows.size)
            total = cot_ref[place, :].astype(f32) + inverse * (
                scaled - normed * jnp.mean(scaled * normed, axis=-1, keepdims=True)
            )
            grad_resid[place, :] = total
            grad_attention[place, :] = total.astype(bf16)

        row_chunks(part, ROWS, resid_rows)
    grad_resid_ref[...] = grad_resid[own_rows, :]
    wait_bytes(w_out, load_sems.at[1])
    for begin, size in spans(QUERY_WIDTH, COLS):
        grad_mixed[:, pl.ds(begin, size)] = dot_nt(grad_attention[...], w_out[pl.ds(begin, size), :]).astype(bf16)
    keys = qkv_ref[:, pl.ds(QUERY_WIDTH, HEAD_DIM)]
    keys_turned = keys.T
    values = qkv_ref[:, pl.ds(QUERY_WIDTH + HEAD_DIM, HEAD_DIM)]

    def rope_back(vector):
        return vector * cos_ref[...] - pltpu.roll(vector, HEAD_DIM // 2, 1) * sin_ref[...]

    grad_keys = jnp.zeros((length, HEAD_DIM), f32)
    grad_values = jnp.zeros((length, HEAD_DIM), f32)
    for head in range(QUERY_COLS):
        columns = pl.ds(head * HEAD_DIM, HEAD_DIM)
        queries = qkv_ref[:, columns]
        scores = scores_turned(keys, queries, allowed_ref[...] > 0)
        probs = jnp.exp(scores - log_ref[pl.ds(head, 1), :])
        grad_values += dot_nn(probs.astype(bf16), grad_mixed[:, columns])
        grad_probs = dot_nt(values, grad_mixed[:, columns])
        row_dot = jnp.sum(probs * grad_probs, axis=0, keepdims=True)
        grad_scores = (probs * (grad_probs - row_dot)).astype(bf16)
        grad_keys += dot_nn(grad_scores, queries)
        grad_queries = dot_nn(keys_turned, grad_scores).T * scaling
        grad_qkv[:, columns] = rope_back(grad_queries).astype(bf16)
    grad_qkv[:, pl.ds(QUERY_WIDTH, HEAD_DIM)] = rope_back(grad_keys * scaling).astype(bf16)
    grad_qkv[:, pl.ds(QUERY_WIDTH + HEAD_DIM, HEAD_DIM)] = grad_values.astype(bf16)

    for begin, size in spans(D, COLS):
        out_stage[:, pl.ds(begin, size)] = dot_nn(
            mixed_turned_ref[...], grad_attention[:, pl.ds(begin, size)]
        ).astype(bf16)
    store_piece(rows_ref, out_stage, grads, OUT_BASE, ROW_BLOCKS, QUERY_COLS, ROW_BLOCKS, 0, store_sems.at[1])
    for begin, size in spans(QKV_WIDTH, COLS):
        qkv_stage[:, pl.ds(begin, size)] = dot_nn(
            normed_turned_ref[...], grad_qkv[:, pl.ds(begin, size)]
        ).astype(bf16)
    store_piece(rows_ref, qkv_stage, grads, 0, QUERY_COLS, ROW_BLOCKS, QUERY_COLS, 0, store_sems.at[0])
    store_piece(rows_ref, qkv_stage, grads, KEY_BASE, PAIR_COLS, ROW_BLOCKS, PAIR_COLS, QUERY_COLS, store_sems.at[0])
    store_piece(
        rows_ref, qkv_stage, grads, VALUE_BASE, PAIR_COLS, ROW_BLOCKS, PAIR_COLS, QUERY_COLS + PAIR_COLS, store_sems.at[0]
    )
    wait_bytes(w_qkv, load_sems.at[0])
    for begin, size in spans(D, COLS):
        grad_sum[:, pl.ds(begin, size)] = dot_nt(grad_qkv[...], w_qkv[pl.ds(begin, size), :])
    grad_own_ref[...] = grad_sum[own_rows, :].astype(bf16)
    grad_other_ref[...] = grad_sum[other_rows, :].astype(bf16)
    gain_part[...] = jnp.zeros_like(gain_part)
    bias_part[...] = jnp.zeros_like(bias_part)

    def gain_rows(rows):
        tokens = x_ref[rows, :].astype(f32)
        gain_part[...] += jnp.sum(grad_sum[rows, :] * tokens * rms_inverse(tokens), axis=0, keepdims=True)
        bias_part[...] += jnp.sum(grad_qkv[rows, :].astype(f32), axis=0, keepdims=True)

    row_chunks(length, ROWS, gain_rows)
    for owner in range(wide_count):
        gain_row, bias_row = small_places(owner, wide_count)[::2]
        small_rows = []
        for row in (gain_row, gain_row + 1):
            columns = pl.ds(row % (D // BLK) * BLK, BLK)
            if row < D // BLK:
                small_rows.append(gain_part[:, columns])
            else:
                small_rows.append(gain_two_low_ref[:, columns] + gain_two_high_ref[:, columns])
        small_rows.append(bias_part[:, pl.ds(bias_row * BLK, BLK)])
        small_rows.append(jnp.zeros((SMALL_ROWS - len(small_rows), BLK), f32))
        small_stage[owner, pl.ds(0, SMALL_ROWS), :] = jnp.concatenate(small_rows, axis=0).astype(bf16)
        pltpu.make_async_copy(
            small_stage.at[owner], grads.at[owner * owner_rows + owner_rows - 1], store_sems.at[3]
        ).start()
    wait_bytes(small_stage, store_sems.at[3])
    wait_bytes(qkv_stage, store_sems.at[0])
    wait_bytes(out_stage, store_sems.at[1])
    if empty_count > 0:
        wait_bytes(blank.at[pl.ds(0, empty_count)], store_sems.at[2])


def soap_update(
    grad_in,
    masters_ref,
    first_ref,
    second_ref,
    left_ref,
    right_ref,
    grad_ref,
    new_masters_ref,
    new_first_ref,
    new_second_ref,
):
    blocks = range(masters_ref.shape[0])
    rights = [right_ref[index].astype(bf16) for index in blocks]
    products = [dot_nn(grad_in[index], rights[index]).astype(bf16) for index in blocks]
    lefts = [left_ref[index].astype(bf16) for index in blocks]
    rotated_blocks = [dot_nn(lefts[index].T, products[index]) for index in blocks]
    normalized = []
    for index in blocks:
        rotated = rotated_blocks[index]
        grad_ref[index] = grad_in[index].astype(f32)
        new_first = beta_first * first_ref[index] + (1.0 - beta_first) * rotated
        new_second = beta_second * second_ref[index] + (1.0 - beta_second) * rotated * rotated
        new_first_ref[index] = new_first
        new_second_ref[index] = new_second
        normalized.append(
            (new_first / first_fix / (jnp.sqrt(new_second / second_fix) + adam_eps)).astype(bf16)
        )
    products = [dot_nt(normalized[index], rights[index]).astype(bf16) for index in blocks]
    for index in blocks:
        new_masters_ref[index] = masters_ref[index] - rate_blocks * dot_nn(lefts[index], products[index])


def params(**options):
    return pltpu.CompilerParams(vmem_limit_bytes=VMEM_LIMIT, **options)


def run_attention_forward(rows, x, gain, bias, cosine, sine, allowed, weights):
    length = x.shape[0]
    shape = jax.ShapeDtypeStruct
    return pl.pallas_call(
        attention_forward,
        out_shape=[
            shape((length // NARROW, D), bf16),
            shape((length // NARROW, D), bf16),
            shape((D, length), bf16),
            shape((length, QKV_WIDTH), bf16),
            shape((QUERY_WIDTH, length), bf16),
            shape((8, length), f32),
        ],
        in_specs=[SMEM_SPEC] + [VMEM_SPEC] * 6 + [ANY_SPEC],
        out_specs=[VMEM_SPEC] * 6,
        scratch_shapes=[
            pltpu.VMEM((D, QKV_WIDTH), bf16),
            pltpu.VMEM((QUERY_WIDTH, D), bf16),
            pltpu.VMEM((length, D), bf16),
            pltpu.VMEM((length, QUERY_WIDTH), bf16),
            pltpu.SemaphoreType.DMA((2,)),
        ],
        compiler_params=params(),
        name="attention_forward",
    )(rows, x, gain, bias, cosine, sine, allowed, weights)


def hidden_cost(length, products, bytes_moved):
    return pl.CostEstimate(
        flops=2 * products * length * D * TILE * TILES, bytes_accessed=bytes_moved, transcendentals=0
    )


def run_active_grads(rows, cotangent, weights):
    length = cotangent.shape[0]
    return pl.pallas_call(
        active_grads,
        out_shape=jax.ShapeDtypeStruct((TILES, length, TILE), f32),
        in_specs=[SMEM_SPEC, VMEM_SPEC, ANY_SPEC],
        out_specs=ANY_SPEC,
        scratch_shapes=[
            pltpu.VMEM((2, TILE, D), bf16),
            pltpu.VMEM((2, length, TILE), f32),
            pltpu.SemaphoreType.DMA((2,)),
            pltpu.SemaphoreType.DMA((2,)),
        ],
        compiler_params=params(),
        cost_estimate=hidden_cost(length, 1, TILES * TILE * (2 * D + 4 * length)),
        name="active_grads",
    )(rows, cotangent, weights)


def run_hidden_grads(first_row, rows, x, own, other, gain, active_grad, weights):
    length = own.shape[0]
    shape = jax.ShapeDtypeStruct
    return pl.pallas_call(
        functools.partial(hidden_grads, first_row),
        out_shape=[
            shape((length, D), bf16),
            shape((length, D), f32),
            shape((D, length), bf16),
            shape((1, D), f32),
            shape((TILES, length, 2 * TILE), bf16),
            shape((TILES, length, TILE), bf16),
            shape((TILES, TILE, length), bf16),
        ],
        in_specs=[SMEM_SPEC] + [VMEM_SPEC] * 4 + [ANY_SPEC] * 2,
        out_specs=[VMEM_SPEC] * 4 + [ANY_SPEC] * 3,
        scratch_shapes=[
            pltpu.VMEM((2, D, 2 * TILE), bf16),
            pltpu.VMEM((2, length, TILE), f32),
            pltpu.VMEM((2, length, TILE), bf16),
            pltpu.VMEM((2, TILE, length), bf16),
            pltpu.VMEM((2, length, 2 * TILE), bf16),
            pltpu.VMEM((length, D), bf16),
            pltpu.VMEM((length, D), f32),
            pltpu.SemaphoreType.DMA((2, 2)),
            pltpu.SemaphoreType.DMA((2, 3)),
        ],
        compiler_params=params(),
        cost_estimate=hidden_cost(length, 4, 2 * TILES * TILE * (2 * D + 6 * length)),
        name="hidden_grads",
    )(rows, x, own, other, gain, active_grad, weights)


def run_hidden_weight_grads(weight_rows, rows, half, cotangent, parts, weights, slots):
    length = cotangent.shape[0]
    shape = jax.ShapeDtypeStruct
    return pl.pallas_call(
        hidden_weight_grads,
        out_shape=[shape((length // NARROW, D), bf16)] * 2 + [shape((slots, BLK, BLK), bf16)],
        in_specs=[SMEM_SPEC] * 3 + [VMEM_SPEC] + [ANY_SPEC] * (4 * NARROW + 1),
        out_specs=[VMEM_SPEC, VMEM_SPEC, ANY_SPEC],
        scratch_shapes=[
            pltpu.VMEM((D, length), bf16),
            pltpu.VMEM((2, length, 2 * TILE), bf16),
            pltpu.VMEM((2, length, TILE), bf16),
            pltpu.VMEM((2, TILE, length), bf16),
            pltpu.VMEM((2, TILE, D), bf16),
            pltpu.VMEM((length, D), f32),
            pltpu.VMEM((2, D, 2 * TILE), bf16),
            pltpu.VMEM((2, TILE, D), bf16),
            pltpu.SemaphoreType.DMA((2, 3 * NARROW + 1)),
            pltpu.SemaphoreType.DMA((2, 2)),
            pltpu.SemaphoreType.DMA((NARROW,)),
        ],
        compiler_params=params(),
        cost_estimate=hidden_cost(length, 4, 2 * TILES * TILE * (4 * D + 4 * length)),
        name="hidden_weight_grads",
    )(weight_rows, rows, half, cotangent, *[array for part in parts for array in part], weights)


def run_attention_backward(
    weight_rows, rows, half, x, low, high, cotangent, gains, cosine, sine, allowed, normed_turned, qkv, mixed_turned,
    log_total, gain_two_parts, weights, grads, wide_count,
):
    length = x.shape[0]
    shape = jax.ShapeDtypeStruct
    empty_count = max(rows.shape[0] - BLOCK_TOTAL, 1)
    operands = (
        weight_rows, rows, half, x, *low, *high, cotangent, gains, cosine, sine, allowed, normed_turned, qkv, mixed_turned,
        log_total, *gain_two_parts, weights, grads,
    )
    return pl.pallas_call(
        attention_backward,
        out_shape=[
            shape((length // NARROW, D), f32),
            shape((length // NARROW, D), bf16),
            shape((length // NARROW, D), bf16),
            shape(grads.shape, bf16),
        ],
        in_specs=[SMEM_SPEC] * 3 + [VMEM_SPEC] * (len(operands) - 5) + [ANY_SPEC] * 2,
        out_specs=[VMEM_SPEC] * 3 + [ANY_SPEC],
        input_output_aliases={len(operands) - 1: 3},
        scratch_shapes=[
            pltpu.VMEM((D, QKV_WIDTH), bf16),
            pltpu.VMEM((QUERY_WIDTH, D), bf16),
            pltpu.VMEM((length, D), f32),
            pltpu.VMEM((length, D), bf16),
            pltpu.VMEM((length, QUERY_WIDTH), bf16),
            pltpu.VMEM((length, QKV_WIDTH), bf16),
            pltpu.VMEM((length, D), f32),
            pltpu.VMEM((1, D), f32),
            pltpu.VMEM((1, QKV_WIDTH), f32),
            pltpu.VMEM((D, QKV_WIDTH), bf16),
            pltpu.VMEM((QUERY_WIDTH, D), bf16),
            pltpu.VMEM((wide_count, BLK, BLK), bf16),
            pltpu.VMEM((empty_count, BLK, BLK), bf16),
            pltpu.SemaphoreType.DMA((2,)),
            pltpu.SemaphoreType.DMA((4,)),
        ],
        compiler_params=params(),
        name="attention_backward",
    )(*operands)


def run_soap(reduced, masters, first_moment, second_moment, left_basis, right_basis):
    slots = masters.shape[0]
    group = max(size for size in range(1, 11) if slots % size == 0)
    spec = pl.BlockSpec((group, BLK, BLK), lambda step: (step, 0, 0))
    shape = jax.ShapeDtypeStruct(masters.shape, f32)
    return pl.pallas_call(
        soap_update,
        grid=(slots // group,),
        out_shape=[shape] * 4,
        in_specs=[spec] * 6,
        out_specs=[spec] * 4,
        compiler_params=params(),
        name="soap_update",
    )(reduced, masters, first_moment, second_moment, left_basis, right_basis)


def sum_for_owners(
    line, steps, late_steps, grads, out,
    a_in, a_own, a_sum, a_keep, a_send, a_cross, a_up, a_down,
    b_in, b_own, b_sum, b_keep, b_send, b_cross, b_up, b_down,
    result,
    core_send, core_recv, own_sems, cross_send, cross_recv, up_send, up_recv, down_send, down_recv,
    b_core_send, b_core_recv, b_own_sems, b_cross_send, b_cross_recv, b_up_send, b_up_recv, b_down_send, b_down_recv,
    out_sem, credits,
):
    wide = lax.axis_index("wide")
    narrow = lax.axis_index("narrow")
    z = wide // 4
    x = lax.rem(wide // 2, 2)
    core = lax.rem(wide, 2)
    mesh_id = pl.DeviceIdType.MESH
    core_peer = (wide + 1 - 2 * core, narrow)
    cross_peer = (wide + 2 - 4 * x, narrow)
    upper = (lax.rem(wide + 4, 4 * line), narrow)
    lower = (lax.rem(wide + 4 * line - 4, 4 * line), narrow)
    has_upper = z < line - 1
    has_lower = z > 0
    sum_depth = a_sum.shape[0]
    hop_depth = a_up.shape[0]
    b_sum_depth = b_sum.shape[0]

    barrier = pltpu.get_barrier_semaphore()
    pl.semaphore_signal(barrier, inc=1, device_id=core_peer, device_id_type=mesh_id)
    pl.semaphore_signal(barrier, inc=1, device_id=cross_peer, device_id_type=mesh_id)

    @pl.when(has_upper)
    def _():
        pl.semaphore_signal(barrier, inc=1, device_id=upper, device_id_type=mesh_id)

    @pl.when(has_lower)
    def _():
        pl.semaphore_signal(barrier, inc=1, device_id=lower, device_id_type=mesh_id)

    pl.semaphore_wait(barrier, 2 + has_upper.astype(jnp.int32) + has_lower.astype(jnp.int32))

    def remote(source, target, send_sem, recv_sem, peer):
        return pltpu.make_async_remote_copy(
            src_ref=source, dst_ref=target, send_sem=send_sem, recv_sem=recv_sem, device_id=peer, device_id_type=mesh_id
        )

    def core_copy(step):
        slot = lax.rem(step, DEPTH)
        source = grads.at[:, :, 1 - core, pl.ds(step * EARLY, EARLY)]
        return remote(source, a_in.at[slot], core_send.at[slot], core_recv.at[slot], core_peer)

    def own_copy(step):
        slot = lax.rem(step, DEPTH)
        return pltpu.make_async_copy(
            grads.at[:, :, core, pl.ds(step * EARLY, EARLY)], a_own.at[slot], own_sems.at[slot]
        )

    def b_core_copy(step):
        slot = lax.rem(step, DEPTH)
        source = grads.at[:, :, 1 - core, steps * EARLY + step]
        return remote(source, b_in.at[slot], b_core_send.at[slot], b_core_recv.at[slot], core_peer)

    def b_own_copy(step):
        slot = lax.rem(step, DEPTH)
        return pltpu.make_async_copy(
            grads.at[:, :, core, steps * EARLY + step], b_own.at[slot], b_own_sems.at[slot]
        )

    def cross_copy(step):
        slot = lax.rem(step, DEPTH)
        return remote(a_send.at[slot], a_cross.at[slot], cross_send.at[slot], cross_recv.at[slot], cross_peer)

    def b_cross_copy(step):
        slot = lax.rem(step, DEPTH)
        return remote(b_send.at[slot], b_cross.at[slot], b_cross_send.at[slot], b_cross_recv.at[slot], cross_peer)

    def up_copy(step, target):
        slot = lax.rem(step, hop_depth)
        return remote(
            a_sum.at[lax.rem(step, sum_depth), target], a_up.at[slot, target],
            up_send.at[slot, target], up_recv.at[slot, target], upper,
        )

    def down_copy(step, target):
        slot = lax.rem(step, hop_depth)
        return remote(
            a_sum.at[lax.rem(step, sum_depth), target], a_down.at[slot, target],
            down_send.at[slot, target], down_recv.at[slot, target], lower,
        )

    def b_up_copy(step, target):
        slot = lax.rem(step, hop_depth)
        return remote(
            b_sum.at[lax.rem(step, b_sum_depth), target], b_up.at[slot, target],
            b_up_send.at[slot, target], b_up_recv.at[slot, target], upper,
        )

    def b_down_copy(step, target):
        slot = lax.rem(step, hop_depth)
        return remote(
            b_sum.at[lax.rem(step, b_sum_depth), target], b_down.at[slot, target],
            b_down_send.at[slot, target], b_down_recv.at[slot, target], lower,
        )

    def give(channel, peer):
        pl.semaphore_signal(credits.at[channel], inc=1, device_id=peer, device_id_type=mesh_id)

    def take(channel, step, depth):
        @pl.when(step >= depth)
        def _():
            pl.semaphore_wait(credits.at[channel], 1)

    def feed(step, count, channel, remote_copy, local_copy):
        @pl.when(step < count)
        def _():
            take(channel, step, DEPTH)
            remote_copy(step).start()
            local_copy(step).start()

    for early in range(DEPTH - 1):
        feed(early, steps, 0, core_copy, own_copy)
        feed(early, late_steps, 1, b_core_copy, b_own_copy)

    def active(step, count):
        return (step >= 0) & (step < count)

    far = jnp.maximum(z, line - 1 - z)

    def hops(step_up, step_down, count, sums, depth, ups, downs, up, down, channel):
        @pl.when(active(step_up, count) & has_upper)
        def _():
            take(channel, step_up, hop_depth)
            slot = lax.rem(step_up, hop_depth)
            place = lax.rem(step_up, depth)

            def one(target, _):
                @pl.when(has_lower)
                def _():
                    up(step_up, target).wait_recv()
                    sums[place, target] += ups[slot, target]

                up(step_up, target).start()
                return 0

            lax.fori_loop(z + 1, line, one, 0)

        @pl.when(active(step_down, count) & has_lower)
        def _():
            take(channel + 1, step_down, hop_depth)
            slot = lax.rem(step_down, hop_depth)
            place = lax.rem(step_down, depth)

            def one(target, _):
                @pl.when(has_upper)
                def _():
                    down(step_down, target).wait_recv()
                    sums[place, target] += downs[slot, target]

                down(step_down, target).start()
                return 0

            lax.fori_loop(0, z, one, 0)

    def gather_hops(step, count, sums, depth, ups, downs, up, down, channel, total):
        slot = lax.rem(step, hop_depth)
        total[...] = sums[lax.rem(step, depth), z].astype(f32)

        @pl.when(has_lower)
        def _():
            up(step, z).wait_recv()
            total[...] += ups[slot, z].astype(f32)

            @pl.when(step < count - hop_depth)
            def _():
                give(channel, lower)

        @pl.when(has_upper)
        def _():
            down(step, z).wait_recv()
            total[...] += downs[slot, z].astype(f32)

            @pl.when(step < count - hop_depth)
            def _():
                give(channel + 1, upper)

    def retire(step, count, up, down):
        @pl.when(active(step, count))
        def _():
            def sent_up(target, _):
                up(step, target).wait_send()
                return 0

            def sent_down(target, _):
                down(step, target).wait_send()
                return 0

            lax.fori_loop(z + 1, line, sent_up, 0)
            lax.fori_loop(0, z, sent_down, 0)

    def iteration(step, _):
        feed(step + DEPTH - 1, steps, 0, core_copy, own_copy)
        feed(step + DEPTH - 1, late_steps, 1, b_core_copy, b_own_copy)

        retire(step - CROSS_LAG - HOP_LAG * far - 1, steps, up_copy, down_copy)
        retire(step - HOP_LAG * far - 1, late_steps, b_up_copy, b_down_copy)

        @pl.when(step < steps)
        def _():
            slot = lax.rem(step, DEPTH)
            place = lax.rem(step, sum_depth)
            core_copy(step).wait()
            own_copy(step).wait()

            @pl.when(step >= DEPTH)
            def _():
                cross_copy(step - DEPTH).wait_send()

            for target in range(line):
                a_send[slot, target] = a_own[slot, target, 1 - x] + a_in[slot, target, 1 - x]
            take(2, step, DEPTH)
            cross_copy(step).start()
            for target in range(line):
                a_sum[place, target] = a_own[slot, target, x] + a_in[slot, target, x]

            @pl.when(step < steps - DEPTH)
            def _():
                give(0, core_peer)

        @pl.when(step < late_steps)
        def _():
            slot = lax.rem(step, DEPTH)
            b_core_copy(step).wait()
            b_own_copy(step).wait()
            b_sum[lax.rem(step, b_sum_depth)] = b_own[slot] + b_in[slot]

            @pl.when(step < late_steps - DEPTH)
            def _():
                give(1, core_peer)

        crossed = step - CROSS_LAG

        @pl.when(active(crossed, steps))
        def _():
            slot = lax.rem(crossed, DEPTH)
            place = lax.rem(crossed, sum_depth)
            cross_copy(crossed).wait_recv()
            for target in range(line):
                a_sum[place, target] += a_cross[slot, target]

            @pl.when(crossed < steps - DEPTH)
            def _():
                give(2, cross_peer)

        hops(
            step - HOP_LAG * z, step - HOP_LAG * (line - 1 - z), late_steps, b_sum, b_sum_depth, b_up, b_down,
            b_up_copy, b_down_copy, 6,
        )
        hops(
            crossed - HOP_LAG * z, crossed - HOP_LAG * (line - 1 - z), steps, a_sum, sum_depth, a_up, a_down,
            up_copy, down_copy, 4,
        )

        last = crossed - HOP_LAG * far

        @pl.when(active(last, steps))
        def _():
            total = result.at[pl.ds(last * EARLY, EARLY)]
            gather_hops(last, steps, a_sum, sum_depth, a_up, a_down, up_copy, down_copy, 4, a_keep)
            total[...] = a_keep[...].astype(bf16)
            pltpu.make_async_copy(total, out.at[pl.ds(last * EARLY, EARLY)], out_sem).start()

        arrived = step - HOP_LAG * far

        @pl.when(active(arrived, late_steps))
        def _():
            slot = lax.rem(arrived, DEPTH)

            @pl.when(arrived >= DEPTH)
            def _():
                b_cross_copy(arrived - DEPTH).wait_send()

            gather_hops(
                arrived, late_steps, b_sum, b_sum_depth, b_up, b_down, b_up_copy, b_down_copy, 6, b_keep.at[slot]
            )
            b_send[slot] = b_keep[slot, 1 - x].astype(bf16)
            take(3, arrived, DEPTH)
            b_cross_copy(arrived).start()

        paired = arrived - CROSS_LAG

        @pl.when(active(paired, late_steps))
        def _():
            slot = lax.rem(paired, DEPTH)
            b_cross_copy(paired).wait_recv()
            place = steps * EARLY + paired
            result[place] = (b_keep[slot, x] + b_cross[slot].astype(f32)).astype(bf16)

            @pl.when(paired < late_steps - DEPTH)
            def _():
                give(3, cross_peer)

            pltpu.make_async_copy(result.at[place], out.at[place], out_sem).start()

        return 0

    lag = HOP_LAG * (line - 1) + CROSS_LAG
    lax.fori_loop(0, max(steps, late_steps) + lag + 2, iteration, 0)
    for step in range(max(steps - DEPTH, 0), steps):
        cross_copy(step).wait_send()
    for step in range(max(late_steps - DEPTH, 0), late_steps):
        b_cross_copy(step).wait_send()
    pltpu.make_async_copy(result, out, out_sem).wait()


def run_sum_for_owners(grads, wide_count):
    line = wide_count // 4
    slots, block = grads.shape[0] // wide_count, grads.shape[1:]
    steps = (slots - 1) // (EARLY + 1)
    late_steps = slots - EARLY * steps
    sum_depth = CROSS_LAG + HOP_LAG * (line - 1) + 2
    b_sum_depth = HOP_LAG * (line - 1) + 2
    hop_depth = 2 * HOP_LAG + 2
    dma = pltpu.SemaphoreType.DMA

    def vmem(*shape):
        return pltpu.VMEM(shape + block, bf16)

    def wide_vmem(*shape):
        return pltpu.VMEM(shape + block, f32)

    return pl.pallas_call(
        functools.partial(sum_for_owners, line, steps, late_steps),
        out_shape=jax.ShapeDtypeStruct((slots,) + block, bf16),
        in_specs=[ANY_SPEC],
        out_specs=ANY_SPEC,
        scratch_shapes=[
            vmem(DEPTH, line, 2, EARLY),
            vmem(DEPTH, line, 2, EARLY),
            vmem(sum_depth, line, EARLY),
            wide_vmem(EARLY),
            vmem(DEPTH, line, EARLY),
            vmem(DEPTH, line, EARLY),
            vmem(hop_depth, line, EARLY),
            vmem(hop_depth, line, EARLY),
            vmem(DEPTH, line, 2),
            vmem(DEPTH, line, 2),
            vmem(b_sum_depth, line, 2),
            wide_vmem(DEPTH, 2),
            vmem(DEPTH),
            vmem(DEPTH),
            vmem(hop_depth, line, 2),
            vmem(hop_depth, line, 2),
            vmem(slots),
        ]
        + ([dma((DEPTH,))] * 5 + [dma((hop_depth, line))] * 4) * 2
        + [dma, pltpu.SemaphoreType.REGULAR((8,))],
        compiler_params=params(collective_id=0, has_side_effects=True),
        cost_estimate=pl.CostEstimate(flops=0, bytes_accessed=2 * grads.size * 8, transcendentals=0),
        name="sum_for_owners",
    )(grads.reshape((line, 2, 2, slots) + block))


def rope_tables(segment_row):
    token_index = jnp.arange(segment_row.shape[0], dtype=jnp.int32)
    changed = jnp.concatenate([jnp.ones((1,), dtype=bool), segment_row[1:] != segment_row[:-1]])
    begins = lax.cummax(jnp.where(changed, token_index, jnp.zeros_like(token_index)), axis=0)
    places = (token_index - begins).astype(f32)
    frequency = rope_base ** (-(jnp.arange(HEAD_DIM // 2, dtype=f32) * 2.0) / HEAD_DIM)
    angles = places[:, None] * frequency[None, :]
    cosine = jnp.concatenate([jnp.cos(angles), jnp.cos(angles)], axis=-1)
    sine_signed = jnp.concatenate([-jnp.sin(angles), jnp.sin(angles)], axis=-1)
    return (cosine, sine_signed)


def rms_parts(values):
    inverse = rms_inverse(values)
    return (inverse, values * inverse)


def norm_back(grad_scaled, normed, inverse):
    return inverse * (grad_scaled - normed * jnp.mean(grad_scaled * normed, axis=-1, keepdims=True))


def adam_small(param_now, gradient, first_now, second_now, rate_here):
    first_new = beta_first * first_now + (1.0 - beta_first) * gradient
    second_new = beta_second * second_now + (1.0 - beta_second) * gradient * gradient
    param_new = param_now - rate_here * (first_new / first_fix) / (
        jnp.sqrt(second_new / second_fix) + adam_eps
    )
    return (param_new, first_new, second_new)


def swap_halves(values):
    return lax.ppermute(values, "narrow", [(0, 1), (1, 0)])


def body(
    tokens,
    cotangent,
    segments,
    owner_list,
    masters,
    first_moment,
    second_moment,
    left_basis,
    right_basis,
    gains,
    gain_first,
    gain_second,
    biases,
    bias_first,
    bias_second,
):
    half = lax.axis_index("narrow")
    wide_index = lax.axis_index("wide")
    wide_count = lax.axis_size("wide")
    tokens_here = tokens.shape[0]
    slots_here = masters.shape[0]
    slots_half = owner_list.shape[0]
    gains_here = gains.shape[0]
    biases_here = biases.shape[1]

    def join_halves(own, other, axis=0):
        return jnp.where(
            half == 0, jnp.concatenate([own, other], axis=axis), jnp.concatenate([other, own], axis=axis)
        )

    masters_low, gains, biases = lax.optimization_barrier((masters.astype(bf16), gains, biases))
    weights = lax.all_gather(masters_low, "wide", axis=0, tiled=True)
    gain_full = lax.all_gather(gains, ("wide", "narrow"), axis=0, tiled=True).reshape(2, D)
    bias_full = lax.all_gather(biases.reshape(-1).astype(bf16), "wide", axis=0, tiled=True)
    bias_full = bias_full.astype(f32).reshape(1, QKV_WIDTH)
    pair_gains = 2 * gains_here

    position = jnp.arange(slots_half, dtype=jnp.int32)
    empty = owner_list == BLOCK_TOTAL
    number = jnp.where(empty, BLOCK_TOTAL - 1 + jnp.cumsum(empty.astype(jnp.int32)), owner_list)
    weight_rows = jnp.zeros((slots_half,), jnp.int32).at[number].set(position, unique_indices=True)
    rows = weight_rows + weight_rows // slots_here
    half_index = half.astype(jnp.int32).reshape(1)

    segment_row = lax.dynamic_index_in_dim(segments, wide_index, 0, keepdims=False)
    cosine, sine = rope_tables(segment_row)
    token_index = jnp.arange(segment_row.shape[0], dtype=jnp.int32)
    allowed_turned = (
        (segment_row[None, :] == segment_row[:, None]) & (token_index[None, :] >= token_index[:, None])
    ).astype(f32)
    tokens_row = join_halves(tokens, swap_halves(tokens))
    cotangent_row = join_halves(cotangent, swap_halves(cotangent))
    weights, tokens_row, cotangent_row, gain_full, bias_full = lax.optimization_barrier(
        (weights, tokens_row, cotangent_row, gain_full, bias_full)
    )

    low_part, high_part, normed_one_turned, qkv, mixed_turned, log_total = run_attention_forward(
        weight_rows, tokens_row, gain_full[0:1], bias_full, cosine, sine, allowed_turned, weights
    )
    low_other = swap_halves(low_part)
    active_grad = run_active_grads(weight_rows, cotangent_row, weights)
    high_sent, low_other = lax.optimization_barrier((high_part, low_other))
    high_other = swap_halves(high_sent)
    gain_two = gain_full[1:2]
    grad_low, resid_low, turned_low, gain_low, *hidden_low = run_hidden_grads(
        0, weight_rows, tokens_row, low_part, low_other, gain_two, active_grad, weights
    )
    grad_low_other = swap_halves(grad_low)
    grad_high, resid_high, turned_high, gain_high, *hidden_high = run_hidden_grads(
        tokens_here, weight_rows, tokens_row, high_part, high_other, gain_two, active_grad, weights
    )
    grad_high_other = swap_halves(grad_high)
    branch_own, branch_sent, grads = run_hidden_weight_grads(
        weight_rows, rows, half_index, cotangent_row, [(turned_low, *hidden_low), (turned_high, *hidden_high)], weights,
        wide_count * (slots_here + 1),
    )
    branch_other = swap_halves(branch_sent)
    grad_resid, grad_one_own, grad_one_sent, grads = run_attention_backward(
        weight_rows, rows, half_index, tokens_row, (resid_low, grad_low, grad_low_other),
        (resid_high, grad_high, grad_high_other), cotangent_row, gain_full, cosine, sine, allowed_turned,
        normed_one_turned, qkv, mixed_turned, log_total, (gain_low, gain_high), weights, grads, wide_count,
    )
    grad_one_other = swap_halves(grad_one_sent)
    resid_own = jnp.where(half == 0, resid_low, resid_high)
    output = (resid_own + branch_own.astype(f32) + branch_other.astype(f32)).astype(bf16)

    if wide_count == 16:
        reduced = run_sum_for_owners(grads, wide_count)
    else:
        reduced = lax.psum_scatter(grads, "wide", scatter_dimension=0, tiled=True)

    block_grad, new_masters, new_first, new_second = run_soap(
        reduced, masters, first_moment, second_moment, left_basis, right_basis
    )
    places = [small_places(owner, wide_count) for owner in range(wide_count)]
    gain_offset = jnp.asarray([place[1] for place in places], jnp.int32)[wide_index]
    bias_offset = jnp.asarray([place[3] for place in places], jnp.int32)[wide_index]
    small_sums = reduced[slots_here, :8].astype(f32)
    gain_sums = lax.dynamic_slice_in_dim(small_sums[:2].reshape(-1), gain_offset, pair_gains, 0)
    gain_sums = gain_sums.reshape(2, gains_here)
    gain_sums = gain_sums + swap_halves(gain_sums)
    gain_grad = lax.dynamic_index_in_dim(gain_sums, half, 0, keepdims=False)
    bias_grad = lax.dynamic_slice_in_dim(small_sums[2], bias_offset, biases_here, 0).reshape(biases.shape)
    new_gains, new_gain_first, new_gain_second = adam_small(gains, gain_grad, gain_first, gain_second, rate_gains)
    new_biases, new_bias_first, new_bias_second = adam_small(biases, bias_grad, bias_first, bias_second, rate_small)

    inverse_one, normed_one = rms_parts(tokens.astype(f32))
    grad_one = grad_one_own.astype(f32) + grad_one_other.astype(f32)
    input_grad = grad_resid + norm_back(grad_one * gain_full[0:1], normed_one, inverse_one)
    return (
        output,
        input_grad,
        block_grad,
        new_masters,
        new_first,
        new_second,
        gain_grad,
        new_gains,
        new_gain_first,
        new_gain_second,
        bias_grad,
        new_biases,
        new_bias_first,
        new_bias_second,
    )


def solution(mesh):
    tokens_spec = P(("wide", "narrow"), None)
    blocks_spec = P(("wide", "narrow"), None, None)
    gains_spec = P(("wide", "narrow"))
    bias_spec = P("narrow", "wide")
    in_specs = (
        (tokens_spec, tokens_spec, P(), P()) + (blocks_spec,) * 5 + (gains_spec,) * 3 + (bias_spec,) * 3
    )
    out_specs = (tokens_spec, tokens_spec) + (blocks_spec,) * 4 + (gains_spec,) * 4 + (bias_spec,) * 4
    return jax.shard_map(body, mesh=mesh, in_specs=in_specs, out_specs=out_specs, check_vma=False)
```

```python
import functools

import jax
import jax.numpy as jnp
from jax import lax
from jax.experimental import pallas as pl
from jax.experimental.pallas import tpu as pltpu
from jax.sharding import PartitionSpec as P

D = 1536
FF = 8960
HEADS = 12
KV_HEADS = 2
HEAD_DIM = 128
BLK = 128
STEP_COUNT = 5


beta_first = 0.95
beta_second = 0.95
adam_eps = 1e-08
rate_blocks = 0.03
rate_small = 0.4
rate_gains = 0.6
norm_eps = 1e-06
rope_base = 10000.0
masked_score = -1e30
first_fix = 1.0 - beta_first**STEP_COUNT
second_fix = 1.0 - beta_second**STEP_COUNT
scaling = HEAD_DIM ** (-0.5)

bf16 = jnp.bfloat16
f32 = jnp.float32

NARROW = 2
ROW_BLOCKS = D // BLK
QUERY_COLS = HEADS * HEAD_DIM // NARROW // BLK
PAIR_COLS = KV_HEADS * HEAD_DIM // NARROW // BLK
HIDDEN_COLS = FF // NARROW // BLK
QKV_COLS = QUERY_COLS + 2 * PAIR_COLS
QUERY_WIDTH = QUERY_COLS * BLK
QKV_WIDTH = QKV_COLS * BLK
KEY_BASE = ROW_BLOCKS * QUERY_COLS
VALUE_BASE = KEY_BASE + ROW_BLOCKS * PAIR_COLS
OUT_BASE = VALUE_BASE + ROW_BLOCKS * PAIR_COLS
GATE_BASE = OUT_BASE + QUERY_COLS * ROW_BLOCKS
UP_BASE = GATE_BASE + ROW_BLOCKS * HIDDEN_COLS
DOWN_BASE = UP_BASE + ROW_BLOCKS * HIDDEN_COLS
BLOCK_TOTAL = DOWN_BASE + HIDDEN_COLS * ROW_BLOCKS

TILE_BLOCKS = 6
TILES = -(-HIDDEN_COLS // TILE_BLOCKS)
LAST_BLOCKS = HIDDEN_COLS - (TILES - 1) * TILE_BLOCKS
TILE = TILE_BLOCKS * BLK
COLS = 256
ROWS = 64
SMALL_ROWS = 16
VMEM_LIMIT = 60 * 2**20
SUM_VMEM = 27 * 2**20
UPDATE_VMEM = 27 * 2**20

EARLY = 4
DEPTH = 3
CROSS_LAG = 2
HOP_LAG = 1
SUM_SCRATCH = 36

VMEM_SPEC = pl.BlockSpec(memory_space=pltpu.VMEM)
SMEM_SPEC = pl.BlockSpec(memory_space=pltpu.SMEM)
ANY_SPEC = pl.BlockSpec(memory_space=pl.ANY)


def spans(total, step):
    return [(begin, min(step, total - begin)) for begin in range(0, total, step)]


def dot_nn(left, right):
    return jnp.dot(left, right, preferred_element_type=f32)


def dot_nt(left, right):
    return lax.dot_general(left, right, (((1,), (1,)), ((), ())), preferred_element_type=f32)


def block_ref(ref, row_block, col_block):
    return ref.at[pl.ds(row_block * BLK, BLK), pl.ds(col_block * BLK, BLK)]


def fetch_piece(rows_ref, weights, target, base, pitch, row_blocks, col_blocks, first_col, sem):
    @pl.loop(0, row_blocks)
    def _(i):
        for j in range(col_blocks):
            pltpu.make_async_copy(
                weights.at[rows_ref[base + i * pitch + j]],
                block_ref(target, i, first_col + j),
                sem,
            ).start()


def store_piece(rows_ref, source, grads, base, pitch, row_blocks, col_blocks, first_col, sem):
    @pl.loop(0, row_blocks)
    def _(i):
        for j in range(col_blocks):
            pltpu.make_async_copy(
                block_ref(source, i, first_col + j),
                grads.at[rows_ref[base + i * pitch + j]],
                sem,
            ).start()


def wait_bytes(ref, sem):
    pltpu.make_async_copy(ref, ref, sem).wait()


def fetch_attention(rows_ref, weights, w_qkv, w_out, sems):
    fetch_piece(rows_ref, weights, w_qkv, 0, QUERY_COLS, ROW_BLOCKS, QUERY_COLS, 0, sems.at[0])
    fetch_piece(rows_ref, weights, w_qkv, KEY_BASE, PAIR_COLS, ROW_BLOCKS, PAIR_COLS, QUERY_COLS, sems.at[0])
    fetch_piece(
        rows_ref, weights, w_qkv, VALUE_BASE, PAIR_COLS, ROW_BLOCKS, PAIR_COLS, QUERY_COLS + PAIR_COLS, sems.at[0]
    )
    fetch_piece(rows_ref, weights, w_out, OUT_BASE, ROW_BLOCKS, QUERY_COLS, ROW_BLOCKS, 0, sems.at[1])


def rms_inverse(values):
    return lax.rsqrt(jnp.mean(values * values, axis=-1, keepdims=True) + norm_eps)


def row_chunks(total, step, run):
    @pl.loop(0, total // step)
    def _(chunk):
        run(pl.ds(pl.multiple_of(chunk * step, step), step))


def small_places(owner, wide_count):
    gain_first = owner * (2 * D // wide_count)
    bias_first = owner * (QKV_WIDTH // wide_count)
    gain_row = min(gain_first // BLK, 2 * D // BLK - 2)
    return (gain_row, gain_first - gain_row * BLK, bias_first // BLK, bias_first % BLK)


def scores_turned(keys, queries, allowed):
    return jnp.where(allowed, dot_nt(keys, queries) * scaling, masked_score)


def attention_forward(
    rows_ref,
    x_ref,
    gain_ref,
    bias_ref,
    cos_ref,
    sin_ref,
    allowed_ref,
    weights,
    part_low_ref,
    part_high_ref,
    normed_turned_ref,
    qkv_ref,
    mixed_turned_ref,
    log_ref,
    w_qkv,
    w_out,
    normed,
    mixed,
    sems,
):
    fetch_attention(rows_ref, weights, w_qkv, w_out, sems)
    length = x_ref.shape[0]

    def norm_rows(rows):
        values = x_ref[rows, :].astype(f32)
        normed[rows, :] = (values * rms_inverse(values) * gain_ref[...]).astype(bf16)

    row_chunks(length, ROWS, norm_rows)
    for begin, size in spans(D, COLS):
        normed_turned_ref[pl.ds(begin, size), :] = normed[:, pl.ds(begin, size)].T
    wait_bytes(w_qkv, sems.at[0])
    for begin, size in spans(QKV_WIDTH, COLS):
        products = dot_nn(normed[...], w_qkv[:, pl.ds(begin, size)]) + bias_ref[:, pl.ds(begin, size)]
        for offset, width in spans(size, HEAD_DIM):
            head = products[:, offset : offset + width]
            if begin + offset < QUERY_WIDTH + PAIR_COLS * BLK:
                head = head * cos_ref[...] + pltpu.roll(head, HEAD_DIM // 2, 1) * sin_ref[...]
            qkv_ref[:, pl.ds(begin + offset, width)] = head.astype(bf16)
    keys = qkv_ref[:, pl.ds(QUERY_WIDTH, HEAD_DIM)]
    values_turned = qkv_ref[:, pl.ds(QUERY_WIDTH + HEAD_DIM, HEAD_DIM)].T
    for head in range(QUERY_COLS):
        columns = pl.ds(head * HEAD_DIM, HEAD_DIM)
        scores = scores_turned(keys, qkv_ref[:, columns], allowed_ref[...] > 0)
        peak = jnp.max(scores, axis=0, keepdims=True)
        expo = jnp.exp(scores - peak)
        total = jnp.sum(expo, axis=0, keepdims=True)
        log_ref[pl.ds(head, 1), :] = peak + jnp.log(total)
        probs = (expo / total).astype(bf16)
        mixed_head = dot_nn(values_turned, probs).astype(bf16)
        mixed_turned_ref[columns, :] = mixed_head
        mixed[:, columns] = mixed_head.T
    wait_bytes(w_out, sems.at[1])
    for part_ref, first in ((part_low_ref, 0), (part_high_ref, length // NARROW)):
        for begin, size in spans(D, COLS):
            part_ref[:, pl.ds(begin, size)] = dot_nn(
                mixed[pl.ds(first, length // NARROW), :], w_out[:, pl.ds(begin, size)]
            ).astype(bf16)


def pair_copies(rows_ref, blocks_hbm, pair, sem, column, place, outward=False):
    return [
        block_copy(blocks_hbm.at[rows_ref[base + i * HIDDEN_COLS + column]], block_ref(pair, i, which), sem, outward)
        for i in range(ROW_BLOCKS)
        for base, which in ((GATE_BASE, 2 * place), (UP_BASE, 2 * place + 1))
    ]


def down_copies(rows_ref, blocks_hbm, down, sem, column, place, outward=False):
    return [
        block_copy(blocks_hbm.at[rows_ref[DOWN_BASE + column * ROW_BLOCKS + i]], block_ref(down, place, i), sem, outward)
        for i in range(ROW_BLOCKS)
    ]


def block_copy(in_hbm, in_vmem, sem, outward):
    return pltpu.make_async_copy(*((in_vmem, in_hbm) if outward else (in_hbm, in_vmem)), sem)


def start_all(copies):
    for copy in copies:
        copy.start()


def half_rows(half_ref, length):
    begin = pl.multiple_of(half_ref[0] * length, length)
    return (pl.ds(begin, length), pl.ds(pl.multiple_of(length - begin, length), length))


def hidden_column(tile, place):
    return jnp.minimum(tile * TILE_BLOCKS + place, HIDDEN_COLS - 1)


def hidden_tiles(run):
    @pl.loop(0, TILES - 1)
    def _(tile):
        run(tile, lax.rem(tile, 2), TILE_BLOCKS, True)

    run(TILES - 1, (TILES - 1) % 2, LAST_BLOCKS, False)


def active_grads(rows_ref, cot_ref, weights, out, w_down, stage, load_sems, store_sems):
    def fetch(tile, slot, place):
        start_all(
            down_copies(rows_ref, weights, w_down.at[slot], load_sems.at[slot], hidden_column(tile, place), place)
        )

    for place in range(TILE_BLOCKS):
        fetch(0, 0, place)

    def run(tile, slot, blocks, more):
        wait_bytes(w_down.at[slot], load_sems.at[slot])

        @pl.when(tile >= 2)
        def _():
            wait_bytes(stage.at[slot], store_sems.at[slot])

        if more:
            for place in range(TILE_BLOCKS):
                fetch(tile + 1, 1 - slot, place)
        for begin, size in spans(blocks * BLK, COLS):
            stage[slot, :, pl.ds(begin, size)] = dot_nt(cot_ref[...], w_down[slot, pl.ds(begin, size), :])
        pltpu.make_async_copy(stage.at[slot], out.at[tile], store_sems.at[slot]).start()

    hidden_tiles(run)
    for tile in range(max(TILES - 2, 0), TILES):
        wait_bytes(stage.at[tile % 2], store_sems.at[tile % 2])


def hidden_grads(
    first_row,
    rows_ref,
    x_ref,
    own_ref,
    other_ref,
    gain_ref,
    active_grad,
    weights,
    grad_ref,
    resid_ref,
    normed_turned_ref,
    gain_part_ref,
    pair_grads,
    active,
    active_turned,
    w_pair,
    grad_active,
    straight,
    turned,
    grads,
    normed,
    grad_sum,
    load_sems,
    store_sems,
):
    length = own_ref.shape[0]

    def fetch(tile, slot, place):
        start_all(
            pair_copies(rows_ref, weights, w_pair.at[slot], load_sems.at[slot, 0], hidden_column(tile, place), place)
        )

    def load_grad(tile, slot):
        return pltpu.make_async_copy(active_grad.at[tile, pl.ds(first_row, length)], grad_active.at[slot], load_sems.at[slot, 1])

    def stores(tile, slot):
        return (
            pltpu.make_async_copy(turned.at[slot], active_turned.at[tile], store_sems.at[slot, 0]),
            pltpu.make_async_copy(grads.at[slot], pair_grads.at[tile], store_sems.at[slot, 1]),
            pltpu.make_async_copy(straight.at[slot], active.at[tile], store_sems.at[slot, 2]),
        )

    for place in range(TILE_BLOCKS):
        fetch(0, 0, place)
    load_grad(0, 0).start()

    def norm_rows(rows):
        tokens = x_ref[pl.ds(rows.start + first_row, rows.size), :]
        values = tokens.astype(f32) + own_ref[rows, :].astype(f32) + other_ref[rows, :].astype(f32)
        resid_ref[rows, :] = values
        normed[rows, :] = (values * rms_inverse(values) * gain_ref[...]).astype(bf16)

    row_chunks(length, ROWS, norm_rows)
    grad_sum[...] = jnp.zeros_like(grad_sum)

    def run(tile, slot, blocks, more):
        wait_bytes(w_pair.at[slot], load_sems.at[slot, 0])
        load_grad(tile, slot).wait()
        if more:
            load_grad(tile + 1, 1 - slot).start()

        @pl.when(tile >= 2)
        def _():
            for copy in stores(tile - 2, slot):
                copy.wait()

        for place in range(blocks):
            columns = pl.ds(place * BLK, BLK)
            pair = dot_nn(normed[...], w_pair[slot, :, pl.ds(2 * place * BLK, 2 * BLK)])
            gate = pair[:, :BLK]
            upper = pair[:, BLK:]
            grad = grad_active[slot, :, columns]
            sigmoid = jax.nn.sigmoid(gate)
            silu = gate * sigmoid
            active_here = (silu * upper).astype(bf16)
            straight[slot, :, columns] = active_here
            turned[slot, columns, :] = active_here.T
            grads[slot, :, pl.ds(2 * place * BLK, BLK)] = (
                grad * upper * sigmoid * (1.0 + gate * (1.0 - sigmoid))
            ).astype(bf16)
            grads[slot, :, pl.ds((2 * place + 1) * BLK, BLK)] = (grad * silu).astype(bf16)
            if more:
                fetch(tile + 1, 1 - slot, place)
        if more:
            for place in range(blocks, TILE_BLOCKS):
                fetch(tile + 1, 1 - slot, place)
        turn = pl.ds(pl.multiple_of(tile * COLS, COLS), COLS)
        normed_turned_ref[turn, :] = normed[:, turn].T
        width = 2 * blocks * BLK
        for begin, size in spans(D, COLS):
            columns = pl.ds(begin, size)
            grad_sum[:, columns] += dot_nt(grads[slot, :, :width], w_pair[slot, columns, :width])
        start_all(stores(tile, slot))

    hidden_tiles(run)
    grad_ref[...] = grad_sum[...].astype(bf16)
    gain_part_ref[...] = jnp.zeros_like(gain_part_ref)

    def gain_rows(rows):
        values = resid_ref[rows, :]
        gain_part_ref[...] += jnp.sum(grad_sum[rows, :] * values * rms_inverse(values), axis=0, keepdims=True)

    row_chunks(length, ROWS, gain_rows)
    for tile in range(max(TILES - 2, 0), TILES):
        for copy in stores(tile, tile % 2):
            copy.wait()


def hidden_weight_grads(
    weight_rows_ref, rows_ref, half_ref, cot_ref, *refs
):
    parts, (weights, branch_own_ref, branch_other_ref, grads), scratch = refs[: 4 * NARROW], refs[8:12], refs[12:]
    normed_turned, pair, straight, turned, w_down, branch_sum, pair_stage, down_stage, load_sems, store_sems, sems = scratch
    length = cot_ref.shape[0] // NARROW

    def loads(tile, slot):
        copies = []
        for part in range(NARROW):
            pair_grads, active, active_turned = parts[part * 4 + 1 : part * 4 + 4]
            tokens = pl.ds(part * length, length)
            copies += [
                pltpu.make_async_copy(pair_grads.at[tile], pair.at[slot, tokens], load_sems.at[slot, part * 3]),
                pltpu.make_async_copy(active.at[tile], straight.at[slot, tokens], load_sems.at[slot, part * 3 + 1]),
                pltpu.make_async_copy(
                    active_turned.at[tile], turned.at[slot, :, tokens], load_sems.at[slot, part * 3 + 2]
                ),
            ]
        return copies

    def fetch(tile, slot, place):
        start_all(
            down_copies(
                weight_rows_ref, weights, w_down.at[slot], load_sems.at[slot, 3 * NARROW], hidden_column(tile, place), place
            )
        )

    def drain(slot, blocks):
        wait_bytes(pair_stage.at[slot, :, pl.ds(0, 2 * blocks * BLK)], store_sems.at[slot, 0])
        wait_bytes(down_stage.at[slot, pl.ds(0, blocks * BLK)], store_sems.at[slot, 1])

    turned_loads = [
        pltpu.make_async_copy(parts[part * 4], normed_turned.at[:, pl.ds(part * length, length)], sems.at[part])
        for part in range(NARROW)
    ]
    start_all(loads(0, 0) + turned_loads)
    for place in range(TILE_BLOCKS):
        fetch(0, 0, place)
    branch_sum[...] = jnp.zeros_like(branch_sum)
    for copy in turned_loads:
        copy.wait()

    def run(tile, slot, blocks, more):
        for copy in loads(tile, slot):
            copy.wait()
        wait_bytes(w_down.at[slot], load_sems.at[slot, 3 * NARROW])
        if more:
            start_all(loads(tile + 1, 1 - slot))

        @pl.when(tile >= 2)
        def _():
            drain(slot, TILE_BLOCKS)

        width = blocks * BLK
        down = turned[slot, pl.ds(0, width), :]
        for begin, size in spans(D, COLS):
            columns = pl.ds(begin, size)
            down_stage[slot, pl.ds(0, width), columns] = dot_nn(down, cot_ref[:, columns]).astype(bf16)
        for place in range(blocks):
            column = tile * TILE_BLOCKS + place
            start_all(
                down_copies(rows_ref, grads, down_stage.at[slot], store_sems.at[slot, 1], column, place, outward=True)
            )
            columns = pl.ds(2 * place * BLK, 2 * BLK)
            for begin, size in spans(D, 512):
                pair_stage[slot, pl.ds(begin, size), columns] = dot_nn(
                    normed_turned[pl.ds(begin, size), :], pair[slot, :, columns]
                ).astype(bf16)
            start_all(
                pair_copies(rows_ref, grads, pair_stage.at[slot], store_sems.at[slot, 0], column, place, outward=True)
            )
            if more:
                fetch(tile + 1, 1 - slot, place)
        if more:
            for place in range(blocks, TILE_BLOCKS):
                fetch(tile + 1, 1 - slot, place)
        for begin, size in spans(D, COLS):
            columns = pl.ds(begin, size)
            branch_sum[:, columns] += dot_nn(straight[slot, :, :width], w_down[slot, :width, columns])

    hidden_tiles(run)
    own, other = half_rows(half_ref, length)
    branch_own_ref[...] = branch_sum[own, :].astype(bf16)
    branch_other_ref[...] = branch_sum[other, :].astype(bf16)
    if TILES > 1:
        drain((TILES - 2) % 2, TILE_BLOCKS)
    drain((TILES - 1) % 2, LAST_BLOCKS)


def attention_backward(
    weight_rows_ref,
    rows_ref,
    half_ref,
    x_ref,
    resid_low_ref,
    own_low_ref,
    other_low_ref,
    resid_high_ref,
    own_high_ref,
    other_high_ref,
    cot_ref,
    gain_ref,
    cos_ref,
    sin_ref,
    allowed_ref,
    normed_turned_ref,
    qkv_ref,
    mixed_turned_ref,
    log_ref,
    gain_two_low_ref,
    gain_two_high_ref,
    weights,
    grads_in,
    grad_resid_ref,
    grad_own_ref,
    grad_other_ref,
    grads,
    w_qkv,
    w_out,
    grad_resid,
    grad_attention,
    grad_mixed,
    grad_qkv,
    grad_sum,
    gain_part,
    bias_part,
    qkv_stage,
    out_stage,
    small_stage,
    blank,
    load_sems,
    store_sems,
):
    del grads_in
    wide_count = small_stage.shape[0]
    owner_rows = grads.shape[0] // wide_count
    small_stage[...] = jnp.zeros_like(small_stage)
    fetch_attention(weight_rows_ref, weights, w_qkv, w_out, load_sems)
    length = x_ref.shape[0]
    empty_count = rows_ref.shape[0] - BLOCK_TOTAL
    blank[...] = jnp.zeros_like(blank)
    for index in range(empty_count):
        pltpu.make_async_copy(blank.at[index], grads.at[rows_ref[BLOCK_TOTAL + index]], store_sems.at[2]).start()

    part = length // NARROW
    own_rows, other_rows = half_rows(half_ref, part)
    for first, resid_ref, own_ref, other_ref in (
        (0, resid_low_ref, own_low_ref, other_low_ref),
        (part, resid_high_ref, own_high_ref, other_high_ref),
    ):

        def resid_rows(rows, first=first, resid_ref=resid_ref, own_ref=own_ref, other_ref=other_ref):
            values = resid_ref[rows, :]
            inverse = rms_inverse(values)
            normed = values * inverse
            scaled = (own_ref[rows, :].astype(f32) + other_ref[rows, :].astype(f32)) * gain_ref[1:2, :]
            place = pl.ds(rows.start + first, rows.size)
            total = cot_ref[place, :].astype(f32) + inverse * (
                scaled - normed * jnp.mean(scaled * normed, axis=-1, keepdims=True)
            )
            grad_resid[place, :] = total
            grad_attention[place, :] = total.astype(bf16)

        row_chunks(part, ROWS, resid_rows)
    grad_resid_ref[...] = grad_resid[own_rows, :]
    wait_bytes(w_out, load_sems.at[1])
    for begin, size in spans(QUERY_WIDTH, COLS):
        grad_mixed[:, pl.ds(begin, size)] = dot_nt(grad_attention[...], w_out[pl.ds(begin, size), :]).astype(bf16)
    keys = qkv_ref[:, pl.ds(QUERY_WIDTH, HEAD_DIM)]
    keys_turned = keys.T
    values = qkv_ref[:, pl.ds(QUERY_WIDTH + HEAD_DIM, HEAD_DIM)]

    def rope_back(vector):
        return vector * cos_ref[...] - pltpu.roll(vector, HEAD_DIM // 2, 1) * sin_ref[...]

    grad_keys = jnp.zeros((length, HEAD_DIM), f32)
    grad_values = jnp.zeros((length, HEAD_DIM), f32)
    for head in range(QUERY_COLS):
        columns = pl.ds(head * HEAD_DIM, HEAD_DIM)
        queries = qkv_ref[:, columns]
        scores = scores_turned(keys, queries, allowed_ref[...] > 0)
        probs = jnp.exp(scores - log_ref[pl.ds(head, 1), :])
        grad_values += dot_nn(probs.astype(bf16), grad_mixed[:, columns])
        grad_probs = dot_nt(values, grad_mixed[:, columns])
        row_dot = jnp.sum(probs * grad_probs, axis=0, keepdims=True)
        grad_scores = (probs * (grad_probs - row_dot)).astype(bf16)
        grad_keys += dot_nn(grad_scores, queries)
        grad_queries = dot_nn(keys_turned, grad_scores).T * scaling
        grad_qkv[:, columns] = rope_back(grad_queries).astype(bf16)
    grad_qkv[:, pl.ds(QUERY_WIDTH, HEAD_DIM)] = rope_back(grad_keys * scaling).astype(bf16)
    grad_qkv[:, pl.ds(QUERY_WIDTH + HEAD_DIM, HEAD_DIM)] = grad_values.astype(bf16)

    for begin, size in spans(D, COLS):
        out_stage[:, pl.ds(begin, size)] = dot_nn(
            mixed_turned_ref[...], grad_attention[:, pl.ds(begin, size)]
        ).astype(bf16)
    store_piece(rows_ref, out_stage, grads, OUT_BASE, ROW_BLOCKS, QUERY_COLS, ROW_BLOCKS, 0, store_sems.at[1])
    for begin, size in spans(QKV_WIDTH, COLS):
        qkv_stage[:, pl.ds(begin, size)] = dot_nn(
            normed_turned_ref[...], grad_qkv[:, pl.ds(begin, size)]
        ).astype(bf16)
    store_piece(rows_ref, qkv_stage, grads, 0, QUERY_COLS, ROW_BLOCKS, QUERY_COLS, 0, store_sems.at[0])
    store_piece(rows_ref, qkv_stage, grads, KEY_BASE, PAIR_COLS, ROW_BLOCKS, PAIR_COLS, QUERY_COLS, store_sems.at[0])
    store_piece(
        rows_ref, qkv_stage, grads, VALUE_BASE, PAIR_COLS, ROW_BLOCKS, PAIR_COLS, QUERY_COLS + PAIR_COLS, store_sems.at[0]
    )
    wait_bytes(w_qkv, load_sems.at[0])
    for begin, size in spans(D, COLS):
        grad_sum[:, pl.ds(begin, size)] = dot_nt(grad_qkv[...], w_qkv[pl.ds(begin, size), :])
    grad_own_ref[...] = grad_sum[own_rows, :].astype(bf16)
    grad_other_ref[...] = grad_sum[other_rows, :].astype(bf16)
    gain_part[...] = jnp.zeros_like(gain_part)
    bias_part[...] = jnp.zeros_like(bias_part)

    def gain_rows(rows):
        tokens = x_ref[rows, :].astype(f32)
        gain_part[...] += jnp.sum(grad_sum[rows, :] * tokens * rms_inverse(tokens), axis=0, keepdims=True)
        bias_part[...] += jnp.sum(grad_qkv[rows, :].astype(f32), axis=0, keepdims=True)

    row_chunks(length, ROWS, gain_rows)
    for owner in range(wide_count):
        gain_row, bias_row = small_places(owner, wide_count)[::2]
        small_rows = []
        for row in (gain_row, gain_row + 1):
            columns = pl.ds(row % (D // BLK) * BLK, BLK)
            if row < D // BLK:
                small_rows.append(gain_part[:, columns])
            else:
                small_rows.append(gain_two_low_ref[:, columns] + gain_two_high_ref[:, columns])
        small_rows.append(bias_part[:, pl.ds(bias_row * BLK, BLK)])
        small_rows.append(jnp.zeros((SMALL_ROWS - len(small_rows), BLK), f32))
        small_stage[owner, pl.ds(0, SMALL_ROWS), :] = jnp.concatenate(small_rows, axis=0).astype(bf16)
        pltpu.make_async_copy(
            small_stage.at[owner], grads.at[owner * owner_rows + owner_rows - 1], store_sems.at[3]
        ).start()
    wait_bytes(small_stage, store_sems.at[3])
    wait_bytes(qkv_stage, store_sems.at[0])
    wait_bytes(out_stage, store_sems.at[1])
    if empty_count > 0:
        wait_bytes(blank.at[pl.ds(0, empty_count)], store_sems.at[2])


def soap_update(
    grad_in,
    masters_ref,
    first_ref,
    second_ref,
    left_ref,
    right_ref,
    grad_out,
    masters_out,
    first_out,
    second_out,
    small_ref,
    grad_stage,
    masters_stage,
    first_stage,
    second_stage,
    sems,
):
    group = grad_stage.shape[1]
    outputs = (
        (grad_stage, grad_out), (masters_stage, masters_out), (first_stage, first_out), (second_stage, second_out)
    )
    steps = masters_ref.shape[0] // group
    small_ref[...] = grad_in[masters_ref.shape[0], :SMALL_ROWS].astype(f32)

    def stores(step):
        slot = lax.rem(step, 2)
        places = pl.ds(step * group, group)
        return [
            pltpu.make_async_copy(stage.at[slot], out.at[places], sems.at[slot, index])
            for index, (stage, out) in enumerate(outputs)
        ]

    @pl.loop(0, steps)
    def _(step):
        @pl.when(step >= 2)
        def _():
            for copy in stores(step - 2):
                copy.wait()

        soap_group(
            step * group, lax.rem(step, 2), grad_in, masters_ref, first_ref, second_ref, left_ref, right_ref,
            *[stage for stage, _ in outputs],
        )
        start_all(stores(step))

    for step in range(max(steps - 2, 0), steps):
        for copy in stores(step):
            copy.wait()


def soap_group(
    first_block, slot, grad_in, masters_ref, first_ref, second_ref, left_ref, right_ref,
    grad_stage, masters_stage, first_stage, second_stage,
):
    places = range(grad_stage.shape[1])
    blocks = [first_block + place for place in places]
    rights = [right_ref[block].astype(bf16) for block in blocks]
    products = [dot_nn(grad_in[blocks[place]], rights[place]).astype(bf16) for place in places]
    lefts = [left_ref[block].astype(bf16) for block in blocks]
    rotated_blocks = [dot_nn(lefts[place].T, products[place]) for place in places]
    normalized = []
    for place, block in enumerate(blocks):
        rotated = rotated_blocks[place]
        grad_stage[slot, place] = grad_in[block].astype(f32)
        new_first = beta_first * first_ref[block] + (1.0 - beta_first) * rotated
        new_second = beta_second * second_ref[block] + (1.0 - beta_second) * rotated * rotated
        first_stage[slot, place] = new_first
        second_stage[slot, place] = new_second
        normalized.append(
            (new_first / first_fix / (jnp.sqrt(new_second / second_fix) + adam_eps)).astype(bf16)
        )
    products = [dot_nt(normalized[place], rights[place]).astype(bf16) for place in places]
    for place, block in enumerate(blocks):
        masters_stage[slot, place] = masters_ref[block] - rate_blocks * dot_nn(lefts[place], products[place])


def params(limit=VMEM_LIMIT, **options):
    return pltpu.CompilerParams(vmem_limit_bytes=limit, **options)


def run_attention_forward(rows, x, gain, bias, cosine, sine, allowed, weights):
    length = x.shape[0]
    shape = jax.ShapeDtypeStruct
    return pl.pallas_call(
        attention_forward,
        out_shape=[
            shape((length // NARROW, D), bf16),
            shape((length // NARROW, D), bf16),
            shape((D, length), bf16),
            shape((length, QKV_WIDTH), bf16),
            shape((QUERY_WIDTH, length), bf16),
            shape((8, length), f32),
        ],
        in_specs=[SMEM_SPEC] + [VMEM_SPEC] * 6 + [ANY_SPEC],
        out_specs=[VMEM_SPEC] * 6,
        scratch_shapes=[
            pltpu.VMEM((D, QKV_WIDTH), bf16),
            pltpu.VMEM((QUERY_WIDTH, D), bf16),
            pltpu.VMEM((length, D), bf16),
            pltpu.VMEM((length, QUERY_WIDTH), bf16),
            pltpu.SemaphoreType.DMA((2,)),
        ],
        compiler_params=params(),
        name="attention_forward",
    )(rows, x, gain, bias, cosine, sine, allowed, weights)


def hidden_cost(length, products, bytes_moved):
    return pl.CostEstimate(
        flops=2 * products * length * D * TILE * TILES, bytes_accessed=bytes_moved, transcendentals=0
    )


def run_active_grads(rows, cotangent, weights):
    length = cotangent.shape[0]
    return pl.pallas_call(
        active_grads,
        out_shape=jax.ShapeDtypeStruct((TILES, length, TILE), f32),
        in_specs=[SMEM_SPEC, VMEM_SPEC, ANY_SPEC],
        out_specs=ANY_SPEC,
        scratch_shapes=[
            pltpu.VMEM((2, TILE, D), bf16),
            pltpu.VMEM((2, length, TILE), f32),
            pltpu.SemaphoreType.DMA((2,)),
            pltpu.SemaphoreType.DMA((2,)),
        ],
        compiler_params=params(),
        cost_estimate=hidden_cost(length, 1, TILES * TILE * (2 * D + 4 * length)),
        name="active_grads",
    )(rows, cotangent, weights)


def run_hidden_grads(first_row, rows, x, own, other, gain, active_grad, weights):
    length = own.shape[0]
    shape = jax.ShapeDtypeStruct
    return pl.pallas_call(
        functools.partial(hidden_grads, first_row),
        out_shape=[
            shape((length, D), bf16),
            shape((length, D), f32),
            shape((D, length), bf16),
            shape((1, D), f32),
            shape((TILES, length, 2 * TILE), bf16),
            shape((TILES, length, TILE), bf16),
            shape((TILES, TILE, length), bf16),
        ],
        in_specs=[SMEM_SPEC] + [VMEM_SPEC] * 4 + [ANY_SPEC] * 2,
        out_specs=[VMEM_SPEC] * 4 + [ANY_SPEC] * 3,
        scratch_shapes=[
            pltpu.VMEM((2, D, 2 * TILE), bf16),
            pltpu.VMEM((2, length, TILE), f32),
            pltpu.VMEM((2, length, TILE), bf16),
            pltpu.VMEM((2, TILE, length), bf16),
            pltpu.VMEM((2, length, 2 * TILE), bf16),
            pltpu.VMEM((length, D), bf16),
            pltpu.VMEM((length, D), f32),
            pltpu.SemaphoreType.DMA((2, 2)),
            pltpu.SemaphoreType.DMA((2, 3)),
        ],
        compiler_params=params(),
        cost_estimate=hidden_cost(length, 4, 2 * TILES * TILE * (2 * D + 6 * length)),
        name="hidden_grads",
    )(rows, x, own, other, gain, active_grad, weights)


def run_hidden_weight_grads(weight_rows, rows, half, cotangent, parts, weights, slots):
    length = cotangent.shape[0]
    shape = jax.ShapeDtypeStruct
    return pl.pallas_call(
        hidden_weight_grads,
        out_shape=[shape((length // NARROW, D), bf16)] * 2 + [shape((slots, BLK, BLK), bf16)],
        in_specs=[SMEM_SPEC] * 3 + [VMEM_SPEC] + [ANY_SPEC] * (4 * NARROW + 1),
        out_specs=[VMEM_SPEC, VMEM_SPEC, ANY_SPEC],
        scratch_shapes=[
            pltpu.VMEM((D, length), bf16),
            pltpu.VMEM((2, length, 2 * TILE), bf16),
            pltpu.VMEM((2, length, TILE), bf16),
            pltpu.VMEM((2, TILE, length), bf16),
            pltpu.VMEM((2, TILE, D), bf16),
            pltpu.VMEM((length, D), f32),
            pltpu.VMEM((2, D, 2 * TILE), bf16),
            pltpu.VMEM((2, TILE, D), bf16),
            pltpu.SemaphoreType.DMA((2, 3 * NARROW + 1)),
            pltpu.SemaphoreType.DMA((2, 2)),
            pltpu.SemaphoreType.DMA((NARROW,)),
        ],
        compiler_params=params(),
        cost_estimate=hidden_cost(length, 4, 2 * TILES * TILE * (4 * D + 4 * length)),
        name="hidden_weight_grads",
    )(weight_rows, rows, half, cotangent, *[array for part in parts for array in part], weights)


def run_attention_backward(
    weight_rows, rows, half, x, low, high, cotangent, gains, cosine, sine, allowed, normed_turned, qkv, mixed_turned,
    log_total, gain_two_parts, weights, grads, wide_count,
):
    length = x.shape[0]
    shape = jax.ShapeDtypeStruct
    empty_count = max(rows.shape[0] - BLOCK_TOTAL, 1)
    operands = (
        weight_rows, rows, half, x, *low, *high, cotangent, gains, cosine, sine, allowed, normed_turned, qkv, mixed_turned,
        log_total, *gain_two_parts, weights, grads,
    )
    return pl.pallas_call(
        attention_backward,
        out_shape=[
            shape((length // NARROW, D), f32),
            shape((length // NARROW, D), bf16),
            shape((length // NARROW, D), bf16),
            shape(grads.shape, bf16),
        ],
        in_specs=[SMEM_SPEC] * 3 + [VMEM_SPEC] * (len(operands) - 5) + [ANY_SPEC] * 2,
        out_specs=[VMEM_SPEC] * 3 + [ANY_SPEC],
        input_output_aliases={len(operands) - 1: 3},
        scratch_shapes=[
            pltpu.VMEM((D, QKV_WIDTH), bf16),
            pltpu.VMEM((QUERY_WIDTH, D), bf16),
            pltpu.VMEM((length, D), f32),
            pltpu.VMEM((length, D), bf16),
            pltpu.VMEM((length, QUERY_WIDTH), bf16),
            pltpu.VMEM((length, QKV_WIDTH), bf16),
            pltpu.VMEM((length, D), f32),
            pltpu.VMEM((1, D), f32),
            pltpu.VMEM((1, QKV_WIDTH), f32),
            pltpu.VMEM((D, QKV_WIDTH), bf16),
            pltpu.VMEM((QUERY_WIDTH, D), bf16),
            pltpu.VMEM((wide_count, BLK, BLK), bf16),
            pltpu.VMEM((empty_count, BLK, BLK), bf16),
            pltpu.SemaphoreType.DMA((2,)),
            pltpu.SemaphoreType.DMA((4,)),
        ],
        compiler_params=params(),
        name="attention_backward",
    )(*operands)


def run_soap(reduced, masters, first_moment, second_moment, left_basis, right_basis):
    slots = masters.shape[0]
    group = max(size for size in range(1, 11) if slots % size == 0)
    shape = jax.ShapeDtypeStruct(masters.shape, f32)
    return pl.pallas_call(
        soap_update,
        out_shape=[shape] * 4 + [jax.ShapeDtypeStruct((SMALL_ROWS, BLK), f32)],
        in_specs=[VMEM_SPEC] * 6,
        out_specs=[ANY_SPEC] * 4 + [VMEM_SPEC],
        scratch_shapes=[pltpu.VMEM((2, group, BLK, BLK), f32)] * 4 + [pltpu.SemaphoreType.DMA((2, 4))],
        compiler_params=params(UPDATE_VMEM),
        name="soap_update",
    )(reduced, masters, first_moment, second_moment, left_basis, right_basis)


def sum_for_owners(
    line, steps, late_steps, grads, *refs
):
    held = len(refs[: -SUM_SCRATCH]) // 2
    sources, (out, *targets), scratch = refs[:held], refs[held:-SUM_SCRATCH], refs[-SUM_SCRATCH:]
    (
        a_in, a_own, a_sum, a_keep, a_send, a_cross, a_up, a_down, b_in, b_own, b_sum, b_keep, b_send,
        b_cross, b_up, b_down, core_send, core_recv, own_sems, cross_send, cross_recv, up_send, up_recv,
        down_send, down_recv, b_core_send, b_core_recv, b_own_sems, b_cross_send, b_cross_recv, b_up_send,
        b_up_recv, b_down_send, b_down_recv, held_sems, credits,
    ) = scratch
    wide = lax.axis_index("wide")
    narrow = lax.axis_index("narrow")
    z = wide // 4
    x = lax.rem(wide // 2, 2)
    core = lax.rem(wide, 2)
    mesh_id = pl.DeviceIdType.MESH
    core_peer = (wide + 1 - 2 * core, narrow)
    cross_peer = (wide + 2 - 4 * x, narrow)
    upper = (lax.rem(wide + 4, 4 * line), narrow)
    lower = (lax.rem(wide + 4 * line - 4, 4 * line), narrow)
    has_upper = z < line - 1
    has_lower = z > 0
    sum_depth = a_sum.shape[0]
    hop_depth = a_up.shape[0]
    b_sum_depth = b_sum.shape[0]

    barrier = pltpu.get_barrier_semaphore()
    pl.semaphore_signal(barrier, inc=1, device_id=core_peer, device_id_type=mesh_id)
    pl.semaphore_signal(barrier, inc=1, device_id=cross_peer, device_id_type=mesh_id)

    @pl.when(has_upper)
    def _():
        pl.semaphore_signal(barrier, inc=1, device_id=upper, device_id_type=mesh_id)

    @pl.when(has_lower)
    def _():
        pl.semaphore_signal(barrier, inc=1, device_id=lower, device_id_type=mesh_id)

    pl.semaphore_wait(barrier, 2 + has_upper.astype(jnp.int32) + has_lower.astype(jnp.int32))

    def remote(source, target, send_sem, recv_sem, peer):
        return pltpu.make_async_remote_copy(
            src_ref=source, dst_ref=target, send_sem=send_sem, recv_sem=recv_sem, device_id=peer, device_id_type=mesh_id
        )

    def core_copy(step):
        slot = lax.rem(step, DEPTH)
        source = grads.at[:, :, 1 - core, pl.ds(step * EARLY, EARLY)]
        return remote(source, a_in.at[slot], core_send.at[slot], core_recv.at[slot], core_peer)

    def own_copy(step):
        slot = lax.rem(step, DEPTH)
        return pltpu.make_async_copy(
            grads.at[:, :, core, pl.ds(step * EARLY, EARLY)], a_own.at[slot], own_sems.at[slot]
        )

    def b_core_copy(step):
        slot = lax.rem(step, DEPTH)
        source = grads.at[:, :, 1 - core, steps * EARLY + step]
        return remote(source, b_in.at[slot], b_core_send.at[slot], b_core_recv.at[slot], core_peer)

    def b_own_copy(step):
        slot = lax.rem(step, DEPTH)
        return pltpu.make_async_copy(
            grads.at[:, :, core, steps * EARLY + step], b_own.at[slot], b_own_sems.at[slot]
        )

    def cross_copy(step):
        slot = lax.rem(step, DEPTH)
        return remote(a_send.at[slot], a_cross.at[slot], cross_send.at[slot], cross_recv.at[slot], cross_peer)

    def b_cross_copy(step):
        slot = lax.rem(step, DEPTH)
        return remote(b_send.at[slot], b_cross.at[slot], b_cross_send.at[slot], b_cross_recv.at[slot], cross_peer)

    def up_copy(step, target):
        slot = lax.rem(step, hop_depth)
        return remote(
            a_sum.at[lax.rem(step, sum_depth), target], a_up.at[slot, target],
            up_send.at[slot, target], up_recv.at[slot, target], upper,
        )

    def down_copy(step, target):
        slot = lax.rem(step, hop_depth)
        return remote(
            a_sum.at[lax.rem(step, sum_depth), target], a_down.at[slot, target],
            down_send.at[slot, target], down_recv.at[slot, target], lower,
        )

    def b_up_copy(step, target):
        slot = lax.rem(step, hop_depth)
        return remote(
            b_sum.at[lax.rem(step, b_sum_depth), target], b_up.at[slot, target],
            b_up_send.at[slot, target], b_up_recv.at[slot, target], upper,
        )

    def b_down_copy(step, target):
        slot = lax.rem(step, hop_depth)
        return remote(
            b_sum.at[lax.rem(step, b_sum_depth), target], b_down.at[slot, target],
            b_down_send.at[slot, target], b_down_recv.at[slot, target], lower,
        )

    def give(channel, peer):
        pl.semaphore_signal(credits.at[channel], inc=1, device_id=peer, device_id_type=mesh_id)

    def take(channel, step, depth):
        @pl.when(step >= depth)
        def _():
            pl.semaphore_wait(credits.at[channel], 1)

    def feed(step, count, channel, remote_copy, local_copy):
        @pl.when(step < count)
        def _():
            take(channel, step, DEPTH)
            remote_copy(step).start()
            local_copy(step).start()

    held_copies = [
        pltpu.make_async_copy(source, target, held_sems.at[index])
        for index, (source, target) in enumerate(zip(sources, targets))
    ]
    start_all(held_copies)
    for early in range(DEPTH - 1):
        feed(early, steps, 0, core_copy, own_copy)
        feed(early, late_steps, 1, b_core_copy, b_own_copy)

    def active(step, count):
        return (step >= 0) & (step < count)

    far = jnp.maximum(z, line - 1 - z)

    def hops(step_up, step_down, count, sums, depth, ups, downs, up, down, channel):
        @pl.when(active(step_up, count) & has_upper)
        def _():
            take(channel, step_up, hop_depth)
            slot = lax.rem(step_up, hop_depth)
            place = lax.rem(step_up, depth)

            def one(target, _):
                @pl.when(has_lower)
                def _():
                    up(step_up, target).wait_recv()
                    sums[place, target] += ups[slot, target]

                up(step_up, target).start()
                return 0

            lax.fori_loop(z + 1, line, one, 0)

        @pl.when(active(step_down, count) & has_lower)
        def _():
            take(channel + 1, step_down, hop_depth)
            slot = lax.rem(step_down, hop_depth)
            place = lax.rem(step_down, depth)

            def one(target, _):
                @pl.when(has_upper)
                def _():
                    down(step_down, target).wait_recv()
                    sums[place, target] += downs[slot, target]

                down(step_down, target).start()
                return 0

            lax.fori_loop(0, z, one, 0)

    def gather_hops(step, count, sums, depth, ups, downs, up, down, channel, total):
        slot = lax.rem(step, hop_depth)
        total[...] = sums[lax.rem(step, depth), z].astype(f32)

        @pl.when(has_lower)
        def _():
            up(step, z).wait_recv()
            total[...] += ups[slot, z].astype(f32)

            @pl.when(step < count - hop_depth)
            def _():
                give(channel, lower)

        @pl.when(has_upper)
        def _():
            down(step, z).wait_recv()
            total[...] += downs[slot, z].astype(f32)

            @pl.when(step < count - hop_depth)
            def _():
                give(channel + 1, upper)

    def retire(step, count, up, down):
        @pl.when(active(step, count))
        def _():
            def sent_up(target, _):
                up(step, target).wait_send()
                return 0

            def sent_down(target, _):
                down(step, target).wait_send()
                return 0

            lax.fori_loop(z + 1, line, sent_up, 0)
            lax.fori_loop(0, z, sent_down, 0)

    def iteration(step, _):
        feed(step + DEPTH - 1, steps, 0, core_copy, own_copy)
        feed(step + DEPTH - 1, late_steps, 1, b_core_copy, b_own_copy)

        retire(step - CROSS_LAG - HOP_LAG * far - 1, steps, up_copy, down_copy)
        retire(step - HOP_LAG * far - 1, late_steps, b_up_copy, b_down_copy)

        @pl.when(step < steps)
        def _():
            slot = lax.rem(step, DEPTH)
            place = lax.rem(step, sum_depth)
            core_copy(step).wait()
            own_copy(step).wait()

            @pl.when(step >= DEPTH)
            def _():
                cross_copy(step - DEPTH).wait_send()

            for target in range(line):
                a_send[slot, target] = a_own[slot, target, 1 - x] + a_in[slot, target, 1 - x]
            take(2, step, DEPTH)
            cross_copy(step).start()
            for target in range(line):
                a_sum[place, target] = a_own[slot, target, x] + a_in[slot, target, x]

            @pl.when(step < steps - DEPTH)
            def _():
                give(0, core_peer)

        @pl.when(step < late_steps)
        def _():
            slot = lax.rem(step, DEPTH)
            b_core_copy(step).wait()
            b_own_copy(step).wait()
            b_sum[lax.rem(step, b_sum_depth)] = b_own[slot] + b_in[slot]

            @pl.when(step < late_steps - DEPTH)
            def _():
                give(1, core_peer)

        crossed = step - CROSS_LAG

        @pl.when(active(crossed, steps))
        def _():
            slot = lax.rem(crossed, DEPTH)
            place = lax.rem(crossed, sum_depth)
            cross_copy(crossed).wait_recv()
            for target in range(line):
                a_sum[place, target] += a_cross[slot, target]

            @pl.when(crossed < steps - DEPTH)
            def _():
                give(2, cross_peer)

        hops(
            step - HOP_LAG * z, step - HOP_LAG * (line - 1 - z), late_steps, b_sum, b_sum_depth, b_up, b_down,
            b_up_copy, b_down_copy, 6,
        )
        hops(
            crossed - HOP_LAG * z, crossed - HOP_LAG * (line - 1 - z), steps, a_sum, sum_depth, a_up, a_down,
            up_copy, down_copy, 4,
        )

        last = crossed - HOP_LAG * far

        @pl.when(active(last, steps))
        def _():
            gather_hops(last, steps, a_sum, sum_depth, a_up, a_down, up_copy, down_copy, 4, a_keep)
            out[pl.ds(last * EARLY, EARLY)] = a_keep[...].astype(bf16)

        arrived = step - HOP_LAG * far

        @pl.when(active(arrived, late_steps))
        def _():
            slot = lax.rem(arrived, DEPTH)

            @pl.when(arrived >= DEPTH)
            def _():
                b_cross_copy(arrived - DEPTH).wait_send()

            gather_hops(
                arrived, late_steps, b_sum, b_sum_depth, b_up, b_down, b_up_copy, b_down_copy, 6, b_keep.at[slot]
            )
            b_send[slot] = b_keep[slot, 1 - x].astype(bf16)
            take(3, arrived, DEPTH)
            b_cross_copy(arrived).start()

        paired = arrived - CROSS_LAG

        @pl.when(active(paired, late_steps))
        def _():
            slot = lax.rem(paired, DEPTH)
            b_cross_copy(paired).wait_recv()
            place = steps * EARLY + paired
            out[place] = (b_keep[slot, x] + b_cross[slot].astype(f32)).astype(bf16)

            @pl.when(paired < late_steps - DEPTH)
            def _():
                give(3, cross_peer)

        return 0

    lag = HOP_LAG * (line - 1) + CROSS_LAG
    lax.fori_loop(0, max(steps, late_steps) + lag + 2, iteration, 0)
    for step in range(max(steps - DEPTH, 0), steps):
        cross_copy(step).wait_send()
    for step in range(max(late_steps - DEPTH, 0), late_steps):
        b_cross_copy(step).wait_send()
    for copy in held_copies:
        copy.wait()


def run_sum_for_owners(grads, wide_count, held):
    line = wide_count // 4
    slots, block = grads.shape[0] // wide_count, grads.shape[1:]
    steps = (slots - 1) // (EARLY + 1)
    late_steps = slots - EARLY * steps
    sum_depth = CROSS_LAG + HOP_LAG * (line - 1) + 2
    b_sum_depth = HOP_LAG * (line - 1) + 2
    hop_depth = 2 * HOP_LAG + 2
    dma = pltpu.SemaphoreType.DMA

    def vmem(*shape):
        return pltpu.VMEM(shape + block, bf16)

    def wide_vmem(*shape):
        return pltpu.VMEM(shape + block, f32)

    return pl.pallas_call(
        functools.partial(sum_for_owners, line, steps, late_steps),
        out_shape=[pltpu.VMEM((slots,) + block, bf16)] + [pltpu.VMEM(array.shape, array.dtype) for array in held],
        in_specs=[ANY_SPEC] * (1 + len(held)),
        out_specs=[VMEM_SPEC] * (1 + len(held)),
        scratch_shapes=[
            vmem(DEPTH, line, 2, EARLY),
            vmem(DEPTH, line, 2, EARLY),
            vmem(sum_depth, line, EARLY),
            wide_vmem(EARLY),
            vmem(DEPTH, line, EARLY),
            vmem(DEPTH, line, EARLY),
            vmem(hop_depth, line, EARLY),
            vmem(hop_depth, line, EARLY),
            vmem(DEPTH, line, 2),
            vmem(DEPTH, line, 2),
            vmem(b_sum_depth, line, 2),
            wide_vmem(DEPTH, 2),
            vmem(DEPTH),
            vmem(DEPTH),
            vmem(hop_depth, line, 2),
            vmem(hop_depth, line, 2),
        ]
        + ([dma((DEPTH,))] * 5 + [dma((hop_depth, line))] * 4) * 2
        + [dma((len(held),)), pltpu.SemaphoreType.REGULAR((8,))],
        compiler_params=params(SUM_VMEM, collective_id=0, has_side_effects=True),
        cost_estimate=pl.CostEstimate(flops=0, bytes_accessed=2 * grads.size * 8, transcendentals=0),
        name="sum_for_owners",
    )(grads.reshape((line, 2, 2, slots) + block), *held)


def rope_tables(segment_row):
    token_index = jnp.arange(segment_row.shape[0], dtype=jnp.int32)
    changed = jnp.concatenate([jnp.ones((1,), dtype=bool), segment_row[1:] != segment_row[:-1]])
    begins = lax.cummax(jnp.where(changed, token_index, jnp.zeros_like(token_index)), axis=0)
    places = (token_index - begins).astype(f32)
    frequency = rope_base ** (-(jnp.arange(HEAD_DIM // 2, dtype=f32) * 2.0) / HEAD_DIM)
    angles = places[:, None] * frequency[None, :]
    cosine = jnp.concatenate([jnp.cos(angles), jnp.cos(angles)], axis=-1)
    sine_signed = jnp.concatenate([-jnp.sin(angles), jnp.sin(angles)], axis=-1)
    return (cosine, sine_signed)


def rms_parts(values):
    inverse = rms_inverse(values)
    return (inverse, values * inverse)


def norm_back(grad_scaled, normed, inverse):
    return inverse * (grad_scaled - normed * jnp.mean(grad_scaled * normed, axis=-1, keepdims=True))


def adam_small(param_now, gradient, first_now, second_now, rate_here):
    first_new = beta_first * first_now + (1.0 - beta_first) * gradient
    second_new = beta_second * second_now + (1.0 - beta_second) * gradient * gradient
    param_new = param_now - rate_here * (first_new / first_fix) / (
        jnp.sqrt(second_new / second_fix) + adam_eps
    )
    return (param_new, first_new, second_new)


def swap_halves(values):
    return lax.ppermute(values, "narrow", [(0, 1), (1, 0)])


def body(
    tokens,
    cotangent,
    segments,
    owner_list,
    masters,
    first_moment,
    second_moment,
    left_basis,
    right_basis,
    gains,
    gain_first,
    gain_second,
    biases,
    bias_first,
    bias_second,
):
    half = lax.axis_index("narrow")
    wide_index = lax.axis_index("wide")
    wide_count = lax.axis_size("wide")
    tokens_here = tokens.shape[0]
    slots_here = masters.shape[0]
    slots_half = owner_list.shape[0]
    gains_here = gains.shape[0]
    biases_here = biases.shape[1]

    def join_halves(own, other, axis=0):
        return jnp.where(
            half == 0, jnp.concatenate([own, other], axis=axis), jnp.concatenate([other, own], axis=axis)
        )

    masters_low, gains, biases = lax.optimization_barrier((masters.astype(bf16), gains, biases))
    weights = lax.all_gather(masters_low, "wide", axis=0, tiled=True)
    gain_full = lax.all_gather(gains, ("wide", "narrow"), axis=0, tiled=True).reshape(2, D)
    bias_full = lax.all_gather(biases.reshape(-1).astype(bf16), "wide", axis=0, tiled=True)
    bias_full = bias_full.astype(f32).reshape(1, QKV_WIDTH)
    pair_gains = 2 * gains_here

    position = jnp.arange(slots_half, dtype=jnp.int32)
    empty = owner_list == BLOCK_TOTAL
    number = jnp.where(empty, BLOCK_TOTAL - 1 + jnp.cumsum(empty.astype(jnp.int32)), owner_list)
    weight_rows = jnp.zeros((slots_half,), jnp.int32).at[number].set(position, unique_indices=True)
    rows = weight_rows + weight_rows // slots_here
    half_index = half.astype(jnp.int32).reshape(1)

    segment_row = lax.dynamic_index_in_dim(segments, wide_index, 0, keepdims=False)
    cosine, sine = rope_tables(segment_row)
    token_index = jnp.arange(segment_row.shape[0], dtype=jnp.int32)
    allowed_turned = (
        (segment_row[None, :] == segment_row[:, None]) & (token_index[None, :] >= token_index[:, None])
    ).astype(f32)
    tokens_row = join_halves(tokens, swap_halves(tokens))
    cotangent_row = join_halves(cotangent, swap_halves(cotangent))
    weights, tokens_row, cotangent_row, gain_full, bias_full = lax.optimization_barrier(
        (weights, tokens_row, cotangent_row, gain_full, bias_full)
    )

    low_part, high_part, normed_one_turned, qkv, mixed_turned, log_total = run_attention_forward(
        weight_rows, tokens_row, gain_full[0:1], bias_full, cosine, sine, allowed_turned, weights
    )
    low_other = swap_halves(low_part)
    active_grad = run_active_grads(weight_rows, cotangent_row, weights)
    high_sent, low_other = lax.optimization_barrier((high_part, low_other))
    high_other = swap_halves(high_sent)
    gain_two = gain_full[1:2]
    grad_low, resid_low, turned_low, gain_low, *hidden_low = run_hidden_grads(
        0, weight_rows, tokens_row, low_part, low_other, gain_two, active_grad, weights
    )
    grad_low_other = swap_halves(grad_low)
    grad_high, resid_high, turned_high, gain_high, *hidden_high = run_hidden_grads(
        tokens_here, weight_rows, tokens_row, high_part, high_other, gain_two, active_grad, weights
    )
    grad_high_other = swap_halves(grad_high)
    branch_own, branch_sent, grads = run_hidden_weight_grads(
        weight_rows, rows, half_index, cotangent_row, [(turned_low, *hidden_low), (turned_high, *hidden_high)], weights,
        wide_count * (slots_here + 1),
    )
    branch_other = swap_halves(branch_sent)
    grad_resid, grad_one_own, grad_one_sent, grads = run_attention_backward(
        weight_rows, rows, half_index, tokens_row, (resid_low, grad_low, grad_low_other),
        (resid_high, grad_high, grad_high_other), cotangent_row, gain_full, cosine, sine, allowed_turned,
        normed_one_turned, qkv, mixed_turned, log_total, (gain_low, gain_high), weights, grads, wide_count,
    )
    grad_one_other = swap_halves(grad_one_sent)
    resid_own = jnp.where(half == 0, resid_low, resid_high)
    output = (resid_own + branch_own.astype(f32) + branch_other.astype(f32)).astype(bf16)

    held = [masters, first_moment, second_moment, left_basis, right_basis]
    if wide_count == 16:
        grads, output = lax.optimization_barrier((grads, output))
        reduced, *held = [
            pltpu.with_memory_space_constraint(array, pltpu.VMEM)
            for array in run_sum_for_owners(grads, wide_count, held)
        ]
    else:
        reduced = lax.psum_scatter(grads, "wide", scatter_dimension=0, tiled=True)

    block_grad, new_masters, new_first, new_second, small_sums = run_soap(reduced, *held)
    inverse_one, normed_one = rms_parts(tokens.astype(f32))
    grad_one = grad_one_own.astype(f32) + grad_one_other.astype(f32)
    input_grad = grad_resid + norm_back(grad_one * gain_full[0:1], normed_one, inverse_one)
    places = [small_places(owner, wide_count) for owner in range(wide_count)]
    gain_offset = jnp.asarray([place[1] for place in places], jnp.int32)[wide_index]
    bias_offset = jnp.asarray([place[3] for place in places], jnp.int32)[wide_index]
    gain_sums = lax.dynamic_slice_in_dim(small_sums[:2].reshape(-1), gain_offset, pair_gains, 0)
    gain_sums = gain_sums.reshape(2, gains_here)
    gain_other, input_grad = lax.optimization_barrier((swap_halves(gain_sums), input_grad))
    gain_sums = gain_sums + gain_other
    gain_grad = lax.dynamic_index_in_dim(gain_sums, half, 0, keepdims=False)
    bias_grad = lax.dynamic_slice_in_dim(small_sums[2], bias_offset, biases_here, 0).reshape(biases.shape)
    new_gains, new_gain_first, new_gain_second = adam_small(gains, gain_grad, gain_first, gain_second, rate_gains)
    new_biases, new_bias_first, new_bias_second = adam_small(biases, bias_grad, bias_first, bias_second, rate_small)

    return (
        output,
        input_grad,
        block_grad,
        new_masters,
        new_first,
        new_second,
        gain_grad,
        new_gains,
        new_gain_first,
        new_gain_second,
        bias_grad,
        new_biases,
        new_bias_first,
        new_bias_second,
    )


def solution(mesh):
    tokens_spec = P(("wide", "narrow"), None)
    blocks_spec = P(("wide", "narrow"), None, None)
    gains_spec = P(("wide", "narrow"))
    bias_spec = P("narrow", "wide")
    in_specs = (
        (tokens_spec, tokens_spec, P(), P()) + (blocks_spec,) * 5 + (gains_spec,) * 3 + (bias_spec,) * 3
    )
    out_specs = (tokens_spec, tokens_spec) + (blocks_spec,) * 4 + (gains_spec,) * 4 + (bias_spec,) * 4
    return jax.shard_map(body, mesh=mesh, in_specs=in_specs, out_specs=out_specs, check_vma=False)
```

```python
import functools

import jax
import jax.numpy as jnp
from jax import lax
from jax.experimental import pallas as pl
from jax.experimental.pallas import tpu as pltpu
from jax.sharding import PartitionSpec as P

D = 1536
FF = 8960
HEADS = 12
KV_HEADS = 2
HEAD_DIM = 128
BLK = 128
STEP_COUNT = 5


beta_first = 0.95
beta_second = 0.95
adam_eps = 1e-08
rate_blocks = 0.03
rate_small = 0.4
rate_gains = 0.6
norm_eps = 1e-06
rope_base = 10000.0
masked_score = -1e30
first_fix = 1.0 - beta_first**STEP_COUNT
second_fix = 1.0 - beta_second**STEP_COUNT
scaling = HEAD_DIM ** (-0.5)

bf16 = jnp.bfloat16
f32 = jnp.float32

NARROW = 2
ROW_BLOCKS = D // BLK
QUERY_COLS = HEADS * HEAD_DIM // NARROW // BLK
PAIR_COLS = KV_HEADS * HEAD_DIM // NARROW // BLK
HIDDEN_COLS = FF // NARROW // BLK
QKV_COLS = QUERY_COLS + 2 * PAIR_COLS
QUERY_WIDTH = QUERY_COLS * BLK
QKV_WIDTH = QKV_COLS * BLK
KEY_BASE = ROW_BLOCKS * QUERY_COLS
VALUE_BASE = KEY_BASE + ROW_BLOCKS * PAIR_COLS
OUT_BASE = VALUE_BASE + ROW_BLOCKS * PAIR_COLS
GATE_BASE = OUT_BASE + QUERY_COLS * ROW_BLOCKS
UP_BASE = GATE_BASE + ROW_BLOCKS * HIDDEN_COLS
DOWN_BASE = UP_BASE + ROW_BLOCKS * HIDDEN_COLS
BLOCK_TOTAL = DOWN_BASE + HIDDEN_COLS * ROW_BLOCKS

TILE_BLOCKS = 6
TILES = -(-HIDDEN_COLS // TILE_BLOCKS)
LAST_BLOCKS = HIDDEN_COLS - (TILES - 1) * TILE_BLOCKS
TILE = TILE_BLOCKS * BLK
COLS = 256
ROWS = 64
SMALL_ROWS = 16
VMEM_LIMIT = 60 * 2**20
SUM_VMEM = 36 * 2**20
WRITE_VMEM = 6 * 2**20

EARLY = 4
DEPTH = 3
CROSS_LAG = 2
HOP_LAG = 1

VMEM_SPEC = pl.BlockSpec(memory_space=pltpu.VMEM)
SMEM_SPEC = pl.BlockSpec(memory_space=pltpu.SMEM)
ANY_SPEC = pl.BlockSpec(memory_space=pl.ANY)


def spans(total, step):
    return [(begin, min(step, total - begin)) for begin in range(0, total, step)]


def dot_nn(left, right):
    return jnp.dot(left, right, preferred_element_type=f32)


def dot_nt(left, right):
    return lax.dot_general(left, right, (((1,), (1,)), ((), ())), preferred_element_type=f32)


def block_ref(ref, row_block, col_block):
    return ref.at[pl.ds(row_block * BLK, BLK), pl.ds(col_block * BLK, BLK)]


def fetch_piece(rows_ref, weights, target, base, pitch, row_blocks, col_blocks, first_col, sem):
    @pl.loop(0, row_blocks)
    def _(i):
        for j in range(col_blocks):
            pltpu.make_async_copy(
                weights.at[rows_ref[base + i * pitch + j]],
                block_ref(target, i, first_col + j),
                sem,
            ).start()


def store_piece(rows_ref, source, grads, base, pitch, row_blocks, col_blocks, first_col, sem):
    @pl.loop(0, row_blocks)
    def _(i):
        for j in range(col_blocks):
            pltpu.make_async_copy(
                block_ref(source, i, first_col + j),
                grads.at[rows_ref[base + i * pitch + j]],
                sem,
            ).start()


def wait_bytes(ref, sem):
    pltpu.make_async_copy(ref, ref, sem).wait()


def fetch_attention(rows_ref, weights, w_qkv, w_out, sems):
    fetch_piece(rows_ref, weights, w_qkv, 0, QUERY_COLS, ROW_BLOCKS, QUERY_COLS, 0, sems.at[0])
    fetch_piece(rows_ref, weights, w_qkv, KEY_BASE, PAIR_COLS, ROW_BLOCKS, PAIR_COLS, QUERY_COLS, sems.at[0])
    fetch_piece(
        rows_ref, weights, w_qkv, VALUE_BASE, PAIR_COLS, ROW_BLOCKS, PAIR_COLS, QUERY_COLS + PAIR_COLS, sems.at[0]
    )
    fetch_piece(rows_ref, weights, w_out, OUT_BASE, ROW_BLOCKS, QUERY_COLS, ROW_BLOCKS, 0, sems.at[1])


def rms_inverse(values):
    return lax.rsqrt(jnp.mean(values * values, axis=-1, keepdims=True) + norm_eps)


def row_chunks(total, step, run):
    @pl.loop(0, total // step)
    def _(chunk):
        run(pl.ds(pl.multiple_of(chunk * step, step), step))


def small_places(owner, wide_count):
    gain_row = min(owner * (2 * D // wide_count) // BLK, 2 * D // BLK - 2)
    return (gain_row, owner * (QKV_WIDTH // wide_count) // BLK)


def scores_turned(keys, queries, allowed):
    return jnp.where(allowed, dot_nt(keys, queries) * scaling, masked_score)


def attention_forward(
    rows_ref,
    x_ref,
    gain_ref,
    bias_ref,
    cos_ref,
    sin_ref,
    allowed_ref,
    weights,
    part_low_ref,
    part_high_ref,
    normed_turned_ref,
    qkv_ref,
    mixed_turned_ref,
    log_ref,
    w_qkv,
    w_out,
    normed,
    mixed,
    sems,
):
    fetch_attention(rows_ref, weights, w_qkv, w_out, sems)
    length = x_ref.shape[0]

    def norm_rows(rows):
        values = x_ref[rows, :].astype(f32)
        normed[rows, :] = (values * rms_inverse(values) * gain_ref[...]).astype(bf16)

    row_chunks(length, ROWS, norm_rows)
    for begin, size in spans(D, COLS):
        normed_turned_ref[pl.ds(begin, size), :] = normed[:, pl.ds(begin, size)].T
    wait_bytes(w_qkv, sems.at[0])
    for begin, size in spans(QKV_WIDTH, COLS):
        products = dot_nn(normed[...], w_qkv[:, pl.ds(begin, size)]) + bias_ref[:, pl.ds(begin, size)]
        for offset, width in spans(size, HEAD_DIM):
            head = products[:, offset : offset + width]
            if begin + offset < QUERY_WIDTH + PAIR_COLS * BLK:
                head = head * cos_ref[...] + pltpu.roll(head, HEAD_DIM // 2, 1) * sin_ref[...]
            qkv_ref[:, pl.ds(begin + offset, width)] = head.astype(bf16)
    keys = qkv_ref[:, pl.ds(QUERY_WIDTH, HEAD_DIM)]
    values_turned = qkv_ref[:, pl.ds(QUERY_WIDTH + HEAD_DIM, HEAD_DIM)].T
    for head in range(QUERY_COLS):
        columns = pl.ds(head * HEAD_DIM, HEAD_DIM)
        scores = scores_turned(keys, qkv_ref[:, columns], allowed_ref[...] > 0)
        peak = jnp.max(scores, axis=0, keepdims=True)
        expo = jnp.exp(scores - peak)
        total = jnp.sum(expo, axis=0, keepdims=True)
        log_ref[pl.ds(head, 1), :] = peak + jnp.log(total)
        probs = (expo / total).astype(bf16)
        mixed_head = dot_nn(values_turned, probs).astype(bf16)
        mixed_turned_ref[columns, :] = mixed_head
        mixed[:, columns] = mixed_head.T
    wait_bytes(w_out, sems.at[1])
    for part_ref, first in ((part_low_ref, 0), (part_high_ref, length // NARROW)):
        for begin, size in spans(D, COLS):
            part_ref[:, pl.ds(begin, size)] = dot_nn(
                mixed[pl.ds(first, length // NARROW), :], w_out[:, pl.ds(begin, size)]
            ).astype(bf16)


def pair_copies(rows_ref, blocks_hbm, pair, sem, column, place, outward=False):
    return [
        block_copy(blocks_hbm.at[rows_ref[base + i * HIDDEN_COLS + column]], block_ref(pair, i, which), sem, outward)
        for i in range(ROW_BLOCKS)
        for base, which in ((GATE_BASE, 2 * place), (UP_BASE, 2 * place + 1))
    ]


def down_copies(rows_ref, blocks_hbm, down, sem, column, place, outward=False):
    return [
        block_copy(blocks_hbm.at[rows_ref[DOWN_BASE + column * ROW_BLOCKS + i]], block_ref(down, place, i), sem, outward)
        for i in range(ROW_BLOCKS)
    ]


def block_copy(in_hbm, in_vmem, sem, outward):
    return pltpu.make_async_copy(*((in_vmem, in_hbm) if outward else (in_hbm, in_vmem)), sem)


def start_all(copies):
    for copy in copies:
        copy.start()


def half_rows(half_ref, length):
    begin = pl.multiple_of(half_ref[0] * length, length)
    return (pl.ds(begin, length), pl.ds(pl.multiple_of(length - begin, length), length))


def hidden_column(tile, place):
    return jnp.minimum(tile * TILE_BLOCKS + place, HIDDEN_COLS - 1)


def hidden_tiles(run):
    @pl.loop(0, TILES - 1)
    def _(tile):
        run(tile, lax.rem(tile, 2), TILE_BLOCKS, True)

    run(TILES - 1, (TILES - 1) % 2, LAST_BLOCKS, False)


def active_grads(rows_ref, cot_ref, weights, out, w_down, stage, load_sems, store_sems):
    def fetch(tile, slot, place):
        start_all(
            down_copies(rows_ref, weights, w_down.at[slot], load_sems.at[slot], hidden_column(tile, place), place)
        )

    for place in range(TILE_BLOCKS):
        fetch(0, 0, place)

    def run(tile, slot, blocks, more):
        wait_bytes(w_down.at[slot], load_sems.at[slot])

        @pl.when(tile >= 2)
        def _():
            wait_bytes(stage.at[slot], store_sems.at[slot])

        if more:
            for place in range(TILE_BLOCKS):
                fetch(tile + 1, 1 - slot, place)
        for begin, size in spans(blocks * BLK, COLS):
            stage[slot, :, pl.ds(begin, size)] = dot_nt(cot_ref[...], w_down[slot, pl.ds(begin, size), :])
        pltpu.make_async_copy(stage.at[slot], out.at[tile], store_sems.at[slot]).start()

    hidden_tiles(run)
    for tile in range(max(TILES - 2, 0), TILES):
        wait_bytes(stage.at[tile % 2], store_sems.at[tile % 2])


def hidden_grads(
    first_row,
    rows_ref,
    x_ref,
    own_ref,
    other_ref,
    gain_ref,
    active_grad,
    weights,
    grad_ref,
    resid_ref,
    normed_turned_ref,
    gain_part_ref,
    pair_grads,
    active,
    active_turned,
    w_pair,
    grad_active,
    straight,
    turned,
    grads,
    normed,
    grad_sum,
    load_sems,
    store_sems,
):
    length = own_ref.shape[0]

    def fetch(tile, slot, place):
        start_all(
            pair_copies(rows_ref, weights, w_pair.at[slot], load_sems.at[slot, 0], hidden_column(tile, place), place)
        )

    def load_grad(tile, slot):
        return pltpu.make_async_copy(active_grad.at[tile, pl.ds(first_row, length)], grad_active.at[slot], load_sems.at[slot, 1])

    def stores(tile, slot):
        return (
            pltpu.make_async_copy(turned.at[slot], active_turned.at[tile], store_sems.at[slot, 0]),
            pltpu.make_async_copy(grads.at[slot], pair_grads.at[tile], store_sems.at[slot, 1]),
            pltpu.make_async_copy(straight.at[slot], active.at[tile], store_sems.at[slot, 2]),
        )

    for place in range(TILE_BLOCKS):
        fetch(0, 0, place)
    load_grad(0, 0).start()

    def norm_rows(rows):
        tokens = x_ref[pl.ds(rows.start + first_row, rows.size), :]
        values = tokens.astype(f32) + own_ref[rows, :].astype(f32) + other_ref[rows, :].astype(f32)
        resid_ref[rows, :] = values
        normed[rows, :] = (values * rms_inverse(values) * gain_ref[...]).astype(bf16)

    row_chunks(length, ROWS, norm_rows)
    grad_sum[...] = jnp.zeros_like(grad_sum)

    def run(tile, slot, blocks, more):
        wait_bytes(w_pair.at[slot], load_sems.at[slot, 0])
        load_grad(tile, slot).wait()
        if more:
            load_grad(tile + 1, 1 - slot).start()

        @pl.when(tile >= 2)
        def _():
            for copy in stores(tile - 2, slot):
                copy.wait()

        for place in range(blocks):
            columns = pl.ds(place * BLK, BLK)
            pair = dot_nn(normed[...], w_pair[slot, :, pl.ds(2 * place * BLK, 2 * BLK)])
            gate = pair[:, :BLK]
            upper = pair[:, BLK:]
            grad = grad_active[slot, :, columns]
            sigmoid = jax.nn.sigmoid(gate)
            silu = gate * sigmoid
            active_here = (silu * upper).astype(bf16)
            straight[slot, :, columns] = active_here
            turned[slot, columns, :] = active_here.T
            grads[slot, :, pl.ds(2 * place * BLK, BLK)] = (
                grad * upper * sigmoid * (1.0 + gate * (1.0 - sigmoid))
            ).astype(bf16)
            grads[slot, :, pl.ds((2 * place + 1) * BLK, BLK)] = (grad * silu).astype(bf16)
            if more:
                fetch(tile + 1, 1 - slot, place)
        if more:
            for place in range(blocks, TILE_BLOCKS):
                fetch(tile + 1, 1 - slot, place)
        turn = pl.ds(pl.multiple_of(tile * COLS, COLS), COLS)
        normed_turned_ref[turn, :] = normed[:, turn].T
        width = 2 * blocks * BLK
        for begin, size in spans(D, COLS):
            columns = pl.ds(begin, size)
            grad_sum[:, columns] += dot_nt(grads[slot, :, :width], w_pair[slot, columns, :width])
        start_all(stores(tile, slot))

    hidden_tiles(run)
    grad_ref[...] = grad_sum[...].astype(bf16)
    gain_part_ref[...] = jnp.zeros_like(gain_part_ref)

    def gain_rows(rows):
        values = resid_ref[rows, :]
        gain_part_ref[...] += jnp.sum(grad_sum[rows, :] * values * rms_inverse(values), axis=0, keepdims=True)

    row_chunks(length, ROWS, gain_rows)
    for tile in range(max(TILES - 2, 0), TILES):
        for copy in stores(tile, tile % 2):
            copy.wait()


def hidden_weight_grads(
    weight_rows_ref, rows_ref, half_ref, cot_ref, *refs
):
    parts, (weights, branch_own_ref, branch_other_ref, grads), scratch = refs[: 4 * NARROW], refs[8:12], refs[12:]
    normed_turned, pair, straight, turned, w_down, branch_sum, pair_stage, down_stage, load_sems, store_sems, sems = scratch
    length = cot_ref.shape[0] // NARROW

    def loads(tile, slot):
        copies = []
        for part in range(NARROW):
            pair_grads, active, active_turned = parts[part * 4 + 1 : part * 4 + 4]
            tokens = pl.ds(part * length, length)
            copies += [
                pltpu.make_async_copy(pair_grads.at[tile], pair.at[slot, tokens], load_sems.at[slot, part * 3]),
                pltpu.make_async_copy(active.at[tile], straight.at[slot, tokens], load_sems.at[slot, part * 3 + 1]),
                pltpu.make_async_copy(
                    active_turned.at[tile], turned.at[slot, :, tokens], load_sems.at[slot, part * 3 + 2]
                ),
            ]
        return copies

    def fetch(tile, slot, place):
        start_all(
            down_copies(
                weight_rows_ref, weights, w_down.at[slot], load_sems.at[slot, 3 * NARROW], hidden_column(tile, place), place
            )
        )

    def drain(slot, blocks):
        wait_bytes(pair_stage.at[slot, :, pl.ds(0, 2 * blocks * BLK)], store_sems.at[slot, 0])
        wait_bytes(down_stage.at[slot, pl.ds(0, blocks * BLK)], store_sems.at[slot, 1])

    turned_loads = [
        pltpu.make_async_copy(parts[part * 4], normed_turned.at[:, pl.ds(part * length, length)], sems.at[part])
        for part in range(NARROW)
    ]
    start_all(loads(0, 0) + turned_loads)
    for place in range(TILE_BLOCKS):
        fetch(0, 0, place)
    branch_sum[...] = jnp.zeros_like(branch_sum)
    for copy in turned_loads:
        copy.wait()

    def run(tile, slot, blocks, more):
        for copy in loads(tile, slot):
            copy.wait()
        wait_bytes(w_down.at[slot], load_sems.at[slot, 3 * NARROW])
        if more:
            start_all(loads(tile + 1, 1 - slot))

        @pl.when(tile >= 2)
        def _():
            drain(slot, TILE_BLOCKS)

        width = blocks * BLK
        down = turned[slot, pl.ds(0, width), :]
        for begin, size in spans(D, COLS):
            columns = pl.ds(begin, size)
            down_stage[slot, pl.ds(0, width), columns] = dot_nn(down, cot_ref[:, columns]).astype(bf16)
        for place in range(blocks):
            column = tile * TILE_BLOCKS + place
            start_all(
                down_copies(rows_ref, grads, down_stage.at[slot], store_sems.at[slot, 1], column, place, outward=True)
            )
            columns = pl.ds(2 * place * BLK, 2 * BLK)
            for begin, size in spans(D, 512):
                pair_stage[slot, pl.ds(begin, size), columns] = dot_nn(
                    normed_turned[pl.ds(begin, size), :], pair[slot, :, columns]
                ).astype(bf16)
            start_all(
                pair_copies(rows_ref, grads, pair_stage.at[slot], store_sems.at[slot, 0], column, place, outward=True)
            )
            if more:
                fetch(tile + 1, 1 - slot, place)
        if more:
            for place in range(blocks, TILE_BLOCKS):
                fetch(tile + 1, 1 - slot, place)
        for begin, size in spans(D, COLS):
            columns = pl.ds(begin, size)
            branch_sum[:, columns] += dot_nn(straight[slot, :, :width], w_down[slot, :width, columns])

    hidden_tiles(run)
    own, other = half_rows(half_ref, length)
    branch_own_ref[...] = branch_sum[own, :].astype(bf16)
    branch_other_ref[...] = branch_sum[other, :].astype(bf16)
    if TILES > 1:
        drain((TILES - 2) % 2, TILE_BLOCKS)
    drain((TILES - 1) % 2, LAST_BLOCKS)


def attention_backward(
    weight_rows_ref,
    rows_ref,
    half_ref,
    x_ref,
    resid_low_ref,
    own_low_ref,
    other_low_ref,
    resid_high_ref,
    own_high_ref,
    other_high_ref,
    cot_ref,
    gain_ref,
    cos_ref,
    sin_ref,
    allowed_ref,
    normed_turned_ref,
    qkv_ref,
    mixed_turned_ref,
    log_ref,
    gain_two_low_ref,
    gain_two_high_ref,
    weights,
    grads_in,
    grad_resid_ref,
    grad_own_ref,
    grad_other_ref,
    grads,
    w_qkv,
    w_out,
    grad_resid,
    grad_attention,
    grad_mixed,
    grad_qkv,
    grad_sum,
    gain_part,
    bias_part,
    qkv_stage,
    out_stage,
    small_stage,
    blank,
    load_sems,
    store_sems,
):
    del grads_in
    wide_count = small_stage.shape[0]
    owner_rows = grads.shape[0] // wide_count
    small_stage[...] = jnp.zeros_like(small_stage)
    fetch_attention(weight_rows_ref, weights, w_qkv, w_out, load_sems)
    length = x_ref.shape[0]
    empty_count = rows_ref.shape[0] - BLOCK_TOTAL
    blank[...] = jnp.zeros_like(blank)
    for index in range(empty_count):
        pltpu.make_async_copy(blank.at[index], grads.at[rows_ref[BLOCK_TOTAL + index]], store_sems.at[2]).start()

    part = length // NARROW
    own_rows, other_rows = half_rows(half_ref, part)
    for first, resid_ref, own_ref, other_ref in (
        (0, resid_low_ref, own_low_ref, other_low_ref),
        (part, resid_high_ref, own_high_ref, other_high_ref),
    ):

        def resid_rows(rows, first=first, resid_ref=resid_ref, own_ref=own_ref, other_ref=other_ref):
            values = resid_ref[rows, :]
            inverse = rms_inverse(values)
            normed = values * inverse
            scaled = (own_ref[rows, :].astype(f32) + other_ref[rows, :].astype(f32)) * gain_ref[1:2, :]
            place = pl.ds(rows.start + first, rows.size)
            total = cot_ref[place, :].astype(f32) + inverse * (
                scaled - normed * jnp.mean(scaled * normed, axis=-1, keepdims=True)
            )
            grad_resid[place, :] = total
            grad_attention[place, :] = total.astype(bf16)

        row_chunks(part, ROWS, resid_rows)
    grad_resid_ref[...] = grad_resid[own_rows, :]
    wait_bytes(w_out, load_sems.at[1])
    for begin, size in spans(QUERY_WIDTH, COLS):
        grad_mixed[:, pl.ds(begin, size)] = dot_nt(grad_attention[...], w_out[pl.ds(begin, size), :]).astype(bf16)
    keys = qkv_ref[:, pl.ds(QUERY_WIDTH, HEAD_DIM)]
    keys_turned = keys.T
    values = qkv_ref[:, pl.ds(QUERY_WIDTH + HEAD_DIM, HEAD_DIM)]

    def rope_back(vector):
        return vector * cos_ref[...] - pltpu.roll(vector, HEAD_DIM // 2, 1) * sin_ref[...]

    grad_keys = jnp.zeros((length, HEAD_DIM), f32)
    grad_values = jnp.zeros((length, HEAD_DIM), f32)
    for head in range(QUERY_COLS):
        columns = pl.ds(head * HEAD_DIM, HEAD_DIM)
        queries = qkv_ref[:, columns]
        scores = scores_turned(keys, queries, allowed_ref[...] > 0)
        probs = jnp.exp(scores - log_ref[pl.ds(head, 1), :])
        grad_values += dot_nn(probs.astype(bf16), grad_mixed[:, columns])
        grad_probs = dot_nt(values, grad_mixed[:, columns])
        row_dot = jnp.sum(probs * grad_probs, axis=0, keepdims=True)
        grad_scores = (probs * (grad_probs - row_dot)).astype(bf16)
        grad_keys += dot_nn(grad_scores, queries)
        grad_queries = dot_nn(keys_turned, grad_scores).T * scaling
        grad_qkv[:, columns] = rope_back(grad_queries).astype(bf16)
    grad_qkv[:, pl.ds(QUERY_WIDTH, HEAD_DIM)] = rope_back(grad_keys * scaling).astype(bf16)
    grad_qkv[:, pl.ds(QUERY_WIDTH + HEAD_DIM, HEAD_DIM)] = grad_values.astype(bf16)

    for begin, size in spans(D, COLS):
        out_stage[:, pl.ds(begin, size)] = dot_nn(
            mixed_turned_ref[...], grad_attention[:, pl.ds(begin, size)]
        ).astype(bf16)
    store_piece(rows_ref, out_stage, grads, OUT_BASE, ROW_BLOCKS, QUERY_COLS, ROW_BLOCKS, 0, store_sems.at[1])
    for begin, size in spans(QKV_WIDTH, COLS):
        qkv_stage[:, pl.ds(begin, size)] = dot_nn(
            normed_turned_ref[...], grad_qkv[:, pl.ds(begin, size)]
        ).astype(bf16)
    store_piece(rows_ref, qkv_stage, grads, 0, QUERY_COLS, ROW_BLOCKS, QUERY_COLS, 0, store_sems.at[0])
    store_piece(rows_ref, qkv_stage, grads, KEY_BASE, PAIR_COLS, ROW_BLOCKS, PAIR_COLS, QUERY_COLS, store_sems.at[0])
    store_piece(
        rows_ref, qkv_stage, grads, VALUE_BASE, PAIR_COLS, ROW_BLOCKS, PAIR_COLS, QUERY_COLS + PAIR_COLS, store_sems.at[0]
    )
    wait_bytes(w_qkv, load_sems.at[0])
    for begin, size in spans(D, COLS):
        grad_sum[:, pl.ds(begin, size)] = dot_nt(grad_qkv[...], w_qkv[pl.ds(begin, size), :])
    grad_own_ref[...] = grad_sum[own_rows, :].astype(bf16)
    grad_other_ref[...] = grad_sum[other_rows, :].astype(bf16)
    gain_part[...] = jnp.zeros_like(gain_part)
    bias_part[...] = jnp.zeros_like(bias_part)

    def gain_rows(rows):
        tokens = x_ref[rows, :].astype(f32)
        gain_part[...] += jnp.sum(grad_sum[rows, :] * tokens * rms_inverse(tokens), axis=0, keepdims=True)
        bias_part[...] += jnp.sum(grad_qkv[rows, :].astype(f32), axis=0, keepdims=True)

    row_chunks(length, ROWS, gain_rows)
    for owner in range(wide_count):
        gain_row, bias_row = small_places(owner, wide_count)
        small_rows = []
        for row in (gain_row, gain_row + 1):
            columns = pl.ds(row % (D // BLK) * BLK, BLK)
            if row < D // BLK:
                small_rows.append(gain_part[:, columns])
            else:
                small_rows.append(gain_two_low_ref[:, columns] + gain_two_high_ref[:, columns])
        small_rows.append(bias_part[:, pl.ds(bias_row * BLK, BLK)])
        small_rows.append(jnp.zeros((SMALL_ROWS - len(small_rows), BLK), f32))
        small_stage[owner, pl.ds(0, SMALL_ROWS), :] = jnp.concatenate(small_rows, axis=0).astype(bf16)
        pltpu.make_async_copy(
            small_stage.at[owner], grads.at[owner * owner_rows + owner_rows - 1], store_sems.at[3]
        ).start()
    wait_bytes(small_stage, store_sems.at[3])
    wait_bytes(qkv_stage, store_sems.at[0])
    wait_bytes(out_stage, store_sems.at[1])
    if empty_count > 0:
        wait_bytes(blank.at[pl.ds(0, empty_count)], store_sems.at[2])


def soap_update(
    grad_in,
    masters_ref,
    first_ref,
    second_ref,
    left_ref,
    right_ref,
    grad_out,
    masters_out,
    first_out,
    second_out,
    small_ref,
    grad_stage,
    masters_stage,
    first_stage,
    second_stage,
    sems,
):
    group = grad_stage.shape[1]
    outputs = (
        (grad_stage, grad_out), (masters_stage, masters_out), (first_stage, first_out), (second_stage, second_out)
    )
    steps = masters_ref.shape[0] // group
    small_ref[...] = grad_in[masters_ref.shape[0], :SMALL_ROWS].astype(f32)

    def stores(step):
        slot = lax.rem(step, 2)
        places = pl.ds(step * group, group)
        return [
            pltpu.make_async_copy(stage.at[slot], out.at[places], sems.at[slot, index])
            for index, (stage, out) in enumerate(outputs)
        ]

    @pl.loop(0, steps)
    def _(step):
        @pl.when(step >= 2)
        def _():
            for copy in stores(step - 2):
                copy.wait()

        soap_group(
            step * group, lax.rem(step, 2), grad_in, masters_ref, first_ref, second_ref, left_ref, right_ref,
            *[stage for stage, _ in outputs],
        )
        start_all(stores(step))

    for step in range(max(steps - 2, 0), steps):
        for copy in stores(step):
            copy.wait()


def soap_group(
    first_block, slot, grad_in, masters_ref, first_ref, second_ref, left_ref, right_ref,
    grad_stage, masters_stage, first_stage, second_stage,
):
    places = range(grad_stage.shape[1])
    blocks = [first_block + place for place in places]
    for place, block in enumerate(blocks):
        grad_stage[slot, place] = grad_in[block].astype(f32)
    soap_blocks(
        [grad_in[block] for block in blocks],
        *[[ref.at[block] for block in blocks] for ref in (masters_ref, first_ref, second_ref, left_ref, right_ref)],
        *[[stage.at[slot, place] for place in places] for stage in (masters_stage, first_stage, second_stage)],
    )


def soap_blocks(grads, masters, firsts, seconds, lefts, rights, masters_out, firsts_out, seconds_out):
    count = range(len(grads))
    rights = [right[...].astype(bf16) for right in rights]
    products = [dot_nn(grads[index].astype(bf16), rights[index]).astype(bf16) for index in count]
    lefts = [left[...].astype(bf16) for left in lefts]
    rotated_blocks = [dot_nn(lefts[index].T, products[index]) for index in count]
    normalized = []
    for index in count:
        rotated = rotated_blocks[index]
        new_first = beta_first * firsts[index][...] + (1.0 - beta_first) * rotated
        new_second = beta_second * seconds[index][...] + (1.0 - beta_second) * rotated * rotated
        firsts_out[index][...] = new_first
        seconds_out[index][...] = new_second
        normalized.append(
            (new_first / first_fix / (jnp.sqrt(new_second / second_fix) + adam_eps)).astype(bf16)
        )
    products = [dot_nt(normalized[index], rights[index]).astype(bf16) for index in count]
    for index in count:
        masters_out[index][...] = masters[index][...] - rate_blocks * dot_nn(lefts[index], products[index])


def params(limit=VMEM_LIMIT, **options):
    return pltpu.CompilerParams(vmem_limit_bytes=limit, **options)


def run_attention_forward(rows, x, gain, bias, cosine, sine, allowed, weights):
    length = x.shape[0]
    shape = jax.ShapeDtypeStruct
    return pl.pallas_call(
        attention_forward,
        out_shape=[
            shape((length // NARROW, D), bf16),
            shape((length // NARROW, D), bf16),
            shape((D, length), bf16),
            shape((length, QKV_WIDTH), bf16),
            shape((QUERY_WIDTH, length), bf16),
            shape((8, length), f32),
        ],
        in_specs=[SMEM_SPEC] + [VMEM_SPEC] * 6 + [ANY_SPEC],
        out_specs=[VMEM_SPEC] * 6,
        scratch_shapes=[
            pltpu.VMEM((D, QKV_WIDTH), bf16),
            pltpu.VMEM((QUERY_WIDTH, D), bf16),
            pltpu.VMEM((length, D), bf16),
            pltpu.VMEM((length, QUERY_WIDTH), bf16),
            pltpu.SemaphoreType.DMA((2,)),
        ],
        compiler_params=params(),
        name="attention_forward",
    )(rows, x, gain, bias, cosine, sine, allowed, weights)


def hidden_cost(length, products, bytes_moved):
    return pl.CostEstimate(
        flops=2 * products * length * D * TILE * TILES, bytes_accessed=bytes_moved, transcendentals=0
    )


def run_active_grads(rows, cotangent, weights):
    length = cotangent.shape[0]
    return pl.pallas_call(
        active_grads,
        out_shape=jax.ShapeDtypeStruct((TILES, length, TILE), f32),
        in_specs=[SMEM_SPEC, VMEM_SPEC, ANY_SPEC],
        out_specs=ANY_SPEC,
        scratch_shapes=[
            pltpu.VMEM((2, TILE, D), bf16),
            pltpu.VMEM((2, length, TILE), f32),
            pltpu.SemaphoreType.DMA((2,)),
            pltpu.SemaphoreType.DMA((2,)),
        ],
        compiler_params=params(),
        cost_estimate=hidden_cost(length, 1, TILES * TILE * (2 * D + 4 * length)),
        name="active_grads",
    )(rows, cotangent, weights)


def run_hidden_grads(first_row, rows, x, own, other, gain, active_grad, weights):
    length = own.shape[0]
    shape = jax.ShapeDtypeStruct
    return pl.pallas_call(
        functools.partial(hidden_grads, first_row),
        out_shape=[
            shape((length, D), bf16),
            shape((length, D), f32),
            shape((D, length), bf16),
            shape((1, D), f32),
            shape((TILES, length, 2 * TILE), bf16),
            shape((TILES, length, TILE), bf16),
            shape((TILES, TILE, length), bf16),
        ],
        in_specs=[SMEM_SPEC] + [VMEM_SPEC] * 4 + [ANY_SPEC] * 2,
        out_specs=[VMEM_SPEC] * 4 + [ANY_SPEC] * 3,
        scratch_shapes=[
            pltpu.VMEM((2, D, 2 * TILE), bf16),
            pltpu.VMEM((2, length, TILE), f32),
            pltpu.VMEM((2, length, TILE), bf16),
            pltpu.VMEM((2, TILE, length), bf16),
            pltpu.VMEM((2, length, 2 * TILE), bf16),
            pltpu.VMEM((length, D), bf16),
            pltpu.VMEM((length, D), f32),
            pltpu.SemaphoreType.DMA((2, 2)),
            pltpu.SemaphoreType.DMA((2, 3)),
        ],
        compiler_params=params(),
        cost_estimate=hidden_cost(length, 4, 2 * TILES * TILE * (2 * D + 6 * length)),
        name="hidden_grads",
    )(rows, x, own, other, gain, active_grad, weights)


def run_hidden_weight_grads(weight_rows, rows, half, cotangent, parts, weights, slots):
    length = cotangent.shape[0]
    shape = jax.ShapeDtypeStruct
    return pl.pallas_call(
        hidden_weight_grads,
        out_shape=[shape((length // NARROW, D), bf16)] * 2 + [shape((slots, BLK, BLK), bf16)],
        in_specs=[SMEM_SPEC] * 3 + [VMEM_SPEC] + [ANY_SPEC] * (4 * NARROW + 1),
        out_specs=[VMEM_SPEC, VMEM_SPEC, ANY_SPEC],
        scratch_shapes=[
            pltpu.VMEM((D, length), bf16),
            pltpu.VMEM((2, length, 2 * TILE), bf16),
            pltpu.VMEM((2, length, TILE), bf16),
            pltpu.VMEM((2, TILE, length), bf16),
            pltpu.VMEM((2, TILE, D), bf16),
            pltpu.VMEM((length, D), f32),
            pltpu.VMEM((2, D, 2 * TILE), bf16),
            pltpu.VMEM((2, TILE, D), bf16),
            pltpu.SemaphoreType.DMA((2, 3 * NARROW + 1)),
            pltpu.SemaphoreType.DMA((2, 2)),
            pltpu.SemaphoreType.DMA((NARROW,)),
        ],
        compiler_params=params(),
        cost_estimate=hidden_cost(length, 4, 2 * TILES * TILE * (4 * D + 4 * length)),
        name="hidden_weight_grads",
    )(weight_rows, rows, half, cotangent, *[array for part in parts for array in part], weights)


def run_attention_backward(
    weight_rows, rows, half, x, low, high, cotangent, gains, cosine, sine, allowed, normed_turned, qkv, mixed_turned,
    log_total, gain_two_parts, weights, grads, wide_count,
):
    length = x.shape[0]
    shape = jax.ShapeDtypeStruct
    empty_count = max(rows.shape[0] - BLOCK_TOTAL, 1)
    operands = (
        weight_rows, rows, half, x, *low, *high, cotangent, gains, cosine, sine, allowed, normed_turned, qkv, mixed_turned,
        log_total, *gain_two_parts, weights, grads,
    )
    return pl.pallas_call(
        attention_backward,
        out_shape=[
            shape((length // NARROW, D), f32),
            shape((length // NARROW, D), bf16),
            shape((length // NARROW, D), bf16),
            shape(grads.shape, bf16),
        ],
        in_specs=[SMEM_SPEC] * 3 + [VMEM_SPEC] * (len(operands) - 5) + [ANY_SPEC] * 2,
        out_specs=[VMEM_SPEC] * 3 + [ANY_SPEC],
        input_output_aliases={len(operands) - 1: 3},
        scratch_shapes=[
            pltpu.VMEM((D, QKV_WIDTH), bf16),
            pltpu.VMEM((QUERY_WIDTH, D), bf16),
            pltpu.VMEM((length, D), f32),
            pltpu.VMEM((length, D), bf16),
            pltpu.VMEM((length, QUERY_WIDTH), bf16),
            pltpu.VMEM((length, QKV_WIDTH), bf16),
            pltpu.VMEM((length, D), f32),
            pltpu.VMEM((1, D), f32),
            pltpu.VMEM((1, QKV_WIDTH), f32),
            pltpu.VMEM((D, QKV_WIDTH), bf16),
            pltpu.VMEM((QUERY_WIDTH, D), bf16),
            pltpu.VMEM((wide_count, BLK, BLK), bf16),
            pltpu.VMEM((empty_count, BLK, BLK), bf16),
            pltpu.SemaphoreType.DMA((2,)),
            pltpu.SemaphoreType.DMA((4,)),
        ],
        compiler_params=params(),
        name="attention_backward",
    )(*operands)


def largest_group(count):
    return max(size for size in range(1, 11) if count % size == 0)


def run_soap(reduced, masters, first_moment, second_moment, left_basis, right_basis):
    slots = masters.shape[0]
    group = largest_group(slots)
    shape = jax.ShapeDtypeStruct(masters.shape, f32)
    return pl.pallas_call(
        soap_update,
        out_shape=[shape] * 4 + [jax.ShapeDtypeStruct((SMALL_ROWS, BLK), f32)],
        in_specs=[VMEM_SPEC] * 6,
        out_specs=[ANY_SPEC] * 4 + [VMEM_SPEC],
        scratch_shapes=[pltpu.VMEM((2, group, BLK, BLK), f32)] * 4 + [pltpu.SemaphoreType.DMA((2, 4))],
        compiler_params=params(),
        name="soap_update",
    )(reduced, masters, first_moment, second_moment, left_basis, right_basis)


def sum_for_owners(
    line, steps, late_steps,
    grads, masters, first_moment, second_moment, left_basis, right_basis,
    grad_resid, grad_own, grad_sent, tokens, gain, resid, branch_own, branch_other,
    out, new_masters, new_first, new_second, input_grad, output, small_own, small_other,
    a_in, a_own, a_sum, a_keep, a_send, a_cross, a_up, a_down,
    b_in, b_own, b_sum, b_keep, b_send, b_cross, b_up, b_down,
    a_params, b_params, grad_resid_here, grad_own_here, grad_other_here, tokens_here, gain_here, resid_here,
    branch_own_here, branch_other_here,
    core_send, core_recv, own_sems, cross_send, cross_recv, up_send, up_recv, down_send, down_recv,
    b_core_send, b_core_recv, b_own_sems, b_cross_send, b_cross_recv, b_up_send, b_up_recv, b_down_send, b_down_recv,
    a_param_sems, b_param_sems, token_sems, swap_send, swap_recv, credits,
):
    wide = lax.axis_index("wide")
    narrow = lax.axis_index("narrow")
    z = wide // 4
    x = lax.rem(wide // 2, 2)
    core = lax.rem(wide, 2)
    mesh_id = pl.DeviceIdType.MESH
    core_peer = (wide + 1 - 2 * core, narrow)
    cross_peer = (wide + 2 - 4 * x, narrow)
    upper = (lax.rem(wide + 4, 4 * line), narrow)
    lower = (lax.rem(wide + 4 * line - 4, 4 * line), narrow)
    swap_peer = (wide, 1 - narrow)
    slots = out.shape[0]
    has_upper = z < line - 1
    has_lower = z > 0
    sum_depth = a_sum.shape[0]
    hop_depth = a_up.shape[0]
    b_sum_depth = b_sum.shape[0]

    barrier = pltpu.get_barrier_semaphore()
    pl.semaphore_signal(barrier, inc=1, device_id=core_peer, device_id_type=mesh_id)
    pl.semaphore_signal(barrier, inc=1, device_id=cross_peer, device_id_type=mesh_id)
    pl.semaphore_signal(barrier, inc=1, device_id=swap_peer, device_id_type=mesh_id)

    @pl.when(has_upper)
    def _():
        pl.semaphore_signal(barrier, inc=1, device_id=upper, device_id_type=mesh_id)

    @pl.when(has_lower)
    def _():
        pl.semaphore_signal(barrier, inc=1, device_id=lower, device_id_type=mesh_id)

    pl.semaphore_wait(barrier, 3 + has_upper.astype(jnp.int32) + has_lower.astype(jnp.int32))

    def remote(source, target, send_sem, recv_sem, peer):
        return pltpu.make_async_remote_copy(
            src_ref=source, dst_ref=target, send_sem=send_sem, recv_sem=recv_sem, device_id=peer, device_id_type=mesh_id
        )

    def core_copy(step):
        slot = lax.rem(step, DEPTH)
        source = grads.at[:, :, 1 - core, pl.ds(step * EARLY, EARLY)]
        return remote(source, a_in.at[slot], core_send.at[slot], core_recv.at[slot], core_peer)

    def own_copy(step):
        slot = lax.rem(step, DEPTH)
        return pltpu.make_async_copy(
            grads.at[:, :, core, pl.ds(step * EARLY, EARLY)], a_own.at[slot], own_sems.at[slot]
        )

    def b_core_copy(step):
        slot = lax.rem(step, DEPTH)
        source = grads.at[:, :, 1 - core, slots - 1 - step]
        return remote(source, b_in.at[slot], b_core_send.at[slot], b_core_recv.at[slot], core_peer)

    def b_own_copy(step):
        slot = lax.rem(step, DEPTH)
        return pltpu.make_async_copy(
            grads.at[:, :, core, slots - 1 - step], b_own.at[slot], b_own_sems.at[slot]
        )

    def cross_copy(step):
        slot = lax.rem(step, DEPTH)
        return remote(a_send.at[slot], a_cross.at[slot], cross_send.at[slot], cross_recv.at[slot], cross_peer)

    def b_cross_copy(step):
        slot = lax.rem(step, DEPTH)
        return remote(b_send.at[slot], b_cross.at[slot], b_cross_send.at[slot], b_cross_recv.at[slot], cross_peer)

    def up_copy(step, target):
        slot = lax.rem(step, hop_depth)
        return remote(
            a_sum.at[lax.rem(step, sum_depth), target], a_up.at[slot, target],
            up_send.at[slot, target], up_recv.at[slot, target], upper,
        )

    def down_copy(step, target):
        slot = lax.rem(step, hop_depth)
        return remote(
            a_sum.at[lax.rem(step, sum_depth), target], a_down.at[slot, target],
            down_send.at[slot, target], down_recv.at[slot, target], lower,
        )

    def b_up_copy(step, target):
        slot = lax.rem(step, hop_depth)
        return remote(
            b_sum.at[lax.rem(step, b_sum_depth), target], b_up.at[slot, target],
            b_up_send.at[slot, target], b_up_recv.at[slot, target], upper,
        )

    def b_down_copy(step, target):
        slot = lax.rem(step, hop_depth)
        return remote(
            b_sum.at[lax.rem(step, b_sum_depth), target], b_down.at[slot, target],
            b_down_send.at[slot, target], b_down_recv.at[slot, target], lower,
        )

    def give(channel, peer):
        pl.semaphore_signal(credits.at[channel], inc=1, device_id=peer, device_id_type=mesh_id)

    def take(channel, step, depth):
        @pl.when(step >= depth)
        def _():
            pl.semaphore_wait(credits.at[channel], 1)

    def feed(step, count, channel, remote_copy, local_copy):
        @pl.when(step < count)
        def _():
            take(channel, step, DEPTH)
            remote_copy(step).start()
            local_copy(step).start()

    sources = (masters, first_moment, second_moment, left_basis, right_basis)

    def param_loads(step):
        slot = lax.rem(step, 2)
        places = pl.ds(step * EARLY, EARLY)
        return [
            pltpu.make_async_copy(source.at[places], a_params.at[slot, index], a_param_sems.at[slot, index])
            for index, source in enumerate(sources)
        ]

    def b_param_loads(step):
        slot = lax.rem(step, 2)
        return [
            pltpu.make_async_copy(
                source.at[slots - 1 - step], b_params.at[slot, index], b_param_sems.at[slot, index]
            )
            for index, source in enumerate(sources)
        ]

    token_loads = [
        pltpu.make_async_copy(source, target, token_sems.at[index])
        for index, (source, target) in enumerate((
            (resid, resid_here), (branch_own, branch_own_here), (branch_other, branch_other_here),
            (grad_resid, grad_resid_here), (grad_own, grad_own_here), (tokens, tokens_here), (gain, gain_here),
        ))
    ]
    grad_swap = remote(grad_sent, grad_other_here, swap_send.at[0], swap_recv.at[0], swap_peer)
    small_swap = remote(small_own, small_other, swap_send.at[1], swap_recv.at[1], swap_peer)

    def finish_output():
        for copy in token_loads[:3]:
            copy.wait()

        def rows_of_output(rows):
            total = resid_here[rows, :] + branch_own_here[rows, :].astype(f32) + branch_other_here[rows, :].astype(f32)
            output[rows, :] = total.astype(bf16)

        row_chunks(output.shape[0], ROWS, rows_of_output)

    def finish_input_grad():
        for copy in token_loads[3:]:
            copy.wait()
        grad_swap.wait()

        def rows_of_grad(rows):
            values = tokens_here[rows, :].astype(f32)
            inverse = rms_inverse(values)
            scaled = grad_own_here[rows, :].astype(f32) + grad_other_here[rows, :].astype(f32)
            input_grad[rows, :] = grad_resid_here[rows, :] + norm_back(
                scaled * gain_here[...], values * inverse, inverse
            )

        row_chunks(input_grad.shape[0], ROWS, rows_of_grad)

    grad_swap.start()
    for early in range(DEPTH - 1):
        feed(early, steps, 0, core_copy, own_copy)
        feed(early, late_steps, 1, b_core_copy, b_own_copy)

    start_all(param_loads(0) + param_loads(1) + b_param_loads(1) + b_param_loads(2) + token_loads)

    def active(step, count):
        return (step >= 0) & (step < count)

    far = jnp.maximum(z, line - 1 - z)

    def hops(step_up, step_down, count, sums, depth, ups, downs, up, down, channel):
        @pl.when(active(step_up, count) & has_upper)
        def _():
            take(channel, step_up, hop_depth)
            slot = lax.rem(step_up, hop_depth)
            place = lax.rem(step_up, depth)

            def one(target, _):
                @pl.when(has_lower)
                def _():
                    up(step_up, target).wait_recv()
                    sums[place, target] += ups[slot, target]

                up(step_up, target).start()
                return 0

            lax.fori_loop(z + 1, line, one, 0)

        @pl.when(active(step_down, count) & has_lower)
        def _():
            take(channel + 1, step_down, hop_depth)
            slot = lax.rem(step_down, hop_depth)
            place = lax.rem(step_down, depth)

            def one(target, _):
                @pl.when(has_upper)
                def _():
                    down(step_down, target).wait_recv()
                    sums[place, target] += downs[slot, target]

                down(step_down, target).start()
                return 0

            lax.fori_loop(0, z, one, 0)

    def gather_hops(step, count, sums, depth, ups, downs, up, down, channel, total):
        slot = lax.rem(step, hop_depth)
        total[...] = sums[lax.rem(step, depth), z].astype(f32)

        @pl.when(has_lower)
        def _():
            up(step, z).wait_recv()
            total[...] += ups[slot, z].astype(f32)

            @pl.when(step < count - hop_depth)
            def _():
                give(channel, lower)

        @pl.when(has_upper)
        def _():
            down(step, z).wait_recv()
            total[...] += downs[slot, z].astype(f32)

            @pl.when(step < count - hop_depth)
            def _():
                give(channel + 1, upper)

    def retire(step, count, up, down):
        @pl.when(active(step, count))
        def _():
            def sent_up(target, _):
                up(step, target).wait_send()
                return 0

            def sent_down(target, _):
                down(step, target).wait_send()
                return 0

            lax.fori_loop(z + 1, line, sent_up, 0)
            lax.fori_loop(0, z, sent_down, 0)

    def iteration(step, _):
        feed(step + DEPTH - 1, steps, 0, core_copy, own_copy)
        feed(step + DEPTH - 1, late_steps, 1, b_core_copy, b_own_copy)

        retire(step - CROSS_LAG - HOP_LAG * far - 1, steps, up_copy, down_copy)
        retire(step - HOP_LAG * far - 1, late_steps, b_up_copy, b_down_copy)

        @pl.when(step < steps)
        def _():
            slot = lax.rem(step, DEPTH)
            place = lax.rem(step, sum_depth)
            core_copy(step).wait()
            own_copy(step).wait()

            @pl.when(step >= DEPTH)
            def _():
                cross_copy(step - DEPTH).wait_send()

            for target in range(line):
                a_send[slot, target] = a_own[slot, target, 1 - x] + a_in[slot, target, 1 - x]
            take(2, step, DEPTH)
            cross_copy(step).start()
            for target in range(line):
                a_sum[place, target] = a_own[slot, target, x] + a_in[slot, target, x]

            @pl.when(step < steps - DEPTH)
            def _():
                give(0, core_peer)

        @pl.when(step < late_steps)
        def _():
            slot = lax.rem(step, DEPTH)
            b_core_copy(step).wait()
            b_own_copy(step).wait()
            b_sum[lax.rem(step, b_sum_depth)] = b_own[slot] + b_in[slot]

            @pl.when(step < late_steps - DEPTH)
            def _():
                give(1, core_peer)

        crossed = step - CROSS_LAG

        @pl.when(active(crossed, steps))
        def _():
            slot = lax.rem(crossed, DEPTH)
            place = lax.rem(crossed, sum_depth)
            cross_copy(crossed).wait_recv()
            for target in range(line):
                a_sum[place, target] += a_cross[slot, target]

            @pl.when(crossed < steps - DEPTH)
            def _():
                give(2, cross_peer)

        hops(
            step - HOP_LAG * z, step - HOP_LAG * (line - 1 - z), late_steps, b_sum, b_sum_depth, b_up, b_down,
            b_up_copy, b_down_copy, 6,
        )
        hops(
            crossed - HOP_LAG * z, crossed - HOP_LAG * (line - 1 - z), steps, a_sum, sum_depth, a_up, a_down,
            up_copy, down_copy, 4,
        )

        last = crossed - HOP_LAG * far

        @pl.when(active(last, steps))
        def _():
            gather_hops(last, steps, a_sum, sum_depth, a_up, a_down, up_copy, down_copy, 4, a_keep)
            out[pl.ds(last * EARLY, EARLY)] = a_keep[...].astype(bf16)
            slot = lax.rem(last, 2)
            for copy in param_loads(last):
                copy.wait()
            soap_blocks(
                [a_keep[index] for index in range(EARLY)],
                *[[a_params.at[slot, kind, index] for index in range(EARLY)] for kind in range(5)],
                *[
                    [target.at[last * EARLY + index] for index in range(EARLY)]
                    for target in (new_masters, new_first, new_second)
                ],
            )

            @pl.when(last + 2 < steps)
            def _():
                start_all(param_loads(last + 2))

        arrived = step - HOP_LAG * far

        @pl.when(active(arrived, late_steps))
        def _():
            slot = lax.rem(arrived, DEPTH)

            @pl.when(arrived >= DEPTH)
            def _():
                b_cross_copy(arrived - DEPTH).wait_send()

            gather_hops(
                arrived, late_steps, b_sum, b_sum_depth, b_up, b_down, b_up_copy, b_down_copy, 6, b_keep.at[slot]
            )
            b_send[slot] = b_keep[slot, 1 - x].astype(bf16)
            take(3, arrived, DEPTH)
            b_cross_copy(arrived).start()

        paired = arrived - CROSS_LAG

        @pl.when(active(paired, late_steps))
        def _():
            slot = lax.rem(paired, DEPTH)
            b_cross_copy(paired).wait_recv()
            place = slots - 1 - paired
            total = b_keep[slot, x] + b_cross[slot].astype(f32)
            out[place] = total.astype(bf16)

            @pl.when(paired < late_steps - DEPTH)
            def _():
                give(3, cross_peer)

            @pl.when(paired == 0)
            def _():
                small_own[...] = total[: small_own.shape[0]]
                small_swap.start()

            @pl.when(paired > 0)
            def _():
                slot = lax.rem(paired, 2)
                for copy in b_param_loads(paired):
                    copy.wait()
                soap_blocks(
                    [total], *[[b_params.at[slot, kind]] for kind in range(5)],
                    [new_masters.at[place]], [new_first.at[place]], [new_second.at[place]],
                )

                @pl.when(paired + 2 < late_steps)
                def _():
                    start_all(b_param_loads(paired + 2))

        pl.when(step == 4)(finish_output)
        pl.when(step == 8)(finish_input_grad)
        return 0

    lag = HOP_LAG * (line - 1) + CROSS_LAG
    lax.fori_loop(0, max(steps, late_steps) + lag + 2, iteration, 0)
    for step in range(max(steps - DEPTH, 0), steps):
        cross_copy(step).wait_send()
    for step in range(max(late_steps - DEPTH, 0), late_steps):
        b_cross_copy(step).wait_send()
    small_swap.wait()


def run_sum_for_owners(grads, wide_count, blocks, token_arrays):
    line = wide_count // 4
    slots, block = grads.shape[0] // wide_count, grads.shape[1:]
    steps = (slots - 1) // (EARLY + 1)
    late_steps = slots - EARLY * steps
    sum_depth = CROSS_LAG + HOP_LAG * (line - 1) + 2
    b_sum_depth = HOP_LAG * (line - 1) + 2
    hop_depth = 2 * HOP_LAG + 2
    dma = pltpu.SemaphoreType.DMA

    def vmem(*shape):
        return pltpu.VMEM(shape + block, bf16)

    def wide_vmem(*shape):
        return pltpu.VMEM(shape + block, f32)

    return pl.pallas_call(
        functools.partial(sum_for_owners, line, steps, late_steps),
        out_shape=[pltpu.VMEM((slots,) + block, bf16)]
        + [pltpu.VMEM(blocks[0].shape, f32)] * 3
        + [pltpu.VMEM(token_arrays[0].shape, f32), pltpu.VMEM(token_arrays[0].shape, bf16)]
        + [pltpu.VMEM((SMALL_ROWS, block[-1]), f32)] * 2,
        in_specs=[ANY_SPEC] * (1 + len(blocks) + len(token_arrays)),
        out_specs=[VMEM_SPEC] * 8,
        scratch_shapes=[
            vmem(DEPTH, line, 2, EARLY),
            vmem(DEPTH, line, 2, EARLY),
            vmem(sum_depth, line, EARLY),
            wide_vmem(EARLY),
            vmem(DEPTH, line, EARLY),
            vmem(DEPTH, line, EARLY),
            vmem(hop_depth, line, EARLY),
            vmem(hop_depth, line, EARLY),
            vmem(DEPTH, line, 2),
            vmem(DEPTH, line, 2),
            vmem(b_sum_depth, line, 2),
            wide_vmem(DEPTH, 2),
            vmem(DEPTH),
            vmem(DEPTH),
            vmem(hop_depth, line, 2),
            vmem(hop_depth, line, 2),
            wide_vmem(2, len(blocks), EARLY),
            wide_vmem(2, len(blocks)),
        ]
        + [pltpu.VMEM(array.shape, array.dtype) for array in token_arrays]
        + ([dma((DEPTH,))] * 5 + [dma((hop_depth, line))] * 4) * 2
        + [dma((2, len(blocks)))] * 2
        + [dma((len(token_arrays) - 1,)), dma((2,)), dma((2,)), pltpu.SemaphoreType.REGULAR((8,))],
        compiler_params=params(SUM_VMEM, collective_id=0, has_side_effects=True),
        cost_estimate=pl.CostEstimate(flops=0, bytes_accessed=2 * grads.size * 8, transcendentals=0),
        name="sum_for_owners",
    )(grads.reshape((line, 2, 2, slots) + block), *blocks, *token_arrays)


def write_results(
    reduced, masters, first_moment, second_moment, input_grad, output, small_own, small_other,
    block_grad_out, masters_out, first_out, second_out, input_grad_out, output_out, small_out,
    stage, stage_sems, sems,
):
    copies = [
        pltpu.make_async_copy(source, target, sems.at[index])
        for index, (source, target) in enumerate((
            (masters, masters_out), (first_moment, first_out), (second_moment, second_out),
            (input_grad, input_grad_out), (output, output_out),
        ))
    ]
    start_all(copies)
    small_out[0] = small_own[...]
    small_out[1] = small_other[...]
    group = stage.shape[1]
    steps = masters.shape[0] // group

    def store(step):
        slot = lax.rem(step, 2)
        return pltpu.make_async_copy(
            stage.at[slot], block_grad_out.at[pl.ds(step * group, group)], stage_sems.at[slot]
        )

    @pl.loop(0, steps)
    def _(step):
        @pl.when(step >= 2)
        def _():
            store(step - 2).wait()

        stage[lax.rem(step, 2)] = reduced[pl.ds(step * group, group)].astype(f32)
        store(step).start()

    for step in range(max(steps - 2, 0), steps):
        store(step).wait()
    for copy in copies:
        copy.wait()


def run_write_results(*arrays):
    arrays = [pltpu.with_memory_space_constraint(array, pltpu.VMEM) for array in arrays]
    blocks, rows, small = arrays[1].shape, arrays[4].shape, arrays[-1].shape
    group = largest_group(blocks[0])
    shape = jax.ShapeDtypeStruct
    return pl.pallas_call(
        write_results,
        out_shape=[shape(blocks, f32)] * 4 + [shape(rows, f32), shape(rows, bf16), shape((2,) + small, f32)],
        in_specs=[VMEM_SPEC] * len(arrays),
        out_specs=[ANY_SPEC] * 6 + [VMEM_SPEC],
        scratch_shapes=[
            pltpu.VMEM((2, group) + blocks[1:], f32),
            pltpu.SemaphoreType.DMA((2,)),
            pltpu.SemaphoreType.DMA((5,)),
        ],
        compiler_params=params(WRITE_VMEM),
        name="write_results",
    )(*arrays)


def rope_tables(segment_row):
    token_index = jnp.arange(segment_row.shape[0], dtype=jnp.int32)
    changed = jnp.concatenate([jnp.ones((1,), dtype=bool), segment_row[1:] != segment_row[:-1]])
    begins = lax.cummax(jnp.where(changed, token_index, jnp.zeros_like(token_index)), axis=0)
    places = (token_index - begins).astype(f32)
    frequency = rope_base ** (-(jnp.arange(HEAD_DIM // 2, dtype=f32) * 2.0) / HEAD_DIM)
    angles = places[:, None] * frequency[None, :]
    cosine = jnp.concatenate([jnp.cos(angles), jnp.cos(angles)], axis=-1)
    sine_signed = jnp.concatenate([-jnp.sin(angles), jnp.sin(angles)], axis=-1)
    return (cosine, sine_signed)


def rms_parts(values):
    inverse = rms_inverse(values)
    return (inverse, values * inverse)


def norm_back(grad_scaled, normed, inverse):
    return inverse * (grad_scaled - normed * jnp.mean(grad_scaled * normed, axis=-1, keepdims=True))


def adam_small(param_now, gradient, first_now, second_now, rate_here):
    first_new = beta_first * first_now + (1.0 - beta_first) * gradient
    second_new = beta_second * second_now + (1.0 - beta_second) * gradient * gradient
    param_new = param_now - rate_here * (first_new / first_fix) / (
        jnp.sqrt(second_new / second_fix) + adam_eps
    )
    return (param_new, first_new, second_new)


def swap_halves(values):
    return lax.ppermute(values, "narrow", [(0, 1), (1, 0)])


def body(
    tokens,
    cotangent,
    segments,
    owner_list,
    masters,
    first_moment,
    second_moment,
    left_basis,
    right_basis,
    gains,
    gain_first,
    gain_second,
    biases,
    bias_first,
    bias_second,
):
    half = lax.axis_index("narrow")
    wide_index = lax.axis_index("wide")
    wide_count = lax.axis_size("wide")
    tokens_here = tokens.shape[0]
    slots_here = masters.shape[0]
    slots_half = owner_list.shape[0]
    gains_here = gains.shape[0]
    biases_here = biases.shape[1]

    def join_halves(own, other, axis=0):
        return jnp.where(
            half == 0, jnp.concatenate([own, other], axis=axis), jnp.concatenate([other, own], axis=axis)
        )

    masters_low, gains, biases = lax.optimization_barrier((masters.astype(bf16), gains, biases))
    weights = lax.all_gather(masters_low, "wide", axis=0, tiled=True)
    gain_full = lax.all_gather(gains, ("wide", "narrow"), axis=0, tiled=True).reshape(2, D)
    bias_full = lax.all_gather(biases.reshape(-1).astype(bf16), "wide", axis=0, tiled=True)
    bias_full = bias_full.astype(f32).reshape(1, QKV_WIDTH)
    pair_gains = 2 * gains_here

    position = jnp.arange(slots_half, dtype=jnp.int32)
    empty = owner_list == BLOCK_TOTAL
    number = jnp.where(empty, BLOCK_TOTAL - 1 + jnp.cumsum(empty.astype(jnp.int32)), owner_list)
    weight_rows = jnp.zeros((slots_half,), jnp.int32).at[number].set(position, unique_indices=True)
    rows = weight_rows + weight_rows // slots_here
    half_index = half.astype(jnp.int32).reshape(1)

    segment_row = lax.dynamic_index_in_dim(segments, wide_index, 0, keepdims=False)
    cosine, sine = rope_tables(segment_row)
    token_index = jnp.arange(segment_row.shape[0], dtype=jnp.int32)
    allowed_turned = (
        (segment_row[None, :] == segment_row[:, None]) & (token_index[None, :] >= token_index[:, None])
    ).astype(f32)
    tokens_row = join_halves(tokens, swap_halves(tokens))
    cotangent_row = join_halves(cotangent, swap_halves(cotangent))
    weights, tokens_row, cotangent_row, gain_full, bias_full = lax.optimization_barrier(
        (weights, tokens_row, cotangent_row, gain_full, bias_full)
    )

    low_part, high_part, normed_one_turned, qkv, mixed_turned, log_total = run_attention_forward(
        weight_rows, tokens_row, gain_full[0:1], bias_full, cosine, sine, allowed_turned, weights
    )
    low_other = swap_halves(low_part)
    active_grad = run_active_grads(weight_rows, cotangent_row, weights)
    high_sent, low_other = lax.optimization_barrier((high_part, low_other))
    high_other = swap_halves(high_sent)
    gain_two = gain_full[1:2]
    grad_low, resid_low, turned_low, gain_low, *hidden_low = run_hidden_grads(
        0, weight_rows, tokens_row, low_part, low_other, gain_two, active_grad, weights
    )
    grad_low_other = swap_halves(grad_low)
    grad_high, resid_high, turned_high, gain_high, *hidden_high = run_hidden_grads(
        tokens_here, weight_rows, tokens_row, high_part, high_other, gain_two, active_grad, weights
    )
    grad_high_other = swap_halves(grad_high)
    branch_own, branch_sent, grads = run_hidden_weight_grads(
        weight_rows, rows, half_index, cotangent_row, [(turned_low, *hidden_low), (turned_high, *hidden_high)], weights,
        wide_count * (slots_here + 1),
    )
    branch_other = swap_halves(branch_sent)
    grad_resid, grad_one_own, grad_one_sent, grads = run_attention_backward(
        weight_rows, rows, half_index, tokens_row, (resid_low, grad_low, grad_low_other),
        (resid_high, grad_high, grad_high_other), cotangent_row, gain_full, cosine, sine, allowed_turned,
        normed_one_turned, qkv, mixed_turned, log_total, (gain_low, gain_high), weights, grads, wide_count,
    )
    resid_own = jnp.where(half == 0, resid_low, resid_high)
    blocks = [masters, first_moment, second_moment, left_basis, right_basis]
    if wide_count == 16:
        token_arrays = [
            grad_resid, grad_one_own, grad_one_sent, tokens, gain_full[0:1], resid_own, branch_own, branch_other
        ]
        block_grad, new_masters, new_first, new_second, input_grad, output, small_sums = run_write_results(
            *run_sum_for_owners(grads, wide_count, blocks, token_arrays)
        )
        gain_parts = small_sums[0, :2] + small_sums[1, :2]
        bias_row = small_sums[0, 2]
    else:
        reduced = lax.psum_scatter(grads, "wide", scatter_dimension=0, tiled=True)
        block_grad, new_masters, new_first, new_second, small_sums = run_soap(reduced, *blocks)
        gain_parts = small_sums[:2] + swap_halves(small_sums[:2])
        bias_row = small_sums[2]
        output = (resid_own + branch_own.astype(f32) + branch_other.astype(f32)).astype(bf16)
        inverse_one, normed_one = rms_parts(tokens.astype(f32))
        grad_one = grad_one_own.astype(f32) + swap_halves(grad_one_sent).astype(f32)
        input_grad = grad_resid + norm_back(grad_one * gain_full[0:1], normed_one, inverse_one)

    gain_first_index = wide_index * pair_gains
    gain_offset = gain_first_index - jnp.minimum(gain_first_index // BLK, 2 * D // BLK - 2) * BLK
    bias_offset = lax.rem(wide_index * biases_here, BLK)
    gain_grad = lax.dynamic_slice_in_dim(gain_parts.reshape(-1), gain_offset + half * gains_here, gains_here, 0)
    bias_grad = lax.dynamic_slice_in_dim(bias_row, bias_offset, biases_here, 0).reshape(biases.shape)
    new_gains, new_gain_first, new_gain_second = adam_small(gains, gain_grad, gain_first, gain_second, rate_gains)
    new_biases, new_bias_first, new_bias_second = adam_small(biases, bias_grad, bias_first, bias_second, rate_small)

    return (
        output,
        input_grad,
        block_grad,
        new_masters,
        new_first,
        new_second,
        gain_grad,
        new_gains,
        new_gain_first,
        new_gain_second,
        bias_grad,
        new_biases,
        new_bias_first,
        new_bias_second,
    )


def solution(mesh):
    tokens_spec = P(("wide", "narrow"), None)
    blocks_spec = P(("wide", "narrow"), None, None)
    gains_spec = P(("wide", "narrow"))
    bias_spec = P("narrow", "wide")
    in_specs = (
        (tokens_spec, tokens_spec, P(), P()) + (blocks_spec,) * 5 + (gains_spec,) * 3 + (bias_spec,) * 3
    )
    out_specs = (tokens_spec, tokens_spec) + (blocks_spec,) * 4 + (gains_spec,) * 4 + (bias_spec,) * 4
    return jax.shard_map(body, mesh=mesh, in_specs=in_specs, out_specs=out_specs, check_vma=False)
```

```python
import functools

import jax
import jax.numpy as jnp
from jax import lax
from jax.experimental import pallas as pl
from jax.experimental.pallas import tpu as pltpu
from jax.sharding import PartitionSpec as P

D = 1536
FF = 8960
HEADS = 12
KV_HEADS = 2
HEAD_DIM = 128
BLK = 128
STEP_COUNT = 5


beta_first = 0.95
beta_second = 0.95
adam_eps = 1e-08
rate_blocks = 0.03
rate_small = 0.4
rate_gains = 0.6
norm_eps = 1e-06
rope_base = 10000.0
masked_score = -1e30
first_fix = 1.0 - beta_first**STEP_COUNT
second_fix = 1.0 - beta_second**STEP_COUNT
scaling = HEAD_DIM ** (-0.5)

bf16 = jnp.bfloat16
f32 = jnp.float32

NARROW = 2
ROW_BLOCKS = D // BLK
QUERY_COLS = HEADS * HEAD_DIM // NARROW // BLK
PAIR_COLS = KV_HEADS * HEAD_DIM // NARROW // BLK
HIDDEN_COLS = FF // NARROW // BLK
QKV_COLS = QUERY_COLS + 2 * PAIR_COLS
QUERY_WIDTH = QUERY_COLS * BLK
QKV_WIDTH = QKV_COLS * BLK
KEY_BASE = ROW_BLOCKS * QUERY_COLS
VALUE_BASE = KEY_BASE + ROW_BLOCKS * PAIR_COLS
OUT_BASE = VALUE_BASE + ROW_BLOCKS * PAIR_COLS
GATE_BASE = OUT_BASE + QUERY_COLS * ROW_BLOCKS
UP_BASE = GATE_BASE + ROW_BLOCKS * HIDDEN_COLS
DOWN_BASE = UP_BASE + ROW_BLOCKS * HIDDEN_COLS
BLOCK_TOTAL = DOWN_BASE + HIDDEN_COLS * ROW_BLOCKS

TILE_BLOCKS = 6
TILES = -(-HIDDEN_COLS // TILE_BLOCKS)
LAST_BLOCKS = HIDDEN_COLS - (TILES - 1) * TILE_BLOCKS
TILE = TILE_BLOCKS * BLK
COLS = 256
ROWS = 64
SMALL_ROWS = 16
VMEM_LIMIT = 60 * 2**20
SUM_VMEM = 39 * 2**20
WRITE_VMEM = 6 * 2**20

EARLY = 4
DEPTH = 3
CROSS_LAG = 2
HOP_LAG = 1

VMEM_SPEC = pl.BlockSpec(memory_space=pltpu.VMEM)
SMEM_SPEC = pl.BlockSpec(memory_space=pltpu.SMEM)
ANY_SPEC = pl.BlockSpec(memory_space=pl.ANY)


def spans(total, step):
    return [(begin, min(step, total - begin)) for begin in range(0, total, step)]


def dot_nn(left, right):
    return jnp.dot(left, right, preferred_element_type=f32)


def dot_nt(left, right):
    return lax.dot_general(left, right, (((1,), (1,)), ((), ())), preferred_element_type=f32)


def block_ref(ref, row_block, col_block):
    return ref.at[pl.ds(row_block * BLK, BLK), pl.ds(col_block * BLK, BLK)]


def fetch_piece(rows_ref, weights, target, base, pitch, row_blocks, col_blocks, first_col, sem):
    @pl.loop(0, row_blocks)
    def _(i):
        for j in range(col_blocks):
            pltpu.make_async_copy(
                weights.at[rows_ref[base + i * pitch + j]],
                block_ref(target, i, first_col + j),
                sem,
            ).start()


def store_piece(rows_ref, source, grads, base, pitch, row_blocks, col_blocks, first_col, sem):
    @pl.loop(0, row_blocks)
    def _(i):
        for j in range(col_blocks):
            pltpu.make_async_copy(
                block_ref(source, i, first_col + j),
                grads.at[rows_ref[base + i * pitch + j]],
                sem,
            ).start()


def wait_bytes(ref, sem):
    pltpu.make_async_copy(ref, ref, sem).wait()


def copies_between(sources, targets, sems):
    return [
        pltpu.make_async_copy(source, target, sems.at[index])
        for index, (source, target) in enumerate(zip(sources, targets, strict=True))
    ]


def wait_all(copies):
    for copy in copies:
        copy.wait()


def fetch_attention(rows_ref, weights, w_qkv, w_out, sems):
    fetch_piece(rows_ref, weights, w_qkv, 0, QUERY_COLS, ROW_BLOCKS, QUERY_COLS, 0, sems.at[0])
    fetch_piece(rows_ref, weights, w_qkv, KEY_BASE, PAIR_COLS, ROW_BLOCKS, PAIR_COLS, QUERY_COLS, sems.at[0])
    fetch_piece(
        rows_ref, weights, w_qkv, VALUE_BASE, PAIR_COLS, ROW_BLOCKS, PAIR_COLS, QUERY_COLS + PAIR_COLS, sems.at[0]
    )
    fetch_piece(rows_ref, weights, w_out, OUT_BASE, ROW_BLOCKS, QUERY_COLS, ROW_BLOCKS, 0, sems.at[1])


def rms_inverse(values):
    return lax.rsqrt(jnp.mean(values * values, axis=-1, keepdims=True) + norm_eps)


def row_chunks(total, step, run):
    @pl.loop(0, total // step)
    def _(chunk):
        run(pl.ds(pl.multiple_of(chunk * step, step), step))


def small_places(owner, wide_count):
    gain_row = min(owner * (2 * D // wide_count) // BLK, 2 * D // BLK - 2)
    return (gain_row, owner * (QKV_WIDTH // wide_count) // BLK)


def scores_turned(keys, queries, allowed):
    return jnp.where(allowed, dot_nt(keys, queries) * scaling, masked_score)


def attention_forward(
    rows_ref,
    gain_ref,
    bias_ref,
    x_hbm,
    cos_hbm,
    sin_hbm,
    allowed_hbm,
    weights,
    part_low_ref,
    part_high_ref,
    log_ref,
    normed_turned_out,
    qkv_out,
    mixed_turned_out,
    x_ref,
    cos_ref,
    sin_ref,
    allowed_ref,
    normed_turned,
    qkv,
    mixed_turned,
    w_qkv,
    w_out,
    normed,
    mixed,
    sems,
    load_sems,
    store_sems,
):
    loads = copies_between(
        (x_hbm, cos_hbm, sin_hbm, allowed_hbm), (x_ref, cos_ref, sin_ref, allowed_ref), load_sems
    )
    stores = copies_between(
        (normed_turned, qkv, mixed_turned), (normed_turned_out, qkv_out, mixed_turned_out), store_sems
    )
    start_all(loads)
    fetch_attention(rows_ref, weights, w_qkv, w_out, sems)
    length = x_ref.shape[0]
    part = length // NARROW

    def norm_rows(rows):
        values = x_ref[rows, :].astype(f32)
        normed[rows, :] = (values * rms_inverse(values) * gain_ref[...]).astype(bf16)

    loads[0].wait()
    row_chunks(length, ROWS, norm_rows)
    wait_all(loads[1:])
    wait_bytes(w_qkv, sems.at[0])
    for begin, size in spans(QKV_WIDTH, COLS):
        products = dot_nn(normed[...], w_qkv[:, pl.ds(begin, size)]) + bias_ref[:, pl.ds(begin, size)]
        for offset, width in spans(size, HEAD_DIM):
            head = products[:, offset : offset + width]
            if begin + offset < QUERY_WIDTH + PAIR_COLS * BLK:
                head = head * cos_ref[...] + pltpu.roll(head, HEAD_DIM // 2, 1) * sin_ref[...]
            qkv[:, pl.ds(begin + offset, width)] = head.astype(bf16)
    for begin, size in spans(D, COLS):
        normed_turned[pl.ds(begin, size), :] = normed[:, pl.ds(begin, size)].T
    start_all(stores[:2])
    values_turned = qkv[:, pl.ds(QUERY_WIDTH + HEAD_DIM, HEAD_DIM)].T
    for head in range(QUERY_COLS):
        columns = pl.ds(head * HEAD_DIM, HEAD_DIM)
        for first in range(0, length, part):
            tokens, seen = pl.ds(first, part), first + part
            scores = scores_turned(
                qkv[:seen, pl.ds(QUERY_WIDTH, HEAD_DIM)], qkv[tokens, columns], allowed_ref[:seen, tokens] > 0
            )
            peak = jnp.max(scores, axis=0, keepdims=True)
            expo = jnp.exp(scores - peak)
            total = jnp.sum(expo, axis=0, keepdims=True)
            log_ref[pl.ds(head, 1), tokens] = peak + jnp.log(total)
            probs = (expo / total).astype(bf16)
            mixed_head = dot_nn(values_turned[:, :seen], probs).astype(bf16)
            mixed_turned[columns, tokens] = mixed_head
            mixed[tokens, columns] = mixed_head.T
    stores[2].start()
    wait_bytes(w_out, sems.at[1])
    for part_ref, first in ((part_low_ref, 0), (part_high_ref, part)):
        for begin, size in spans(D, COLS):
            part_ref[:, pl.ds(begin, size)] = dot_nn(
                mixed[pl.ds(first, part), :], w_out[:, pl.ds(begin, size)]
            ).astype(bf16)
    wait_all(stores)


def pair_copies(rows_ref, blocks_hbm, pair, sem, column, place, outward=False):
    return [
        block_copy(blocks_hbm.at[rows_ref[base + i * HIDDEN_COLS + column]], block_ref(pair, i, which), sem, outward)
        for i in range(ROW_BLOCKS)
        for base, which in ((GATE_BASE, 2 * place), (UP_BASE, 2 * place + 1))
    ]


def down_copies(rows_ref, blocks_hbm, down, sem, column, place, outward=False):
    return [
        block_copy(blocks_hbm.at[rows_ref[DOWN_BASE + column * ROW_BLOCKS + i]], block_ref(down, place, i), sem, outward)
        for i in range(ROW_BLOCKS)
    ]


def block_copy(in_hbm, in_vmem, sem, outward):
    return pltpu.make_async_copy(*((in_vmem, in_hbm) if outward else (in_hbm, in_vmem)), sem)


def start_all(copies):
    for copy in copies:
        copy.start()


def half_rows(half_ref, length):
    begin = pl.multiple_of(half_ref[0] * length, length)
    return (pl.ds(begin, length), pl.ds(pl.multiple_of(length - begin, length), length))


def hidden_column(tile, place):
    return jnp.minimum(tile * TILE_BLOCKS + place, HIDDEN_COLS - 1)


def hidden_tiles(run):
    @pl.loop(0, TILES - 1)
    def _(tile):
        run(tile, lax.rem(tile, 2), TILE_BLOCKS, True)

    run(TILES - 1, (TILES - 1) % 2, LAST_BLOCKS, False)


def active_grads(rows_ref, cot_ref, weights, out, down_out, w_down, stage, load_sems, store_sems, down_sems):
    ring = w_down.shape[0]

    def fetch(tile):
        slot = lax.rem(tile, ring)
        for place in range(TILE_BLOCKS):
            start_all(
                down_copies(rows_ref, weights, w_down.at[slot], load_sems.at[slot], hidden_column(tile, place), place)
            )

    def store(tile):
        return pltpu.make_async_copy(stage.at[lax.rem(tile, 2)], out.at[tile], store_sems.at[lax.rem(tile, 2)])

    def store_down(tile):
        slot = lax.rem(tile, ring)
        return pltpu.make_async_copy(w_down.at[slot], down_out.at[tile], down_sems.at[slot])

    fetch(0)

    def run(tile, slot, blocks, more):
        here = lax.rem(tile, ring)

        @pl.when(tile >= ring - 1)
        def _():
            store_down(tile - ring + 1).wait()

        if more:
            fetch(tile + 1)
        wait_bytes(w_down.at[here], load_sems.at[here])
        if blocks < TILE_BLOCKS:
            w_down[here, pl.ds(blocks * BLK, (TILE_BLOCKS - blocks) * BLK), :] = jnp.zeros(
                ((TILE_BLOCKS - blocks) * BLK, D), bf16
            )
        store_down(tile).start()

        @pl.when(tile >= 2)
        def _():
            store(tile - 2).wait()

        for begin, size in spans(blocks * BLK, COLS):
            stage[slot, :, pl.ds(begin, size)] = dot_nt(cot_ref[...], w_down[here, pl.ds(begin, size), :])
        store(tile).start()

    hidden_tiles(run)
    for tile in range(max(TILES - 2, 0), TILES):
        store(tile).wait()
    for tile in range(max(TILES - ring + 1, 0), TILES):
        store_down(tile).wait()


def hidden_grads(
    first_row,
    rows_ref,
    gain_ref,
    x_hbm,
    own_hbm,
    other_hbm,
    active_grad,
    weights,
    grad_ref,
    gain_part_ref,
    resid_out,
    normed_turned_out,
    pair_grads,
    active,
    active_turned,
    x_ref,
    own_ref,
    other_ref,
    resid_ref,
    normed_turned_ref,
    w_pair,
    grad_active,
    straight,
    turned,
    grads,
    normed,
    grad_sum,
    load_sems,
    store_sems,
    token_sems,
):
    length = own_ref.shape[0]
    token_loads = copies_between(
        (x_hbm.at[pl.ds(first_row, length)], own_hbm, other_hbm), (x_ref, own_ref, other_ref), token_sems
    )
    store_resid = pltpu.make_async_copy(resid_ref, resid_out, token_sems.at[3])
    store_turned = pltpu.make_async_copy(normed_turned_ref, normed_turned_out, token_sems.at[4])
    start_all(token_loads)

    def fetch(tile, slot, place):
        start_all(
            pair_copies(rows_ref, weights, w_pair.at[slot], load_sems.at[slot, 0], hidden_column(tile, place), place)
        )

    def load_grad(tile, slot):
        return pltpu.make_async_copy(active_grad.at[tile, pl.ds(first_row, length)], grad_active.at[slot], load_sems.at[slot, 1])

    def stores(tile, slot):
        return (
            pltpu.make_async_copy(turned.at[slot], active_turned.at[tile], store_sems.at[slot, 0]),
            pltpu.make_async_copy(grads.at[slot], pair_grads.at[tile], store_sems.at[slot, 1]),
            pltpu.make_async_copy(straight.at[slot], active.at[tile], store_sems.at[slot, 2]),
        )

    for place in range(TILE_BLOCKS):
        fetch(0, 0, place)
    load_grad(0, 0).start()

    def norm_rows(rows):
        values = x_ref[rows, :].astype(f32) + own_ref[rows, :].astype(f32) + other_ref[rows, :].astype(f32)
        resid_ref[rows, :] = values
        normed[rows, :] = (values * rms_inverse(values) * gain_ref[...]).astype(bf16)

    wait_all(token_loads)
    row_chunks(length, ROWS, norm_rows)
    store_resid.start()
    grad_sum[...] = jnp.zeros_like(grad_sum)

    def run(tile, slot, blocks, more):
        wait_bytes(w_pair.at[slot], load_sems.at[slot, 0])
        load_grad(tile, slot).wait()
        if more:
            load_grad(tile + 1, 1 - slot).start()

        @pl.when(tile >= 2)
        def _():
            for copy in stores(tile - 2, slot):
                copy.wait()

        for place in range(blocks):
            columns = pl.ds(place * BLK, BLK)
            pair = dot_nn(normed[...], w_pair[slot, :, pl.ds(2 * place * BLK, 2 * BLK)])
            gate = pair[:, :BLK]
            upper = pair[:, BLK:]
            grad = grad_active[slot, :, columns]
            sigmoid = jax.nn.sigmoid(gate)
            silu = gate * sigmoid
            active_here = (silu * upper).astype(bf16)
            straight[slot, :, columns] = active_here
            turned[slot, columns, :] = active_here.T
            grads[slot, :, pl.ds(2 * place * BLK, BLK)] = (
                grad * upper * sigmoid * (1.0 + gate * (1.0 - sigmoid))
            ).astype(bf16)
            grads[slot, :, pl.ds((2 * place + 1) * BLK, BLK)] = (grad * silu).astype(bf16)
            if more:
                fetch(tile + 1, 1 - slot, place)
        if more:
            for place in range(blocks, TILE_BLOCKS):
                fetch(tile + 1, 1 - slot, place)
        turn = pl.ds(pl.multiple_of(tile * COLS, COLS), COLS)
        normed_turned_ref[turn, :] = normed[:, turn].T
        width = 2 * blocks * BLK
        for begin, size in spans(D, COLS):
            columns = pl.ds(begin, size)
            grad_sum[:, columns] += dot_nt(grads[slot, :, :width], w_pair[slot, columns, :width])
        start_all(stores(tile, slot))

    hidden_tiles(run)
    store_turned.start()
    grad_ref[...] = grad_sum[...].astype(bf16)
    gain_part_ref[...] = jnp.zeros_like(gain_part_ref)

    def gain_rows(rows):
        values = resid_ref[rows, :]
        gain_part_ref[...] += jnp.sum(grad_sum[rows, :] * values * rms_inverse(values), axis=0, keepdims=True)

    row_chunks(length, ROWS, gain_rows)
    for tile in range(max(TILES - 2, 0), TILES):
        wait_all(stores(tile, tile % 2))
    store_resid.wait()
    store_turned.wait()


def hidden_weight_grads(rows_ref, cot_ref, *refs):
    parts, grads, scratch = refs[: 3 * NARROW], refs[3 * NARROW], refs[3 * NARROW + 1 :]
    normed_turned, pair, turned, pair_stage, down_stage, load_sems, store_sems, sems = scratch
    length = cot_ref.shape[0] // NARROW

    def loads(tile, slot):
        copies = []
        for part in range(NARROW):
            pair_grads, active_turned = parts[part * 3 + 1 : part * 3 + 3]
            tokens = pl.ds(part * length, length)
            copies += [
                pltpu.make_async_copy(pair_grads.at[tile], pair.at[slot, tokens], load_sems.at[slot, part * 2]),
                pltpu.make_async_copy(
                    active_turned.at[tile], turned.at[slot, :, tokens], load_sems.at[slot, part * 2 + 1]
                ),
            ]
        return copies

    def drain(slot, blocks):
        wait_bytes(pair_stage.at[slot, :, pl.ds(0, 2 * blocks * BLK)], store_sems.at[slot, 0])
        wait_bytes(down_stage.at[slot, pl.ds(0, blocks * BLK)], store_sems.at[slot, 1])

    turned_loads = [
        pltpu.make_async_copy(parts[part * 3], normed_turned.at[:, pl.ds(part * length, length)], sems.at[part])
        for part in range(NARROW)
    ]
    start_all(loads(0, 0) + turned_loads)
    wait_all(turned_loads)

    def run(tile, slot, blocks, more):
        wait_all(loads(tile, slot))
        if more:
            start_all(loads(tile + 1, 1 - slot))

        @pl.when(tile >= 2)
        def _():
            drain(slot, TILE_BLOCKS)

        width = blocks * BLK
        down = turned[slot, pl.ds(0, width), :]
        for begin, size in spans(D, COLS):
            columns = pl.ds(begin, size)
            down_stage[slot, pl.ds(0, width), columns] = dot_nn(down, cot_ref[:, columns]).astype(bf16)
        for place in range(blocks):
            column = tile * TILE_BLOCKS + place
            start_all(
                down_copies(rows_ref, grads, down_stage.at[slot], store_sems.at[slot, 1], column, place, outward=True)
            )
            columns = pl.ds(2 * place * BLK, 2 * BLK)
            for begin, size in spans(D, 512):
                pair_stage[slot, pl.ds(begin, size), columns] = dot_nn(
                    normed_turned[pl.ds(begin, size), :], pair[slot, :, columns]
                ).astype(bf16)
            start_all(
                pair_copies(rows_ref, grads, pair_stage.at[slot], store_sems.at[slot, 0], column, place, outward=True)
            )

    hidden_tiles(run)
    if TILES > 1:
        drain((TILES - 2) % 2, TILE_BLOCKS)
    drain((TILES - 1) % 2, LAST_BLOCKS)


def attention_backward(
    weight_rows_ref,
    rows_ref,
    half_ref,
    gain_ref,
    log_ref,
    gain_two_low_ref,
    gain_two_high_ref,
    resid_low_hbm,
    own_low_hbm,
    other_low_hbm,
    resid_high_hbm,
    own_high_hbm,
    other_high_hbm,
    cot_hbm,
    qkv_hbm,
    cos_hbm,
    sin_hbm,
    allowed_hbm,
    mixed_turned_hbm,
    normed_turned_hbm,
    x_hbm,
    weights,
    grads_in,
    grad_resid_ref,
    grad_own_ref,
    grad_other_ref,
    grads,
    resid_low_ref,
    own_low_ref,
    other_low_ref,
    resid_high_ref,
    own_high_ref,
    other_high_ref,
    cot_ref,
    qkv_ref,
    cos_ref,
    sin_ref,
    allowed_ref,
    mixed_turned_ref,
    normed_turned_ref,
    x_ref,
    w_qkv,
    w_out,
    grad_resid,
    grad_attention,
    grad_mixed,
    grad_qkv,
    grad_sum,
    grad_keys,
    grad_values,
    gain_part,
    bias_part,
    qkv_stage,
    out_stage,
    small_stage,
    blank,
    load_sems,
    store_sems,
    token_sems,
):
    del grads_in
    loads = copies_between(
        (
            cot_hbm, resid_low_hbm, own_low_hbm, other_low_hbm, resid_high_hbm, own_high_hbm, other_high_hbm, qkv_hbm,
            cos_hbm, sin_hbm, allowed_hbm, mixed_turned_hbm, normed_turned_hbm, x_hbm,
        ),
        (
            cot_ref, resid_low_ref, own_low_ref, other_low_ref, resid_high_ref, own_high_ref, other_high_ref, qkv_ref,
            cos_ref, sin_ref, allowed_ref, mixed_turned_ref, normed_turned_ref, x_ref,
        ),
        token_sems,
    )
    start_all(loads[:7])
    wide_count = small_stage.shape[0]
    owner_rows = grads.shape[0] // wide_count
    small_stage[...] = jnp.zeros_like(small_stage)
    fetch_attention(weight_rows_ref, weights, w_qkv, w_out, load_sems)
    start_all(loads[7:])
    length = x_ref.shape[0]
    empty_count = rows_ref.shape[0] - BLOCK_TOTAL
    blank[...] = jnp.zeros_like(blank)
    for index in range(empty_count):
        pltpu.make_async_copy(blank.at[index], grads.at[rows_ref[BLOCK_TOTAL + index]], store_sems.at[2]).start()

    part = length // NARROW
    own_rows, other_rows = half_rows(half_ref, part)
    for first, resid_ref, own_ref, other_ref, needed in (
        (0, resid_low_ref, own_low_ref, other_low_ref, loads[:4]),
        (part, resid_high_ref, own_high_ref, other_high_ref, loads[4:7]),
    ):
        wait_all(needed)

        def resid_rows(rows, first=first, resid_ref=resid_ref, own_ref=own_ref, other_ref=other_ref):
            values = resid_ref[rows, :]
            inverse = rms_inverse(values)
            normed = values * inverse
            scaled = (own_ref[rows, :].astype(f32) + other_ref[rows, :].astype(f32)) * gain_ref[1:2, :]
            place = pl.ds(rows.start + first, rows.size)
            total = cot_ref[place, :].astype(f32) + inverse * (
                scaled - normed * jnp.mean(scaled * normed, axis=-1, keepdims=True)
            )
            grad_resid[place, :] = total
            grad_attention[place, :] = total.astype(bf16)

        row_chunks(part, ROWS, resid_rows)
    grad_resid_ref[...] = grad_resid[own_rows, :]
    wait_bytes(w_out, load_sems.at[1])
    for begin, size in spans(QUERY_WIDTH, COLS):
        grad_mixed[:, pl.ds(begin, size)] = dot_nt(grad_attention[...], w_out[pl.ds(begin, size), :]).astype(bf16)
    wait_all(loads[7:11])
    keys_turned = qkv_ref[:, pl.ds(QUERY_WIDTH, HEAD_DIM)].T

    def rope_back(vector):
        return vector * cos_ref[...] - pltpu.roll(vector, HEAD_DIM // 2, 1) * sin_ref[...]

    grad_keys[...] = jnp.zeros_like(grad_keys)
    grad_values[...] = jnp.zeros_like(grad_values)
    for head in range(QUERY_COLS):
        columns = pl.ds(head * HEAD_DIM, HEAD_DIM)
        grad_queries = []
        for first in range(0, length, part):
            tokens, seen = pl.ds(first, part), first + part
            queries = qkv_ref[tokens, columns]
            grad_mixed_here = grad_mixed[tokens, columns]
            scores = scores_turned(
                qkv_ref[:seen, pl.ds(QUERY_WIDTH, HEAD_DIM)], queries, allowed_ref[:seen, tokens] > 0
            )
            probs = jnp.exp(scores - log_ref[pl.ds(head, 1), tokens])
            grad_values[:seen, :] += dot_nn(probs.astype(bf16), grad_mixed_here)
            grad_probs = dot_nt(qkv_ref[:seen, pl.ds(QUERY_WIDTH + HEAD_DIM, HEAD_DIM)], grad_mixed_here)
            row_dot = jnp.sum(probs * grad_probs, axis=0, keepdims=True)
            grad_scores = (probs * (grad_probs - row_dot)).astype(bf16)
            grad_keys[:seen, :] += dot_nn(grad_scores, queries)
            grad_queries.append(dot_nn(keys_turned[:, :seen], grad_scores).T * scaling)
        grad_qkv[:, columns] = rope_back(jnp.concatenate(grad_queries, axis=0)).astype(bf16)
    grad_qkv[:, pl.ds(QUERY_WIDTH, HEAD_DIM)] = rope_back(grad_keys[...] * scaling).astype(bf16)
    grad_qkv[:, pl.ds(QUERY_WIDTH + HEAD_DIM, HEAD_DIM)] = grad_values[...].astype(bf16)
    wait_all(loads[11:])

    for begin, size in spans(D, COLS):
        out_stage[:, pl.ds(begin, size)] = dot_nn(
            mixed_turned_ref[...], grad_attention[:, pl.ds(begin, size)]
        ).astype(bf16)
    store_piece(rows_ref, out_stage, grads, OUT_BASE, ROW_BLOCKS, QUERY_COLS, ROW_BLOCKS, 0, store_sems.at[1])
    for begin, size in spans(QKV_WIDTH, COLS):
        qkv_stage[:, pl.ds(begin, size)] = dot_nn(
            normed_turned_ref[...], grad_qkv[:, pl.ds(begin, size)]
        ).astype(bf16)
    store_piece(rows_ref, qkv_stage, grads, 0, QUERY_COLS, ROW_BLOCKS, QUERY_COLS, 0, store_sems.at[0])
    store_piece(rows_ref, qkv_stage, grads, KEY_BASE, PAIR_COLS, ROW_BLOCKS, PAIR_COLS, QUERY_COLS, store_sems.at[0])
    store_piece(
        rows_ref, qkv_stage, grads, VALUE_BASE, PAIR_COLS, ROW_BLOCKS, PAIR_COLS, QUERY_COLS + PAIR_COLS, store_sems.at[0]
    )
    wait_bytes(w_qkv, load_sems.at[0])
    for begin, size in spans(D, COLS):
        grad_sum[:, pl.ds(begin, size)] = dot_nt(grad_qkv[...], w_qkv[pl.ds(begin, size), :])
    grad_own_ref[...] = grad_sum[own_rows, :].astype(bf16)
    grad_other_ref[...] = grad_sum[other_rows, :].astype(bf16)
    gain_part[...] = jnp.zeros_like(gain_part)
    bias_part[...] = jnp.zeros_like(bias_part)

    def gain_rows(rows):
        tokens = x_ref[rows, :].astype(f32)
        gain_part[...] += jnp.sum(grad_sum[rows, :] * tokens * rms_inverse(tokens), axis=0, keepdims=True)
        bias_part[...] += jnp.sum(grad_qkv[rows, :].astype(f32), axis=0, keepdims=True)

    row_chunks(length, ROWS, gain_rows)
    for owner in range(wide_count):
        gain_row, bias_row = small_places(owner, wide_count)
        small_rows = []
        for row in (gain_row, gain_row + 1):
            columns = pl.ds(row % (D // BLK) * BLK, BLK)
            if row < D // BLK:
                small_rows.append(gain_part[:, columns])
            else:
                small_rows.append(gain_two_low_ref[:, columns] + gain_two_high_ref[:, columns])
        small_rows.append(bias_part[:, pl.ds(bias_row * BLK, BLK)])
        small_rows.append(jnp.zeros((SMALL_ROWS - len(small_rows), BLK), f32))
        small_stage[owner, pl.ds(0, SMALL_ROWS), :] = jnp.concatenate(small_rows, axis=0).astype(bf16)
        pltpu.make_async_copy(
            small_stage.at[owner], grads.at[owner * owner_rows + owner_rows - 1], store_sems.at[3]
        ).start()
    wait_bytes(small_stage, store_sems.at[3])
    wait_bytes(qkv_stage, store_sems.at[0])
    wait_bytes(out_stage, store_sems.at[1])
    if empty_count > 0:
        wait_bytes(blank.at[pl.ds(0, empty_count)], store_sems.at[2])


def soap_update(
    grad_in,
    masters_ref,
    first_ref,
    second_ref,
    left_ref,
    right_ref,
    grad_out,
    masters_out,
    first_out,
    second_out,
    small_ref,
    grad_stage,
    masters_stage,
    first_stage,
    second_stage,
    sems,
):
    group = grad_stage.shape[1]
    outputs = (
        (grad_stage, grad_out), (masters_stage, masters_out), (first_stage, first_out), (second_stage, second_out)
    )
    steps = masters_ref.shape[0] // group
    small_ref[...] = grad_in[masters_ref.shape[0], :SMALL_ROWS].astype(f32)

    def stores(step):
        slot = lax.rem(step, 2)
        places = pl.ds(step * group, group)
        return [
            pltpu.make_async_copy(stage.at[slot], out.at[places], sems.at[slot, index])
            for index, (stage, out) in enumerate(outputs)
        ]

    @pl.loop(0, steps)
    def _(step):
        @pl.when(step >= 2)
        def _():
            for copy in stores(step - 2):
                copy.wait()

        soap_group(
            step * group, lax.rem(step, 2), grad_in, masters_ref, first_ref, second_ref, left_ref, right_ref,
            *[stage for stage, _ in outputs],
        )
        start_all(stores(step))

    for step in range(max(steps - 2, 0), steps):
        for copy in stores(step):
            copy.wait()


def soap_group(
    first_block, slot, grad_in, masters_ref, first_ref, second_ref, left_ref, right_ref,
    grad_stage, masters_stage, first_stage, second_stage,
):
    places = range(grad_stage.shape[1])
    blocks = [first_block + place for place in places]
    for place, block in enumerate(blocks):
        grad_stage[slot, place] = grad_in[block].astype(f32)
    soap_blocks(
        [grad_in[block] for block in blocks],
        *[[ref.at[block] for block in blocks] for ref in (masters_ref, first_ref, second_ref, left_ref, right_ref)],
        *[[stage.at[slot, place] for place in places] for stage in (masters_stage, first_stage, second_stage)],
    )


def soap_blocks(grads, masters, firsts, seconds, lefts, rights, masters_out, firsts_out, seconds_out):
    count = range(len(grads))
    rights = [right[...].astype(bf16) for right in rights]
    products = [dot_nn(grads[index].astype(bf16), rights[index]).astype(bf16) for index in count]
    lefts = [left[...].astype(bf16) for left in lefts]
    rotated_blocks = [dot_nn(lefts[index].T, products[index]) for index in count]
    normalized = []
    for index in count:
        rotated = rotated_blocks[index]
        new_first = beta_first * firsts[index][...] + (1.0 - beta_first) * rotated
        new_second = beta_second * seconds[index][...] + (1.0 - beta_second) * rotated * rotated
        firsts_out[index][...] = new_first
        seconds_out[index][...] = new_second
        normalized.append(
            (new_first / first_fix / (jnp.sqrt(new_second / second_fix) + adam_eps)).astype(bf16)
        )
    products = [dot_nt(normalized[index], rights[index]).astype(bf16) for index in count]
    for index in count:
        masters_out[index][...] = masters[index][...] - rate_blocks * dot_nn(lefts[index], products[index])


def params(limit=VMEM_LIMIT, **options):
    return pltpu.CompilerParams(vmem_limit_bytes=limit, **options)


def run_attention_forward(rows, x, gain, bias, cosine, sine, allowed, weights):
    length = x.shape[0]
    shape = jax.ShapeDtypeStruct
    kept = [((D, length), bf16), ((length, QKV_WIDTH), bf16), ((QUERY_WIDTH, length), bf16)]
    low, high, log_total, *kept_arrays = pl.pallas_call(
        attention_forward,
        out_shape=[
            shape((length // NARROW, D), bf16),
            shape((length // NARROW, D), bf16),
            shape((8, length), f32),
        ]
        + [shape(*one) for one in kept],
        in_specs=[SMEM_SPEC] + [VMEM_SPEC] * 2 + [ANY_SPEC] * 5,
        out_specs=[VMEM_SPEC] * 3 + [ANY_SPEC] * 3,
        scratch_shapes=[pltpu.VMEM(array.shape, array.dtype) for array in (x, cosine, sine, allowed)]
        + [pltpu.VMEM(*one) for one in kept]
        + [
            pltpu.VMEM((D, QKV_WIDTH), bf16),
            pltpu.VMEM((QUERY_WIDTH, D), bf16),
            pltpu.VMEM((length, D), bf16),
            pltpu.VMEM((length, QUERY_WIDTH), bf16),
            pltpu.SemaphoreType.DMA((2,)),
            pltpu.SemaphoreType.DMA((4,)),
            pltpu.SemaphoreType.DMA((3,)),
        ],
        compiler_params=params(),
        name="attention_forward",
    )(rows, gain, bias, x, cosine, sine, allowed, weights)
    return (low, high, *kept_arrays, log_total)


def hidden_cost(length, products, bytes_moved):
    return pl.CostEstimate(
        flops=2 * products * length * D * TILE * TILES, bytes_accessed=bytes_moved, transcendentals=0
    )


def run_active_grads(rows, cotangent, weights):
    length = cotangent.shape[0]
    return pl.pallas_call(
        active_grads,
        out_shape=[
            jax.ShapeDtypeStruct((TILES, length, TILE), f32),
            jax.ShapeDtypeStruct((TILES, TILE, D), bf16),
        ],
        in_specs=[SMEM_SPEC, VMEM_SPEC, ANY_SPEC],
        out_specs=[ANY_SPEC] * 2,
        scratch_shapes=[
            pltpu.VMEM((4, TILE, D), bf16),
            pltpu.VMEM((2, length, TILE), f32),
            pltpu.SemaphoreType.DMA((4,)),
            pltpu.SemaphoreType.DMA((2,)),
            pltpu.SemaphoreType.DMA((4,)),
        ],
        compiler_params=params(),
        cost_estimate=hidden_cost(length, 1, TILES * TILE * (2 * D + 4 * length)),
        name="active_grads",
    )(rows, cotangent, weights)


def run_hidden_grads(first_row, rows, x, own, other, gain, active_grad, weights):
    length = own.shape[0]
    shape = jax.ShapeDtypeStruct
    grad, gain_part, *kept = pl.pallas_call(
        functools.partial(hidden_grads, first_row),
        out_shape=[
            shape((length, D), bf16),
            shape((1, D), f32),
            shape((length, D), f32),
            shape((D, length), bf16),
            shape((TILES, length, 2 * TILE), bf16),
            shape((TILES, length, TILE), bf16),
            shape((TILES, TILE, length), bf16),
        ],
        in_specs=[SMEM_SPEC, VMEM_SPEC] + [ANY_SPEC] * 5,
        out_specs=[VMEM_SPEC] * 2 + [ANY_SPEC] * 5,
        scratch_shapes=[
            pltpu.VMEM((length, D), bf16),
            pltpu.VMEM((length, D), bf16),
            pltpu.VMEM((length, D), bf16),
            pltpu.VMEM((length, D), f32),
            pltpu.VMEM((D, length), bf16),
            pltpu.VMEM((2, D, 2 * TILE), bf16),
            pltpu.VMEM((2, length, TILE), f32),
            pltpu.VMEM((2, length, TILE), bf16),
            pltpu.VMEM((2, TILE, length), bf16),
            pltpu.VMEM((2, length, 2 * TILE), bf16),
            pltpu.VMEM((length, D), bf16),
            pltpu.VMEM((length, D), f32),
            pltpu.SemaphoreType.DMA((2, 2)),
            pltpu.SemaphoreType.DMA((2, 3)),
            pltpu.SemaphoreType.DMA((5,)),
        ],
        compiler_params=params(),
        cost_estimate=hidden_cost(length, 4, 2 * TILES * TILE * (2 * D + 6 * length)),
        name="hidden_grads",
    )(rows, gain, x, own, other, active_grad, weights)
    resid, normed_turned, *hidden = kept
    return (grad, resid, normed_turned, gain_part, *hidden)


def run_hidden_weight_grads(rows, cotangent, parts, slots):
    length = cotangent.shape[0]
    return pl.pallas_call(
        hidden_weight_grads,
        out_shape=jax.ShapeDtypeStruct((slots, BLK, BLK), bf16),
        in_specs=[SMEM_SPEC, VMEM_SPEC] + [ANY_SPEC] * (3 * NARROW),
        out_specs=ANY_SPEC,
        scratch_shapes=[
            pltpu.VMEM((D, length), bf16),
            pltpu.VMEM((2, length, 2 * TILE), bf16),
            pltpu.VMEM((2, TILE, length), bf16),
            pltpu.VMEM((2, D, 2 * TILE), bf16),
            pltpu.VMEM((2, TILE, D), bf16),
            pltpu.SemaphoreType.DMA((2, 2 * NARROW)),
            pltpu.SemaphoreType.DMA((2, 2)),
            pltpu.SemaphoreType.DMA((NARROW,)),
        ],
        compiler_params=params(),
        cost_estimate=hidden_cost(length, 3, 2 * TILES * TILE * 3 * (D + length)),
        name="hidden_weight_grads",
    )(rows, cotangent, *[array for part in parts for array in part])


def run_attention_backward(
    weight_rows, rows, half, x, low, high, cotangent, gains, cosine, sine, allowed, normed_turned, qkv, mixed_turned,
    log_total, gain_two_parts, weights, grads, wide_count,
):
    length = x.shape[0]
    shape = jax.ShapeDtypeStruct
    empty_count = max(rows.shape[0] - BLOCK_TOTAL, 1)
    loaded = (*low, *high, cotangent, qkv, cosine, sine, allowed, mixed_turned, normed_turned, x)
    operands = (weight_rows, rows, half, gains, log_total, *gain_two_parts, *loaded, weights, grads)
    return pl.pallas_call(
        attention_backward,
        out_shape=[
            shape((length // NARROW, D), f32),
            shape((length // NARROW, D), bf16),
            shape((length // NARROW, D), bf16),
            shape(grads.shape, bf16),
        ],
        in_specs=[SMEM_SPEC] * 3 + [VMEM_SPEC] * 4 + [ANY_SPEC] * (len(loaded) + 2),
        out_specs=[VMEM_SPEC] * 3 + [ANY_SPEC],
        input_output_aliases={len(operands) - 1: 3},
        scratch_shapes=[pltpu.VMEM(array.shape, array.dtype) for array in loaded]
        + [
            pltpu.VMEM((D, QKV_WIDTH), bf16),
            pltpu.VMEM((QUERY_WIDTH, D), bf16),
            pltpu.VMEM((length, D), f32),
            pltpu.VMEM((length, D), bf16),
            pltpu.VMEM((length, QUERY_WIDTH), bf16),
            pltpu.VMEM((length, QKV_WIDTH), bf16),
            pltpu.VMEM((length, D), f32),
            pltpu.VMEM((length, HEAD_DIM), f32),
            pltpu.VMEM((length, HEAD_DIM), f32),
            pltpu.VMEM((1, D), f32),
            pltpu.VMEM((1, QKV_WIDTH), f32),
            pltpu.VMEM((D, QKV_WIDTH), bf16),
            pltpu.VMEM((QUERY_WIDTH, D), bf16),
            pltpu.VMEM((wide_count, BLK, BLK), bf16),
            pltpu.VMEM((empty_count, BLK, BLK), bf16),
            pltpu.SemaphoreType.DMA((2,)),
            pltpu.SemaphoreType.DMA((4,)),
            pltpu.SemaphoreType.DMA((len(loaded),)),
        ],
        compiler_params=params(),
        name="attention_backward",
    )(*operands)


def largest_group(count):
    return max(size for size in range(1, 11) if count % size == 0)


def run_soap(reduced, masters, first_moment, second_moment, left_basis, right_basis):
    slots = masters.shape[0]
    group = largest_group(slots)
    shape = jax.ShapeDtypeStruct(masters.shape, f32)
    return pl.pallas_call(
        soap_update,
        out_shape=[shape] * 4 + [jax.ShapeDtypeStruct((SMALL_ROWS, BLK), f32)],
        in_specs=[VMEM_SPEC] * 6,
        out_specs=[ANY_SPEC] * 4 + [VMEM_SPEC],
        scratch_shapes=[pltpu.VMEM((2, group, BLK, BLK), f32)] * 4 + [pltpu.SemaphoreType.DMA((2, 4))],
        compiler_params=params(),
        name="soap_update",
    )(reduced, masters, first_moment, second_moment, left_basis, right_basis)


def sum_for_owners(
    line, steps, late_steps,
    grads, masters, first_moment, second_moment, left_basis, right_basis,
    grad_resid, grad_own, grad_sent, tokens, gain, resid, active_low, active_high, down,
    out, new_masters, new_first, new_second, input_grad, output, small_own, small_other,
    a_in, a_own, a_sum, a_keep, a_send, a_cross, a_up, a_down,
    b_in, b_own, b_sum, b_keep, b_send, b_cross, b_up, b_down,
    a_params, b_params, grad_resid_here, grad_own_here, grad_other_here, tokens_here, gain_here, resid_here,
    active_here, down_here, branch_sum, branch_sent, branch_other,
    core_send, core_recv, own_sems, cross_send, cross_recv, up_send, up_recv, down_send, down_recv,
    b_core_send, b_core_recv, b_own_sems, b_cross_send, b_cross_recv, b_up_send, b_up_recv, b_down_send, b_down_recv,
    a_param_sems, b_param_sems, token_sems, branch_sems, swap_send, swap_recv, credits,
):
    wide = lax.axis_index("wide")
    narrow = lax.axis_index("narrow")
    z = wide // 4
    x = lax.rem(wide // 2, 2)
    core = lax.rem(wide, 2)
    mesh_id = pl.DeviceIdType.MESH
    core_peer = (wide + 1 - 2 * core, narrow)
    cross_peer = (wide + 2 - 4 * x, narrow)
    upper = (lax.rem(wide + 4, 4 * line), narrow)
    lower = (lax.rem(wide + 4 * line - 4, 4 * line), narrow)
    swap_peer = (wide, 1 - narrow)
    slots = out.shape[0]
    has_upper = z < line - 1
    has_lower = z > 0
    sum_depth = a_sum.shape[0]
    hop_depth = a_up.shape[0]
    b_sum_depth = b_sum.shape[0]

    barrier = pltpu.get_barrier_semaphore()
    pl.semaphore_signal(barrier, inc=1, device_id=core_peer, device_id_type=mesh_id)
    pl.semaphore_signal(barrier, inc=1, device_id=cross_peer, device_id_type=mesh_id)
    pl.semaphore_signal(barrier, inc=1, device_id=swap_peer, device_id_type=mesh_id)

    @pl.when(has_upper)
    def _():
        pl.semaphore_signal(barrier, inc=1, device_id=upper, device_id_type=mesh_id)

    @pl.when(has_lower)
    def _():
        pl.semaphore_signal(barrier, inc=1, device_id=lower, device_id_type=mesh_id)

    pl.semaphore_wait(barrier, 3 + has_upper.astype(jnp.int32) + has_lower.astype(jnp.int32))

    def remote(source, target, send_sem, recv_sem, peer):
        return pltpu.make_async_remote_copy(
            src_ref=source, dst_ref=target, send_sem=send_sem, recv_sem=recv_sem, device_id=peer, device_id_type=mesh_id
        )

    def core_copy(step):
        slot = lax.rem(step, DEPTH)
        source = grads.at[:, :, 1 - core, pl.ds(step * EARLY, EARLY)]
        return remote(source, a_in.at[slot], core_send.at[slot], core_recv.at[slot], core_peer)

    def own_copy(step):
        slot = lax.rem(step, DEPTH)
        return pltpu.make_async_copy(
            grads.at[:, :, core, pl.ds(step * EARLY, EARLY)], a_own.at[slot], own_sems.at[slot]
        )

    def b_core_copy(step):
        slot = lax.rem(step, DEPTH)
        source = grads.at[:, :, 1 - core, slots - 1 - step]
        return remote(source, b_in.at[slot], b_core_send.at[slot], b_core_recv.at[slot], core_peer)

    def b_own_copy(step):
        slot = lax.rem(step, DEPTH)
        return pltpu.make_async_copy(
            grads.at[:, :, core, slots - 1 - step], b_own.at[slot], b_own_sems.at[slot]
        )

    def cross_copy(step):
        slot = lax.rem(step, DEPTH)
        return remote(a_send.at[slot], a_cross.at[slot], cross_send.at[slot], cross_recv.at[slot], cross_peer)

    def b_cross_copy(step):
        slot = lax.rem(step, DEPTH)
        return remote(b_send.at[slot], b_cross.at[slot], b_cross_send.at[slot], b_cross_recv.at[slot], cross_peer)

    def up_copy(step, target):
        slot = lax.rem(step, hop_depth)
        return remote(
            a_sum.at[lax.rem(step, sum_depth), target], a_up.at[slot, target],
            up_send.at[slot, target], up_recv.at[slot, target], upper,
        )

    def down_copy(step, target):
        slot = lax.rem(step, hop_depth)
        return remote(
            a_sum.at[lax.rem(step, sum_depth), target], a_down.at[slot, target],
            down_send.at[slot, target], down_recv.at[slot, target], lower,
        )

    def b_up_copy(step, target):
        slot = lax.rem(step, hop_depth)
        return remote(
            b_sum.at[lax.rem(step, b_sum_depth), target], b_up.at[slot, target],
            b_up_send.at[slot, target], b_up_recv.at[slot, target], upper,
        )

    def b_down_copy(step, target):
        slot = lax.rem(step, hop_depth)
        return remote(
            b_sum.at[lax.rem(step, b_sum_depth), target], b_down.at[slot, target],
            b_down_send.at[slot, target], b_down_recv.at[slot, target], lower,
        )

    def give(channel, peer):
        pl.semaphore_signal(credits.at[channel], inc=1, device_id=peer, device_id_type=mesh_id)

    def take(channel, step, depth):
        @pl.when(step >= depth)
        def _():
            pl.semaphore_wait(credits.at[channel], 1)

    def feed(step, count, channel, remote_copy, local_copy):
        @pl.when(step < count)
        def _():
            take(channel, step, DEPTH)
            remote_copy(step).start()
            local_copy(step).start()

    sources = (masters, first_moment, second_moment, left_basis, right_basis)

    def param_loads(step):
        slot = lax.rem(step, 2)
        places = pl.ds(step * EARLY, EARLY)
        return [
            pltpu.make_async_copy(source.at[places], a_params.at[slot, index], a_param_sems.at[slot, index])
            for index, source in enumerate(sources)
        ]

    def b_param_loads(step):
        slot = lax.rem(step, 2)
        return [
            pltpu.make_async_copy(
                source.at[slots - 1 - step], b_params.at[slot, index], b_param_sems.at[slot, index]
            )
            for index, source in enumerate(sources)
        ]

    token_loads = [
        pltpu.make_async_copy(source, target, token_sems.at[index])
        for index, (source, target) in enumerate((
            (resid, resid_here), (grad_resid, grad_resid_here), (grad_own, grad_own_here), (tokens, tokens_here), (gain, gain_here),
        ))
    ]
    grad_swap = remote(grad_sent, grad_other_here, swap_send.at[0], swap_recv.at[0], swap_peer)
    small_swap = remote(small_own, small_other, swap_send.at[1], swap_recv.at[1], swap_peer)

    branch_swap = remote(branch_sent, branch_other, swap_send.at[2], swap_recv.at[2], swap_peer)

    def branch_load(index):
        tile = lax.rem(index, TILES)
        takes_low = narrow == jnp.where(index < TILES, 1, 0)

        @pl.when(takes_low)
        def _():
            pltpu.make_async_copy(active_low.at[tile], active_here, branch_sems.at[0]).start()

        @pl.when(jnp.logical_not(takes_low))
        def _():
            pltpu.make_async_copy(active_high.at[tile], active_here, branch_sems.at[0]).start()

        pltpu.make_async_copy(down.at[tile], down_here, branch_sems.at[1]).start()

    def branch_step(index):
        pltpu.make_async_copy(active_low.at[0], active_here, branch_sems.at[0]).wait()
        pltpu.make_async_copy(down.at[0], down_here, branch_sems.at[1]).wait()

        @pl.when(lax.rem(index, TILES) == 0)
        def _():
            branch_sum[...] = jnp.zeros_like(branch_sum)

        for begin, size in spans(D, COLS):
            columns = pl.ds(begin, size)
            branch_sum[:, columns] += dot_nn(active_here[...], down_here[:, columns])

        @pl.when(index < 2 * TILES - 1)
        def _():
            branch_load(index + 1)

        @pl.when(index == TILES - 1)
        def _():
            branch_sent[...] = branch_sum[...].astype(bf16)
            branch_swap.start()

    def finish_output():
        token_loads[0].wait()
        branch_swap.wait()

        def rows_of_output(rows):
            total = resid_here[rows, :] + branch_sum[rows, :] + branch_other[rows, :].astype(f32)
            output[rows, :] = total.astype(bf16)

        row_chunks(output.shape[0], ROWS, rows_of_output)

    def finish_input_grad():
        wait_all(token_loads[1:])
        grad_swap.wait()

        def rows_of_grad(rows):
            values = tokens_here[rows, :].astype(f32)
            inverse = rms_inverse(values)
            scaled = grad_own_here[rows, :].astype(f32) + grad_other_here[rows, :].astype(f32)
            input_grad[rows, :] = grad_resid_here[rows, :] + norm_back(
                scaled * gain_here[...], values * inverse, inverse
            )

        row_chunks(input_grad.shape[0], ROWS, rows_of_grad)

    grad_swap.start()
    for early in range(DEPTH - 1):
        feed(early, steps, 0, core_copy, own_copy)
        feed(early, late_steps, 1, b_core_copy, b_own_copy)

    start_all(param_loads(0) + param_loads(1) + b_param_loads(1) + b_param_loads(2) + token_loads)
    branch_load(0)

    def active(step, count):
        return (step >= 0) & (step < count)

    far = jnp.maximum(z, line - 1 - z)

    def hops(step_up, step_down, count, sums, depth, ups, downs, up, down, channel):
        @pl.when(active(step_up, count) & has_upper)
        def _():
            take(channel, step_up, hop_depth)
            slot = lax.rem(step_up, hop_depth)
            place = lax.rem(step_up, depth)

            def one(target, _):
                @pl.when(has_lower)
                def _():
                    up(step_up, target).wait_recv()
                    sums[place, target] += ups[slot, target]

                up(step_up, target).start()
                return 0

            lax.fori_loop(z + 1, line, one, 0)

        @pl.when(active(step_down, count) & has_lower)
        def _():
            take(channel + 1, step_down, hop_depth)
            slot = lax.rem(step_down, hop_depth)
            place = lax.rem(step_down, depth)

            def one(target, _):
                @pl.when(has_upper)
                def _():
                    down(step_down, target).wait_recv()
                    sums[place, target] += downs[slot, target]

                down(step_down, target).start()
                return 0

            lax.fori_loop(0, z, one, 0)

    def gather_hops(step, count, sums, depth, ups, downs, up, down, channel, total):
        slot = lax.rem(step, hop_depth)
        total[...] = sums[lax.rem(step, depth), z].astype(f32)

        @pl.when(has_lower)
        def _():
            up(step, z).wait_recv()
            total[...] += ups[slot, z].astype(f32)

            @pl.when(step < count - hop_depth)
            def _():
                give(channel, lower)

        @pl.when(has_upper)
        def _():
            down(step, z).wait_recv()
            total[...] += downs[slot, z].astype(f32)

            @pl.when(step < count - hop_depth)
            def _():
                give(channel + 1, upper)

    def retire(step, count, up, down):
        @pl.when(active(step, count))
        def _():
            def sent_up(target, _):
                up(step, target).wait_send()
                return 0

            def sent_down(target, _):
                down(step, target).wait_send()
                return 0

            lax.fori_loop(z + 1, line, sent_up, 0)
            lax.fori_loop(0, z, sent_down, 0)

    def iteration(step, _):
        feed(step + DEPTH - 1, steps, 0, core_copy, own_copy)
        feed(step + DEPTH - 1, late_steps, 1, b_core_copy, b_own_copy)

        retire(step - CROSS_LAG - HOP_LAG * far - 1, steps, up_copy, down_copy)
        retire(step - HOP_LAG * far - 1, late_steps, b_up_copy, b_down_copy)

        @pl.when(step < steps)
        def _():
            slot = lax.rem(step, DEPTH)
            place = lax.rem(step, sum_depth)
            core_copy(step).wait()
            own_copy(step).wait()

            @pl.when(step >= DEPTH)
            def _():
                cross_copy(step - DEPTH).wait_send()

            for target in range(line):
                a_send[slot, target] = a_own[slot, target, 1 - x] + a_in[slot, target, 1 - x]
            take(2, step, DEPTH)
            cross_copy(step).start()
            for target in range(line):
                a_sum[place, target] = a_own[slot, target, x] + a_in[slot, target, x]

            @pl.when(step < steps - DEPTH)
            def _():
                give(0, core_peer)

        @pl.when(step < late_steps)
        def _():
            slot = lax.rem(step, DEPTH)
            b_core_copy(step).wait()
            b_own_copy(step).wait()
            b_sum[lax.rem(step, b_sum_depth)] = b_own[slot] + b_in[slot]

            @pl.when(step < late_steps - DEPTH)
            def _():
                give(1, core_peer)

        crossed = step - CROSS_LAG

        @pl.when(active(crossed, steps))
        def _():
            slot = lax.rem(crossed, DEPTH)
            place = lax.rem(crossed, sum_depth)
            cross_copy(crossed).wait_recv()
            for target in range(line):
                a_sum[place, target] += a_cross[slot, target]

            @pl.when(crossed < steps - DEPTH)
            def _():
                give(2, cross_peer)

        hops(
            step - HOP_LAG * z, step - HOP_LAG * (line - 1 - z), late_steps, b_sum, b_sum_depth, b_up, b_down,
            b_up_copy, b_down_copy, 6,
        )
        hops(
            crossed - HOP_LAG * z, crossed - HOP_LAG * (line - 1 - z), steps, a_sum, sum_depth, a_up, a_down,
            up_copy, down_copy, 4,
        )

        last = crossed - HOP_LAG * far

        @pl.when(active(last, steps))
        def _():
            gather_hops(last, steps, a_sum, sum_depth, a_up, a_down, up_copy, down_copy, 4, a_keep)
            out[pl.ds(last * EARLY, EARLY)] = a_keep[...].astype(bf16)
            slot = lax.rem(last, 2)
            for copy in param_loads(last):
                copy.wait()
            soap_blocks(
                [a_keep[index] for index in range(EARLY)],
                *[[a_params.at[slot, kind, index] for index in range(EARLY)] for kind in range(5)],
                *[
                    [target.at[last * EARLY + index] for index in range(EARLY)]
                    for target in (new_masters, new_first, new_second)
                ],
            )

            @pl.when(last + 2 < steps)
            def _():
                start_all(param_loads(last + 2))

        arrived = step - HOP_LAG * far

        @pl.when(active(arrived, late_steps))
        def _():
            slot = lax.rem(arrived, DEPTH)

            @pl.when(arrived >= DEPTH)
            def _():
                b_cross_copy(arrived - DEPTH).wait_send()

            gather_hops(
                arrived, late_steps, b_sum, b_sum_depth, b_up, b_down, b_up_copy, b_down_copy, 6, b_keep.at[slot]
            )
            b_send[slot] = b_keep[slot, 1 - x].astype(bf16)
            take(3, arrived, DEPTH)
            b_cross_copy(arrived).start()

        paired = arrived - CROSS_LAG

        @pl.when(active(paired, late_steps))
        def _():
            slot = lax.rem(paired, DEPTH)
            b_cross_copy(paired).wait_recv()
            place = slots - 1 - paired
            total = b_keep[slot, x] + b_cross[slot].astype(f32)
            out[place] = total.astype(bf16)

            @pl.when(paired < late_steps - DEPTH)
            def _():
                give(3, cross_peer)

            @pl.when(paired == 0)
            def _():
                small_own[...] = total[: small_own.shape[0]]
                small_swap.start()

            @pl.when(paired > 0)
            def _():
                slot = lax.rem(paired, 2)
                for copy in b_param_loads(paired):
                    copy.wait()
                soap_blocks(
                    [total], *[[b_params.at[slot, kind]] for kind in range(5)],
                    [new_masters.at[place]], [new_first.at[place]], [new_second.at[place]],
                )

                @pl.when(paired + 2 < late_steps)
                def _():
                    start_all(b_param_loads(paired + 2))

        @pl.when((step >= 1) & (step < 2 * TILES + 1))
        def _():
            branch_step(step - 1)

        pl.when(step == 2 * TILES + 1)(finish_output)
        pl.when(step == 4)(finish_input_grad)
        return 0

    lag = HOP_LAG * (line - 1) + CROSS_LAG
    lax.fori_loop(0, max(max(steps, late_steps) + lag, 2 * TILES) + 2, iteration, 0)
    for step in range(max(steps - DEPTH, 0), steps):
        cross_copy(step).wait_send()
    for step in range(max(late_steps - DEPTH, 0), late_steps):
        b_cross_copy(step).wait_send()
    small_swap.wait()


def run_sum_for_owners(grads, wide_count, blocks, token_arrays):
    line = wide_count // 4
    slots, block = grads.shape[0] // wide_count, grads.shape[1:]
    steps = (slots - 1) // (EARLY + 1)
    late_steps = slots - EARLY * steps
    sum_depth = CROSS_LAG + HOP_LAG * (line - 1) + 2
    b_sum_depth = HOP_LAG * (line - 1) + 2
    hop_depth = 2 * HOP_LAG + 2
    dma = pltpu.SemaphoreType.DMA

    def vmem(*shape):
        return pltpu.VMEM(shape + block, bf16)

    def wide_vmem(*shape):
        return pltpu.VMEM(shape + block, f32)

    return pl.pallas_call(
        functools.partial(sum_for_owners, line, steps, late_steps),
        out_shape=[pltpu.VMEM((slots,) + block, bf16)]
        + [pltpu.VMEM(blocks[0].shape, f32)] * 3
        + [pltpu.VMEM(token_arrays[0].shape, f32), pltpu.VMEM(token_arrays[0].shape, bf16)]
        + [pltpu.VMEM((SMALL_ROWS, block[-1]), f32)] * 2,
        in_specs=[ANY_SPEC] * (1 + len(blocks) + len(token_arrays)),
        out_specs=[VMEM_SPEC] * 8,
        scratch_shapes=[
            vmem(DEPTH, line, 2, EARLY),
            vmem(DEPTH, line, 2, EARLY),
            vmem(sum_depth, line, EARLY),
            wide_vmem(EARLY),
            vmem(DEPTH, line, EARLY),
            vmem(DEPTH, line, EARLY),
            vmem(hop_depth, line, EARLY),
            vmem(hop_depth, line, EARLY),
            vmem(DEPTH, line, 2),
            vmem(DEPTH, line, 2),
            vmem(b_sum_depth, line, 2),
            wide_vmem(DEPTH, 2),
            vmem(DEPTH),
            vmem(DEPTH),
            vmem(hop_depth, line, 2),
            vmem(hop_depth, line, 2),
            wide_vmem(2, len(blocks), EARLY),
            wide_vmem(2, len(blocks)),
        ]
        + [pltpu.VMEM(array.shape, array.dtype) for array in token_arrays[:6]]
        + [
            pltpu.VMEM(token_arrays[6].shape[1:], bf16),
            pltpu.VMEM(token_arrays[8].shape[1:], bf16),
            pltpu.VMEM(token_arrays[0].shape, f32),
            pltpu.VMEM(token_arrays[0].shape, bf16),
            pltpu.VMEM(token_arrays[0].shape, bf16),
        ]
        + ([dma((DEPTH,))] * 5 + [dma((hop_depth, line))] * 4) * 2
        + [dma((2, len(blocks)))] * 2
        + [dma((5,)), dma((2,)), dma((3,)), dma((3,)), pltpu.SemaphoreType.REGULAR((8,))],
        compiler_params=params(SUM_VMEM, collective_id=0, has_side_effects=True),
        cost_estimate=pl.CostEstimate(flops=0, bytes_accessed=2 * grads.size * 8, transcendentals=0),
        name="sum_for_owners",
    )(grads.reshape((line, 2, 2, slots) + block), *blocks, *token_arrays)


def write_results(
    reduced, masters, first_moment, second_moment, input_grad, output, small_own, small_other,
    block_grad_out, masters_out, first_out, second_out, input_grad_out, output_out, small_out,
    stage, stage_sems, sems,
):
    copies = [
        pltpu.make_async_copy(source, target, sems.at[index])
        for index, (source, target) in enumerate((
            (masters, masters_out), (first_moment, first_out), (second_moment, second_out),
            (input_grad, input_grad_out), (output, output_out),
        ))
    ]
    start_all(copies)
    small_out[0] = small_own[...]
    small_out[1] = small_other[...]
    group = stage.shape[1]
    steps = masters.shape[0] // group

    def store(step):
        slot = lax.rem(step, 2)
        return pltpu.make_async_copy(
            stage.at[slot], block_grad_out.at[pl.ds(step * group, group)], stage_sems.at[slot]
        )

    @pl.loop(0, steps)
    def _(step):
        @pl.when(step >= 2)
        def _():
            store(step - 2).wait()

        stage[lax.rem(step, 2)] = reduced[pl.ds(step * group, group)].astype(f32)
        store(step).start()

    for step in range(max(steps - 2, 0), steps):
        store(step).wait()
    for copy in copies:
        copy.wait()


def run_write_results(*arrays):
    arrays = [pltpu.with_memory_space_constraint(array, pltpu.VMEM) for array in arrays]
    blocks, rows, small = arrays[1].shape, arrays[4].shape, arrays[-1].shape
    group = largest_group(blocks[0])
    shape = jax.ShapeDtypeStruct
    return pl.pallas_call(
        write_results,
        out_shape=[shape(blocks, f32)] * 4 + [shape(rows, f32), shape(rows, bf16), shape((2,) + small, f32)],
        in_specs=[VMEM_SPEC] * len(arrays),
        out_specs=[ANY_SPEC] * 6 + [VMEM_SPEC],
        scratch_shapes=[
            pltpu.VMEM((2, group) + blocks[1:], f32),
            pltpu.SemaphoreType.DMA((2,)),
            pltpu.SemaphoreType.DMA((5,)),
        ],
        compiler_params=params(WRITE_VMEM),
        name="write_results",
    )(*arrays)


def rope_tables(segment_row):
    token_index = jnp.arange(segment_row.shape[0], dtype=jnp.int32)
    changed = jnp.concatenate([jnp.ones((1,), dtype=bool), segment_row[1:] != segment_row[:-1]])
    begins = lax.cummax(jnp.where(changed, token_index, jnp.zeros_like(token_index)), axis=0)
    places = (token_index - begins).astype(f32)
    frequency = rope_base ** (-(jnp.arange(HEAD_DIM // 2, dtype=f32) * 2.0) / HEAD_DIM)
    angles = places[:, None] * frequency[None, :]
    cosine = jnp.concatenate([jnp.cos(angles), jnp.cos(angles)], axis=-1)
    sine_signed = jnp.concatenate([-jnp.sin(angles), jnp.sin(angles)], axis=-1)
    return (cosine, sine_signed)


def rms_parts(values):
    inverse = rms_inverse(values)
    return (inverse, values * inverse)


def norm_back(grad_scaled, normed, inverse):
    return inverse * (grad_scaled - normed * jnp.mean(grad_scaled * normed, axis=-1, keepdims=True))


def adam_small(param_now, gradient, first_now, second_now, rate_here):
    first_new = beta_first * first_now + (1.0 - beta_first) * gradient
    second_new = beta_second * second_now + (1.0 - beta_second) * gradient * gradient
    param_new = param_now - rate_here * (first_new / first_fix) / (
        jnp.sqrt(second_new / second_fix) + adam_eps
    )
    return (param_new, first_new, second_new)


def swap_halves(values):
    return lax.ppermute(values, "narrow", [(0, 1), (1, 0)])


def body(
    tokens,
    cotangent,
    segments,
    owner_list,
    masters,
    first_moment,
    second_moment,
    left_basis,
    right_basis,
    gains,
    gain_first,
    gain_second,
    biases,
    bias_first,
    bias_second,
):
    half = lax.axis_index("narrow")
    wide_index = lax.axis_index("wide")
    wide_count = lax.axis_size("wide")
    tokens_here = tokens.shape[0]
    slots_here = masters.shape[0]
    slots_half = owner_list.shape[0]
    gains_here = gains.shape[0]
    biases_here = biases.shape[1]

    def join_halves(own, other, axis=0):
        return jnp.where(
            half == 0, jnp.concatenate([own, other], axis=axis), jnp.concatenate([other, own], axis=axis)
        )

    masters_low, gains, biases = lax.optimization_barrier((masters.astype(bf16), gains, biases))
    weights = lax.all_gather(masters_low, "wide", axis=0, tiled=True)
    gain_full = lax.all_gather(gains, ("wide", "narrow"), axis=0, tiled=True).reshape(2, D)
    bias_full = lax.all_gather(biases.reshape(-1).astype(bf16), "wide", axis=0, tiled=True)
    bias_full = bias_full.astype(f32).reshape(1, QKV_WIDTH)
    pair_gains = 2 * gains_here

    position = jnp.arange(slots_half, dtype=jnp.int32)
    empty = owner_list == BLOCK_TOTAL
    number = jnp.where(empty, BLOCK_TOTAL - 1 + jnp.cumsum(empty.astype(jnp.int32)), owner_list)
    weight_rows = jnp.zeros((slots_half,), jnp.int32).at[number].set(position, unique_indices=True)
    rows = weight_rows + weight_rows // slots_here
    half_index = half.astype(jnp.int32).reshape(1)

    segment_row = lax.dynamic_index_in_dim(segments, wide_index, 0, keepdims=False)
    cosine, sine = rope_tables(segment_row)
    token_index = jnp.arange(segment_row.shape[0], dtype=jnp.int32)
    allowed_turned = (
        (segment_row[None, :] == segment_row[:, None]) & (token_index[None, :] >= token_index[:, None])
    ).astype(f32)
    tokens_row = join_halves(tokens, swap_halves(tokens))
    cotangent_row = join_halves(cotangent, swap_halves(cotangent))
    weights, tokens_row, cotangent_row, gain_full, bias_full = lax.optimization_barrier(
        (weights, tokens_row, cotangent_row, gain_full, bias_full)
    )

    low_part, high_part, normed_one_turned, qkv, mixed_turned, log_total = run_attention_forward(
        weight_rows, tokens_row, gain_full[0:1], bias_full, cosine, sine, allowed_turned, weights
    )
    low_other = swap_halves(low_part)
    active_grad, down_tiles = run_active_grads(weight_rows, cotangent_row, weights)
    high_sent, low_other = lax.optimization_barrier((high_part, low_other))
    high_other = swap_halves(high_sent)
    gain_two = gain_full[1:2]
    grad_low, resid_low, turned_low, gain_low, *hidden_low = run_hidden_grads(
        0, weight_rows, tokens_row, low_part, low_other, gain_two, active_grad, weights
    )
    grad_low_other = swap_halves(grad_low)
    grad_high, resid_high, turned_high, gain_high, *hidden_high = run_hidden_grads(
        tokens_here, weight_rows, tokens_row, high_part, high_other, gain_two, active_grad, weights
    )
    grad_high_other = swap_halves(grad_high)
    pair_low, active_low, active_turned_low = hidden_low
    pair_high, active_high, active_turned_high = hidden_high
    grads = run_hidden_weight_grads(
        rows, cotangent_row, [(turned_low, pair_low, active_turned_low), (turned_high, pair_high, active_turned_high)],
        wide_count * (slots_here + 1),
    )
    grad_resid, grad_one_own, grad_one_sent, grads = run_attention_backward(
        weight_rows, rows, half_index, tokens_row, (resid_low, grad_low, grad_low_other),
        (resid_high, grad_high, grad_high_other), cotangent_row, gain_full, cosine, sine, allowed_turned,
        normed_one_turned, qkv, mixed_turned, log_total, (gain_low, gain_high), weights, grads, wide_count,
    )
    resid_own = jnp.where(half == 0, resid_low, resid_high)
    blocks = [masters, first_moment, second_moment, left_basis, right_basis]
    if wide_count == 16:
        token_arrays = [
            grad_resid, grad_one_own, grad_one_sent, tokens, gain_full[0:1], resid_own, active_low, active_high, down_tiles
        ]
        block_grad, new_masters, new_first, new_second, input_grad, output, small_sums = run_write_results(
            *run_sum_for_owners(grads, wide_count, blocks, token_arrays)
        )
        gain_parts = small_sums[0, :2] + small_sums[1, :2]
        bias_row = small_sums[0, 2]
    else:
        reduced = lax.psum_scatter(grads, "wide", scatter_dimension=0, tiled=True)
        block_grad, new_masters, new_first, new_second, small_sums = run_soap(reduced, *blocks)
        gain_parts = small_sums[:2] + swap_halves(small_sums[:2])
        bias_row = small_sums[2]
        branch_low, branch_high = [
            jnp.einsum("tik,tkd->id", active, down_tiles, preferred_element_type=f32)
            for active in (active_low, active_high)
        ]
        branch_own = jnp.where(half == 0, branch_low, branch_high)
        branch_sent = jnp.where(half == 0, branch_high, branch_low).astype(bf16)
        output = (resid_own + branch_own + swap_halves(branch_sent).astype(f32)).astype(bf16)
        inverse_one, normed_one = rms_parts(tokens.astype(f32))
        grad_one = grad_one_own.astype(f32) + swap_halves(grad_one_sent).astype(f32)
        input_grad = grad_resid + norm_back(grad_one * gain_full[0:1], normed_one, inverse_one)

    gain_first_index = wide_index * pair_gains
    gain_offset = gain_first_index - jnp.minimum(gain_first_index // BLK, 2 * D // BLK - 2) * BLK
    bias_offset = lax.rem(wide_index * biases_here, BLK)
    gain_grad = lax.dynamic_slice_in_dim(gain_parts.reshape(-1), gain_offset + half * gains_here, gains_here, 0)
    bias_grad = lax.dynamic_slice_in_dim(bias_row, bias_offset, biases_here, 0).reshape(biases.shape)
    new_gains, new_gain_first, new_gain_second = adam_small(gains, gain_grad, gain_first, gain_second, rate_gains)
    new_biases, new_bias_first, new_bias_second = adam_small(biases, bias_grad, bias_first, bias_second, rate_small)

    return (
        output,
        input_grad,
        block_grad,
        new_masters,
        new_first,
        new_second,
        gain_grad,
        new_gains,
        new_gain_first,
        new_gain_second,
        bias_grad,
        new_biases,
        new_bias_first,
        new_bias_second,
    )


def solution(mesh):
    tokens_spec = P(("wide", "narrow"), None)
    blocks_spec = P(("wide", "narrow"), None, None)
    gains_spec = P(("wide", "narrow"))
    bias_spec = P("narrow", "wide")
    in_specs = (
        (tokens_spec, tokens_spec, P(), P()) + (blocks_spec,) * 5 + (gains_spec,) * 3 + (bias_spec,) * 3
    )
    out_specs = (tokens_spec, tokens_spec) + (blocks_spec,) * 4 + (gains_spec,) * 4 + (bias_spec,) * 4
    return jax.shard_map(body, mesh=mesh, in_specs=in_specs, out_specs=out_specs, check_vma=False)
```

```python
import functools

import jax
import jax.numpy as jnp
from jax import lax
from jax.experimental import pallas as pl
from jax.experimental.pallas import tpu as pltpu
from jax.sharding import PartitionSpec as P

D = 1536
FF = 8960
HEADS = 12
KV_HEADS = 2
HEAD_DIM = 128
BLK = 128
STEP_COUNT = 5


beta_first = 0.95
beta_second = 0.95
adam_eps = 1e-08
rate_blocks = 0.03
rate_small = 0.4
rate_gains = 0.6
norm_eps = 1e-06
rope_base = 10000.0
masked_score = -1e30
first_fix = 1.0 - beta_first**STEP_COUNT
second_fix = 1.0 - beta_second**STEP_COUNT
scaling = HEAD_DIM ** (-0.5)

bf16 = jnp.bfloat16
f32 = jnp.float32

NARROW = 2
ROW_BLOCKS = D // BLK
QUERY_COLS = HEADS * HEAD_DIM // NARROW // BLK
PAIR_COLS = KV_HEADS * HEAD_DIM // NARROW // BLK
HIDDEN_COLS = FF // NARROW // BLK
QKV_COLS = QUERY_COLS + 2 * PAIR_COLS
QUERY_WIDTH = QUERY_COLS * BLK
QKV_WIDTH = QKV_COLS * BLK
KEY_BASE = ROW_BLOCKS * QUERY_COLS
VALUE_BASE = KEY_BASE + ROW_BLOCKS * PAIR_COLS
OUT_BASE = VALUE_BASE + ROW_BLOCKS * PAIR_COLS
GATE_BASE = OUT_BASE + QUERY_COLS * ROW_BLOCKS
UP_BASE = GATE_BASE + ROW_BLOCKS * HIDDEN_COLS
DOWN_BASE = UP_BASE + ROW_BLOCKS * HIDDEN_COLS
BLOCK_TOTAL = DOWN_BASE + HIDDEN_COLS * ROW_BLOCKS

TILE_BLOCKS = 6
TILES = -(-HIDDEN_COLS // TILE_BLOCKS)
LAST_BLOCKS = HIDDEN_COLS - (TILES - 1) * TILE_BLOCKS
TILE = TILE_BLOCKS * BLK
COLS = 256
ROWS = 64
SMALL_ROWS = 16
VMEM_LIMIT = 60 * 2**20
SUM_VMEM = 39 * 2**20
WRITE_VMEM = 6 * 2**20

EARLY = 4
DEPTH = 3
CROSS_LAG = 2
HOP_LAG = 1

VMEM_SPEC = pl.BlockSpec(memory_space=pltpu.VMEM)
SMEM_SPEC = pl.BlockSpec(memory_space=pltpu.SMEM)
ANY_SPEC = pl.BlockSpec(memory_space=pl.ANY)


def spans(total, step):
    return [(begin, min(step, total - begin)) for begin in range(0, total, step)]


def dot_nn(left, right):
    return jnp.dot(left, right, preferred_element_type=f32)


def dot_nt(left, right):
    return lax.dot_general(left, right, (((1,), (1,)), ((), ())), preferred_element_type=f32)


def block_ref(ref, row_block, col_block):
    return ref.at[pl.ds(row_block * BLK, BLK), pl.ds(col_block * BLK, BLK)]


def fetch_piece(rows_ref, weights, target, base, pitch, row_blocks, col_blocks, first_col, sem):
    @pl.loop(0, row_blocks)
    def _(i):
        for j in range(col_blocks):
            pltpu.make_async_copy(
                weights.at[rows_ref[base + i * pitch + j]],
                block_ref(target, i, first_col + j),
                sem,
            ).start()


def store_piece(rows_ref, source, grads, base, pitch, row_blocks, col_blocks, first_col, sem):
    @pl.loop(0, row_blocks)
    def _(i):
        for j in range(col_blocks):
            pltpu.make_async_copy(
                block_ref(source, i, first_col + j),
                grads.at[rows_ref[base + i * pitch + j]],
                sem,
            ).start()


def wait_bytes(ref, sem):
    pltpu.make_async_copy(ref, ref, sem).wait()


def copies_between(sources, targets, sems):
    return [
        pltpu.make_async_copy(source, target, sems.at[index])
        for index, (source, target) in enumerate(zip(sources, targets, strict=True))
    ]


def wait_all(copies):
    for copy in copies:
        copy.wait()


def fetch_qkv(rows_ref, weights, w_qkv, sem):
    fetch_piece(rows_ref, weights, w_qkv, 0, QUERY_COLS, ROW_BLOCKS, QUERY_COLS, 0, sem)
    fetch_piece(rows_ref, weights, w_qkv, KEY_BASE, PAIR_COLS, ROW_BLOCKS, PAIR_COLS, QUERY_COLS, sem)
    fetch_piece(
        rows_ref, weights, w_qkv, VALUE_BASE, PAIR_COLS, ROW_BLOCKS, PAIR_COLS, QUERY_COLS + PAIR_COLS, sem
    )


def fetch_out(rows_ref, weights, w_out, sem):
    fetch_piece(rows_ref, weights, w_out, OUT_BASE, ROW_BLOCKS, QUERY_COLS, ROW_BLOCKS, 0, sem)


def rms_inverse(values):
    return lax.rsqrt(jnp.mean(values * values, axis=-1, keepdims=True) + norm_eps)


def row_chunks(total, step, run):
    @pl.loop(0, total // step)
    def _(chunk):
        run(pl.ds(pl.multiple_of(chunk * step, step), step))


def small_places(owner, wide_count):
    gain_row = min(owner * (2 * D // wide_count) // BLK, 2 * D // BLK - 2)
    return (gain_row, owner * (QKV_WIDTH // wide_count) // BLK)


def scores_turned(keys, queries, allowed):
    return jnp.where(allowed, dot_nt(keys, queries) * scaling, masked_score)


def attention_forward(
    rows_ref,
    gain_ref,
    bias_ref,
    x_hbm,
    cos_hbm,
    sin_hbm,
    allowed_hbm,
    weights,
    part_low_ref,
    part_high_ref,
    log_ref,
    normed_turned_out,
    qkv_out,
    mixed_turned_out,
    x_ref,
    cos_ref,
    sin_ref,
    allowed_ref,
    normed_turned,
    qkv,
    mixed_turned,
    w_qkv,
    w_out,
    normed,
    mixed,
    sems,
    load_sems,
    store_sems,
):
    loads = copies_between(
        (x_hbm, cos_hbm, sin_hbm, allowed_hbm), (x_ref, cos_ref, sin_ref, allowed_ref), load_sems
    )
    stores = copies_between(
        (normed_turned, qkv, mixed_turned), (normed_turned_out, qkv_out, mixed_turned_out), store_sems
    )
    start_all(loads)
    fetch_qkv(rows_ref, weights, w_qkv, sems.at[0])
    fetch_out(rows_ref, weights, w_out, sems.at[1])
    length = x_ref.shape[0]
    part = length // NARROW

    def norm_rows(rows):
        values = x_ref[rows, :].astype(f32)
        normed[rows, :] = (values * rms_inverse(values) * gain_ref[...]).astype(bf16)

    loads[0].wait()
    row_chunks(length, ROWS, norm_rows)
    wait_all(loads[1:])
    wait_bytes(w_qkv, sems.at[0])
    for begin, size in spans(QKV_WIDTH, COLS):
        products = dot_nn(normed[...], w_qkv[:, pl.ds(begin, size)]) + bias_ref[:, pl.ds(begin, size)]
        for offset, width in spans(size, HEAD_DIM):
            head = products[:, offset : offset + width]
            if begin + offset < QUERY_WIDTH + PAIR_COLS * BLK:
                head = head * cos_ref[...] + pltpu.roll(head, HEAD_DIM // 2, 1) * sin_ref[...]
            qkv[:, pl.ds(begin + offset, width)] = head.astype(bf16)
    for begin, size in spans(D, COLS):
        normed_turned[pl.ds(begin, size), :] = normed[:, pl.ds(begin, size)].T
    start_all(stores[:2])
    values_turned = qkv[:, pl.ds(QUERY_WIDTH + HEAD_DIM, HEAD_DIM)].T
    for head in range(QUERY_COLS):
        columns = pl.ds(head * HEAD_DIM, HEAD_DIM)
        for first in range(0, length, part):
            tokens, seen = pl.ds(first, part), first + part
            scores = scores_turned(
                qkv[:seen, pl.ds(QUERY_WIDTH, HEAD_DIM)], qkv[tokens, columns], allowed_ref[:seen, tokens] > 0
            )
            peak = jnp.max(scores, axis=0, keepdims=True)
            expo = jnp.exp(scores - peak)
            total = jnp.sum(expo, axis=0, keepdims=True)
            log_ref[pl.ds(head, 1), tokens] = peak + jnp.log(total)
            probs = (expo / total).astype(bf16)
            mixed_head = dot_nn(values_turned[:, :seen], probs).astype(bf16)
            mixed_turned[columns, tokens] = mixed_head
            mixed[tokens, columns] = mixed_head.T
    stores[2].start()
    wait_bytes(w_out, sems.at[1])
    for part_ref, first in ((part_low_ref, 0), (part_high_ref, part)):
        for begin, size in spans(D, COLS):
            part_ref[:, pl.ds(begin, size)] = dot_nn(
                mixed[pl.ds(first, part), :], w_out[:, pl.ds(begin, size)]
            ).astype(bf16)
    wait_all(stores)


def pair_copies(rows_ref, blocks_hbm, pair, sem, column, place, outward=False):
    return [
        block_copy(blocks_hbm.at[rows_ref[base + i * HIDDEN_COLS + column]], block_ref(pair, i, which), sem, outward)
        for i in range(ROW_BLOCKS)
        for base, which in ((GATE_BASE, 2 * place), (UP_BASE, 2 * place + 1))
    ]


def down_copies(rows_ref, blocks_hbm, down, sem, column, place, outward=False):
    return [
        block_copy(blocks_hbm.at[rows_ref[DOWN_BASE + column * ROW_BLOCKS + i]], block_ref(down, place, i), sem, outward)
        for i in range(ROW_BLOCKS)
    ]


def block_copy(in_hbm, in_vmem, sem, outward):
    return pltpu.make_async_copy(*((in_vmem, in_hbm) if outward else (in_hbm, in_vmem)), sem)


def start_all(copies):
    for copy in copies:
        copy.start()


def half_rows(half_ref, length):
    begin = pl.multiple_of(half_ref[0] * length, length)
    return (pl.ds(begin, length), pl.ds(pl.multiple_of(length - begin, length), length))


def hidden_column(tile, place):
    return jnp.minimum(tile * TILE_BLOCKS + place, HIDDEN_COLS - 1)


def hidden_tiles(run):
    @pl.loop(0, TILES - 1)
    def _(tile):
        run(tile, lax.rem(tile, 2), TILE_BLOCKS, True)

    run(TILES - 1, (TILES - 1) % 2, LAST_BLOCKS, False)


def active_grads(rows_ref, cot_ref, weights, out, down_out, w_down, stage, load_sems, store_sems, down_sems):
    ring = w_down.shape[0]

    def fetch(tile):
        slot = lax.rem(tile, ring)
        for place in range(TILE_BLOCKS):
            start_all(
                down_copies(rows_ref, weights, w_down.at[slot], load_sems.at[slot], hidden_column(tile, place), place)
            )

    def store(tile):
        return pltpu.make_async_copy(stage.at[lax.rem(tile, 2)], out.at[tile], store_sems.at[lax.rem(tile, 2)])

    def store_down(tile):
        slot = lax.rem(tile, ring)
        return pltpu.make_async_copy(w_down.at[slot], down_out.at[tile], down_sems.at[slot])

    fetch(0)

    def run(tile, slot, blocks, more):
        here = lax.rem(tile, ring)

        @pl.when(tile >= ring - 1)
        def _():
            store_down(tile - ring + 1).wait()

        if more:
            fetch(tile + 1)
        wait_bytes(w_down.at[here], load_sems.at[here])
        if blocks < TILE_BLOCKS:
            w_down[here, pl.ds(blocks * BLK, (TILE_BLOCKS - blocks) * BLK), :] = jnp.zeros(
                ((TILE_BLOCKS - blocks) * BLK, D), bf16
            )
        store_down(tile).start()

        @pl.when(tile >= 2)
        def _():
            store(tile - 2).wait()

        for begin, size in spans(blocks * BLK, COLS):
            stage[slot, :, pl.ds(begin, size)] = dot_nt(cot_ref[...], w_down[here, pl.ds(begin, size), :])
        store(tile).start()

    hidden_tiles(run)
    for tile in range(max(TILES - 2, 0), TILES):
        store(tile).wait()
    for tile in range(max(TILES - ring + 1, 0), TILES):
        store_down(tile).wait()


def hidden_grads(
    first_row,
    rows_ref,
    gain_ref,
    x_hbm,
    own_hbm,
    other_hbm,
    active_grad,
    weights,
    grad_ref,
    resid_out,
    normed_turned_out,
    pair_grads,
    active,
    active_turned,
    x_ref,
    own_ref,
    other_ref,
    resid_ref,
    normed_turned_ref,
    w_pair,
    grad_active,
    straight,
    turned,
    grads,
    normed,
    grad_sum,
    load_sems,
    store_sems,
    token_sems,
):
    length = own_ref.shape[0]
    token_loads = copies_between(
        (x_hbm.at[pl.ds(first_row, length)], own_hbm, other_hbm), (x_ref, own_ref, other_ref), token_sems
    )
    store_resid = pltpu.make_async_copy(resid_ref, resid_out, token_sems.at[3])
    store_turned = pltpu.make_async_copy(normed_turned_ref, normed_turned_out, token_sems.at[4])
    start_all(token_loads)

    def fetch(tile, slot, place):
        start_all(
            pair_copies(rows_ref, weights, w_pair.at[slot], load_sems.at[slot, 0], hidden_column(tile, place), place)
        )

    def load_grad(tile, slot):
        return pltpu.make_async_copy(active_grad.at[tile, pl.ds(first_row, length)], grad_active.at[slot], load_sems.at[slot, 1])

    def stores(tile, slot):
        return (
            pltpu.make_async_copy(turned.at[slot], active_turned.at[tile], store_sems.at[slot, 0]),
            pltpu.make_async_copy(grads.at[slot], pair_grads.at[tile], store_sems.at[slot, 1]),
            pltpu.make_async_copy(straight.at[slot], active.at[tile], store_sems.at[slot, 2]),
        )

    for place in range(TILE_BLOCKS):
        fetch(0, 0, place)
    load_grad(0, 0).start()

    def norm_rows(rows):
        values = x_ref[rows, :].astype(f32) + own_ref[rows, :].astype(f32) + other_ref[rows, :].astype(f32)
        resid_ref[rows, :] = values
        normed[rows, :] = (values * rms_inverse(values) * gain_ref[...]).astype(bf16)

    wait_all(token_loads)
    row_chunks(length, ROWS, norm_rows)
    store_resid.start()
    grad_sum[...] = jnp.zeros_like(grad_sum)

    def run(tile, slot, blocks, more):
        wait_bytes(w_pair.at[slot], load_sems.at[slot, 0])
        load_grad(tile, slot).wait()
        if more:
            load_grad(tile + 1, 1 - slot).start()

        @pl.when(tile >= 2)
        def _():
            for copy in stores(tile - 2, slot):
                copy.wait()

        for place in range(blocks):
            columns = pl.ds(place * BLK, BLK)
            pair = dot_nn(normed[...], w_pair[slot, :, pl.ds(2 * place * BLK, 2 * BLK)])
            gate = pair[:, :BLK]
            upper = pair[:, BLK:]
            grad = grad_active[slot, :, columns]
            sigmoid = jax.nn.sigmoid(gate)
            silu = gate * sigmoid
            active_here = (silu * upper).astype(bf16)
            straight[slot, :, columns] = active_here
            turned[slot, columns, :] = active_here.T
            grads[slot, :, pl.ds(2 * place * BLK, BLK)] = (
                grad * upper * sigmoid * (1.0 + gate * (1.0 - sigmoid))
            ).astype(bf16)
            grads[slot, :, pl.ds((2 * place + 1) * BLK, BLK)] = (grad * silu).astype(bf16)
            if more:
                fetch(tile + 1, 1 - slot, place)
        if more:
            for place in range(blocks, TILE_BLOCKS):
                fetch(tile + 1, 1 - slot, place)
        turn = pl.ds(pl.multiple_of(tile * COLS, COLS), COLS)
        normed_turned_ref[turn, :] = normed[:, turn].T
        width = 2 * blocks * BLK
        for begin, size in spans(D, COLS):
            columns = pl.ds(begin, size)
            grad_sum[:, columns] += dot_nt(grads[slot, :, :width], w_pair[slot, columns, :width])
        start_all(stores(tile, slot))

    hidden_tiles(run)
    store_turned.start()
    grad_ref[...] = grad_sum[...].astype(bf16)
    for tile in range(max(TILES - 2, 0), TILES):
        wait_all(stores(tile, tile % 2))
    store_resid.wait()
    store_turned.wait()


def hidden_weight_grads(rows_ref, cot_ref, *refs):
    parts, grads, scratch = refs[: 3 * NARROW], refs[3 * NARROW], refs[3 * NARROW + 1 :]
    normed_turned, pair, turned, pair_stage, down_stage, load_sems, store_sems, sems = scratch
    length = cot_ref.shape[0] // NARROW

    def loads(tile, slot):
        copies = []
        for part in range(NARROW):
            pair_grads, active_turned = parts[part * 3 + 1 : part * 3 + 3]
            tokens = pl.ds(part * length, length)
            copies += [
                pltpu.make_async_copy(pair_grads.at[tile], pair.at[slot, tokens], load_sems.at[slot, part * 2]),
                pltpu.make_async_copy(
                    active_turned.at[tile], turned.at[slot, :, tokens], load_sems.at[slot, part * 2 + 1]
                ),
            ]
        return copies

    def drain(slot, blocks):
        wait_bytes(pair_stage.at[slot, :, pl.ds(0, 2 * blocks * BLK)], store_sems.at[slot, 0])
        wait_bytes(down_stage.at[slot, pl.ds(0, blocks * BLK)], store_sems.at[slot, 1])

    turned_loads = [
        pltpu.make_async_copy(parts[part * 3], normed_turned.at[:, pl.ds(part * length, length)], sems.at[part])
        for part in range(NARROW)
    ]
    start_all(loads(0, 0) + turned_loads)
    wait_all(turned_loads)

    def run(tile, slot, blocks, more):
        wait_all(loads(tile, slot))
        if more:
            start_all(loads(tile + 1, 1 - slot))

        @pl.when(tile >= 2)
        def _():
            drain(slot, TILE_BLOCKS)

        width = blocks * BLK
        down = turned[slot, pl.ds(0, width), :]
        for begin, size in spans(D, COLS):
            columns = pl.ds(begin, size)
            down_stage[slot, pl.ds(0, width), columns] = dot_nn(down, cot_ref[:, columns]).astype(bf16)
        for place in range(blocks):
            column = tile * TILE_BLOCKS + place
            start_all(
                down_copies(rows_ref, grads, down_stage.at[slot], store_sems.at[slot, 1], column, place, outward=True)
            )
            columns = pl.ds(2 * place * BLK, 2 * BLK)
            for begin, size in spans(D, 512):
                pair_stage[slot, pl.ds(begin, size), columns] = dot_nn(
                    normed_turned[pl.ds(begin, size), :], pair[slot, :, columns]
                ).astype(bf16)
            start_all(
                pair_copies(rows_ref, grads, pair_stage.at[slot], store_sems.at[slot, 0], column, place, outward=True)
            )

    hidden_tiles(run)
    if TILES > 1:
        drain((TILES - 2) % 2, TILE_BLOCKS)
    drain((TILES - 1) % 2, LAST_BLOCKS)


def attention_backward(
    weight_rows_ref,
    rows_ref,
    half_ref,
    gain_ref,
    log_ref,
    resid_low_hbm,
    own_low_hbm,
    other_low_hbm,
    resid_high_hbm,
    own_high_hbm,
    other_high_hbm,
    cot_hbm,
    qkv_hbm,
    cos_hbm,
    sin_hbm,
    allowed_hbm,
    mixed_turned_hbm,
    normed_turned_hbm,
    x_hbm,
    weights,
    grads_in,
    grad_resid_ref,
    grad_own_ref,
    grad_other_ref,
    grads,
    resid_low_ref,
    own_low_ref,
    other_low_ref,
    resid_high_ref,
    own_high_ref,
    other_high_ref,
    cot_ref,
    qkv_ref,
    cos_ref,
    sin_ref,
    allowed_ref,
    mixed_turned_ref,
    normed_turned_ref,
    x_ref,
    w_qkv,
    w_out,
    grad_resid,
    grad_attention,
    grad_mixed,
    grad_qkv,
    grad_sum,
    grad_keys,
    grad_values,
    gain_part,
    gain_two_part,
    bias_part,
    qkv_stage,
    out_stage,
    small_stage,
    blank,
    load_sems,
    store_sems,
    token_sems,
):
    del grads_in
    loads = copies_between(
        (
            cot_hbm, resid_low_hbm, own_low_hbm, other_low_hbm, resid_high_hbm, own_high_hbm, other_high_hbm, qkv_hbm,
            cos_hbm, sin_hbm, allowed_hbm, mixed_turned_hbm, normed_turned_hbm, x_hbm,
        ),
        (
            cot_ref, resid_low_ref, own_low_ref, other_low_ref, resid_high_ref, own_high_ref, other_high_ref, qkv_ref,
            cos_ref, sin_ref, allowed_ref, mixed_turned_ref, normed_turned_ref, x_ref,
        ),
        token_sems,
    )
    start_all(loads[:7])
    wide_count = small_stage.shape[0]
    owner_rows = grads.shape[0] // wide_count
    small_stage[...] = jnp.zeros_like(small_stage)
    fetch_out(weight_rows_ref, weights, w_out, load_sems.at[1])
    start_all(loads[7:])
    fetch_qkv(weight_rows_ref, weights, w_qkv, load_sems.at[0])
    length = x_ref.shape[0]
    empty_count = rows_ref.shape[0] - BLOCK_TOTAL
    blank[...] = jnp.zeros_like(blank)
    for index in range(empty_count):
        pltpu.make_async_copy(blank.at[index], grads.at[rows_ref[BLOCK_TOTAL + index]], store_sems.at[2]).start()

    gain_two_part[...] = jnp.zeros_like(gain_two_part)
    part = length // NARROW
    own_rows, other_rows = half_rows(half_ref, part)
    for first, resid_ref, own_ref, other_ref, needed in (
        (0, resid_low_ref, own_low_ref, other_low_ref, loads[:4]),
        (part, resid_high_ref, own_high_ref, other_high_ref, loads[4:7]),
    ):
        wait_all(needed)

        def resid_rows(rows, first=first, resid_ref=resid_ref, own_ref=own_ref, other_ref=other_ref):
            values = resid_ref[rows, :]
            inverse = rms_inverse(values)
            normed = values * inverse
            grad_normed = own_ref[rows, :].astype(f32) + other_ref[rows, :].astype(f32)
            gain_two_part[...] += jnp.sum(grad_normed * normed, axis=0, keepdims=True) / NARROW
            scaled = grad_normed * gain_ref[1:2, :]
            place = pl.ds(rows.start + first, rows.size)
            total = cot_ref[place, :].astype(f32) + inverse * (
                scaled - normed * jnp.mean(scaled * normed, axis=-1, keepdims=True)
            )
            grad_resid[place, :] = total
            grad_attention[place, :] = total.astype(bf16)

        row_chunks(part, ROWS, resid_rows)
    grad_resid_ref[...] = grad_resid[own_rows, :]
    wait_bytes(w_out, load_sems.at[1])
    for begin, size in spans(QUERY_WIDTH, COLS):
        grad_mixed[:, pl.ds(begin, size)] = dot_nt(grad_attention[...], w_out[pl.ds(begin, size), :]).astype(bf16)
    wait_all(loads[7:11])
    keys_turned = qkv_ref[:, pl.ds(QUERY_WIDTH, HEAD_DIM)].T

    def rope_back(vector):
        return vector * cos_ref[...] - pltpu.roll(vector, HEAD_DIM // 2, 1) * sin_ref[...]

    grad_keys[...] = jnp.zeros_like(grad_keys)
    grad_values[...] = jnp.zeros_like(grad_values)
    for head in range(QUERY_COLS):
        columns = pl.ds(head * HEAD_DIM, HEAD_DIM)
        grad_queries = []
        for first in range(0, length, part):
            tokens, seen = pl.ds(first, part), first + part
            queries = qkv_ref[tokens, columns]
            grad_mixed_here = grad_mixed[tokens, columns]
            scores = scores_turned(
                qkv_ref[:seen, pl.ds(QUERY_WIDTH, HEAD_DIM)], queries, allowed_ref[:seen, tokens] > 0
            )
            probs = jnp.exp(scores - log_ref[pl.ds(head, 1), tokens])
            grad_values[:seen, :] += dot_nn(probs.astype(bf16), grad_mixed_here)
            grad_probs = dot_nt(qkv_ref[:seen, pl.ds(QUERY_WIDTH + HEAD_DIM, HEAD_DIM)], grad_mixed_here)
            row_dot = jnp.sum(probs * grad_probs, axis=0, keepdims=True)
            grad_scores = (probs * (grad_probs - row_dot)).astype(bf16)
            grad_keys[:seen, :] += dot_nn(grad_scores, queries)
            grad_queries.append(dot_nn(keys_turned[:, :seen], grad_scores).T * scaling)
        grad_qkv[:, columns] = rope_back(jnp.concatenate(grad_queries, axis=0)).astype(bf16)
    grad_qkv[:, pl.ds(QUERY_WIDTH, HEAD_DIM)] = rope_back(grad_keys[...] * scaling).astype(bf16)
    grad_qkv[:, pl.ds(QUERY_WIDTH + HEAD_DIM, HEAD_DIM)] = grad_values[...].astype(bf16)
    wait_all(loads[11:])

    for begin, size in spans(D, COLS):
        out_stage[:, pl.ds(begin, size)] = dot_nn(
            mixed_turned_ref[...], grad_attention[:, pl.ds(begin, size)]
        ).astype(bf16)
    store_piece(rows_ref, out_stage, grads, OUT_BASE, ROW_BLOCKS, QUERY_COLS, ROW_BLOCKS, 0, store_sems.at[1])
    for begin, size in spans(QKV_WIDTH, COLS):
        qkv_stage[:, pl.ds(begin, size)] = dot_nn(
            normed_turned_ref[...], grad_qkv[:, pl.ds(begin, size)]
        ).astype(bf16)
    store_piece(rows_ref, qkv_stage, grads, 0, QUERY_COLS, ROW_BLOCKS, QUERY_COLS, 0, store_sems.at[0])
    store_piece(rows_ref, qkv_stage, grads, KEY_BASE, PAIR_COLS, ROW_BLOCKS, PAIR_COLS, QUERY_COLS, store_sems.at[0])
    store_piece(
        rows_ref, qkv_stage, grads, VALUE_BASE, PAIR_COLS, ROW_BLOCKS, PAIR_COLS, QUERY_COLS + PAIR_COLS, store_sems.at[0]
    )
    wait_bytes(w_qkv, load_sems.at[0])
    for begin, size in spans(D, COLS):
        grad_sum[:, pl.ds(begin, size)] = dot_nt(grad_qkv[...], w_qkv[pl.ds(begin, size), :])
    grad_own_ref[...] = grad_sum[own_rows, :].astype(bf16)
    grad_other_ref[...] = grad_sum[other_rows, :].astype(bf16)
    gain_part[...] = jnp.zeros_like(gain_part)
    bias_part[...] = dot_nn(jnp.ones((SMALL_ROWS, length), bf16), grad_qkv[...])[:1]

    def gain_rows(rows):
        tokens = x_ref[rows, :].astype(f32)
        gain_part[...] += jnp.sum(grad_sum[rows, :] * tokens * rms_inverse(tokens), axis=0, keepdims=True)

    row_chunks(length, ROWS, gain_rows)
    for owner in range(wide_count):
        gain_row, bias_row = small_places(owner, wide_count)
        small_rows = []
        for row in (gain_row, gain_row + 1):
            columns = pl.ds(row % (D // BLK) * BLK, BLK)
            if row < D // BLK:
                small_rows.append(gain_part[:, columns])
            else:
                small_rows.append(gain_two_part[:, columns])
        small_rows.append(bias_part[:, pl.ds(bias_row * BLK, BLK)])
        small_rows.append(jnp.zeros((SMALL_ROWS - len(small_rows), BLK), f32))
        small_stage[owner, pl.ds(0, SMALL_ROWS), :] = jnp.concatenate(small_rows, axis=0).astype(bf16)
        pltpu.make_async_copy(
            small_stage.at[owner], grads.at[owner * owner_rows + owner_rows - 1], store_sems.at[3]
        ).start()
    wait_bytes(small_stage, store_sems.at[3])
    wait_bytes(qkv_stage, store_sems.at[0])
    wait_bytes(out_stage, store_sems.at[1])
    if empty_count > 0:
        wait_bytes(blank.at[pl.ds(0, empty_count)], store_sems.at[2])


def soap_update(
    grad_in,
    masters_ref,
    first_ref,
    second_ref,
    left_ref,
    right_ref,
    grad_out,
    masters_out,
    first_out,
    second_out,
    small_ref,
    grad_stage,
    masters_stage,
    first_stage,
    second_stage,
    sems,
):
    group = grad_stage.shape[1]
    outputs = (
        (grad_stage, grad_out), (masters_stage, masters_out), (first_stage, first_out), (second_stage, second_out)
    )
    steps = masters_ref.shape[0] // group
    small_ref[...] = grad_in[masters_ref.shape[0], :SMALL_ROWS].astype(f32)

    def stores(step):
        slot = lax.rem(step, 2)
        places = pl.ds(step * group, group)
        return [
            pltpu.make_async_copy(stage.at[slot], out.at[places], sems.at[slot, index])
            for index, (stage, out) in enumerate(outputs)
        ]

    @pl.loop(0, steps)
    def _(step):
        @pl.when(step >= 2)
        def _():
            for copy in stores(step - 2):
                copy.wait()

        soap_group(
            step * group, lax.rem(step, 2), grad_in, masters_ref, first_ref, second_ref, left_ref, right_ref,
            *[stage for stage, _ in outputs],
        )
        start_all(stores(step))

    for step in range(max(steps - 2, 0), steps):
        for copy in stores(step):
            copy.wait()


def soap_group(
    first_block, slot, grad_in, masters_ref, first_ref, second_ref, left_ref, right_ref,
    grad_stage, masters_stage, first_stage, second_stage,
):
    places = range(grad_stage.shape[1])
    blocks = [first_block + place for place in places]
    for place, block in enumerate(blocks):
        grad_stage[slot, place] = grad_in[block].astype(f32)
    soap_blocks(
        [grad_in[block] for block in blocks],
        *[[ref.at[block] for block in blocks] for ref in (masters_ref, first_ref, second_ref, left_ref, right_ref)],
        *[[stage.at[slot, place] for place in places] for stage in (masters_stage, first_stage, second_stage)],
    )


def soap_blocks(grads, masters, firsts, seconds, lefts, rights, masters_out, firsts_out, seconds_out):
    count = range(len(grads))
    rights = [right[...].astype(bf16) for right in rights]
    products = [dot_nn(grads[index].astype(bf16), rights[index]).astype(bf16) for index in count]
    lefts = [left[...].astype(bf16) for left in lefts]
    rotated_blocks = [dot_nn(lefts[index].T, products[index]) for index in count]
    normalized = []
    for index in count:
        rotated = rotated_blocks[index]
        new_first = beta_first * firsts[index][...] + (1.0 - beta_first) * rotated
        new_second = beta_second * seconds[index][...] + (1.0 - beta_second) * rotated * rotated
        firsts_out[index][...] = new_first
        seconds_out[index][...] = new_second
        normalized.append(
            (new_first / first_fix / (jnp.sqrt(new_second / second_fix) + adam_eps)).astype(bf16)
        )
    products = [dot_nt(normalized[index], rights[index]).astype(bf16) for index in count]
    for index in count:
        masters_out[index][...] = masters[index][...] - rate_blocks * dot_nn(lefts[index], products[index])


def params(limit=VMEM_LIMIT, **options):
    return pltpu.CompilerParams(vmem_limit_bytes=limit, **options)


def run_attention_forward(rows, x, gain, bias, cosine, sine, allowed, weights):
    length = x.shape[0]
    shape = jax.ShapeDtypeStruct
    kept = [((D, length), bf16), ((length, QKV_WIDTH), bf16), ((QUERY_WIDTH, length), bf16)]
    low, high, log_total, *kept_arrays = pl.pallas_call(
        attention_forward,
        out_shape=[
            shape((length // NARROW, D), bf16),
            shape((length // NARROW, D), bf16),
            shape((8, length), f32),
        ]
        + [shape(*one) for one in kept],
        in_specs=[SMEM_SPEC] + [VMEM_SPEC] * 2 + [ANY_SPEC] * 5,
        out_specs=[VMEM_SPEC] * 3 + [ANY_SPEC] * 3,
        scratch_shapes=[pltpu.VMEM(array.shape, array.dtype) for array in (x, cosine, sine, allowed)]
        + [pltpu.VMEM(*one) for one in kept]
        + [
            pltpu.VMEM((D, QKV_WIDTH), bf16),
            pltpu.VMEM((QUERY_WIDTH, D), bf16),
            pltpu.VMEM((length, D), bf16),
            pltpu.VMEM((length, QUERY_WIDTH), bf16),
            pltpu.SemaphoreType.DMA((2,)),
            pltpu.SemaphoreType.DMA((4,)),
            pltpu.SemaphoreType.DMA((3,)),
        ],
        compiler_params=params(),
        name="attention_forward",
    )(rows, gain, bias, x, cosine, sine, allowed, weights)
    return (low, high, *kept_arrays, log_total)


def hidden_cost(length, products, bytes_moved):
    return pl.CostEstimate(
        flops=2 * products * length * D * TILE * TILES, bytes_accessed=bytes_moved, transcendentals=0
    )


def run_active_grads(rows, cotangent, weights):
    length = cotangent.shape[0]
    return pl.pallas_call(
        active_grads,
        out_shape=[
            jax.ShapeDtypeStruct((TILES, length, TILE), f32),
            jax.ShapeDtypeStruct((TILES, TILE, D), bf16),
        ],
        in_specs=[SMEM_SPEC, VMEM_SPEC, ANY_SPEC],
        out_specs=[ANY_SPEC] * 2,
        scratch_shapes=[
            pltpu.VMEM((4, TILE, D), bf16),
            pltpu.VMEM((2, length, TILE), f32),
            pltpu.SemaphoreType.DMA((4,)),
            pltpu.SemaphoreType.DMA((2,)),
            pltpu.SemaphoreType.DMA((4,)),
        ],
        compiler_params=params(),
        cost_estimate=hidden_cost(length, 1, TILES * TILE * (2 * D + 4 * length)),
        name="active_grads",
    )(rows, cotangent, weights)


def run_hidden_grads(first_row, rows, x, own, other, gain, active_grad, weights):
    length = own.shape[0]
    shape = jax.ShapeDtypeStruct
    return pl.pallas_call(
        functools.partial(hidden_grads, first_row),
        out_shape=[
            shape((length, D), bf16),
            shape((length, D), f32),
            shape((D, length), bf16),
            shape((TILES, length, 2 * TILE), bf16),
            shape((TILES, length, TILE), bf16),
            shape((TILES, TILE, length), bf16),
        ],
        in_specs=[SMEM_SPEC, VMEM_SPEC] + [ANY_SPEC] * 5,
        out_specs=[VMEM_SPEC] + [ANY_SPEC] * 5,
        scratch_shapes=[
            pltpu.VMEM((length, D), bf16),
            pltpu.VMEM((length, D), bf16),
            pltpu.VMEM((length, D), bf16),
            pltpu.VMEM((length, D), f32),
            pltpu.VMEM((D, length), bf16),
            pltpu.VMEM((2, D, 2 * TILE), bf16),
            pltpu.VMEM((2, length, TILE), f32),
            pltpu.VMEM((2, length, TILE), bf16),
            pltpu.VMEM((2, TILE, length), bf16),
            pltpu.VMEM((2, length, 2 * TILE), bf16),
            pltpu.VMEM((length, D), bf16),
            pltpu.VMEM((length, D), f32),
            pltpu.SemaphoreType.DMA((2, 2)),
            pltpu.SemaphoreType.DMA((2, 3)),
            pltpu.SemaphoreType.DMA((5,)),
        ],
        compiler_params=params(),
        cost_estimate=hidden_cost(length, 4, 2 * TILES * TILE * (2 * D + 6 * length)),
        name="hidden_grads",
    )(rows, gain, x, own, other, active_grad, weights)


def run_hidden_weight_grads(rows, cotangent, parts, slots):
    length = cotangent.shape[0]
    return pl.pallas_call(
        hidden_weight_grads,
        out_shape=jax.ShapeDtypeStruct((slots, BLK, BLK), bf16),
        in_specs=[SMEM_SPEC, VMEM_SPEC] + [ANY_SPEC] * (3 * NARROW),
        out_specs=ANY_SPEC,
        scratch_shapes=[
            pltpu.VMEM((D, length), bf16),
            pltpu.VMEM((2, length, 2 * TILE), bf16),
            pltpu.VMEM((2, TILE, length), bf16),
            pltpu.VMEM((2, D, 2 * TILE), bf16),
            pltpu.VMEM((2, TILE, D), bf16),
            pltpu.SemaphoreType.DMA((2, 2 * NARROW)),
            pltpu.SemaphoreType.DMA((2, 2)),
            pltpu.SemaphoreType.DMA((NARROW,)),
        ],
        compiler_params=params(),
        cost_estimate=hidden_cost(length, 3, 2 * TILES * TILE * 3 * (D + length)),
        name="hidden_weight_grads",
    )(rows, cotangent, *[array for part in parts for array in part])


def run_attention_backward(
    weight_rows, rows, half, x, low, high, cotangent, gains, cosine, sine, allowed, normed_turned, qkv, mixed_turned,
    log_total, weights, grads, wide_count,
):
    length = x.shape[0]
    shape = jax.ShapeDtypeStruct
    empty_count = max(rows.shape[0] - BLOCK_TOTAL, 1)
    loaded = (*low, *high, cotangent, qkv, cosine, sine, allowed, mixed_turned, normed_turned, x)
    operands = (weight_rows, rows, half, gains, log_total, *loaded, weights, grads)
    return pl.pallas_call(
        attention_backward,
        out_shape=[
            shape((length // NARROW, D), f32),
            shape((length // NARROW, D), bf16),
            shape((length // NARROW, D), bf16),
            shape(grads.shape, bf16),
        ],
        in_specs=[SMEM_SPEC] * 3 + [VMEM_SPEC] * 2 + [ANY_SPEC] * (len(loaded) + 2),
        out_specs=[VMEM_SPEC] * 3 + [ANY_SPEC],
        input_output_aliases={len(operands) - 1: 3},
        scratch_shapes=[pltpu.VMEM(array.shape, array.dtype) for array in loaded]
        + [
            pltpu.VMEM((D, QKV_WIDTH), bf16),
            pltpu.VMEM((QUERY_WIDTH, D), bf16),
            pltpu.VMEM((length, D), f32),
            pltpu.VMEM((length, D), bf16),
            pltpu.VMEM((length, QUERY_WIDTH), bf16),
            pltpu.VMEM((length, QKV_WIDTH), bf16),
            pltpu.VMEM((length, D), f32),
            pltpu.VMEM((length, HEAD_DIM), f32),
            pltpu.VMEM((length, HEAD_DIM), f32),
            pltpu.VMEM((1, D), f32),
            pltpu.VMEM((1, D), f32),
            pltpu.VMEM((1, QKV_WIDTH), f32),
            pltpu.VMEM((D, QKV_WIDTH), bf16),
            pltpu.VMEM((QUERY_WIDTH, D), bf16),
            pltpu.VMEM((wide_count, BLK, BLK), bf16),
            pltpu.VMEM((empty_count, BLK, BLK), bf16),
            pltpu.SemaphoreType.DMA((2,)),
            pltpu.SemaphoreType.DMA((4,)),
            pltpu.SemaphoreType.DMA((len(loaded),)),
        ],
        compiler_params=params(),
        name="attention_backward",
    )(*operands)


def largest_group(count):
    return max(size for size in range(1, 11) if count % size == 0)


def run_soap(reduced, masters, first_moment, second_moment, left_basis, right_basis):
    slots = masters.shape[0]
    group = largest_group(slots)
    shape = jax.ShapeDtypeStruct(masters.shape, f32)
    return pl.pallas_call(
        soap_update,
        out_shape=[shape] * 4 + [jax.ShapeDtypeStruct((SMALL_ROWS, BLK), f32)],
        in_specs=[VMEM_SPEC] * 6,
        out_specs=[ANY_SPEC] * 4 + [VMEM_SPEC],
        scratch_shapes=[pltpu.VMEM((2, group, BLK, BLK), f32)] * 4 + [pltpu.SemaphoreType.DMA((2, 4))],
        compiler_params=params(),
        name="soap_update",
    )(reduced, masters, first_moment, second_moment, left_basis, right_basis)


def sum_for_owners(
    line, steps, late_steps,
    grads, masters, first_moment, second_moment, left_basis, right_basis,
    grad_resid, grad_own, grad_sent, tokens, gain, resid_low, resid_high, active_low, active_high, down,
    out, new_masters, new_first, new_second, input_grad, output, small_own, small_other,
    a_in, a_own, a_sum, a_keep, a_send, a_cross, a_up, a_down,
    b_in, b_own, b_sum, b_keep, b_send, b_cross, b_up, b_down,
    a_params, b_params, grad_resid_here, grad_own_here, grad_other_here, tokens_here, gain_here, resid_here,
    active_here, down_here, branch_sum, branch_sent, branch_other,
    core_send, core_recv, own_sems, cross_send, cross_recv, up_send, up_recv, down_send, down_recv,
    b_core_send, b_core_recv, b_own_sems, b_cross_send, b_cross_recv, b_up_send, b_up_recv, b_down_send, b_down_recv,
    a_param_sems, b_param_sems, token_sems, branch_sems, swap_send, swap_recv, credits,
):
    wide = lax.axis_index("wide")
    narrow = lax.axis_index("narrow")
    z = wide // 4
    x = lax.rem(wide // 2, 2)
    core = lax.rem(wide, 2)
    mesh_id = pl.DeviceIdType.MESH
    core_peer = (wide + 1 - 2 * core, narrow)
    cross_peer = (wide + 2 - 4 * x, narrow)
    upper = (lax.rem(wide + 4, 4 * line), narrow)
    lower = (lax.rem(wide + 4 * line - 4, 4 * line), narrow)
    swap_peer = (wide, 1 - narrow)
    slots = out.shape[0]
    has_upper = z < line - 1
    has_lower = z > 0
    sum_depth = a_sum.shape[0]
    hop_depth = a_up.shape[0]
    b_sum_depth = b_sum.shape[0]

    barrier = pltpu.get_barrier_semaphore()
    pl.semaphore_signal(barrier, inc=1, device_id=core_peer, device_id_type=mesh_id)
    pl.semaphore_signal(barrier, inc=1, device_id=cross_peer, device_id_type=mesh_id)
    pl.semaphore_signal(barrier, inc=1, device_id=swap_peer, device_id_type=mesh_id)

    @pl.when(has_upper)
    def _():
        pl.semaphore_signal(barrier, inc=1, device_id=upper, device_id_type=mesh_id)

    @pl.when(has_lower)
    def _():
        pl.semaphore_signal(barrier, inc=1, device_id=lower, device_id_type=mesh_id)

    pl.semaphore_wait(barrier, 3 + has_upper.astype(jnp.int32) + has_lower.astype(jnp.int32))

    def remote(source, target, send_sem, recv_sem, peer):
        return pltpu.make_async_remote_copy(
            src_ref=source, dst_ref=target, send_sem=send_sem, recv_sem=recv_sem, device_id=peer, device_id_type=mesh_id
        )

    def core_copy(step):
        slot = lax.rem(step, DEPTH)
        source = grads.at[:, :, 1 - core, pl.ds(step * EARLY, EARLY)]
        return remote(source, a_in.at[slot], core_send.at[slot], core_recv.at[slot], core_peer)

    def own_copy(step):
        slot = lax.rem(step, DEPTH)
        return pltpu.make_async_copy(
            grads.at[:, :, core, pl.ds(step * EARLY, EARLY)], a_own.at[slot], own_sems.at[slot]
        )

    def b_core_copy(step):
        slot = lax.rem(step, DEPTH)
        source = grads.at[:, :, 1 - core, slots - 1 - step]
        return remote(source, b_in.at[slot], b_core_send.at[slot], b_core_recv.at[slot], core_peer)

    def b_own_copy(step):
        slot = lax.rem(step, DEPTH)
        return pltpu.make_async_copy(
            grads.at[:, :, core, slots - 1 - step], b_own.at[slot], b_own_sems.at[slot]
        )

    def cross_copy(step):
        slot = lax.rem(step, DEPTH)
        return remote(a_send.at[slot], a_cross.at[slot], cross_send.at[slot], cross_recv.at[slot], cross_peer)

    def b_cross_copy(step):
        slot = lax.rem(step, DEPTH)
        return remote(b_send.at[slot], b_cross.at[slot], b_cross_send.at[slot], b_cross_recv.at[slot], cross_peer)

    def up_copy(step, target):
        slot = lax.rem(step, hop_depth)
        return remote(
            a_sum.at[lax.rem(step, sum_depth), target], a_up.at[slot, target],
            up_send.at[slot, target], up_recv.at[slot, target], upper,
        )

    def down_copy(step, target):
        slot = lax.rem(step, hop_depth)
        return remote(
            a_sum.at[lax.rem(step, sum_depth), target], a_down.at[slot, target],
            down_send.at[slot, target], down_recv.at[slot, target], lower,
        )

    def b_up_copy(step, target):
        slot = lax.rem(step, hop_depth)
        return remote(
            b_sum.at[lax.rem(step, b_sum_depth), target], b_up.at[slot, target],
            b_up_send.at[slot, target], b_up_recv.at[slot, target], upper,
        )

    def b_down_copy(step, target):
        slot = lax.rem(step, hop_depth)
        return remote(
            b_sum.at[lax.rem(step, b_sum_depth), target], b_down.at[slot, target],
            b_down_send.at[slot, target], b_down_recv.at[slot, target], lower,
        )

    def give(channel, peer):
        pl.semaphore_signal(credits.at[channel], inc=1, device_id=peer, device_id_type=mesh_id)

    def take(channel, step, depth):
        @pl.when(step >= depth)
        def _():
            pl.semaphore_wait(credits.at[channel], 1)

    def feed(step, count, channel, remote_copy, local_copy):
        @pl.when(step < count)
        def _():
            take(channel, step, DEPTH)
            remote_copy(step).start()
            local_copy(step).start()

    sources = (masters, first_moment, second_moment, left_basis, right_basis)

    def param_loads(step):
        slot = lax.rem(step, 2)
        places = pl.ds(step * EARLY, EARLY)
        return [
            pltpu.make_async_copy(source.at[places], a_params.at[slot, index], a_param_sems.at[slot, index])
            for index, source in enumerate(sources)
        ]

    def b_param_loads(step):
        slot = lax.rem(step, 2)
        return [
            pltpu.make_async_copy(
                source.at[slots - 1 - step], b_params.at[slot, index], b_param_sems.at[slot, index]
            )
            for index, source in enumerate(sources)
        ]

    token_loads = [
        pltpu.make_async_copy(source, target, token_sems.at[1 + index])
        for index, (source, target) in enumerate((
            (grad_resid, grad_resid_here), (grad_own, grad_own_here), (tokens, tokens_here), (gain, gain_here),
        ))
    ]
    grad_swap = remote(grad_sent, grad_other_here, swap_send.at[0], swap_recv.at[0], swap_peer)
    small_swap = remote(small_own, small_other, swap_send.at[1], swap_recv.at[1], swap_peer)

    branch_swap = remote(branch_sent, branch_other, swap_send.at[2], swap_recv.at[2], swap_peer)

    def branch_load(index):
        tile = lax.rem(index, TILES)
        takes_low = narrow == jnp.where(index < TILES, 1, 0)

        @pl.when(takes_low)
        def _():
            pltpu.make_async_copy(active_low.at[tile], active_here, branch_sems.at[0]).start()

        @pl.when(jnp.logical_not(takes_low))
        def _():
            pltpu.make_async_copy(active_high.at[tile], active_here, branch_sems.at[0]).start()

        pltpu.make_async_copy(down.at[tile], down_here, branch_sems.at[1]).start()

    def branch_step(index):
        pltpu.make_async_copy(active_low.at[0], active_here, branch_sems.at[0]).wait()
        pltpu.make_async_copy(down.at[0], down_here, branch_sems.at[1]).wait()

        @pl.when(lax.rem(index, TILES) == 0)
        def _():
            branch_sum[...] = jnp.zeros_like(branch_sum)

        for begin, size in spans(D, COLS):
            columns = pl.ds(begin, size)
            branch_sum[:, columns] += dot_nn(active_here[...], down_here[:, columns])

        @pl.when(index < 2 * TILES - 1)
        def _():
            branch_load(index + 1)

        @pl.when(index == TILES - 1)
        def _():
            branch_sent[...] = branch_sum[...].astype(bf16)
            branch_swap.start()

    def resid_load(source):
        return pltpu.make_async_copy(source, resid_here, token_sems.at[0])

    def finish_output():
        resid_load(resid_low).wait()
        branch_swap.wait()

        def rows_of_output(rows):
            total = resid_here[rows, :] + branch_sum[rows, :] + branch_other[rows, :].astype(f32)
            output[rows, :] = total.astype(bf16)

        row_chunks(output.shape[0], ROWS, rows_of_output)

    def finish_input_grad():
        wait_all(token_loads)
        grad_swap.wait()

        def rows_of_grad(rows):
            values = tokens_here[rows, :].astype(f32)
            inverse = rms_inverse(values)
            scaled = grad_own_here[rows, :].astype(f32) + grad_other_here[rows, :].astype(f32)
            input_grad[rows, :] = grad_resid_here[rows, :] + norm_back(
                scaled * gain_here[...], values * inverse, inverse
            )

        row_chunks(input_grad.shape[0], ROWS, rows_of_grad)

    grad_swap.start()
    for early in range(DEPTH - 1):
        feed(early, steps, 0, core_copy, own_copy)
        feed(early, late_steps, 1, b_core_copy, b_own_copy)

    start_all(param_loads(0) + param_loads(1) + b_param_loads(1) + b_param_loads(2) + token_loads)
    branch_load(0)
    pl.when(narrow == 0)(lambda: resid_load(resid_low).start())
    pl.when(narrow != 0)(lambda: resid_load(resid_high).start())

    def active(step, count):
        return (step >= 0) & (step < count)

    far = jnp.maximum(z, line - 1 - z)

    def hops(step_up, step_down, count, sums, depth, ups, downs, up, down, channel):
        @pl.when(active(step_up, count) & has_upper)
        def _():
            take(channel, step_up, hop_depth)
            slot = lax.rem(step_up, hop_depth)
            place = lax.rem(step_up, depth)

            def one(target, _):
                @pl.when(has_lower)
                def _():
                    up(step_up, target).wait_recv()
                    sums[place, target] += ups[slot, target]

                up(step_up, target).start()
                return 0

            lax.fori_loop(z + 1, line, one, 0)

        @pl.when(active(step_down, count) & has_lower)
        def _():
            take(channel + 1, step_down, hop_depth)
            slot = lax.rem(step_down, hop_depth)
            place = lax.rem(step_down, depth)

            def one(target, _):
                @pl.when(has_upper)
                def _():
                    down(step_down, target).wait_recv()
                    sums[place, target] += downs[slot, target]

                down(step_down, target).start()
                return 0

            lax.fori_loop(0, z, one, 0)

    def gather_hops(step, count, sums, depth, ups, downs, up, down, channel, total):
        slot = lax.rem(step, hop_depth)
        total[...] = sums[lax.rem(step, depth), z].astype(f32)

        @pl.when(has_lower)
        def _():
            up(step, z).wait_recv()
            total[...] += ups[slot, z].astype(f32)

            @pl.when(step < count - hop_depth)
            def _():
                give(channel, lower)

        @pl.when(has_upper)
        def _():
            down(step, z).wait_recv()
            total[...] += downs[slot, z].astype(f32)

            @pl.when(step < count - hop_depth)
            def _():
                give(channel + 1, upper)

    def retire(step, count, up, down):
        @pl.when(active(step, count))
        def _():
            def sent_up(target, _):
                up(step, target).wait_send()
                return 0

            def sent_down(target, _):
                down(step, target).wait_send()
                return 0

            lax.fori_loop(z + 1, line, sent_up, 0)
            lax.fori_loop(0, z, sent_down, 0)

    def iteration(step, _):
        feed(step + DEPTH - 1, steps, 0, core_copy, own_copy)
        feed(step + DEPTH - 1, late_steps, 1, b_core_copy, b_own_copy)

        retire(step - CROSS_LAG - HOP_LAG * far - 1, steps, up_copy, down_copy)
        retire(step - HOP_LAG * far - 1, late_steps, b_up_copy, b_down_copy)

        @pl.when(step < steps)
        def _():
            slot = lax.rem(step, DEPTH)
            place = lax.rem(step, sum_depth)
            core_copy(step).wait()
            own_copy(step).wait()

            @pl.when(step >= DEPTH)
            def _():
                cross_copy(step - DEPTH).wait_send()

            for target in range(line):
                a_send[slot, target] = a_own[slot, target, 1 - x] + a_in[slot, target, 1 - x]
            take(2, step, DEPTH)
            cross_copy(step).start()
            for target in range(line):
                a_sum[place, target] = a_own[slot, target, x] + a_in[slot, target, x]

            @pl.when(step < steps - DEPTH)
            def _():
                give(0, core_peer)

        @pl.when(step < late_steps)
        def _():
            slot = lax.rem(step, DEPTH)
            b_core_copy(step).wait()
            b_own_copy(step).wait()
            b_sum[lax.rem(step, b_sum_depth)] = b_own[slot] + b_in[slot]

            @pl.when(step < late_steps - DEPTH)
            def _():
                give(1, core_peer)

        crossed = step - CROSS_LAG

        @pl.when(active(crossed, steps))
        def _():
            slot = lax.rem(crossed, DEPTH)
            place = lax.rem(crossed, sum_depth)
            cross_copy(crossed).wait_recv()
            for target in range(line):
                a_sum[place, target] += a_cross[slot, target]

            @pl.when(crossed < steps - DEPTH)
            def _():
                give(2, cross_peer)

        hops(
            step - HOP_LAG * z, step - HOP_LAG * (line - 1 - z), late_steps, b_sum, b_sum_depth, b_up, b_down,
            b_up_copy, b_down_copy, 6,
        )
        hops(
            crossed - HOP_LAG * z, crossed - HOP_LAG * (line - 1 - z), steps, a_sum, sum_depth, a_up, a_down,
            up_copy, down_copy, 4,
        )

        last = crossed - HOP_LAG * far

        @pl.when(active(last, steps))
        def _():
            gather_hops(last, steps, a_sum, sum_depth, a_up, a_down, up_copy, down_copy, 4, a_keep)
            out[pl.ds(last * EARLY, EARLY)] = a_keep[...].astype(bf16)
            slot = lax.rem(last, 2)
            for copy in param_loads(last):
                copy.wait()
            soap_blocks(
                [a_keep[index] for index in range(EARLY)],
                *[[a_params.at[slot, kind, index] for index in range(EARLY)] for kind in range(5)],
                *[
                    [target.at[last * EARLY + index] for index in range(EARLY)]
                    for target in (new_masters, new_first, new_second)
                ],
            )

            @pl.when(last + 2 < steps)
            def _():
                start_all(param_loads(last + 2))

        arrived = step - HOP_LAG * far

        @pl.when(active(arrived, late_steps))
        def _():
            slot = lax.rem(arrived, DEPTH)

            @pl.when(arrived >= DEPTH)
            def _():
                b_cross_copy(arrived - DEPTH).wait_send()

            gather_hops(
                arrived, late_steps, b_sum, b_sum_depth, b_up, b_down, b_up_copy, b_down_copy, 6, b_keep.at[slot]
            )
            b_send[slot] = b_keep[slot, 1 - x].astype(bf16)
            take(3, arrived, DEPTH)
            b_cross_copy(arrived).start()

        paired = arrived - CROSS_LAG

        @pl.when(active(paired, late_steps))
        def _():
            slot = lax.rem(paired, DEPTH)
            b_cross_copy(paired).wait_recv()
            place = slots - 1 - paired
            total = b_keep[slot, x] + b_cross[slot].astype(f32)
            out[place] = total.astype(bf16)

            @pl.when(paired < late_steps - DEPTH)
            def _():
                give(3, cross_peer)

            @pl.when(paired == 0)
            def _():
                small_own[...] = total[: small_own.shape[0]]
                small_swap.start()

            @pl.when(paired > 0)
            def _():
                slot = lax.rem(paired, 2)
                for copy in b_param_loads(paired):
                    copy.wait()
                soap_blocks(
                    [total], *[[b_params.at[slot, kind]] for kind in range(5)],
                    [new_masters.at[place]], [new_first.at[place]], [new_second.at[place]],
                )

                @pl.when(paired + 2 < late_steps)
                def _():
                    start_all(b_param_loads(paired + 2))

        @pl.when((step >= 1) & (step < 2 * TILES + 1))
        def _():
            branch_step(step - 1)

        pl.when(step == 2 * TILES + 1)(finish_output)
        pl.when(step == 4)(finish_input_grad)
        return 0

    lag = HOP_LAG * (line - 1) + CROSS_LAG
    lax.fori_loop(0, max(max(steps, late_steps) + lag, 2 * TILES) + 2, iteration, 0)
    for step in range(max(steps - DEPTH, 0), steps):
        cross_copy(step).wait_send()
    for step in range(max(late_steps - DEPTH, 0), late_steps):
        b_cross_copy(step).wait_send()
    small_swap.wait()


def run_sum_for_owners(grads, wide_count, blocks, token_arrays):
    line = wide_count // 4
    slots, block = grads.shape[0] // wide_count, grads.shape[1:]
    steps = (slots - 1) // (EARLY + 1)
    late_steps = slots - EARLY * steps
    sum_depth = CROSS_LAG + HOP_LAG * (line - 1) + 2
    b_sum_depth = HOP_LAG * (line - 1) + 2
    hop_depth = 2 * HOP_LAG + 2
    dma = pltpu.SemaphoreType.DMA

    def vmem(*shape):
        return pltpu.VMEM(shape + block, bf16)

    def wide_vmem(*shape):
        return pltpu.VMEM(shape + block, f32)

    return pl.pallas_call(
        functools.partial(sum_for_owners, line, steps, late_steps),
        out_shape=[pltpu.VMEM((slots,) + block, bf16)]
        + [pltpu.VMEM(blocks[0].shape, f32)] * 3
        + [pltpu.VMEM(token_arrays[0].shape, f32), pltpu.VMEM(token_arrays[0].shape, bf16)]
        + [pltpu.VMEM((SMALL_ROWS, block[-1]), f32)] * 2,
        in_specs=[ANY_SPEC] * (1 + len(blocks) + len(token_arrays)),
        out_specs=[VMEM_SPEC] * 8,
        scratch_shapes=[
            vmem(DEPTH, line, 2, EARLY),
            vmem(DEPTH, line, 2, EARLY),
            vmem(sum_depth, line, EARLY),
            wide_vmem(EARLY),
            vmem(DEPTH, line, EARLY),
            vmem(DEPTH, line, EARLY),
            vmem(hop_depth, line, EARLY),
            vmem(hop_depth, line, EARLY),
            vmem(DEPTH, line, 2),
            vmem(DEPTH, line, 2),
            vmem(b_sum_depth, line, 2),
            wide_vmem(DEPTH, 2),
            vmem(DEPTH),
            vmem(DEPTH),
            vmem(hop_depth, line, 2),
            vmem(hop_depth, line, 2),
            wide_vmem(2, len(blocks), EARLY),
            wide_vmem(2, len(blocks)),
        ]
        + [pltpu.VMEM(array.shape, array.dtype) for array in token_arrays[:6]]
        + [
            pltpu.VMEM(token_arrays[7].shape[1:], bf16),
            pltpu.VMEM(token_arrays[9].shape[1:], bf16),
            pltpu.VMEM(token_arrays[0].shape, f32),
            pltpu.VMEM(token_arrays[0].shape, bf16),
            pltpu.VMEM(token_arrays[0].shape, bf16),
        ]
        + ([dma((DEPTH,))] * 5 + [dma((hop_depth, line))] * 4) * 2
        + [dma((2, len(blocks)))] * 2
        + [dma((5,)), dma((2,)), dma((3,)), dma((3,)), pltpu.SemaphoreType.REGULAR((8,))],
        compiler_params=params(SUM_VMEM, collective_id=0, has_side_effects=True),
        cost_estimate=pl.CostEstimate(flops=0, bytes_accessed=2 * grads.size * 8, transcendentals=0),
        name="sum_for_owners",
    )(grads.reshape((line, 2, 2, slots) + block), *blocks, *token_arrays)


def write_results(
    reduced, masters, first_moment, second_moment, input_grad, output, small_own, small_other,
    block_grad_out, masters_out, first_out, second_out, input_grad_out, output_out, small_out,
    stage, stage_sems, sems,
):
    copies = [
        pltpu.make_async_copy(source, target, sems.at[index])
        for index, (source, target) in enumerate((
            (masters, masters_out), (first_moment, first_out), (second_moment, second_out),
            (input_grad, input_grad_out), (output, output_out),
        ))
    ]
    start_all(copies)
    small_out[0] = small_own[...]
    small_out[1] = small_other[...]
    group = stage.shape[1]
    steps = masters.shape[0] // group

    def store(step):
        slot = lax.rem(step, 2)
        return pltpu.make_async_copy(
            stage.at[slot], block_grad_out.at[pl.ds(step * group, group)], stage_sems.at[slot]
        )

    @pl.loop(0, steps)
    def _(step):
        @pl.when(step >= 2)
        def _():
            store(step - 2).wait()

        stage[lax.rem(step, 2)] = reduced[pl.ds(step * group, group)].astype(f32)
        store(step).start()

    for step in range(max(steps - 2, 0), steps):
        store(step).wait()
    for copy in copies:
        copy.wait()


def run_write_results(*arrays):
    arrays = [pltpu.with_memory_space_constraint(array, pltpu.VMEM) for array in arrays]
    blocks, rows, small = arrays[1].shape, arrays[4].shape, arrays[-1].shape
    group = largest_group(blocks[0])
    shape = jax.ShapeDtypeStruct
    return pl.pallas_call(
        write_results,
        out_shape=[shape(blocks, f32)] * 4 + [shape(rows, f32), shape(rows, bf16), shape((2,) + small, f32)],
        in_specs=[VMEM_SPEC] * len(arrays),
        out_specs=[ANY_SPEC] * 6 + [VMEM_SPEC],
        scratch_shapes=[
            pltpu.VMEM((2, group) + blocks[1:], f32),
            pltpu.SemaphoreType.DMA((2,)),
            pltpu.SemaphoreType.DMA((5,)),
        ],
        compiler_params=params(WRITE_VMEM),
        name="write_results",
    )(*arrays)


def rope_tables(segment_row):
    token_index = jnp.arange(segment_row.shape[0], dtype=jnp.int32)
    changed = jnp.concatenate([jnp.ones((1,), dtype=bool), segment_row[1:] != segment_row[:-1]])
    begins = lax.cummax(jnp.where(changed, token_index, jnp.zeros_like(token_index)), axis=0)
    places = (token_index - begins).astype(f32)
    frequency = rope_base ** (-(jnp.arange(HEAD_DIM // 2, dtype=f32) * 2.0) / HEAD_DIM)
    angles = places[:, None] * frequency[None, :]
    cosine = jnp.concatenate([jnp.cos(angles), jnp.cos(angles)], axis=-1)
    sine_signed = jnp.concatenate([-jnp.sin(angles), jnp.sin(angles)], axis=-1)
    return (cosine, sine_signed)


def rms_parts(values):
    inverse = rms_inverse(values)
    return (inverse, values * inverse)


def norm_back(grad_scaled, normed, inverse):
    return inverse * (grad_scaled - normed * jnp.mean(grad_scaled * normed, axis=-1, keepdims=True))


def adam_small(param_now, gradient, first_now, second_now, rate_here):
    first_new = beta_first * first_now + (1.0 - beta_first) * gradient
    second_new = beta_second * second_now + (1.0 - beta_second) * gradient * gradient
    param_new = param_now - rate_here * (first_new / first_fix) / (
        jnp.sqrt(second_new / second_fix) + adam_eps
    )
    return (param_new, first_new, second_new)


def swap_halves(values):
    return lax.ppermute(values, "narrow", [(0, 1), (1, 0)])


def body(
    tokens,
    cotangent,
    segments,
    owner_list,
    masters,
    first_moment,
    second_moment,
    left_basis,
    right_basis,
    gains,
    gain_first,
    gain_second,
    biases,
    bias_first,
    bias_second,
):
    half = lax.axis_index("narrow")
    wide_index = lax.axis_index("wide")
    wide_count = lax.axis_size("wide")
    tokens_here = tokens.shape[0]
    slots_here = masters.shape[0]
    slots_half = owner_list.shape[0]
    gains_here = gains.shape[0]
    biases_here = biases.shape[1]

    def join_halves(own, other, axis=0):
        return jnp.where(
            half == 0, jnp.concatenate([own, other], axis=axis), jnp.concatenate([other, own], axis=axis)
        )

    masters_low, gains, biases = lax.optimization_barrier((masters.astype(bf16), gains, biases))
    weights = lax.all_gather(masters_low, "wide", axis=0, tiled=True)
    gain_full = lax.all_gather(gains, ("wide", "narrow"), axis=0, tiled=True).reshape(2, D)
    bias_full = lax.all_gather(biases.reshape(-1).astype(bf16), "wide", axis=0, tiled=True)
    bias_full = bias_full.astype(f32).reshape(1, QKV_WIDTH)
    pair_gains = 2 * gains_here

    position = jnp.arange(slots_half, dtype=jnp.int32)
    empty = owner_list == BLOCK_TOTAL
    number = jnp.where(empty, BLOCK_TOTAL - 1 + jnp.cumsum(empty.astype(jnp.int32)), owner_list)
    weight_rows = jnp.zeros((slots_half,), jnp.int32).at[number].set(position, unique_indices=True)
    rows = weight_rows + weight_rows // slots_here
    half_index = half.astype(jnp.int32).reshape(1)

    segment_row = lax.dynamic_index_in_dim(segments, wide_index, 0, keepdims=False)
    cosine, sine = rope_tables(segment_row)
    token_index = jnp.arange(segment_row.shape[0], dtype=jnp.int32)
    allowed_turned = (
        (segment_row[None, :] == segment_row[:, None]) & (token_index[None, :] >= token_index[:, None])
    ).astype(f32)
    tokens_row = join_halves(tokens, swap_halves(tokens))
    cotangent_row = join_halves(cotangent, swap_halves(cotangent))
    weights, tokens_row, cotangent_row = lax.optimization_barrier((weights, tokens_row, cotangent_row))

    low_part, high_part, normed_one_turned, qkv, mixed_turned, log_total = run_attention_forward(
        weight_rows, tokens_row, gain_full[0:1], bias_full, cosine, sine, allowed_turned, weights
    )
    low_other = swap_halves(low_part)
    active_grad, down_tiles = run_active_grads(weight_rows, cotangent_row, weights)
    high_sent, low_other = lax.optimization_barrier((high_part, low_other))
    high_other = swap_halves(high_sent)
    gain_two = gain_full[1:2]
    grad_low, resid_low, turned_low, *hidden_low = run_hidden_grads(
        0, weight_rows, tokens_row, low_part, low_other, gain_two, active_grad, weights
    )
    grad_low_other = swap_halves(grad_low)
    grad_high, resid_high, turned_high, *hidden_high = run_hidden_grads(
        tokens_here, weight_rows, tokens_row, high_part, high_other, gain_two, active_grad, weights
    )
    grad_high_other = swap_halves(grad_high)
    pair_low, active_low, active_turned_low = hidden_low
    pair_high, active_high, active_turned_high = hidden_high
    grads = run_hidden_weight_grads(
        rows, cotangent_row, [(turned_low, pair_low, active_turned_low), (turned_high, pair_high, active_turned_high)],
        wide_count * (slots_here + 1),
    )
    grad_resid, grad_one_own, grad_one_sent, grads = run_attention_backward(
        weight_rows, rows, half_index, tokens_row, (resid_low, grad_low, grad_low_other),
        (resid_high, grad_high, grad_high_other), cotangent_row, gain_full, cosine, sine, allowed_turned,
        normed_one_turned, qkv, mixed_turned, log_total, weights, grads, wide_count,
    )
    blocks = [masters, first_moment, second_moment, left_basis, right_basis]
    if wide_count == 16:
        token_arrays = [
            grad_resid, grad_one_own, grad_one_sent, tokens, gain_full[0:1], resid_low, resid_high, active_low,
            active_high, down_tiles,
        ]
        block_grad, new_masters, new_first, new_second, input_grad, output, small_sums = run_write_results(
            *run_sum_for_owners(grads, wide_count, blocks, token_arrays)
        )
        gain_parts = small_sums[0, :2] + small_sums[1, :2]
        bias_row = small_sums[0, 2]
    else:
        reduced = lax.psum_scatter(grads, "wide", scatter_dimension=0, tiled=True)
        block_grad, new_masters, new_first, new_second, small_sums = run_soap(reduced, *blocks)
        gain_parts = small_sums[:2] + swap_halves(small_sums[:2])
        bias_row = small_sums[2]
        branch_low, branch_high = [
            jnp.einsum("tik,tkd->id", active, down_tiles, preferred_element_type=f32)
            for active in (active_low, active_high)
        ]
        resid_own = jnp.where(half == 0, resid_low, resid_high)
        branch_own = jnp.where(half == 0, branch_low, branch_high)
        branch_sent = jnp.where(half == 0, branch_high, branch_low).astype(bf16)
        output = (resid_own + branch_own + swap_halves(branch_sent).astype(f32)).astype(bf16)
        inverse_one, normed_one = rms_parts(tokens.astype(f32))
        grad_one = grad_one_own.astype(f32) + swap_halves(grad_one_sent).astype(f32)
        input_grad = grad_resid + norm_back(grad_one * gain_full[0:1], normed_one, inverse_one)

    gain_first_index = wide_index * pair_gains
    gain_offset = gain_first_index - jnp.minimum(gain_first_index // BLK, 2 * D // BLK - 2) * BLK
    bias_offset = lax.rem(wide_index * biases_here, BLK)
    gain_grad = lax.dynamic_slice_in_dim(gain_parts.reshape(-1), gain_offset + half * gains_here, gains_here, 0)
    bias_grad = lax.dynamic_slice_in_dim(bias_row, bias_offset, biases_here, 0).reshape(biases.shape)
    new_gains, new_gain_first, new_gain_second = adam_small(gains, gain_grad, gain_first, gain_second, rate_gains)
    new_biases, new_bias_first, new_bias_second = adam_small(biases, bias_grad, bias_first, bias_second, rate_small)

    return (
        output,
        input_grad,
        block_grad,
        new_masters,
        new_first,
        new_second,
        gain_grad,
        new_gains,
        new_gain_first,
        new_gain_second,
        bias_grad,
        new_biases,
        new_bias_first,
        new_bias_second,
    )


def solution(mesh):
    tokens_spec = P(("wide", "narrow"), None)
    blocks_spec = P(("wide", "narrow"), None, None)
    gains_spec = P(("wide", "narrow"))
    bias_spec = P("narrow", "wide")
    in_specs = (
        (tokens_spec, tokens_spec, P(), P()) + (blocks_spec,) * 5 + (gains_spec,) * 3 + (bias_spec,) * 3
    )
    out_specs = (tokens_spec, tokens_spec) + (blocks_spec,) * 4 + (gains_spec,) * 4 + (bias_spec,) * 4
    return jax.shard_map(body, mesh=mesh, in_specs=in_specs, out_specs=out_specs, check_vma=False)
```

```python
import functools

import jax
import jax.numpy as jnp
from jax import lax
from jax.experimental import pallas as pl
from jax.experimental.pallas import tpu as pltpu
from jax.sharding import PartitionSpec as P

D = 1536
FF = 8960
HEADS = 12
KV_HEADS = 2
HEAD_DIM = 128
BLK = 128
STEP_COUNT = 5


beta_first = 0.95
beta_second = 0.95
adam_eps = 1e-08
rate_blocks = 0.03
rate_small = 0.4
rate_gains = 0.6
norm_eps = 1e-06
rope_base = 10000.0
masked_score = -1e30
first_fix = 1.0 - beta_first**STEP_COUNT
second_fix = 1.0 - beta_second**STEP_COUNT
scaling = HEAD_DIM ** (-0.5)

bf16 = jnp.bfloat16
f32 = jnp.float32

NARROW = 2
ROW_BLOCKS = D // BLK
QUERY_COLS = HEADS * HEAD_DIM // NARROW // BLK
PAIR_COLS = KV_HEADS * HEAD_DIM // NARROW // BLK
HIDDEN_COLS = FF // NARROW // BLK
QKV_COLS = QUERY_COLS + 2 * PAIR_COLS
QUERY_WIDTH = QUERY_COLS * BLK
QKV_WIDTH = QKV_COLS * BLK
KEY_BASE = ROW_BLOCKS * QUERY_COLS
VALUE_BASE = KEY_BASE + ROW_BLOCKS * PAIR_COLS
OUT_BASE = VALUE_BASE + ROW_BLOCKS * PAIR_COLS
GATE_BASE = OUT_BASE + QUERY_COLS * ROW_BLOCKS
UP_BASE = GATE_BASE + ROW_BLOCKS * HIDDEN_COLS
DOWN_BASE = UP_BASE + ROW_BLOCKS * HIDDEN_COLS
BLOCK_TOTAL = DOWN_BASE + HIDDEN_COLS * ROW_BLOCKS

TILE_BLOCKS = 6
TILES = -(-HIDDEN_COLS // TILE_BLOCKS)
LAST_BLOCKS = HIDDEN_COLS - (TILES - 1) * TILE_BLOCKS
TILE = TILE_BLOCKS * BLK
COLS = 256
ROWS = 64
SMALL_ROWS = 16
VMEM_LIMIT = 60 * 2**20
SUM_VMEM = 39 * 2**20
WRITE_VMEM = 6 * 2**20

EARLY = 4
DEPTH = 3
CROSS_LAG = 2
HOP_LAG = 1

VMEM_SPEC = pl.BlockSpec(memory_space=pltpu.VMEM)
SMEM_SPEC = pl.BlockSpec(memory_space=pltpu.SMEM)
ANY_SPEC = pl.BlockSpec(memory_space=pl.ANY)


def spans(total, step):
    return [(begin, min(step, total - begin)) for begin in range(0, total, step)]


def dot_nn(left, right):
    return jnp.dot(left, right, preferred_element_type=f32)


def dot_nt(left, right):
    return lax.dot_general(left, right, (((1,), (1,)), ((), ())), preferred_element_type=f32)


def block_ref(ref, row_block, col_block):
    return ref.at[pl.ds(row_block * BLK, BLK), pl.ds(col_block * BLK, BLK)]


def fetch_piece(rows_ref, weights, target, base, pitch, row_blocks, col_blocks, first_col, sem):
    @pl.loop(0, row_blocks)
    def _(i):
        for j in range(col_blocks):
            pltpu.make_async_copy(
                weights.at[rows_ref[base + i * pitch + j]],
                block_ref(target, i, first_col + j),
                sem,
            ).start()


def store_piece(rows_ref, source, grads, base, pitch, row_blocks, col_blocks, first_col, sem):
    @pl.loop(0, row_blocks)
    def _(i):
        for j in range(col_blocks):
            pltpu.make_async_copy(
                block_ref(source, i, first_col + j),
                grads.at[rows_ref[base + i * pitch + j]],
                sem,
            ).start()


def wait_bytes(ref, sem):
    pltpu.make_async_copy(ref, ref, sem).wait()


def copies_between(sources, targets, sems):
    return [
        pltpu.make_async_copy(source, target, sems.at[index])
        for index, (source, target) in enumerate(zip(sources, targets, strict=True))
    ]


def wait_all(copies):
    for copy in copies:
        copy.wait()


def fetch_qkv(rows_ref, weights, w_qkv, sem):
    fetch_piece(rows_ref, weights, w_qkv, 0, QUERY_COLS, ROW_BLOCKS, QUERY_COLS, 0, sem)
    fetch_piece(rows_ref, weights, w_qkv, KEY_BASE, PAIR_COLS, ROW_BLOCKS, PAIR_COLS, QUERY_COLS, sem)
    fetch_piece(
        rows_ref, weights, w_qkv, VALUE_BASE, PAIR_COLS, ROW_BLOCKS, PAIR_COLS, QUERY_COLS + PAIR_COLS, sem
    )


def fetch_out(rows_ref, weights, w_out, sem):
    fetch_piece(rows_ref, weights, w_out, OUT_BASE, ROW_BLOCKS, QUERY_COLS, ROW_BLOCKS, 0, sem)


def rms_inverse(values):
    return lax.rsqrt(jnp.mean(values * values, axis=-1, keepdims=True) + norm_eps)


def row_chunks(total, step, run):
    @pl.loop(0, total // step)
    def _(chunk):
        run(pl.ds(pl.multiple_of(chunk * step, step), step))


def small_places(owner, wide_count):
    gain_row = min(owner * (2 * D // wide_count) // BLK, 2 * D // BLK - 2)
    return (gain_row, owner * (QKV_WIDTH // wide_count) // BLK)


def scores_turned(keys, queries, allowed):
    return jnp.where(allowed, dot_nt(keys, queries) * scaling, masked_score)


def attention_forward(
    rows_ref,
    gain_ref,
    bias_ref,
    x_hbm,
    cos_hbm,
    sin_hbm,
    allowed_hbm,
    weights,
    part_low_ref,
    part_high_ref,
    log_ref,
    normed_turned_out,
    qkv_out,
    mixed_turned_out,
    x_ref,
    cos_ref,
    sin_ref,
    allowed_ref,
    normed_turned,
    qkv,
    mixed_turned,
    w_qkv,
    w_out,
    normed,
    mixed,
    sems,
    load_sems,
    store_sems,
):
    loads = copies_between(
        (x_hbm, cos_hbm, sin_hbm, allowed_hbm), (x_ref, cos_ref, sin_ref, allowed_ref), load_sems
    )
    stores = copies_between(
        (normed_turned, qkv, mixed_turned), (normed_turned_out, qkv_out, mixed_turned_out), store_sems
    )
    start_all(loads)
    fetch_qkv(rows_ref, weights, w_qkv, sems.at[0])
    fetch_out(rows_ref, weights, w_out, sems.at[1])
    length = x_ref.shape[0]
    part = length // NARROW

    def norm_rows(rows):
        values = x_ref[rows, :].astype(f32)
        normed[rows, :] = (values * rms_inverse(values) * gain_ref[...]).astype(bf16)

    loads[0].wait()
    row_chunks(length, ROWS, norm_rows)
    wait_all(loads[1:])
    wait_bytes(w_qkv, sems.at[0])
    for begin, size in spans(QKV_WIDTH, COLS):
        products = dot_nn(normed[...], w_qkv[:, pl.ds(begin, size)]) + bias_ref[:, pl.ds(begin, size)]
        for offset, width in spans(size, HEAD_DIM):
            head = products[:, offset : offset + width]
            if begin + offset < QUERY_WIDTH + PAIR_COLS * BLK:
                head = head * cos_ref[...] + pltpu.roll(head, HEAD_DIM // 2, 1) * sin_ref[...]
            qkv[:, pl.ds(begin + offset, width)] = head.astype(bf16)
    for begin, size in spans(D, COLS):
        normed_turned[pl.ds(begin, size), :] = normed[:, pl.ds(begin, size)].T
    start_all(stores[:2])
    values_turned = qkv[:, pl.ds(QUERY_WIDTH + HEAD_DIM, HEAD_DIM)].T
    for head in range(QUERY_COLS):
        columns = pl.ds(head * HEAD_DIM, HEAD_DIM)
        for first in range(0, length, part):
            tokens, seen = pl.ds(first, part), first + part
            scores = scores_turned(
                qkv[:seen, pl.ds(QUERY_WIDTH, HEAD_DIM)], qkv[tokens, columns], allowed_ref[:seen, tokens] > 0
            )
            peak = jnp.max(scores, axis=0, keepdims=True)
            expo = jnp.exp(scores - peak)
            total = jnp.sum(expo, axis=0, keepdims=True)
            log_ref[pl.ds(head, 1), tokens] = peak + jnp.log(total)
            probs = (expo / total).astype(bf16)
            mixed_head = dot_nn(values_turned[:, :seen], probs).astype(bf16)
            mixed_turned[columns, tokens] = mixed_head
            mixed[tokens, columns] = mixed_head.T
    stores[2].start()
    wait_bytes(w_out, sems.at[1])
    for part_ref, first in ((part_low_ref, 0), (part_high_ref, part)):
        for begin, size in spans(D, COLS):
            part_ref[:, pl.ds(begin, size)] = dot_nn(
                mixed[pl.ds(first, part), :], w_out[:, pl.ds(begin, size)]
            ).astype(bf16)
    wait_all(stores)


def pair_copies(rows_ref, blocks_hbm, pair, sem, column, place, outward=False):
    return [
        block_copy(blocks_hbm.at[rows_ref[base + i * HIDDEN_COLS + column]], block_ref(pair, i, which), sem, outward)
        for i in range(ROW_BLOCKS)
        for base, which in ((GATE_BASE, 2 * place), (UP_BASE, 2 * place + 1))
    ]


def down_copies(rows_ref, blocks_hbm, down, sem, column, place, outward=False):
    return [
        block_copy(blocks_hbm.at[rows_ref[DOWN_BASE + column * ROW_BLOCKS + i]], block_ref(down, place, i), sem, outward)
        for i in range(ROW_BLOCKS)
    ]


def block_copy(in_hbm, in_vmem, sem, outward):
    return pltpu.make_async_copy(*((in_vmem, in_hbm) if outward else (in_hbm, in_vmem)), sem)


def start_all(copies):
    for copy in copies:
        copy.start()


def half_rows(half_ref, length):
    begin = pl.multiple_of(half_ref[0] * length, length)
    return (pl.ds(begin, length), pl.ds(pl.multiple_of(length - begin, length), length))


def hidden_column(tile, place):
    return jnp.minimum(tile * TILE_BLOCKS + place, HIDDEN_COLS - 1)


def hidden_tiles(run):
    @pl.loop(0, TILES - 1)
    def _(tile):
        run(tile, lax.rem(tile, 2), TILE_BLOCKS, True)

    run(TILES - 1, (TILES - 1) % 2, LAST_BLOCKS, False)


def active_grads(rows_ref, cot_ref, weights, out, down_out, w_down, stage, load_sems, store_sems, down_sems):
    ring = w_down.shape[0]

    def fetch(tile):
        slot = lax.rem(tile, ring)
        for place in range(TILE_BLOCKS):
            start_all(
                down_copies(rows_ref, weights, w_down.at[slot], load_sems.at[slot], hidden_column(tile, place), place)
            )

    def store(tile):
        return pltpu.make_async_copy(stage.at[lax.rem(tile, 2)], out.at[tile], store_sems.at[lax.rem(tile, 2)])

    def store_down(tile):
        slot = lax.rem(tile, ring)
        return pltpu.make_async_copy(w_down.at[slot], down_out.at[tile], down_sems.at[slot])

    fetch(0)

    def run(tile, slot, blocks, more):
        here = lax.rem(tile, ring)

        @pl.when(tile >= ring - 1)
        def _():
            store_down(tile - ring + 1).wait()

        if more:
            fetch(tile + 1)
        wait_bytes(w_down.at[here], load_sems.at[here])
        if blocks < TILE_BLOCKS:
            w_down[here, pl.ds(blocks * BLK, (TILE_BLOCKS - blocks) * BLK), :] = jnp.zeros(
                ((TILE_BLOCKS - blocks) * BLK, D), bf16
            )
        store_down(tile).start()

        @pl.when(tile >= 2)
        def _():
            store(tile - 2).wait()

        for begin, size in spans(blocks * BLK, COLS):
            stage[slot, :, pl.ds(begin, size)] = dot_nt(cot_ref[...], w_down[here, pl.ds(begin, size), :])
        store(tile).start()

    hidden_tiles(run)
    for tile in range(max(TILES - 2, 0), TILES):
        store(tile).wait()
    for tile in range(max(TILES - ring + 1, 0), TILES):
        store_down(tile).wait()


def hidden_grads(
    first_row,
    rows_ref,
    gain_ref,
    other_ref,
    x_hbm,
    own_hbm,
    active_grad,
    weights,
    grad_ref,
    resid_out,
    normed_turned_out,
    pair_grads,
    active,
    active_turned,
    x_ref,
    own_ref,
    resid_ref,
    normed_turned_ref,
    w_pair,
    grad_active,
    straight,
    turned,
    grads,
    normed,
    grad_sum,
    load_sems,
    store_sems,
    token_sems,
):
    length = own_ref.shape[0]
    token_loads = copies_between(
        (x_hbm.at[pl.ds(first_row, length)], own_hbm), (x_ref, own_ref), token_sems
    )
    store_resid = pltpu.make_async_copy(resid_ref, resid_out, token_sems.at[3])
    store_turned = pltpu.make_async_copy(normed_turned_ref, normed_turned_out, token_sems.at[4])
    start_all(token_loads)

    def fetch(tile, slot, place):
        start_all(
            pair_copies(rows_ref, weights, w_pair.at[slot], load_sems.at[slot, 0], hidden_column(tile, place), place)
        )

    def load_grad(tile, slot):
        return pltpu.make_async_copy(active_grad.at[tile, pl.ds(first_row, length)], grad_active.at[slot], load_sems.at[slot, 1])

    def stores(tile, slot):
        return (
            pltpu.make_async_copy(turned.at[slot], active_turned.at[tile], store_sems.at[slot, 0]),
            pltpu.make_async_copy(grads.at[slot], pair_grads.at[tile], store_sems.at[slot, 1]),
            pltpu.make_async_copy(straight.at[slot], active.at[tile], store_sems.at[slot, 2]),
        )

    for place in range(TILE_BLOCKS):
        fetch(0, 0, place)
    load_grad(0, 0).start()

    def norm_rows(rows):
        values = x_ref[rows, :].astype(f32) + own_ref[rows, :].astype(f32) + other_ref[rows, :].astype(f32)
        resid_ref[rows, :] = values
        normed[rows, :] = (values * rms_inverse(values) * gain_ref[...]).astype(bf16)

    wait_all(token_loads)
    row_chunks(length, ROWS, norm_rows)
    store_resid.start()
    grad_sum[...] = jnp.zeros_like(grad_sum)

    def run(tile, slot, blocks, more):
        wait_bytes(w_pair.at[slot], load_sems.at[slot, 0])
        load_grad(tile, slot).wait()
        if more:
            load_grad(tile + 1, 1 - slot).start()

        @pl.when(tile >= 2)
        def _():
            for copy in stores(tile - 2, slot):
                copy.wait()

        for place in range(blocks):
            columns = pl.ds(place * BLK, BLK)
            pair = dot_nn(normed[...], w_pair[slot, :, pl.ds(2 * place * BLK, 2 * BLK)])
            gate = pair[:, :BLK]
            upper = pair[:, BLK:]
            grad = grad_active[slot, :, columns]
            sigmoid = jax.nn.sigmoid(gate)
            silu = gate * sigmoid
            active_here = (silu * upper).astype(bf16)
            straight[slot, :, columns] = active_here
            turned[slot, columns, :] = active_here.T
            grads[slot, :, pl.ds(2 * place * BLK, BLK)] = (
                grad * upper * sigmoid * (1.0 + gate * (1.0 - sigmoid))
            ).astype(bf16)
            grads[slot, :, pl.ds((2 * place + 1) * BLK, BLK)] = (grad * silu).astype(bf16)
            if more:
                fetch(tile + 1, 1 - slot, place)
        if more:
            for place in range(blocks, TILE_BLOCKS):
                fetch(tile + 1, 1 - slot, place)
        turn = pl.ds(pl.multiple_of(tile * COLS, COLS), COLS)
        normed_turned_ref[turn, :] = normed[:, turn].T
        width = 2 * blocks * BLK
        for begin, size in spans(D, COLS):
            columns = pl.ds(begin, size)
            grad_sum[:, columns] += dot_nt(grads[slot, :, :width], w_pair[slot, columns, :width])
        start_all(stores(tile, slot))

    hidden_tiles(run)
    store_turned.start()
    grad_ref[...] = grad_sum[...].astype(bf16)
    for tile in range(max(TILES - 2, 0), TILES):
        wait_all(stores(tile, tile % 2))
    store_resid.wait()
    store_turned.wait()


def hidden_weight_grads(rows_ref, cot_ref, *refs):
    parts, grads, scratch = refs[: 3 * NARROW], refs[3 * NARROW], refs[3 * NARROW + 1 :]
    normed_turned, pair, turned, pair_stage, down_stage, load_sems, store_sems, sems = scratch
    length = cot_ref.shape[0] // NARROW

    def loads(tile, slot):
        copies = []
        for part in range(NARROW):
            pair_grads, active_turned = parts[part * 3 + 1 : part * 3 + 3]
            tokens = pl.ds(part * length, length)
            copies += [
                pltpu.make_async_copy(pair_grads.at[tile], pair.at[slot, tokens], load_sems.at[slot, part * 2]),
                pltpu.make_async_copy(
                    active_turned.at[tile], turned.at[slot, :, tokens], load_sems.at[slot, part * 2 + 1]
                ),
            ]
        return copies

    def drain(slot, blocks):
        wait_bytes(pair_stage.at[slot, :, pl.ds(0, 2 * blocks * BLK)], store_sems.at[slot, 0])
        wait_bytes(down_stage.at[slot, pl.ds(0, blocks * BLK)], store_sems.at[slot, 1])

    turned_loads = [
        pltpu.make_async_copy(parts[part * 3], normed_turned.at[:, pl.ds(part * length, length)], sems.at[part])
        for part in range(NARROW)
    ]
    start_all(loads(0, 0) + turned_loads)
    wait_all(turned_loads)

    def run(tile, slot, blocks, more):
        wait_all(loads(tile, slot))
        if more:
            start_all(loads(tile + 1, 1 - slot))

        @pl.when(tile >= 2)
        def _():
            drain(slot, TILE_BLOCKS)

        width = blocks * BLK
        down = turned[slot, pl.ds(0, width), :]
        for begin, size in spans(D, COLS):
            columns = pl.ds(begin, size)
            down_stage[slot, pl.ds(0, width), columns] = dot_nn(down, cot_ref[:, columns]).astype(bf16)
        for place in range(blocks):
            column = tile * TILE_BLOCKS + place
            start_all(
                down_copies(rows_ref, grads, down_stage.at[slot], store_sems.at[slot, 1], column, place, outward=True)
            )
            columns = pl.ds(2 * place * BLK, 2 * BLK)
            for begin, size in spans(D, 512):
                pair_stage[slot, pl.ds(begin, size), columns] = dot_nn(
                    normed_turned[pl.ds(begin, size), :], pair[slot, :, columns]
                ).astype(bf16)
            start_all(
                pair_copies(rows_ref, grads, pair_stage.at[slot], store_sems.at[slot, 0], column, place, outward=True)
            )

    hidden_tiles(run)
    if TILES > 1:
        drain((TILES - 2) % 2, TILE_BLOCKS)
    drain((TILES - 1) % 2, LAST_BLOCKS)


def attention_backward(
    weight_rows_ref,
    rows_ref,
    half_ref,
    gain_ref,
    log_ref,
    other_low_ref,
    other_high_ref,
    resid_low_hbm,
    own_low_hbm,
    resid_high_hbm,
    own_high_hbm,
    cot_hbm,
    qkv_hbm,
    cos_hbm,
    sin_hbm,
    allowed_hbm,
    mixed_turned_hbm,
    normed_turned_hbm,
    x_hbm,
    weights,
    grads_in,
    grad_resid_ref,
    grad_own_ref,
    grad_other_ref,
    grads,
    resid_low_ref,
    own_low_ref,
    resid_high_ref,
    own_high_ref,
    cot_ref,
    qkv_ref,
    cos_ref,
    sin_ref,
    allowed_ref,
    mixed_turned_ref,
    normed_turned_ref,
    x_ref,
    w_qkv,
    w_out,
    grad_resid,
    grad_attention,
    grad_mixed,
    grad_qkv,
    grad_sum,
    grad_keys,
    grad_values,
    gain_part,
    gain_two_part,
    bias_part,
    qkv_stage,
    out_stage,
    small_stage,
    blank,
    load_sems,
    store_sems,
    token_sems,
):
    del grads_in
    loads = copies_between(
        (
            cot_hbm, resid_low_hbm, own_low_hbm, resid_high_hbm, own_high_hbm, qkv_hbm, cos_hbm, sin_hbm, allowed_hbm, mixed_turned_hbm, normed_turned_hbm, x_hbm,
        ),
        (
            cot_ref, resid_low_ref, own_low_ref, resid_high_ref, own_high_ref, qkv_ref, cos_ref, sin_ref, allowed_ref, mixed_turned_ref, normed_turned_ref, x_ref,
        ),
        token_sems,
    )
    start_all(loads[:5])
    wide_count = small_stage.shape[0]
    owner_rows = grads.shape[0] // wide_count
    small_stage[...] = jnp.zeros_like(small_stage)
    fetch_out(weight_rows_ref, weights, w_out, load_sems.at[1])
    start_all(loads[5:])
    fetch_qkv(weight_rows_ref, weights, w_qkv, load_sems.at[0])
    length = x_ref.shape[0]
    empty_count = rows_ref.shape[0] - BLOCK_TOTAL
    blank[...] = jnp.zeros_like(blank)
    for index in range(empty_count):
        pltpu.make_async_copy(blank.at[index], grads.at[rows_ref[BLOCK_TOTAL + index]], store_sems.at[2]).start()

    gain_two_part[...] = jnp.zeros_like(gain_two_part)
    part = length // NARROW
    own_rows, other_rows = half_rows(half_ref, part)
    for first, resid_ref, own_ref, other_ref, needed in (
        (0, resid_low_ref, own_low_ref, other_low_ref, loads[:3]),
        (part, resid_high_ref, own_high_ref, other_high_ref, loads[3:5]),
    ):
        wait_all(needed)

        def resid_rows(rows, first=first, resid_ref=resid_ref, own_ref=own_ref, other_ref=other_ref):
            values = resid_ref[rows, :]
            inverse = rms_inverse(values)
            normed = values * inverse
            grad_normed = own_ref[rows, :].astype(f32) + other_ref[rows, :].astype(f32)
            gain_two_part[...] += jnp.sum(grad_normed * normed, axis=0, keepdims=True) / NARROW
            scaled = grad_normed * gain_ref[1:2, :]
            place = pl.ds(rows.start + first, rows.size)
            total = cot_ref[place, :].astype(f32) + inverse * (
                scaled - normed * jnp.mean(scaled * normed, axis=-1, keepdims=True)
            )
            grad_resid[place, :] = total
            grad_attention[place, :] = total.astype(bf16)

        row_chunks(part, ROWS, resid_rows)
    grad_resid_ref[...] = grad_resid[own_rows, :]
    wait_bytes(w_out, load_sems.at[1])
    for begin, size in spans(QUERY_WIDTH, COLS):
        grad_mixed[:, pl.ds(begin, size)] = dot_nt(grad_attention[...], w_out[pl.ds(begin, size), :]).astype(bf16)
    wait_all(loads[5:9])
    keys_turned = qkv_ref[:, pl.ds(QUERY_WIDTH, HEAD_DIM)].T

    def rope_back(vector):
        return vector * cos_ref[...] - pltpu.roll(vector, HEAD_DIM // 2, 1) * sin_ref[...]

    grad_keys[...] = jnp.zeros_like(grad_keys)
    grad_values[...] = jnp.zeros_like(grad_values)
    for head in range(QUERY_COLS):
        columns = pl.ds(head * HEAD_DIM, HEAD_DIM)
        grad_queries = []
        for first in range(0, length, part):
            tokens, seen = pl.ds(first, part), first + part
            queries = qkv_ref[tokens, columns]
            grad_mixed_here = grad_mixed[tokens, columns]
            scores = scores_turned(
                qkv_ref[:seen, pl.ds(QUERY_WIDTH, HEAD_DIM)], queries, allowed_ref[:seen, tokens] > 0
            )
            probs = jnp.exp(scores - log_ref[pl.ds(head, 1), tokens])
            grad_values[:seen, :] += dot_nn(probs.astype(bf16), grad_mixed_here)
            grad_probs = dot_nt(qkv_ref[:seen, pl.ds(QUERY_WIDTH + HEAD_DIM, HEAD_DIM)], grad_mixed_here)
            row_dot = jnp.sum(probs * grad_probs, axis=0, keepdims=True)
            grad_scores = (probs * (grad_probs - row_dot)).astype(bf16)
            grad_keys[:seen, :] += dot_nn(grad_scores, queries)
            grad_queries.append(dot_nn(keys_turned[:, :seen], grad_scores).T * scaling)
        grad_qkv[:, columns] = rope_back(jnp.concatenate(grad_queries, axis=0)).astype(bf16)
    grad_qkv[:, pl.ds(QUERY_WIDTH, HEAD_DIM)] = rope_back(grad_keys[...] * scaling).astype(bf16)
    grad_qkv[:, pl.ds(QUERY_WIDTH + HEAD_DIM, HEAD_DIM)] = grad_values[...].astype(bf16)
    wait_all(loads[9:])

    for begin, size in spans(D, COLS):
        out_stage[:, pl.ds(begin, size)] = dot_nn(
            mixed_turned_ref[...], grad_attention[:, pl.ds(begin, size)]
        ).astype(bf16)
    store_piece(rows_ref, out_stage, grads, OUT_BASE, ROW_BLOCKS, QUERY_COLS, ROW_BLOCKS, 0, store_sems.at[1])
    for begin, size in spans(QKV_WIDTH, COLS):
        qkv_stage[:, pl.ds(begin, size)] = dot_nn(
            normed_turned_ref[...], grad_qkv[:, pl.ds(begin, size)]
        ).astype(bf16)
    store_piece(rows_ref, qkv_stage, grads, 0, QUERY_COLS, ROW_BLOCKS, QUERY_COLS, 0, store_sems.at[0])
    store_piece(rows_ref, qkv_stage, grads, KEY_BASE, PAIR_COLS, ROW_BLOCKS, PAIR_COLS, QUERY_COLS, store_sems.at[0])
    store_piece(
        rows_ref, qkv_stage, grads, VALUE_BASE, PAIR_COLS, ROW_BLOCKS, PAIR_COLS, QUERY_COLS + PAIR_COLS, store_sems.at[0]
    )
    wait_bytes(w_qkv, load_sems.at[0])
    for begin, size in spans(D, COLS):
        grad_sum[:, pl.ds(begin, size)] = dot_nt(grad_qkv[...], w_qkv[pl.ds(begin, size), :])
    grad_own_ref[...] = grad_sum[own_rows, :].astype(bf16)
    grad_other_ref[...] = grad_sum[other_rows, :].astype(bf16)
    gain_part[...] = jnp.zeros_like(gain_part)
    bias_part[...] = dot_nn(jnp.ones((SMALL_ROWS, length), bf16), grad_qkv[...])[:1]

    def gain_rows(rows):
        tokens = x_ref[rows, :].astype(f32)
        gain_part[...] += jnp.sum(grad_sum[rows, :] * tokens * rms_inverse(tokens), axis=0, keepdims=True)

    row_chunks(length, ROWS, gain_rows)
    for owner in range(wide_count):
        gain_row, bias_row = small_places(owner, wide_count)
        small_rows = []
        for row in (gain_row, gain_row + 1):
            columns = pl.ds(row % (D // BLK) * BLK, BLK)
            if row < D // BLK:
                small_rows.append(gain_part[:, columns])
            else:
                small_rows.append(gain_two_part[:, columns])
        small_rows.append(bias_part[:, pl.ds(bias_row * BLK, BLK)])
        small_rows.append(jnp.zeros((SMALL_ROWS - len(small_rows), BLK), f32))
        small_stage[owner, pl.ds(0, SMALL_ROWS), :] = jnp.concatenate(small_rows, axis=0).astype(bf16)
        pltpu.make_async_copy(
            small_stage.at[owner], grads.at[owner * owner_rows + owner_rows - 1], store_sems.at[3]
        ).start()
    wait_bytes(small_stage, store_sems.at[3])
    wait_bytes(qkv_stage, store_sems.at[0])
    wait_bytes(out_stage, store_sems.at[1])
    if empty_count > 0:
        wait_bytes(blank.at[pl.ds(0, empty_count)], store_sems.at[2])


def soap_update(
    grad_in,
    masters_ref,
    first_ref,
    second_ref,
    left_ref,
    right_ref,
    grad_out,
    masters_out,
    first_out,
    second_out,
    small_ref,
    grad_stage,
    masters_stage,
    first_stage,
    second_stage,
    sems,
):
    group = grad_stage.shape[1]
    outputs = (
        (grad_stage, grad_out), (masters_stage, masters_out), (first_stage, first_out), (second_stage, second_out)
    )
    steps = masters_ref.shape[0] // group
    small_ref[...] = grad_in[masters_ref.shape[0], :SMALL_ROWS].astype(f32)

    def stores(step):
        slot = lax.rem(step, 2)
        places = pl.ds(step * group, group)
        return [
            pltpu.make_async_copy(stage.at[slot], out.at[places], sems.at[slot, index])
            for index, (stage, out) in enumerate(outputs)
        ]

    @pl.loop(0, steps)
    def _(step):
        @pl.when(step >= 2)
        def _():
            for copy in stores(step - 2):
                copy.wait()

        soap_group(
            step * group, lax.rem(step, 2), grad_in, masters_ref, first_ref, second_ref, left_ref, right_ref,
            *[stage for stage, _ in outputs],
        )
        start_all(stores(step))

    for step in range(max(steps - 2, 0), steps):
        for copy in stores(step):
            copy.wait()


def soap_group(
    first_block, slot, grad_in, masters_ref, first_ref, second_ref, left_ref, right_ref,
    grad_stage, masters_stage, first_stage, second_stage,
):
    places = range(grad_stage.shape[1])
    blocks = [first_block + place for place in places]
    for place, block in enumerate(blocks):
        grad_stage[slot, place] = grad_in[block].astype(f32)
    soap_blocks(
        [grad_in[block] for block in blocks],
        *[[ref.at[block] for block in blocks] for ref in (masters_ref, first_ref, second_ref, left_ref, right_ref)],
        *[[stage.at[slot, place] for place in places] for stage in (masters_stage, first_stage, second_stage)],
    )


def soap_blocks(grads, masters, firsts, seconds, lefts, rights, masters_out, firsts_out, seconds_out):
    count = range(len(grads))
    rights = [right[...].astype(bf16) for right in rights]
    products = [dot_nn(grads[index].astype(bf16), rights[index]).astype(bf16) for index in count]
    lefts = [left[...].astype(bf16) for left in lefts]
    rotated_blocks = [dot_nn(lefts[index].T, products[index]) for index in count]
    normalized = []
    for index in count:
        rotated = rotated_blocks[index]
        new_first = beta_first * firsts[index][...] + (1.0 - beta_first) * rotated
        new_second = beta_second * seconds[index][...] + (1.0 - beta_second) * rotated * rotated
        firsts_out[index][...] = new_first
        seconds_out[index][...] = new_second
        normalized.append(
            (new_first / first_fix / (jnp.sqrt(new_second / second_fix) + adam_eps)).astype(bf16)
        )
    products = [dot_nt(normalized[index], rights[index]).astype(bf16) for index in count]
    for index in count:
        masters_out[index][...] = masters[index][...] - rate_blocks * dot_nn(lefts[index], products[index])


def params(limit=VMEM_LIMIT, **options):
    return pltpu.CompilerParams(vmem_limit_bytes=limit, **options)


def run_attention_forward(rows, x, gain, bias, cosine, sine, allowed, weights):
    length = x.shape[0]
    shape = jax.ShapeDtypeStruct
    kept = [((D, length), bf16), ((length, QKV_WIDTH), bf16), ((QUERY_WIDTH, length), bf16)]
    low, high, log_total, *kept_arrays = pl.pallas_call(
        attention_forward,
        out_shape=[
            shape((length // NARROW, D), bf16),
            shape((length // NARROW, D), bf16),
            shape((8, length), f32),
        ]
        + [shape(*one) for one in kept],
        in_specs=[SMEM_SPEC] + [VMEM_SPEC] * 2 + [ANY_SPEC] * 5,
        out_specs=[VMEM_SPEC] * 3 + [ANY_SPEC] * 3,
        scratch_shapes=[pltpu.VMEM(array.shape, array.dtype) for array in (x, cosine, sine, allowed)]
        + [pltpu.VMEM(*one) for one in kept]
        + [
            pltpu.VMEM((D, QKV_WIDTH), bf16),
            pltpu.VMEM((QUERY_WIDTH, D), bf16),
            pltpu.VMEM((length, D), bf16),
            pltpu.VMEM((length, QUERY_WIDTH), bf16),
            pltpu.SemaphoreType.DMA((2,)),
            pltpu.SemaphoreType.DMA((4,)),
            pltpu.SemaphoreType.DMA((3,)),
        ],
        compiler_params=params(),
        name="attention_forward",
    )(rows, gain, bias, x, cosine, sine, allowed, weights)
    return (low, high, *kept_arrays, log_total)


def hidden_cost(length, products, bytes_moved):
    return pl.CostEstimate(
        flops=2 * products * length * D * TILE * TILES, bytes_accessed=bytes_moved, transcendentals=0
    )


def run_active_grads(rows, cotangent, weights):
    length = cotangent.shape[0]
    return pl.pallas_call(
        active_grads,
        out_shape=[
            jax.ShapeDtypeStruct((TILES, length, TILE), f32),
            jax.ShapeDtypeStruct((TILES, TILE, D), bf16),
        ],
        in_specs=[SMEM_SPEC, VMEM_SPEC, ANY_SPEC],
        out_specs=[ANY_SPEC] * 2,
        scratch_shapes=[
            pltpu.VMEM((4, TILE, D), bf16),
            pltpu.VMEM((2, length, TILE), f32),
            pltpu.SemaphoreType.DMA((4,)),
            pltpu.SemaphoreType.DMA((2,)),
            pltpu.SemaphoreType.DMA((4,)),
        ],
        compiler_params=params(),
        cost_estimate=hidden_cost(length, 1, TILES * TILE * (2 * D + 4 * length)),
        name="active_grads",
    )(rows, cotangent, weights)


def run_hidden_grads(first_row, rows, x, own, other, gain, active_grad, weights):
    length = own.shape[0]
    shape = jax.ShapeDtypeStruct
    return pl.pallas_call(
        functools.partial(hidden_grads, first_row),
        out_shape=[
            shape((length, D), bf16),
            shape((length, D), f32),
            shape((D, length), bf16),
            shape((TILES, length, 2 * TILE), bf16),
            shape((TILES, length, TILE), bf16),
            shape((TILES, TILE, length), bf16),
        ],
        in_specs=[SMEM_SPEC, VMEM_SPEC, VMEM_SPEC] + [ANY_SPEC] * 4,
        out_specs=[VMEM_SPEC] + [ANY_SPEC] * 5,
        scratch_shapes=[
            pltpu.VMEM((length, D), bf16),
            pltpu.VMEM((length, D), bf16),
            pltpu.VMEM((length, D), f32),
            pltpu.VMEM((D, length), bf16),
            pltpu.VMEM((2, D, 2 * TILE), bf16),
            pltpu.VMEM((2, length, TILE), f32),
            pltpu.VMEM((2, length, TILE), bf16),
            pltpu.VMEM((2, TILE, length), bf16),
            pltpu.VMEM((2, length, 2 * TILE), bf16),
            pltpu.VMEM((length, D), bf16),
            pltpu.VMEM((length, D), f32),
            pltpu.SemaphoreType.DMA((2, 2)),
            pltpu.SemaphoreType.DMA((2, 3)),
            pltpu.SemaphoreType.DMA((5,)),
        ],
        compiler_params=params(),
        cost_estimate=hidden_cost(length, 4, 2 * TILES * TILE * (2 * D + 6 * length)),
        name="hidden_grads",
    )(rows, gain, in_vmem(other), x, own, active_grad, weights)


def run_hidden_weight_grads(rows, cotangent, parts, slots):
    length = cotangent.shape[0]
    return pl.pallas_call(
        hidden_weight_grads,
        out_shape=jax.ShapeDtypeStruct((slots, BLK, BLK), bf16),
        in_specs=[SMEM_SPEC, VMEM_SPEC] + [ANY_SPEC] * (3 * NARROW),
        out_specs=ANY_SPEC,
        scratch_shapes=[
            pltpu.VMEM((D, length), bf16),
            pltpu.VMEM((2, length, 2 * TILE), bf16),
            pltpu.VMEM((2, TILE, length), bf16),
            pltpu.VMEM((2, D, 2 * TILE), bf16),
            pltpu.VMEM((2, TILE, D), bf16),
            pltpu.SemaphoreType.DMA((2, 2 * NARROW)),
            pltpu.SemaphoreType.DMA((2, 2)),
            pltpu.SemaphoreType.DMA((NARROW,)),
        ],
        compiler_params=params(),
        cost_estimate=hidden_cost(length, 3, 2 * TILES * TILE * 3 * (D + length)),
        name="hidden_weight_grads",
    )(rows, cotangent, *[array for part in parts for array in part])


def run_attention_backward(
    weight_rows, rows, half, x, low, high, cotangent, gains, cosine, sine, allowed, normed_turned, qkv, mixed_turned,
    log_total, weights, grads, wide_count,
):
    length = x.shape[0]
    shape = jax.ShapeDtypeStruct
    empty_count = max(rows.shape[0] - BLOCK_TOTAL, 1)
    (resid_low, own_low, other_low), (resid_high, own_high, other_high) = low, high
    loaded = (resid_low, own_low, resid_high, own_high, cotangent, qkv, cosine, sine, allowed, mixed_turned, normed_turned, x)
    operands = (weight_rows, rows, half, gains, log_total, in_vmem(other_low), in_vmem(other_high), *loaded, weights, grads)
    return pl.pallas_call(
        attention_backward,
        out_shape=[
            shape((length // NARROW, D), f32),
            shape((length // NARROW, D), bf16),
            shape((length // NARROW, D), bf16),
            shape(grads.shape, bf16),
        ],
        in_specs=[SMEM_SPEC] * 3 + [VMEM_SPEC] * 4 + [ANY_SPEC] * (len(loaded) + 2),
        out_specs=[VMEM_SPEC] * 3 + [ANY_SPEC],
        input_output_aliases={len(operands) - 1: 3},
        scratch_shapes=[pltpu.VMEM(array.shape, array.dtype) for array in loaded]
        + [
            pltpu.VMEM((D, QKV_WIDTH), bf16),
            pltpu.VMEM((QUERY_WIDTH, D), bf16),
            pltpu.VMEM((length, D), f32),
            pltpu.VMEM((length, D), bf16),
            pltpu.VMEM((length, QUERY_WIDTH), bf16),
            pltpu.VMEM((length, QKV_WIDTH), bf16),
            pltpu.VMEM((length, D), f32),
            pltpu.VMEM((length, HEAD_DIM), f32),
            pltpu.VMEM((length, HEAD_DIM), f32),
            pltpu.VMEM((1, D), f32),
            pltpu.VMEM((1, D), f32),
            pltpu.VMEM((1, QKV_WIDTH), f32),
            pltpu.VMEM((D, QKV_WIDTH), bf16),
            pltpu.VMEM((QUERY_WIDTH, D), bf16),
            pltpu.VMEM((wide_count, BLK, BLK), bf16),
            pltpu.VMEM((empty_count, BLK, BLK), bf16),
            pltpu.SemaphoreType.DMA((2,)),
            pltpu.SemaphoreType.DMA((4,)),
            pltpu.SemaphoreType.DMA((len(loaded),)),
        ],
        compiler_params=params(),
        name="attention_backward",
    )(*operands)


def largest_group(count):
    return max(size for size in range(1, 11) if count % size == 0)


def run_soap(reduced, masters, first_moment, second_moment, left_basis, right_basis):
    slots = masters.shape[0]
    group = largest_group(slots)
    shape = jax.ShapeDtypeStruct(masters.shape, f32)
    return pl.pallas_call(
        soap_update,
        out_shape=[shape] * 4 + [jax.ShapeDtypeStruct((SMALL_ROWS, BLK), f32)],
        in_specs=[VMEM_SPEC] * 6,
        out_specs=[ANY_SPEC] * 4 + [VMEM_SPEC],
        scratch_shapes=[pltpu.VMEM((2, group, BLK, BLK), f32)] * 4 + [pltpu.SemaphoreType.DMA((2, 4))],
        compiler_params=params(),
        name="soap_update",
    )(reduced, masters, first_moment, second_moment, left_basis, right_basis)


def sum_for_owners(
    line, steps, late_steps,
    grads, masters, first_moment, second_moment, left_basis, right_basis,
    grad_resid, grad_own, grad_sent, tokens, gain, resid_low, resid_high, active_low, active_high, down,
    out, new_masters, new_first, new_second, input_grad, output, small_own, small_other,
    a_in, a_own, a_sum, a_keep, a_send, a_cross, a_up, a_down,
    b_in, b_own, b_sum, b_keep, b_send, b_cross, b_up, b_down,
    a_params, b_params, grad_resid_here, grad_own_here, grad_other_here, tokens_here, gain_here, resid_here,
    active_here, down_here, branch_sum, branch_sent, branch_other,
    core_send, core_recv, own_sems, cross_send, cross_recv, up_send, up_recv, down_send, down_recv,
    b_core_send, b_core_recv, b_own_sems, b_cross_send, b_cross_recv, b_up_send, b_up_recv, b_down_send, b_down_recv,
    a_param_sems, b_param_sems, token_sems, branch_sems, swap_send, swap_recv, credits,
):
    wide = lax.axis_index("wide")
    narrow = lax.axis_index("narrow")
    z = wide // 4
    x = lax.rem(wide // 2, 2)
    core = lax.rem(wide, 2)
    mesh_id = pl.DeviceIdType.MESH
    core_peer = (wide + 1 - 2 * core, narrow)
    cross_peer = (wide + 2 - 4 * x, narrow)
    upper = (lax.rem(wide + 4, 4 * line), narrow)
    lower = (lax.rem(wide + 4 * line - 4, 4 * line), narrow)
    swap_peer = (wide, 1 - narrow)
    slots = out.shape[0]
    has_upper = z < line - 1
    has_lower = z > 0
    sum_depth = a_sum.shape[0]
    hop_depth = a_up.shape[0]
    b_sum_depth = b_sum.shape[0]

    barrier = pltpu.get_barrier_semaphore()
    pl.semaphore_signal(barrier, inc=1, device_id=core_peer, device_id_type=mesh_id)
    pl.semaphore_signal(barrier, inc=1, device_id=cross_peer, device_id_type=mesh_id)
    pl.semaphore_signal(barrier, inc=1, device_id=swap_peer, device_id_type=mesh_id)

    @pl.when(has_upper)
    def _():
        pl.semaphore_signal(barrier, inc=1, device_id=upper, device_id_type=mesh_id)

    @pl.when(has_lower)
    def _():
        pl.semaphore_signal(barrier, inc=1, device_id=lower, device_id_type=mesh_id)

    pl.semaphore_wait(barrier, 3 + has_upper.astype(jnp.int32) + has_lower.astype(jnp.int32))

    def remote(source, target, send_sem, recv_sem, peer):
        return pltpu.make_async_remote_copy(
            src_ref=source, dst_ref=target, send_sem=send_sem, recv_sem=recv_sem, device_id=peer, device_id_type=mesh_id
        )

    def core_copy(step):
        slot = lax.rem(step, DEPTH)
        source = grads.at[:, :, 1 - core, pl.ds(step * EARLY, EARLY)]
        return remote(source, a_in.at[slot], core_send.at[slot], core_recv.at[slot], core_peer)

    def own_copy(step):
        slot = lax.rem(step, DEPTH)
        return pltpu.make_async_copy(
            grads.at[:, :, core, pl.ds(step * EARLY, EARLY)], a_own.at[slot], own_sems.at[slot]
        )

    def b_core_copy(step):
        slot = lax.rem(step, DEPTH)
        source = grads.at[:, :, 1 - core, slots - 1 - step]
        return remote(source, b_in.at[slot], b_core_send.at[slot], b_core_recv.at[slot], core_peer)

    def b_own_copy(step):
        slot = lax.rem(step, DEPTH)
        return pltpu.make_async_copy(
            grads.at[:, :, core, slots - 1 - step], b_own.at[slot], b_own_sems.at[slot]
        )

    def cross_copy(step):
        slot = lax.rem(step, DEPTH)
        return remote(a_send.at[slot], a_cross.at[slot], cross_send.at[slot], cross_recv.at[slot], cross_peer)

    def b_cross_copy(step):
        slot = lax.rem(step, DEPTH)
        return remote(b_send.at[slot], b_cross.at[slot], b_cross_send.at[slot], b_cross_recv.at[slot], cross_peer)

    def up_copy(step, target):
        slot = lax.rem(step, hop_depth)
        return remote(
            a_sum.at[lax.rem(step, sum_depth), target], a_up.at[slot, target],
            up_send.at[slot, target], up_recv.at[slot, target], upper,
        )

    def down_copy(step, target):
        slot = lax.rem(step, hop_depth)
        return remote(
            a_sum.at[lax.rem(step, sum_depth), target], a_down.at[slot, target],
            down_send.at[slot, target], down_recv.at[slot, target], lower,
        )

    def b_up_copy(step, target):
        slot = lax.rem(step, hop_depth)
        return remote(
            b_sum.at[lax.rem(step, b_sum_depth), target], b_up.at[slot, target],
            b_up_send.at[slot, target], b_up_recv.at[slot, target], upper,
        )

    def b_down_copy(step, target):
        slot = lax.rem(step, hop_depth)
        return remote(
            b_sum.at[lax.rem(step, b_sum_depth), target], b_down.at[slot, target],
            b_down_send.at[slot, target], b_down_recv.at[slot, target], lower,
        )

    def give(channel, peer):
        pl.semaphore_signal(credits.at[channel], inc=1, device_id=peer, device_id_type=mesh_id)

    def take(channel, step, depth):
        @pl.when(step >= depth)
        def _():
            pl.semaphore_wait(credits.at[channel], 1)

    def feed(step, count, channel, remote_copy, local_copy):
        @pl.when(step < count)
        def _():
            take(channel, step, DEPTH)
            remote_copy(step).start()
            local_copy(step).start()

    sources = (masters, first_moment, second_moment, left_basis, right_basis)

    def param_loads(step):
        slot = lax.rem(step, 2)
        places = pl.ds(step * EARLY, EARLY)
        return [
            pltpu.make_async_copy(source.at[places], a_params.at[slot, index], a_param_sems.at[slot, index])
            for index, source in enumerate(sources)
        ]

    def b_param_loads(step):
        slot = lax.rem(step, 2)
        return [
            pltpu.make_async_copy(
                source.at[slots - 1 - step], b_params.at[slot, index], b_param_sems.at[slot, index]
            )
            for index, source in enumerate(sources)
        ]

    token_loads = [
        pltpu.make_async_copy(source, target, token_sems.at[1 + index])
        for index, (source, target) in enumerate((
            (grad_resid, grad_resid_here), (grad_own, grad_own_here), (tokens, tokens_here), (gain, gain_here),
        ))
    ]
    grad_swap = remote(grad_sent, grad_other_here, swap_send.at[0], swap_recv.at[0], swap_peer)
    small_swap = remote(small_own, small_other, swap_send.at[1], swap_recv.at[1], swap_peer)

    branch_swap = remote(branch_sent, branch_other, swap_send.at[2], swap_recv.at[2], swap_peer)

    def branch_load(index):
        tile = lax.rem(index, TILES)
        takes_low = narrow == jnp.where(index < TILES, 1, 0)

        @pl.when(takes_low)
        def _():
            pltpu.make_async_copy(active_low.at[tile], active_here, branch_sems.at[0]).start()

        @pl.when(jnp.logical_not(takes_low))
        def _():
            pltpu.make_async_copy(active_high.at[tile], active_here, branch_sems.at[0]).start()

        pltpu.make_async_copy(down.at[tile], down_here, branch_sems.at[1]).start()

    def branch_step(index):
        pltpu.make_async_copy(active_low.at[0], active_here, branch_sems.at[0]).wait()
        pltpu.make_async_copy(down.at[0], down_here, branch_sems.at[1]).wait()

        @pl.when(lax.rem(index, TILES) == 0)
        def _():
            branch_sum[...] = jnp.zeros_like(branch_sum)

        for begin, size in spans(D, COLS):
            columns = pl.ds(begin, size)
            branch_sum[:, columns] += dot_nn(active_here[...], down_here[:, columns])

        @pl.when(index < 2 * TILES - 1)
        def _():
            branch_load(index + 1)

        @pl.when(index == TILES - 1)
        def _():
            branch_sent[...] = branch_sum[...].astype(bf16)
            branch_swap.start()

    def resid_load(source):
        return pltpu.make_async_copy(source, resid_here, token_sems.at[0])

    def finish_output():
        resid_load(resid_low).wait()
        branch_swap.wait()

        def rows_of_output(rows):
            total = resid_here[rows, :] + branch_sum[rows, :] + branch_other[rows, :].astype(f32)
            output[rows, :] = total.astype(bf16)

        row_chunks(output.shape[0], ROWS, rows_of_output)

    def finish_input_grad():
        wait_all(token_loads)
        grad_swap.wait()

        def rows_of_grad(rows):
            values = tokens_here[rows, :].astype(f32)
            inverse = rms_inverse(values)
            scaled = grad_own_here[rows, :].astype(f32) + grad_other_here[rows, :].astype(f32)
            input_grad[rows, :] = grad_resid_here[rows, :] + norm_back(
                scaled * gain_here[...], values * inverse, inverse
            )

        row_chunks(input_grad.shape[0], ROWS, rows_of_grad)

    grad_swap.start()
    for early in range(DEPTH - 1):
        feed(early, steps, 0, core_copy, own_copy)
        feed(early, late_steps, 1, b_core_copy, b_own_copy)

    start_all(param_loads(0) + param_loads(1) + b_param_loads(1) + b_param_loads(2) + token_loads)
    branch_load(0)
    pl.when(narrow == 0)(lambda: resid_load(resid_low).start())
    pl.when(narrow != 0)(lambda: resid_load(resid_high).start())

    def active(step, count):
        return (step >= 0) & (step < count)

    far = jnp.maximum(z, line - 1 - z)

    def hops(step_up, step_down, count, sums, depth, ups, downs, up, down, channel):
        @pl.when(active(step_up, count) & has_upper)
        def _():
            take(channel, step_up, hop_depth)
            slot = lax.rem(step_up, hop_depth)
            place = lax.rem(step_up, depth)

            def one(target, _):
                @pl.when(has_lower)
                def _():
                    up(step_up, target).wait_recv()
                    sums[place, target] += ups[slot, target]

                up(step_up, target).start()
                return 0

            lax.fori_loop(z + 1, line, one, 0)

        @pl.when(active(step_down, count) & has_lower)
        def _():
            take(channel + 1, step_down, hop_depth)
            slot = lax.rem(step_down, hop_depth)
            place = lax.rem(step_down, depth)

            def one(target, _):
                @pl.when(has_upper)
                def _():
                    down(step_down, target).wait_recv()
                    sums[place, target] += downs[slot, target]

                down(step_down, target).start()
                return 0

            lax.fori_loop(0, z, one, 0)

    def gather_hops(step, count, sums, depth, ups, downs, up, down, channel, total):
        slot = lax.rem(step, hop_depth)
        total[...] = sums[lax.rem(step, depth), z].astype(f32)

        @pl.when(has_lower)
        def _():
            up(step, z).wait_recv()
            total[...] += ups[slot, z].astype(f32)

            @pl.when(step < count - hop_depth)
            def _():
                give(channel, lower)

        @pl.when(has_upper)
        def _():
            down(step, z).wait_recv()
            total[...] += downs[slot, z].astype(f32)

            @pl.when(step < count - hop_depth)
            def _():
                give(channel + 1, upper)

    def retire(step, count, up, down):
        @pl.when(active(step, count))
        def _():
            def sent_up(target, _):
                up(step, target).wait_send()
                return 0

            def sent_down(target, _):
                down(step, target).wait_send()
                return 0

            lax.fori_loop(z + 1, line, sent_up, 0)
            lax.fori_loop(0, z, sent_down, 0)

    def iteration(step, _):
        feed(step + DEPTH - 1, steps, 0, core_copy, own_copy)
        feed(step + DEPTH - 1, late_steps, 1, b_core_copy, b_own_copy)

        retire(step - CROSS_LAG - HOP_LAG * far - 1, steps, up_copy, down_copy)
        retire(step - HOP_LAG * far - 1, late_steps, b_up_copy, b_down_copy)

        @pl.when(step < steps)
        def _():
            slot = lax.rem(step, DEPTH)
            place = lax.rem(step, sum_depth)
            core_copy(step).wait()
            own_copy(step).wait()

            @pl.when(step >= DEPTH)
            def _():
                cross_copy(step - DEPTH).wait_send()

            for target in range(line):
                a_send[slot, target] = a_own[slot, target, 1 - x] + a_in[slot, target, 1 - x]
            take(2, step, DEPTH)
            cross_copy(step).start()
            for target in range(line):
                a_sum[place, target] = a_own[slot, target, x] + a_in[slot, target, x]

            @pl.when(step < steps - DEPTH)
            def _():
                give(0, core_peer)

        @pl.when(step < late_steps)
        def _():
            slot = lax.rem(step, DEPTH)
            b_core_copy(step).wait()
            b_own_copy(step).wait()
            b_sum[lax.rem(step, b_sum_depth)] = b_own[slot] + b_in[slot]

            @pl.when(step < late_steps - DEPTH)
            def _():
                give(1, core_peer)

        crossed = step - CROSS_LAG

        @pl.when(active(crossed, steps))
        def _():
            slot = lax.rem(crossed, DEPTH)
            place = lax.rem(crossed, sum_depth)
            cross_copy(crossed).wait_recv()
            for target in range(line):
                a_sum[place, target] += a_cross[slot, target]

            @pl.when(crossed < steps - DEPTH)
            def _():
                give(2, cross_peer)

        hops(
            step - HOP_LAG * z, step - HOP_LAG * (line - 1 - z), late_steps, b_sum, b_sum_depth, b_up, b_down,
            b_up_copy, b_down_copy, 6,
        )
        hops(
            crossed - HOP_LAG * z, crossed - HOP_LAG * (line - 1 - z), steps, a_sum, sum_depth, a_up, a_down,
            up_copy, down_copy, 4,
        )

        last = crossed - HOP_LAG * far

        @pl.when(active(last, steps))
        def _():
            gather_hops(last, steps, a_sum, sum_depth, a_up, a_down, up_copy, down_copy, 4, a_keep)
            out[pl.ds(last * EARLY, EARLY)] = a_keep[...].astype(bf16)
            slot = lax.rem(last, 2)
            for copy in param_loads(last):
                copy.wait()
            soap_blocks(
                [a_keep[index] for index in range(EARLY)],
                *[[a_params.at[slot, kind, index] for index in range(EARLY)] for kind in range(5)],
                *[
                    [target.at[last * EARLY + index] for index in range(EARLY)]
                    for target in (new_masters, new_first, new_second)
                ],
            )

            @pl.when(last + 2 < steps)
            def _():
                start_all(param_loads(last + 2))

        arrived = step - HOP_LAG * far

        @pl.when(active(arrived, late_steps))
        def _():
            slot = lax.rem(arrived, DEPTH)

            @pl.when(arrived >= DEPTH)
            def _():
                b_cross_copy(arrived - DEPTH).wait_send()

            gather_hops(
                arrived, late_steps, b_sum, b_sum_depth, b_up, b_down, b_up_copy, b_down_copy, 6, b_keep.at[slot]
            )
            b_send[slot] = b_keep[slot, 1 - x].astype(bf16)
            take(3, arrived, DEPTH)
            b_cross_copy(arrived).start()

        paired = arrived - CROSS_LAG

        @pl.when(active(paired, late_steps))
        def _():
            slot = lax.rem(paired, DEPTH)
            b_cross_copy(paired).wait_recv()
            place = slots - 1 - paired
            total = b_keep[slot, x] + b_cross[slot].astype(f32)
            out[place] = total.astype(bf16)

            @pl.when(paired < late_steps - DEPTH)
            def _():
                give(3, cross_peer)

            @pl.when(paired == 0)
            def _():
                small_own[...] = total[: small_own.shape[0]]
                small_swap.start()

            @pl.when(paired > 0)
            def _():
                slot = lax.rem(paired, 2)
                for copy in b_param_loads(paired):
                    copy.wait()
                soap_blocks(
                    [total], *[[b_params.at[slot, kind]] for kind in range(5)],
                    [new_masters.at[place]], [new_first.at[place]], [new_second.at[place]],
                )

                @pl.when(paired + 2 < late_steps)
                def _():
                    start_all(b_param_loads(paired + 2))

        @pl.when((step >= 1) & (step < 2 * TILES + 1))
        def _():
            branch_step(step - 1)

        pl.when(step == 2 * TILES + 1)(finish_output)
        pl.when(step == 4)(finish_input_grad)
        return 0

    lag = HOP_LAG * (line - 1) + CROSS_LAG
    lax.fori_loop(0, max(max(steps, late_steps) + lag, 2 * TILES) + 2, iteration, 0)
    for step in range(max(steps - DEPTH, 0), steps):
        cross_copy(step).wait_send()
    for step in range(max(late_steps - DEPTH, 0), late_steps):
        b_cross_copy(step).wait_send()
    small_swap.wait()


def run_sum_for_owners(grads, wide_count, blocks, token_arrays):
    line = wide_count // 4
    slots, block = grads.shape[0] // wide_count, grads.shape[1:]
    steps = (slots - 1) // (EARLY + 1)
    late_steps = slots - EARLY * steps
    sum_depth = CROSS_LAG + HOP_LAG * (line - 1) + 2
    b_sum_depth = HOP_LAG * (line - 1) + 2
    hop_depth = 2 * HOP_LAG + 2
    dma = pltpu.SemaphoreType.DMA

    def vmem(*shape):
        return pltpu.VMEM(shape + block, bf16)

    def wide_vmem(*shape):
        return pltpu.VMEM(shape + block, f32)

    return pl.pallas_call(
        functools.partial(sum_for_owners, line, steps, late_steps),
        out_shape=[pltpu.VMEM((slots,) + block, bf16)]
        + [pltpu.VMEM(blocks[0].shape, f32)] * 3
        + [pltpu.VMEM(token_arrays[0].shape, f32), pltpu.VMEM(token_arrays[0].shape, bf16)]
        + [pltpu.VMEM((SMALL_ROWS, block[-1]), f32)] * 2,
        in_specs=[ANY_SPEC] * (1 + len(blocks) + len(token_arrays)),
        out_specs=[VMEM_SPEC] * 8,
        scratch_shapes=[
            vmem(DEPTH, line, 2, EARLY),
            vmem(DEPTH, line, 2, EARLY),
            vmem(sum_depth, line, EARLY),
            wide_vmem(EARLY),
            vmem(DEPTH, line, EARLY),
            vmem(DEPTH, line, EARLY),
            vmem(hop_depth, line, EARLY),
            vmem(hop_depth, line, EARLY),
            vmem(DEPTH, line, 2),
            vmem(DEPTH, line, 2),
            vmem(b_sum_depth, line, 2),
            wide_vmem(DEPTH, 2),
            vmem(DEPTH),
            vmem(DEPTH),
            vmem(hop_depth, line, 2),
            vmem(hop_depth, line, 2),
            wide_vmem(2, len(blocks), EARLY),
            wide_vmem(2, len(blocks)),
        ]
        + [pltpu.VMEM(array.shape, array.dtype) for array in token_arrays[:6]]
        + [
            pltpu.VMEM(token_arrays[7].shape[1:], bf16),
            pltpu.VMEM(token_arrays[9].shape[1:], bf16),
            pltpu.VMEM(token_arrays[0].shape, f32),
            pltpu.VMEM(token_arrays[0].shape, bf16),
            pltpu.VMEM(token_arrays[0].shape, bf16),
        ]
        + ([dma((DEPTH,))] * 5 + [dma((hop_depth, line))] * 4) * 2
        + [dma((2, len(blocks)))] * 2
        + [dma((5,)), dma((2,)), dma((3,)), dma((3,)), pltpu.SemaphoreType.REGULAR((8,))],
        compiler_params=params(SUM_VMEM, collective_id=0, has_side_effects=True),
        cost_estimate=pl.CostEstimate(flops=0, bytes_accessed=2 * grads.size * 8, transcendentals=0),
        name="sum_for_owners",
    )(grads.reshape((line, 2, 2, slots) + block), *blocks, *token_arrays)


def write_results(
    reduced, masters, first_moment, second_moment, input_grad, output, small_own, small_other,
    block_grad_out, masters_out, first_out, second_out, input_grad_out, output_out, small_out,
    stage, stage_sems, sems,
):
    copies = [
        pltpu.make_async_copy(source, target, sems.at[index])
        for index, (source, target) in enumerate((
            (masters, masters_out), (first_moment, first_out), (second_moment, second_out),
            (input_grad, input_grad_out), (output, output_out),
        ))
    ]
    start_all(copies)
    small_out[0] = small_own[...]
    small_out[1] = small_other[...]
    group = stage.shape[1]
    steps = masters.shape[0] // group

    def store(step):
        slot = lax.rem(step, 2)
        return pltpu.make_async_copy(
            stage.at[slot], block_grad_out.at[pl.ds(step * group, group)], stage_sems.at[slot]
        )

    @pl.loop(0, steps)
    def _(step):
        @pl.when(step >= 2)
        def _():
            store(step - 2).wait()

        stage[lax.rem(step, 2)] = reduced[pl.ds(step * group, group)].astype(f32)
        store(step).start()

    for step in range(max(steps - 2, 0), steps):
        store(step).wait()
    for copy in copies:
        copy.wait()


def run_write_results(*arrays):
    arrays = [pltpu.with_memory_space_constraint(array, pltpu.VMEM) for array in arrays]
    blocks, rows, small = arrays[1].shape, arrays[4].shape, arrays[-1].shape
    group = largest_group(blocks[0])
    shape = jax.ShapeDtypeStruct
    return pl.pallas_call(
        write_results,
        out_shape=[shape(blocks, f32)] * 4 + [shape(rows, f32), shape(rows, bf16), shape((2,) + small, f32)],
        in_specs=[VMEM_SPEC] * len(arrays),
        out_specs=[ANY_SPEC] * 6 + [VMEM_SPEC],
        scratch_shapes=[
            pltpu.VMEM((2, group) + blocks[1:], f32),
            pltpu.SemaphoreType.DMA((2,)),
            pltpu.SemaphoreType.DMA((5,)),
        ],
        compiler_params=params(WRITE_VMEM),
        name="write_results",
    )(*arrays)


def rope_tables(segment_row):
    token_index = jnp.arange(segment_row.shape[0], dtype=jnp.int32)
    changed = jnp.concatenate([jnp.ones((1,), dtype=bool), segment_row[1:] != segment_row[:-1]])
    begins = lax.cummax(jnp.where(changed, token_index, jnp.zeros_like(token_index)), axis=0)
    places = (token_index - begins).astype(f32)
    frequency = rope_base ** (-(jnp.arange(HEAD_DIM // 2, dtype=f32) * 2.0) / HEAD_DIM)
    angles = places[:, None] * frequency[None, :]
    cosine = jnp.concatenate([jnp.cos(angles), jnp.cos(angles)], axis=-1)
    sine_signed = jnp.concatenate([-jnp.sin(angles), jnp.sin(angles)], axis=-1)
    return (cosine, sine_signed)


def rms_parts(values):
    inverse = rms_inverse(values)
    return (inverse, values * inverse)


def norm_back(grad_scaled, normed, inverse):
    return inverse * (grad_scaled - normed * jnp.mean(grad_scaled * normed, axis=-1, keepdims=True))


def adam_small(param_now, gradient, first_now, second_now, rate_here):
    first_new = beta_first * first_now + (1.0 - beta_first) * gradient
    second_new = beta_second * second_now + (1.0 - beta_second) * gradient * gradient
    param_new = param_now - rate_here * (first_new / first_fix) / (
        jnp.sqrt(second_new / second_fix) + adam_eps
    )
    return (param_new, first_new, second_new)


def swap_halves(values):
    return lax.ppermute(values, "narrow", [(0, 1), (1, 0)])


def in_vmem(array):
    return pltpu.with_memory_space_constraint(array, pltpu.VMEM)


def body(
    tokens,
    cotangent,
    segments,
    owner_list,
    masters,
    first_moment,
    second_moment,
    left_basis,
    right_basis,
    gains,
    gain_first,
    gain_second,
    biases,
    bias_first,
    bias_second,
):
    half = lax.axis_index("narrow")
    wide_index = lax.axis_index("wide")
    wide_count = lax.axis_size("wide")
    tokens_here = tokens.shape[0]
    slots_here = masters.shape[0]
    slots_half = owner_list.shape[0]
    gains_here = gains.shape[0]
    biases_here = biases.shape[1]

    def join_halves(own, other, axis=0):
        return jnp.where(
            half == 0, jnp.concatenate([own, other], axis=axis), jnp.concatenate([other, own], axis=axis)
        )

    masters_low, gains, biases = lax.optimization_barrier((masters.astype(bf16), gains, biases))
    weights = lax.all_gather(masters_low, "wide", axis=0, tiled=True)
    gain_full = lax.all_gather(gains, ("wide", "narrow"), axis=0, tiled=True).reshape(2, D)
    bias_full = lax.all_gather(biases.reshape(-1).astype(bf16), "wide", axis=0, tiled=True)
    bias_full = bias_full.astype(f32).reshape(1, QKV_WIDTH)
    pair_gains = 2 * gains_here

    position = jnp.arange(slots_half, dtype=jnp.int32)
    empty = owner_list == BLOCK_TOTAL
    number = jnp.where(empty, BLOCK_TOTAL - 1 + jnp.cumsum(empty.astype(jnp.int32)), owner_list)
    weight_rows = jnp.zeros((slots_half,), jnp.int32).at[number].set(position, unique_indices=True)
    rows = weight_rows + weight_rows // slots_here
    half_index = half.astype(jnp.int32).reshape(1)

    segment_row = lax.dynamic_index_in_dim(segments, wide_index, 0, keepdims=False)
    cosine, sine = rope_tables(segment_row)
    token_index = jnp.arange(segment_row.shape[0], dtype=jnp.int32)
    allowed_turned = (
        (segment_row[None, :] == segment_row[:, None]) & (token_index[None, :] >= token_index[:, None])
    ).astype(f32)
    tokens_row = join_halves(tokens, swap_halves(tokens))
    cotangent_row = join_halves(cotangent, swap_halves(cotangent))
    weights, tokens_row, cotangent_row, rows, gain_full, gain_one, gain_two = lax.optimization_barrier(
        (weights, tokens_row, cotangent_row, rows, gain_full, gain_full[0:1], gain_full[1:2])
    )

    low_part, high_part, normed_one_turned, qkv, mixed_turned, log_total = run_attention_forward(
        weight_rows, tokens_row, gain_one, bias_full, cosine, sine, allowed_turned, weights
    )
    low_other = swap_halves(low_part)
    active_grad, down_tiles = run_active_grads(weight_rows, cotangent_row, weights)
    high_sent, low_other = lax.optimization_barrier((high_part, low_other))
    high_other = swap_halves(high_sent)
    grad_low, resid_low, turned_low, *hidden_low = run_hidden_grads(
        0, weight_rows, tokens_row, low_part, low_other, gain_two, active_grad, weights
    )
    grad_low_other = swap_halves(grad_low)
    grad_high, resid_high, turned_high, *hidden_high = run_hidden_grads(
        tokens_here, weight_rows, tokens_row, high_part, high_other, gain_two, active_grad, weights
    )
    grad_high_other = swap_halves(grad_high)
    pair_low, active_low, active_turned_low = hidden_low
    pair_high, active_high, active_turned_high = hidden_high
    grads = run_hidden_weight_grads(
        rows, cotangent_row, [(turned_low, pair_low, active_turned_low), (turned_high, pair_high, active_turned_high)],
        wide_count * (slots_here + 1),
    )
    grad_resid, grad_one_own, grad_one_sent, grads = run_attention_backward(
        weight_rows, rows, half_index, tokens_row, (resid_low, grad_low, grad_low_other),
        (resid_high, grad_high, grad_high_other), cotangent_row, gain_full, cosine, sine, allowed_turned,
        normed_one_turned, qkv, mixed_turned, log_total, weights, grads, wide_count,
    )
    blocks = [masters, first_moment, second_moment, left_basis, right_basis]
    if wide_count == 16:
        token_arrays = [
            grad_resid, grad_one_own, grad_one_sent, tokens, gain_one, resid_low, resid_high, active_low,
            active_high, down_tiles,
        ]
        block_grad, new_masters, new_first, new_second, input_grad, output, small_sums = run_write_results(
            *run_sum_for_owners(grads, wide_count, blocks, token_arrays)
        )
        gain_parts = small_sums[0, :2] + small_sums[1, :2]
        bias_row = small_sums[0, 2]
    else:
        reduced = lax.psum_scatter(grads, "wide", scatter_dimension=0, tiled=True)
        block_grad, new_masters, new_first, new_second, small_sums = run_soap(reduced, *blocks)
        gain_parts = small_sums[:2] + swap_halves(small_sums[:2])
        bias_row = small_sums[2]
        branch_low, branch_high = [
            jnp.einsum("tik,tkd->id", active, down_tiles, preferred_element_type=f32)
            for active in (active_low, active_high)
        ]
        resid_own = jnp.where(half == 0, resid_low, resid_high)
        branch_own = jnp.where(half == 0, branch_low, branch_high)
        branch_sent = jnp.where(half == 0, branch_high, branch_low).astype(bf16)
        output = (resid_own + branch_own + swap_halves(branch_sent).astype(f32)).astype(bf16)
        inverse_one, normed_one = rms_parts(tokens.astype(f32))
        grad_one = grad_one_own.astype(f32) + swap_halves(grad_one_sent).astype(f32)
        input_grad = grad_resid + norm_back(grad_one * gain_full[0:1], normed_one, inverse_one)

    gain_first_index = wide_index * pair_gains
    gain_offset = gain_first_index - jnp.minimum(gain_first_index // BLK, 2 * D // BLK - 2) * BLK
    bias_offset = lax.rem(wide_index * biases_here, BLK)
    gain_grad = lax.dynamic_slice_in_dim(gain_parts.reshape(-1), gain_offset + half * gains_here, gains_here, 0)
    bias_grad = lax.dynamic_slice_in_dim(bias_row, bias_offset, biases_here, 0).reshape(biases.shape)
    new_gains, new_gain_first, new_gain_second = adam_small(gains, gain_grad, gain_first, gain_second, rate_gains)
    new_biases, new_bias_first, new_bias_second = adam_small(biases, bias_grad, bias_first, bias_second, rate_small)

    return (
        output,
        input_grad,
        block_grad,
        new_masters,
        new_first,
        new_second,
        gain_grad,
        new_gains,
        new_gain_first,
        new_gain_second,
        bias_grad,
        new_biases,
        new_bias_first,
        new_bias_second,
    )


def solution(mesh):
    tokens_spec = P(("wide", "narrow"), None)
    blocks_spec = P(("wide", "narrow"), None, None)
    gains_spec = P(("wide", "narrow"))
    bias_spec = P("narrow", "wide")
    in_specs = (
        (tokens_spec, tokens_spec, P(), P()) + (blocks_spec,) * 5 + (gains_spec,) * 3 + (bias_spec,) * 3
    )
    out_specs = (tokens_spec, tokens_spec) + (blocks_spec,) * 4 + (gains_spec,) * 4 + (bias_spec,) * 4
    return jax.shard_map(body, mesh=mesh, in_specs=in_specs, out_specs=out_specs, check_vma=False)
```

```python
import functools

import jax
import jax.numpy as jnp
from jax import lax
from jax.experimental import pallas as pl
from jax.experimental.pallas import tpu as pltpu
from jax.sharding import PartitionSpec as P

D = 1536
FF = 8960
HEADS = 12
KV_HEADS = 2
HEAD_DIM = 128
BLK = 128
STEP_COUNT = 5


beta_first = 0.95
beta_second = 0.95
adam_eps = 1e-08
rate_blocks = 0.03
rate_small = 0.4
rate_gains = 0.6
norm_eps = 1e-06
rope_base = 10000.0
masked_score = -1e30
first_fix = 1.0 - beta_first**STEP_COUNT
second_fix = 1.0 - beta_second**STEP_COUNT
scaling = HEAD_DIM ** (-0.5)

bf16 = jnp.bfloat16
f32 = jnp.float32

NARROW = 2
ROW_BLOCKS = D // BLK
QUERY_COLS = HEADS * HEAD_DIM // NARROW // BLK
PAIR_COLS = KV_HEADS * HEAD_DIM // NARROW // BLK
HIDDEN_COLS = FF // NARROW // BLK
QKV_COLS = QUERY_COLS + 2 * PAIR_COLS
QUERY_WIDTH = QUERY_COLS * BLK
QKV_WIDTH = QKV_COLS * BLK
KEY_BASE = ROW_BLOCKS * QUERY_COLS
VALUE_BASE = KEY_BASE + ROW_BLOCKS * PAIR_COLS
OUT_BASE = VALUE_BASE + ROW_BLOCKS * PAIR_COLS
GATE_BASE = OUT_BASE + QUERY_COLS * ROW_BLOCKS
UP_BASE = GATE_BASE + ROW_BLOCKS * HIDDEN_COLS
DOWN_BASE = UP_BASE + ROW_BLOCKS * HIDDEN_COLS
BLOCK_TOTAL = DOWN_BASE + HIDDEN_COLS * ROW_BLOCKS

TILE_BLOCKS = 6
TILES = -(-HIDDEN_COLS // TILE_BLOCKS)
LAST_BLOCKS = HIDDEN_COLS - (TILES - 1) * TILE_BLOCKS
TILE = TILE_BLOCKS * BLK
COLS = 256
ROWS = 64
SMALL_ROWS = 16
VMEM_LIMIT = 60 * 2**20
SUM_VMEM = 39 * 2**20
WRITE_VMEM = 6 * 2**20

EARLY = 4
DEPTH = 3
CROSS_LAG = 2
HOP_LAG = 1

VMEM_SPEC = pl.BlockSpec(memory_space=pltpu.VMEM)
SMEM_SPEC = pl.BlockSpec(memory_space=pltpu.SMEM)
ANY_SPEC = pl.BlockSpec(memory_space=pl.ANY)


def spans(total, step):
    return [(begin, min(step, total - begin)) for begin in range(0, total, step)]


def dot_nn(left, right):
    return jnp.dot(left, right, preferred_element_type=f32)


def dot_nt(left, right):
    return lax.dot_general(left, right, (((1,), (1,)), ((), ())), preferred_element_type=f32)


def block_ref(ref, row_block, col_block):
    return ref.at[pl.ds(row_block * BLK, BLK), pl.ds(col_block * BLK, BLK)]


def fetch_piece(rows_ref, weights, target, base, pitch, row_blocks, col_blocks, first_col, sem):
    @pl.loop(0, row_blocks)
    def _(i):
        for j in range(col_blocks):
            pltpu.make_async_copy(
                weights.at[rows_ref[base + i * pitch + j]],
                block_ref(target, i, first_col + j),
                sem,
            ).start()


def store_piece(rows_ref, source, grads, base, pitch, row_blocks, col_blocks, first_col, sem):
    @pl.loop(0, row_blocks)
    def _(i):
        for j in range(col_blocks):
            pltpu.make_async_copy(
                block_ref(source, i, first_col + j),
                grads.at[rows_ref[base + i * pitch + j]],
                sem,
            ).start()


def wait_bytes(ref, sem):
    pltpu.make_async_copy(ref, ref, sem).wait()


def copies_between(sources, targets, sems):
    return [
        pltpu.make_async_copy(source, target, sems.at[index])
        for index, (source, target) in enumerate(zip(sources, targets, strict=True))
    ]


def wait_all(copies):
    for copy in copies:
        copy.wait()


def fetch_qkv(rows_ref, weights, w_qkv, sem):
    fetch_piece(rows_ref, weights, w_qkv, 0, QUERY_COLS, ROW_BLOCKS, QUERY_COLS, 0, sem)
    fetch_piece(rows_ref, weights, w_qkv, KEY_BASE, PAIR_COLS, ROW_BLOCKS, PAIR_COLS, QUERY_COLS, sem)
    fetch_piece(
        rows_ref, weights, w_qkv, VALUE_BASE, PAIR_COLS, ROW_BLOCKS, PAIR_COLS, QUERY_COLS + PAIR_COLS, sem
    )


def fetch_out(rows_ref, weights, w_out, sem):
    fetch_piece(rows_ref, weights, w_out, OUT_BASE, ROW_BLOCKS, QUERY_COLS, ROW_BLOCKS, 0, sem)


def rms_inverse(values):
    return lax.rsqrt(jnp.mean(values * values, axis=-1, keepdims=True) + norm_eps)


def row_chunks(total, step, run):
    @pl.loop(0, total // step)
    def _(chunk):
        run(pl.ds(pl.multiple_of(chunk * step, step), step))


def small_places(owner, wide_count):
    gain_row = min(owner * (2 * D // wide_count) // BLK, 2 * D // BLK - 2)
    return (gain_row, owner * (QKV_WIDTH // wide_count) // BLK)


def scores_turned(keys, queries, allowed):
    return jnp.where(allowed, dot_nt(keys, queries) * scaling, masked_score)


def attention_forward(
    rows_ref,
    gain_ref,
    bias_ref,
    x_hbm,
    cos_hbm,
    sin_hbm,
    allowed_hbm,
    weights,
    part_low_ref,
    part_high_ref,
    log_ref,
    normed_turned_out,
    qkv_out,
    mixed_turned_out,
    x_ref,
    cos_ref,
    sin_ref,
    allowed_ref,
    normed_turned,
    qkv,
    mixed_turned,
    w_qkv,
    w_out,
    normed,
    mixed,
    sems,
    load_sems,
    store_sems,
):
    loads = copies_between(
        (x_hbm, cos_hbm, sin_hbm, allowed_hbm), (x_ref, cos_ref, sin_ref, allowed_ref), load_sems
    )
    stores = copies_between(
        (normed_turned, qkv, mixed_turned), (normed_turned_out, qkv_out, mixed_turned_out), store_sems
    )
    start_all(loads)
    fetch_qkv(rows_ref, weights, w_qkv, sems.at[0])
    fetch_out(rows_ref, weights, w_out, sems.at[1])
    length = x_ref.shape[0]
    part = length // NARROW

    def norm_rows(rows):
        values = x_ref[rows, :].astype(f32)
        normed[rows, :] = (values * rms_inverse(values) * gain_ref[...]).astype(bf16)

    loads[0].wait()
    row_chunks(length, ROWS, norm_rows)
    wait_all(loads[1:])
    wait_bytes(w_qkv, sems.at[0])
    for begin, size in spans(QKV_WIDTH, COLS):
        products = dot_nn(normed[...], w_qkv[:, pl.ds(begin, size)]) + bias_ref[:, pl.ds(begin, size)]
        for offset, width in spans(size, HEAD_DIM):
            head = products[:, offset : offset + width]
            if begin + offset < QUERY_WIDTH + PAIR_COLS * BLK:
                head = head * cos_ref[...] + pltpu.roll(head, HEAD_DIM // 2, 1) * sin_ref[...]
            qkv[:, pl.ds(begin + offset, width)] = head.astype(bf16)
    for begin, size in spans(D, COLS):
        normed_turned[pl.ds(begin, size), :] = normed[:, pl.ds(begin, size)].T
    start_all(stores[:2])
    values_turned = qkv[:, pl.ds(QUERY_WIDTH + HEAD_DIM, HEAD_DIM)].T
    for head in range(QUERY_COLS):
        columns = pl.ds(head * HEAD_DIM, HEAD_DIM)
        for first in range(0, length, part):
            tokens, seen = pl.ds(first, part), first + part
            scores = scores_turned(
                qkv[:seen, pl.ds(QUERY_WIDTH, HEAD_DIM)], qkv[tokens, columns], allowed_ref[:seen, tokens] > 0
            )
            peak = jnp.max(scores, axis=0, keepdims=True)
            expo = jnp.exp(scores - peak)
            total = jnp.sum(expo, axis=0, keepdims=True)
            log_ref[pl.ds(head, 1), tokens] = peak + jnp.log(total)
            probs = (expo / total).astype(bf16)
            mixed_head = dot_nn(values_turned[:, :seen], probs).astype(bf16)
            mixed_turned[columns, tokens] = mixed_head
            mixed[tokens, columns] = mixed_head.T
    stores[2].start()
    wait_bytes(w_out, sems.at[1])
    for part_ref, first in ((part_low_ref, 0), (part_high_ref, part)):
        for begin, size in spans(D, COLS):
            part_ref[:, pl.ds(begin, size)] = dot_nn(
                mixed[pl.ds(first, part), :], w_out[:, pl.ds(begin, size)]
            ).astype(bf16)
    wait_all(stores)


def pair_copies(rows_ref, blocks_hbm, pair, sem, column, place, outward=False):
    return [
        block_copy(blocks_hbm.at[rows_ref[base + i * HIDDEN_COLS + column]], block_ref(pair, i, which), sem, outward)
        for i in range(ROW_BLOCKS)
        for base, which in ((GATE_BASE, 2 * place), (UP_BASE, 2 * place + 1))
    ]


def down_copies(rows_ref, blocks_hbm, down, sem, column, place, outward=False):
    return [
        block_copy(blocks_hbm.at[rows_ref[DOWN_BASE + column * ROW_BLOCKS + i]], block_ref(down, place, i), sem, outward)
        for i in range(ROW_BLOCKS)
    ]


def block_copy(in_hbm, in_vmem, sem, outward):
    return pltpu.make_async_copy(*((in_vmem, in_hbm) if outward else (in_hbm, in_vmem)), sem)


def start_all(copies):
    for copy in copies:
        copy.start()


def half_rows(half_ref, length):
    begin = pl.multiple_of(half_ref[0] * length, length)
    return (pl.ds(begin, length), pl.ds(pl.multiple_of(length - begin, length), length))


def hidden_column(tile, place):
    return jnp.minimum(tile * TILE_BLOCKS + place, HIDDEN_COLS - 1)


def hidden_tiles(run):
    @pl.loop(0, TILES - 1)
    def _(tile):
        run(tile, lax.rem(tile, 2), TILE_BLOCKS, True)

    run(TILES - 1, (TILES - 1) % 2, LAST_BLOCKS, False)


def active_grads(rows_ref, cot_ref, weights, out, down_out, w_down, stage, load_sems, store_sems, down_sems):
    ring = w_down.shape[0]

    def fetch(tile):
        slot = lax.rem(tile, ring)
        for place in range(TILE_BLOCKS):
            start_all(
                down_copies(rows_ref, weights, w_down.at[slot], load_sems.at[slot], hidden_column(tile, place), place)
            )

    def store(tile):
        return pltpu.make_async_copy(stage.at[lax.rem(tile, 2)], out.at[tile], store_sems.at[lax.rem(tile, 2)])

    def store_down(tile):
        slot = lax.rem(tile, ring)
        return pltpu.make_async_copy(w_down.at[slot], down_out.at[tile], down_sems.at[slot])

    fetch(0)

    def run(tile, slot, blocks, more):
        here = lax.rem(tile, ring)

        @pl.when(tile >= ring - 1)
        def _():
            store_down(tile - ring + 1).wait()

        if more:
            fetch(tile + 1)
        wait_bytes(w_down.at[here], load_sems.at[here])
        if blocks < TILE_BLOCKS:
            w_down[here, pl.ds(blocks * BLK, (TILE_BLOCKS - blocks) * BLK), :] = jnp.zeros(
                ((TILE_BLOCKS - blocks) * BLK, D), bf16
            )
        store_down(tile).start()

        @pl.when(tile >= 2)
        def _():
            store(tile - 2).wait()

        for begin, size in spans(blocks * BLK, COLS):
            stage[slot, :, pl.ds(begin, size)] = dot_nt(cot_ref[...], w_down[here, pl.ds(begin, size), :])
        store(tile).start()

    hidden_tiles(run)
    for tile in range(max(TILES - 2, 0), TILES):
        store(tile).wait()
    for tile in range(max(TILES - ring + 1, 0), TILES):
        store_down(tile).wait()


def hidden_grads(
    first_row,
    rows_ref,
    gain_ref,
    other_ref,
    x_hbm,
    own_hbm,
    active_grad,
    weights,
    grad_ref,
    resid_out,
    normed_turned_out,
    pair_grads,
    active,
    active_turned,
    x_ref,
    own_ref,
    resid_ref,
    normed_turned_ref,
    w_pair,
    grad_active,
    straight,
    turned,
    grads,
    normed,
    grad_sum,
    load_sems,
    store_sems,
    token_sems,
):
    length = own_ref.shape[0]
    token_loads = copies_between(
        (x_hbm.at[pl.ds(first_row, length)], own_hbm), (x_ref, own_ref), token_sems
    )
    store_resid = pltpu.make_async_copy(resid_ref, resid_out, token_sems.at[3])
    store_turned = pltpu.make_async_copy(normed_turned_ref, normed_turned_out, token_sems.at[4])
    start_all(token_loads)

    def fetch(tile, slot, place):
        start_all(
            pair_copies(rows_ref, weights, w_pair.at[slot], load_sems.at[slot, 0], hidden_column(tile, place), place)
        )

    def load_grad(tile, slot):
        return pltpu.make_async_copy(active_grad.at[tile, pl.ds(first_row, length)], grad_active.at[slot], load_sems.at[slot, 1])

    def stores(tile, slot):
        return (
            pltpu.make_async_copy(turned.at[slot], active_turned.at[tile], store_sems.at[slot, 0]),
            pltpu.make_async_copy(grads.at[slot], pair_grads.at[tile], store_sems.at[slot, 1]),
            pltpu.make_async_copy(straight.at[slot], active.at[tile], store_sems.at[slot, 2]),
        )

    for place in range(TILE_BLOCKS):
        fetch(0, 0, place)
    load_grad(0, 0).start()

    def norm_rows(rows):
        values = x_ref[rows, :].astype(f32) + own_ref[rows, :].astype(f32) + other_ref[rows, :].astype(f32)
        resid_ref[rows, :] = values
        normed[rows, :] = (values * rms_inverse(values) * gain_ref[...]).astype(bf16)

    wait_all(token_loads)
    row_chunks(length, ROWS, norm_rows)
    store_resid.start()
    grad_sum[...] = jnp.zeros_like(grad_sum)

    def run(tile, slot, blocks, more):
        wait_bytes(w_pair.at[slot], load_sems.at[slot, 0])
        load_grad(tile, slot).wait()
        if more:
            load_grad(tile + 1, 1 - slot).start()

        @pl.when(tile >= 2)
        def _():
            for copy in stores(tile - 2, slot):
                copy.wait()

        for place in range(blocks):
            columns = pl.ds(place * BLK, BLK)
            pair = dot_nn(normed[...], w_pair[slot, :, pl.ds(2 * place * BLK, 2 * BLK)])
            gate = pair[:, :BLK]
            upper = pair[:, BLK:]
            grad = grad_active[slot, :, columns]
            sigmoid = jax.nn.sigmoid(gate)
            silu = gate * sigmoid
            active_here = (silu * upper).astype(bf16)
            straight[slot, :, columns] = active_here
            turned[slot, columns, :] = active_here.T
            grads[slot, :, pl.ds(2 * place * BLK, BLK)] = (
                grad * upper * sigmoid * (1.0 + gate * (1.0 - sigmoid))
            ).astype(bf16)
            grads[slot, :, pl.ds((2 * place + 1) * BLK, BLK)] = (grad * silu).astype(bf16)
            if more:
                fetch(tile + 1, 1 - slot, place)
        if more:
            for place in range(blocks, TILE_BLOCKS):
                fetch(tile + 1, 1 - slot, place)
        turn = pl.ds(pl.multiple_of(tile * COLS, COLS), COLS)
        normed_turned_ref[turn, :] = normed[:, turn].T
        width = 2 * blocks * BLK
        for begin, size in spans(D, COLS):
            columns = pl.ds(begin, size)
            grad_sum[:, columns] += dot_nt(grads[slot, :, :width], w_pair[slot, columns, :width])
        start_all(stores(tile, slot))

    hidden_tiles(run)
    store_turned.start()
    grad_ref[...] = grad_sum[...].astype(bf16)
    for tile in range(max(TILES - 2, 0), TILES):
        wait_all(stores(tile, tile % 2))
    store_resid.wait()
    store_turned.wait()


def hidden_weight_grads(rows_ref, cot_ref, *refs):
    parts, grads, scratch = refs[: 3 * NARROW], refs[3 * NARROW], refs[3 * NARROW + 1 :]
    normed_turned, pair, turned, pair_stage, down_stage, load_sems, store_sems, sems = scratch
    length = cot_ref.shape[0] // NARROW

    def loads(tile, slot):
        copies = []
        for part in range(NARROW):
            pair_grads, active_turned = parts[part * 3 + 1 : part * 3 + 3]
            tokens = pl.ds(part * length, length)
            copies += [
                pltpu.make_async_copy(pair_grads.at[tile], pair.at[slot, tokens], load_sems.at[slot, part * 2]),
                pltpu.make_async_copy(
                    active_turned.at[tile], turned.at[slot, :, tokens], load_sems.at[slot, part * 2 + 1]
                ),
            ]
        return copies

    def drain(slot, blocks):
        wait_bytes(pair_stage.at[slot, :, pl.ds(0, 2 * blocks * BLK)], store_sems.at[slot, 0])
        wait_bytes(down_stage.at[slot, pl.ds(0, blocks * BLK)], store_sems.at[slot, 1])

    turned_loads = [
        pltpu.make_async_copy(parts[part * 3], normed_turned.at[:, pl.ds(part * length, length)], sems.at[part])
        for part in range(NARROW)
    ]
    start_all(loads(0, 0) + turned_loads)
    wait_all(turned_loads)

    def run(tile, slot, blocks, more):
        wait_all(loads(tile, slot))
        if more:
            start_all(loads(tile + 1, 1 - slot))

        @pl.when(tile >= 2)
        def _():
            drain(slot, TILE_BLOCKS)

        width = blocks * BLK
        down = turned[slot, pl.ds(0, width), :]
        for begin, size in spans(D, COLS):
            columns = pl.ds(begin, size)
            down_stage[slot, pl.ds(0, width), columns] = dot_nn(down, cot_ref[:, columns]).astype(bf16)
        for place in range(blocks):
            column = tile * TILE_BLOCKS + place
            start_all(
                down_copies(rows_ref, grads, down_stage.at[slot], store_sems.at[slot, 1], column, place, outward=True)
            )
            columns = pl.ds(2 * place * BLK, 2 * BLK)
            for begin, size in spans(D, 512):
                pair_stage[slot, pl.ds(begin, size), columns] = dot_nn(
                    normed_turned[pl.ds(begin, size), :], pair[slot, :, columns]
                ).astype(bf16)
            start_all(
                pair_copies(rows_ref, grads, pair_stage.at[slot], store_sems.at[slot, 0], column, place, outward=True)
            )

    hidden_tiles(run)
    if TILES > 1:
        drain((TILES - 2) % 2, TILE_BLOCKS)
    drain((TILES - 1) % 2, LAST_BLOCKS)


def attention_backward(
    weight_rows_ref,
    rows_ref,
    half_ref,
    gain_ref,
    log_ref,
    other_low_ref,
    other_high_ref,
    resid_low_hbm,
    own_low_hbm,
    resid_high_hbm,
    own_high_hbm,
    cot_hbm,
    qkv_hbm,
    cos_hbm,
    sin_hbm,
    allowed_hbm,
    mixed_turned_hbm,
    normed_turned_hbm,
    x_hbm,
    weights,
    grads_in,
    grad_resid_ref,
    grad_own_ref,
    grad_other_ref,
    grads,
    resid_low_ref,
    own_low_ref,
    resid_high_ref,
    own_high_ref,
    cot_ref,
    qkv_ref,
    cos_ref,
    sin_ref,
    allowed_ref,
    mixed_turned_ref,
    normed_turned_ref,
    x_ref,
    w_qkv,
    w_out,
    grad_resid,
    grad_attention,
    grad_mixed,
    grad_qkv,
    grad_sum,
    grad_keys,
    grad_values,
    gain_part,
    gain_two_part,
    bias_part,
    qkv_stage,
    out_stage,
    small_stage,
    blank,
    load_sems,
    store_sems,
    token_sems,
):
    del grads_in
    loads = copies_between(
        (
            cot_hbm, resid_low_hbm, own_low_hbm, resid_high_hbm, own_high_hbm, qkv_hbm, cos_hbm, sin_hbm, allowed_hbm, mixed_turned_hbm, normed_turned_hbm, x_hbm,
        ),
        (
            cot_ref, resid_low_ref, own_low_ref, resid_high_ref, own_high_ref, qkv_ref, cos_ref, sin_ref, allowed_ref, mixed_turned_ref, normed_turned_ref, x_ref,
        ),
        token_sems,
    )
    start_all(loads[:5])
    wide_count = small_stage.shape[0]
    owner_rows = grads.shape[0] // wide_count
    small_stage[...] = jnp.zeros_like(small_stage)
    fetch_out(weight_rows_ref, weights, w_out, load_sems.at[1])
    start_all(loads[5:])
    fetch_qkv(weight_rows_ref, weights, w_qkv, load_sems.at[0])
    length = x_ref.shape[0]
    empty_count = rows_ref.shape[0] - BLOCK_TOTAL
    blank[...] = jnp.zeros_like(blank)
    for index in range(empty_count):
        pltpu.make_async_copy(blank.at[index], grads.at[rows_ref[BLOCK_TOTAL + index]], store_sems.at[2]).start()

    gain_two_part[...] = jnp.zeros_like(gain_two_part)
    part = length // NARROW
    own_rows, other_rows = half_rows(half_ref, part)
    for first, resid_ref, own_ref, other_ref, needed in (
        (0, resid_low_ref, own_low_ref, other_low_ref, loads[:3]),
        (part, resid_high_ref, own_high_ref, other_high_ref, loads[3:5]),
    ):
        wait_all(needed)

        def resid_rows(rows, first=first, resid_ref=resid_ref, own_ref=own_ref, other_ref=other_ref):
            values = resid_ref[rows, :]
            inverse = rms_inverse(values)
            normed = values * inverse
            grad_normed = own_ref[rows, :].astype(f32) + other_ref[rows, :].astype(f32)
            gain_two_part[...] += jnp.sum(grad_normed * normed, axis=0, keepdims=True) / NARROW
            scaled = grad_normed * gain_ref[1:2, :]
            place = pl.ds(rows.start + first, rows.size)
            total = cot_ref[place, :].astype(f32) + inverse * (
                scaled - normed * jnp.mean(scaled * normed, axis=-1, keepdims=True)
            )
            grad_resid[place, :] = total
            grad_attention[place, :] = total.astype(bf16)

        row_chunks(part, ROWS, resid_rows)
    grad_resid_ref[...] = grad_resid[own_rows, :]
    wait_bytes(w_out, load_sems.at[1])
    for begin, size in spans(QUERY_WIDTH, COLS):
        grad_mixed[:, pl.ds(begin, size)] = dot_nt(grad_attention[...], w_out[pl.ds(begin, size), :]).astype(bf16)
    wait_all(loads[5:9])
    keys_turned = qkv_ref[:, pl.ds(QUERY_WIDTH, HEAD_DIM)].T

    def rope_back(vector):
        return vector * cos_ref[...] - pltpu.roll(vector, HEAD_DIM // 2, 1) * sin_ref[...]

    grad_keys[...] = jnp.zeros_like(grad_keys)
    grad_values[...] = jnp.zeros_like(grad_values)
    for head in range(QUERY_COLS):
        columns = pl.ds(head * HEAD_DIM, HEAD_DIM)
        grad_queries = []
        for first in range(0, length, part):
            tokens, seen = pl.ds(first, part), first + part
            queries = qkv_ref[tokens, columns]
            grad_mixed_here = grad_mixed[tokens, columns]
            scores = scores_turned(
                qkv_ref[:seen, pl.ds(QUERY_WIDTH, HEAD_DIM)], queries, allowed_ref[:seen, tokens] > 0
            )
            probs = jnp.exp(scores - log_ref[pl.ds(head, 1), tokens])
            grad_values[:seen, :] += dot_nn(probs.astype(bf16), grad_mixed_here)
            grad_probs = dot_nt(qkv_ref[:seen, pl.ds(QUERY_WIDTH + HEAD_DIM, HEAD_DIM)], grad_mixed_here)
            row_dot = jnp.sum(probs * grad_probs, axis=0, keepdims=True)
            grad_scores = (probs * (grad_probs - row_dot)).astype(bf16)
            grad_keys[:seen, :] += dot_nn(grad_scores, queries)
            grad_queries.append(dot_nn(keys_turned[:, :seen], grad_scores).T * scaling)
        grad_qkv[:, columns] = rope_back(jnp.concatenate(grad_queries, axis=0)).astype(bf16)
    grad_qkv[:, pl.ds(QUERY_WIDTH, HEAD_DIM)] = rope_back(grad_keys[...] * scaling).astype(bf16)
    grad_qkv[:, pl.ds(QUERY_WIDTH + HEAD_DIM, HEAD_DIM)] = grad_values[...].astype(bf16)
    wait_all(loads[9:])

    for begin, size in spans(D, COLS):
        out_stage[:, pl.ds(begin, size)] = dot_nn(
            mixed_turned_ref[...], grad_attention[:, pl.ds(begin, size)]
        ).astype(bf16)
    store_piece(rows_ref, out_stage, grads, OUT_BASE, ROW_BLOCKS, QUERY_COLS, ROW_BLOCKS, 0, store_sems.at[1])
    for begin, size in spans(QKV_WIDTH, COLS):
        qkv_stage[:, pl.ds(begin, size)] = dot_nn(
            normed_turned_ref[...], grad_qkv[:, pl.ds(begin, size)]
        ).astype(bf16)
    store_piece(rows_ref, qkv_stage, grads, 0, QUERY_COLS, ROW_BLOCKS, QUERY_COLS, 0, store_sems.at[0])
    store_piece(rows_ref, qkv_stage, grads, KEY_BASE, PAIR_COLS, ROW_BLOCKS, PAIR_COLS, QUERY_COLS, store_sems.at[0])
    store_piece(
        rows_ref, qkv_stage, grads, VALUE_BASE, PAIR_COLS, ROW_BLOCKS, PAIR_COLS, QUERY_COLS + PAIR_COLS, store_sems.at[0]
    )
    wait_bytes(w_qkv, load_sems.at[0])
    for begin, size in spans(D, COLS):
        grad_sum[:, pl.ds(begin, size)] = dot_nt(grad_qkv[...], w_qkv[pl.ds(begin, size), :])
    grad_own_ref[...] = grad_sum[own_rows, :].astype(bf16)
    grad_other_ref[...] = grad_sum[other_rows, :].astype(bf16)
    gain_part[...] = jnp.zeros_like(gain_part)
    bias_part[...] = dot_nn(jnp.ones((SMALL_ROWS, length), bf16), grad_qkv[...])[:1]

    def gain_rows(rows):
        tokens = x_ref[rows, :].astype(f32)
        gain_part[...] += jnp.sum(grad_sum[rows, :] * tokens * rms_inverse(tokens), axis=0, keepdims=True)

    row_chunks(length, ROWS, gain_rows)
    for owner in range(wide_count):
        gain_row, bias_row = small_places(owner, wide_count)
        small_rows = []
        for row in (gain_row, gain_row + 1):
            columns = pl.ds(row % (D // BLK) * BLK, BLK)
            if row < D // BLK:
                small_rows.append(gain_part[:, columns])
            else:
                small_rows.append(gain_two_part[:, columns])
        small_rows.append(bias_part[:, pl.ds(bias_row * BLK, BLK)])
        small_rows.append(jnp.zeros((SMALL_ROWS - len(small_rows), BLK), f32))
        small_stage[owner, pl.ds(0, SMALL_ROWS), :] = jnp.concatenate(small_rows, axis=0).astype(bf16)
        pltpu.make_async_copy(
            small_stage.at[owner], grads.at[owner * owner_rows + owner_rows - 1], store_sems.at[3]
        ).start()
    wait_bytes(small_stage, store_sems.at[3])
    wait_bytes(qkv_stage, store_sems.at[0])
    wait_bytes(out_stage, store_sems.at[1])
    if empty_count > 0:
        wait_bytes(blank.at[pl.ds(0, empty_count)], store_sems.at[2])


def soap_update(
    grad_in,
    masters_ref,
    first_ref,
    second_ref,
    left_ref,
    right_ref,
    grad_out,
    masters_out,
    first_out,
    second_out,
    small_ref,
    grad_stage,
    masters_stage,
    first_stage,
    second_stage,
    sems,
):
    group = grad_stage.shape[1]
    outputs = (
        (grad_stage, grad_out), (masters_stage, masters_out), (first_stage, first_out), (second_stage, second_out)
    )
    steps = masters_ref.shape[0] // group
    small_ref[...] = grad_in[masters_ref.shape[0], :SMALL_ROWS].astype(f32)

    def stores(step):
        slot = lax.rem(step, 2)
        places = pl.ds(step * group, group)
        return [
            pltpu.make_async_copy(stage.at[slot], out.at[places], sems.at[slot, index])
            for index, (stage, out) in enumerate(outputs)
        ]

    @pl.loop(0, steps)
    def _(step):
        @pl.when(step >= 2)
        def _():
            for copy in stores(step - 2):
                copy.wait()

        soap_group(
            step * group, lax.rem(step, 2), grad_in, masters_ref, first_ref, second_ref, left_ref, right_ref,
            *[stage for stage, _ in outputs],
        )
        start_all(stores(step))

    for step in range(max(steps - 2, 0), steps):
        for copy in stores(step):
            copy.wait()


def soap_group(
    first_block, slot, grad_in, masters_ref, first_ref, second_ref, left_ref, right_ref,
    grad_stage, masters_stage, first_stage, second_stage,
):
    places = range(grad_stage.shape[1])
    blocks = [first_block + place for place in places]
    for place, block in enumerate(blocks):
        grad_stage[slot, place] = grad_in[block].astype(f32)
    soap_blocks(
        [grad_in[block] for block in blocks],
        *[[ref.at[block] for block in blocks] for ref in (masters_ref, first_ref, second_ref, left_ref, right_ref)],
        *[[stage.at[slot, place] for place in places] for stage in (masters_stage, first_stage, second_stage)],
    )


def soap_blocks(grads, masters, firsts, seconds, lefts, rights, masters_out, firsts_out, seconds_out):
    count = range(len(grads))
    rights = [right[...].astype(bf16) for right in rights]
    products = [dot_nn(grads[index].astype(bf16), rights[index]).astype(bf16) for index in count]
    lefts = [left[...].astype(bf16) for left in lefts]
    rotated_blocks = [dot_nn(lefts[index].T, products[index]) for index in count]
    normalized = []
    for index in count:
        rotated = rotated_blocks[index]
        new_first = beta_first * firsts[index][...] + (1.0 - beta_first) * rotated
        new_second = beta_second * seconds[index][...] + (1.0 - beta_second) * rotated * rotated
        firsts_out[index][...] = new_first
        seconds_out[index][...] = new_second
        normalized.append(
            (new_first / first_fix / (jnp.sqrt(new_second / second_fix) + adam_eps)).astype(bf16)
        )
    products = [dot_nt(normalized[index], rights[index]).astype(bf16) for index in count]
    for index in count:
        masters_out[index][...] = masters[index][...] - rate_blocks * dot_nn(lefts[index], products[index])


def params(limit=VMEM_LIMIT, **options):
    return pltpu.CompilerParams(vmem_limit_bytes=limit, **options)


def cast_blocks(source, out, wide, low, load_sems, store_sems):
    parts = load_sems.shape[0]
    group = source.shape[0] // parts
    places = [pl.ds(part * group, group) for part in range(parts)]
    loads = copies_between([source.at[place] for place in places], [wide.at[place] for place in places], load_sems)
    stores = copies_between([low.at[place] for place in places], [out.at[place] for place in places], store_sems)
    start_all(loads)
    for place, load, store in zip(places, loads, stores):
        load.wait()
        low[place] = wide[place].astype(bf16)
        store.start()
    wait_all(stores)


def run_cast(blocks):
    parts = blocks.shape[0] // largest_group(blocks.shape[0])
    return pl.pallas_call(
        cast_blocks,
        out_shape=jax.ShapeDtypeStruct(blocks.shape, bf16),
        in_specs=[ANY_SPEC],
        out_specs=ANY_SPEC,
        scratch_shapes=[
            pltpu.VMEM(blocks.shape, f32),
            pltpu.VMEM(blocks.shape, bf16),
            pltpu.SemaphoreType.DMA((parts,)),
            pltpu.SemaphoreType.DMA((parts,)),
        ],
        compiler_params=params(),
        name="cast_blocks",
    )(blocks)


def run_attention_forward(rows, x, gain, bias, cosine, sine, allowed, weights):
    length = x.shape[0]
    shape = jax.ShapeDtypeStruct
    kept = [((D, length), bf16), ((length, QKV_WIDTH), bf16), ((QUERY_WIDTH, length), bf16)]
    low, high, log_total, *kept_arrays = pl.pallas_call(
        attention_forward,
        out_shape=[
            shape((length // NARROW, D), bf16),
            shape((length // NARROW, D), bf16),
            shape((8, length), f32),
        ]
        + [shape(*one) for one in kept],
        in_specs=[SMEM_SPEC] + [VMEM_SPEC] * 2 + [ANY_SPEC] * 5,
        out_specs=[VMEM_SPEC] * 3 + [ANY_SPEC] * 3,
        scratch_shapes=[pltpu.VMEM(array.shape, array.dtype) for array in (x, cosine, sine, allowed)]
        + [pltpu.VMEM(*one) for one in kept]
        + [
            pltpu.VMEM((D, QKV_WIDTH), bf16),
            pltpu.VMEM((QUERY_WIDTH, D), bf16),
            pltpu.VMEM((length, D), bf16),
            pltpu.VMEM((length, QUERY_WIDTH), bf16),
            pltpu.SemaphoreType.DMA((2,)),
            pltpu.SemaphoreType.DMA((4,)),
            pltpu.SemaphoreType.DMA((3,)),
        ],
        compiler_params=params(),
        name="attention_forward",
    )(rows, gain, bias, x, cosine, sine, allowed, weights)
    return (low, high, *kept_arrays, log_total)


def hidden_cost(length, products, bytes_moved):
    return pl.CostEstimate(
        flops=2 * products * length * D * TILE * TILES, bytes_accessed=bytes_moved, transcendentals=0
    )


def run_active_grads(rows, cotangent, weights):
    length = cotangent.shape[0]
    return pl.pallas_call(
        active_grads,
        out_shape=[
            jax.ShapeDtypeStruct((TILES, length, TILE), f32),
            jax.ShapeDtypeStruct((TILES, TILE, D), bf16),
        ],
        in_specs=[SMEM_SPEC, VMEM_SPEC, ANY_SPEC],
        out_specs=[ANY_SPEC] * 2,
        scratch_shapes=[
            pltpu.VMEM((4, TILE, D), bf16),
            pltpu.VMEM((2, length, TILE), f32),
            pltpu.SemaphoreType.DMA((4,)),
            pltpu.SemaphoreType.DMA((2,)),
            pltpu.SemaphoreType.DMA((4,)),
        ],
        compiler_params=params(),
        cost_estimate=hidden_cost(length, 1, TILES * TILE * (2 * D + 4 * length)),
        name="active_grads",
    )(rows, cotangent, weights)


def run_hidden_grads(first_row, rows, x, own, other, gain, active_grad, weights):
    length = own.shape[0]
    shape = jax.ShapeDtypeStruct
    return pl.pallas_call(
        functools.partial(hidden_grads, first_row),
        out_shape=[
            shape((length, D), bf16),
            shape((length, D), f32),
            shape((D, length), bf16),
            shape((TILES, length, 2 * TILE), bf16),
            shape((TILES, length, TILE), bf16),
            shape((TILES, TILE, length), bf16),
        ],
        in_specs=[SMEM_SPEC, VMEM_SPEC, VMEM_SPEC] + [ANY_SPEC] * 4,
        out_specs=[VMEM_SPEC] + [ANY_SPEC] * 5,
        scratch_shapes=[
            pltpu.VMEM((length, D), bf16),
            pltpu.VMEM((length, D), bf16),
            pltpu.VMEM((length, D), f32),
            pltpu.VMEM((D, length), bf16),
            pltpu.VMEM((2, D, 2 * TILE), bf16),
            pltpu.VMEM((2, length, TILE), f32),
            pltpu.VMEM((2, length, TILE), bf16),
            pltpu.VMEM((2, TILE, length), bf16),
            pltpu.VMEM((2, length, 2 * TILE), bf16),
            pltpu.VMEM((length, D), bf16),
            pltpu.VMEM((length, D), f32),
            pltpu.SemaphoreType.DMA((2, 2)),
            pltpu.SemaphoreType.DMA((2, 3)),
            pltpu.SemaphoreType.DMA((5,)),
        ],
        compiler_params=params(),
        cost_estimate=hidden_cost(length, 4, 2 * TILES * TILE * (2 * D + 6 * length)),
        name="hidden_grads",
    )(rows, gain, in_vmem(other), x, own, active_grad, weights)


def run_hidden_weight_grads(rows, cotangent, parts, slots):
    length = cotangent.shape[0]
    return pl.pallas_call(
        hidden_weight_grads,
        out_shape=jax.ShapeDtypeStruct((slots, BLK, BLK), bf16),
        in_specs=[SMEM_SPEC, VMEM_SPEC] + [ANY_SPEC] * (3 * NARROW),
        out_specs=ANY_SPEC,
        scratch_shapes=[
            pltpu.VMEM((D, length), bf16),
            pltpu.VMEM((2, length, 2 * TILE), bf16),
            pltpu.VMEM((2, TILE, length), bf16),
            pltpu.VMEM((2, D, 2 * TILE), bf16),
            pltpu.VMEM((2, TILE, D), bf16),
            pltpu.SemaphoreType.DMA((2, 2 * NARROW)),
            pltpu.SemaphoreType.DMA((2, 2)),
            pltpu.SemaphoreType.DMA((NARROW,)),
        ],
        compiler_params=params(),
        cost_estimate=hidden_cost(length, 3, 2 * TILES * TILE * 3 * (D + length)),
        name="hidden_weight_grads",
    )(rows, cotangent, *[array for part in parts for array in part])


def run_attention_backward(
    weight_rows, rows, half, x, low, high, cotangent, gains, cosine, sine, allowed, normed_turned, qkv, mixed_turned,
    log_total, weights, grads, wide_count,
):
    length = x.shape[0]
    shape = jax.ShapeDtypeStruct
    empty_count = max(rows.shape[0] - BLOCK_TOTAL, 1)
    (resid_low, own_low, other_low), (resid_high, own_high, other_high) = low, high
    loaded = (resid_low, own_low, resid_high, own_high, cotangent, qkv, cosine, sine, allowed, mixed_turned, normed_turned, x)
    operands = (weight_rows, rows, half, gains, log_total, in_vmem(other_low), in_vmem(other_high), *loaded, weights, grads)
    return pl.pallas_call(
        attention_backward,
        out_shape=[
            shape((length // NARROW, D), f32),
            shape((length // NARROW, D), bf16),
            shape((length // NARROW, D), bf16),
            shape(grads.shape, bf16),
        ],
        in_specs=[SMEM_SPEC] * 3 + [VMEM_SPEC] * 4 + [ANY_SPEC] * (len(loaded) + 2),
        out_specs=[VMEM_SPEC] * 3 + [ANY_SPEC],
        input_output_aliases={len(operands) - 1: 3},
        scratch_shapes=[pltpu.VMEM(array.shape, array.dtype) for array in loaded]
        + [
            pltpu.VMEM((D, QKV_WIDTH), bf16),
            pltpu.VMEM((QUERY_WIDTH, D), bf16),
            pltpu.VMEM((length, D), f32),
            pltpu.VMEM((length, D), bf16),
            pltpu.VMEM((length, QUERY_WIDTH), bf16),
            pltpu.VMEM((length, QKV_WIDTH), bf16),
            pltpu.VMEM((length, D), f32),
            pltpu.VMEM((length, HEAD_DIM), f32),
            pltpu.VMEM((length, HEAD_DIM), f32),
            pltpu.VMEM((1, D), f32),
            pltpu.VMEM((1, D), f32),
            pltpu.VMEM((1, QKV_WIDTH), f32),
            pltpu.VMEM((D, QKV_WIDTH), bf16),
            pltpu.VMEM((QUERY_WIDTH, D), bf16),
            pltpu.VMEM((wide_count, BLK, BLK), bf16),
            pltpu.VMEM((empty_count, BLK, BLK), bf16),
            pltpu.SemaphoreType.DMA((2,)),
            pltpu.SemaphoreType.DMA((4,)),
            pltpu.SemaphoreType.DMA((len(loaded),)),
        ],
        compiler_params=params(),
        name="attention_backward",
    )(*operands)


def largest_group(count):
    return max(size for size in range(1, 11) if count % size == 0)


def run_soap(reduced, masters, first_moment, second_moment, left_basis, right_basis):
    slots = masters.shape[0]
    group = largest_group(slots)
    shape = jax.ShapeDtypeStruct(masters.shape, f32)
    return pl.pallas_call(
        soap_update,
        out_shape=[shape] * 4 + [jax.ShapeDtypeStruct((SMALL_ROWS, BLK), f32)],
        in_specs=[VMEM_SPEC] * 6,
        out_specs=[ANY_SPEC] * 4 + [VMEM_SPEC],
        scratch_shapes=[pltpu.VMEM((2, group, BLK, BLK), f32)] * 4 + [pltpu.SemaphoreType.DMA((2, 4))],
        compiler_params=params(),
        name="soap_update",
    )(reduced, masters, first_moment, second_moment, left_basis, right_basis)


def sum_for_owners(
    line, steps, late_steps,
    grads, masters, first_moment, second_moment, left_basis, right_basis,
    grad_resid, grad_own, grad_sent, tokens, gain, resid_low, resid_high, active_low, active_high, down,
    out, new_masters, new_first, new_second, input_grad, output, small_own, small_other,
    a_in, a_own, a_sum, a_keep, a_send, a_cross, a_up, a_down,
    b_in, b_own, b_sum, b_keep, b_send, b_cross, b_up, b_down,
    a_params, b_params, grad_resid_here, grad_own_here, grad_other_here, tokens_here, gain_here, resid_here,
    active_here, down_here, branch_sum, branch_sent, branch_other,
    core_send, core_recv, own_sems, cross_send, cross_recv, up_send, up_recv, down_send, down_recv,
    b_core_send, b_core_recv, b_own_sems, b_cross_send, b_cross_recv, b_up_send, b_up_recv, b_down_send, b_down_recv,
    a_param_sems, b_param_sems, token_sems, branch_sems, swap_send, swap_recv, credits,
):
    wide = lax.axis_index("wide")
    narrow = lax.axis_index("narrow")
    z = wide // 4
    x = lax.rem(wide // 2, 2)
    core = lax.rem(wide, 2)
    mesh_id = pl.DeviceIdType.MESH
    core_peer = (wide + 1 - 2 * core, narrow)
    cross_peer = (wide + 2 - 4 * x, narrow)
    upper = (lax.rem(wide + 4, 4 * line), narrow)
    lower = (lax.rem(wide + 4 * line - 4, 4 * line), narrow)
    swap_peer = (wide, 1 - narrow)
    slots = out.shape[0]
    has_upper = z < line - 1
    has_lower = z > 0
    sum_depth = a_sum.shape[0]
    hop_depth = a_up.shape[0]
    b_sum_depth = b_sum.shape[0]

    barrier = pltpu.get_barrier_semaphore()
    pl.semaphore_signal(barrier, inc=1, device_id=core_peer, device_id_type=mesh_id)
    pl.semaphore_signal(barrier, inc=1, device_id=cross_peer, device_id_type=mesh_id)
    pl.semaphore_signal(barrier, inc=1, device_id=swap_peer, device_id_type=mesh_id)

    @pl.when(has_upper)
    def _():
        pl.semaphore_signal(barrier, inc=1, device_id=upper, device_id_type=mesh_id)

    @pl.when(has_lower)
    def _():
        pl.semaphore_signal(barrier, inc=1, device_id=lower, device_id_type=mesh_id)

    pl.semaphore_wait(barrier, 3 + has_upper.astype(jnp.int32) + has_lower.astype(jnp.int32))

    def remote(source, target, send_sem, recv_sem, peer):
        return pltpu.make_async_remote_copy(
            src_ref=source, dst_ref=target, send_sem=send_sem, recv_sem=recv_sem, device_id=peer, device_id_type=mesh_id
        )

    def core_copy(step):
        slot = lax.rem(step, DEPTH)
        source = grads.at[:, :, 1 - core, pl.ds(step * EARLY, EARLY)]
        return remote(source, a_in.at[slot], core_send.at[slot], core_recv.at[slot], core_peer)

    def own_copy(step):
        slot = lax.rem(step, DEPTH)
        return pltpu.make_async_copy(
            grads.at[:, :, core, pl.ds(step * EARLY, EARLY)], a_own.at[slot], own_sems.at[slot]
        )

    def b_core_copy(step):
        slot = lax.rem(step, DEPTH)
        source = grads.at[:, :, 1 - core, slots - 1 - step]
        return remote(source, b_in.at[slot], b_core_send.at[slot], b_core_recv.at[slot], core_peer)

    def b_own_copy(step):
        slot = lax.rem(step, DEPTH)
        return pltpu.make_async_copy(
            grads.at[:, :, core, slots - 1 - step], b_own.at[slot], b_own_sems.at[slot]
        )

    def cross_copy(step):
        slot = lax.rem(step, DEPTH)
        return remote(a_send.at[slot], a_cross.at[slot], cross_send.at[slot], cross_recv.at[slot], cross_peer)

    def b_cross_copy(step):
        slot = lax.rem(step, DEPTH)
        return remote(b_send.at[slot], b_cross.at[slot], b_cross_send.at[slot], b_cross_recv.at[slot], cross_peer)

    def up_copy(step, target):
        slot = lax.rem(step, hop_depth)
        return remote(
            a_sum.at[lax.rem(step, sum_depth), target], a_up.at[slot, target],
            up_send.at[slot, target], up_recv.at[slot, target], upper,
        )

    def down_copy(step, target):
        slot = lax.rem(step, hop_depth)
        return remote(
            a_sum.at[lax.rem(step, sum_depth), target], a_down.at[slot, target],
            down_send.at[slot, target], down_recv.at[slot, target], lower,
        )

    def b_up_copy(step, target):
        slot = lax.rem(step, hop_depth)
        return remote(
            b_sum.at[lax.rem(step, b_sum_depth), target], b_up.at[slot, target],
            b_up_send.at[slot, target], b_up_recv.at[slot, target], upper,
        )

    def b_down_copy(step, target):
        slot = lax.rem(step, hop_depth)
        return remote(
            b_sum.at[lax.rem(step, b_sum_depth), target], b_down.at[slot, target],
            b_down_send.at[slot, target], b_down_recv.at[slot, target], lower,
        )

    def give(channel, peer):
        pl.semaphore_signal(credits.at[channel], inc=1, device_id=peer, device_id_type=mesh_id)

    def take(channel, step, depth):
        @pl.when(step >= depth)
        def _():
            pl.semaphore_wait(credits.at[channel], 1)

    def feed(step, count, channel, remote_copy, local_copy):
        @pl.when(step < count)
        def _():
            take(channel, step, DEPTH)
            remote_copy(step).start()
            local_copy(step).start()

    sources = (masters, first_moment, second_moment, left_basis, right_basis)

    def param_loads(step):
        slot = lax.rem(step, 2)
        places = pl.ds(step * EARLY, EARLY)
        return [
            pltpu.make_async_copy(source.at[places], a_params.at[slot, index], a_param_sems.at[slot, index])
            for index, source in enumerate(sources)
        ]

    def b_param_loads(step):
        slot = lax.rem(step, 2)
        return [
            pltpu.make_async_copy(
                source.at[slots - 1 - step], b_params.at[slot, index], b_param_sems.at[slot, index]
            )
            for index, source in enumerate(sources)
        ]

    token_loads = [
        pltpu.make_async_copy(source, target, token_sems.at[1 + index])
        for index, (source, target) in enumerate((
            (grad_resid, grad_resid_here), (grad_own, grad_own_here), (tokens, tokens_here), (gain, gain_here),
        ))
    ]
    grad_swap = remote(grad_sent, grad_other_here, swap_send.at[0], swap_recv.at[0], swap_peer)
    small_swap = remote(small_own, small_other, swap_send.at[1], swap_recv.at[1], swap_peer)

    branch_swap = remote(branch_sent, branch_other, swap_send.at[2], swap_recv.at[2], swap_peer)

    def branch_load(index):
        tile = lax.rem(index, TILES)
        takes_low = narrow == jnp.where(index < TILES, 1, 0)

        @pl.when(takes_low)
        def _():
            pltpu.make_async_copy(active_low.at[tile], active_here, branch_sems.at[0]).start()

        @pl.when(jnp.logical_not(takes_low))
        def _():
            pltpu.make_async_copy(active_high.at[tile], active_here, branch_sems.at[0]).start()

        pltpu.make_async_copy(down.at[tile], down_here, branch_sems.at[1]).start()

    def branch_step(index):
        pltpu.make_async_copy(active_low.at[0], active_here, branch_sems.at[0]).wait()
        pltpu.make_async_copy(down.at[0], down_here, branch_sems.at[1]).wait()

        @pl.when(lax.rem(index, TILES) == 0)
        def _():
            branch_sum[...] = jnp.zeros_like(branch_sum)

        for begin, size in spans(D, COLS):
            columns = pl.ds(begin, size)
            branch_sum[:, columns] += dot_nn(active_here[...], down_here[:, columns])

        @pl.when(index < 2 * TILES - 1)
        def _():
            branch_load(index + 1)

        @pl.when(index == TILES - 1)
        def _():
            branch_sent[...] = branch_sum[...].astype(bf16)
            branch_swap.start()

    def resid_load(source):
        return pltpu.make_async_copy(source, resid_here, token_sems.at[0])

    def finish_output():
        resid_load(resid_low).wait()
        branch_swap.wait()

        def rows_of_output(rows):
            total = resid_here[rows, :] + branch_sum[rows, :] + branch_other[rows, :].astype(f32)
            output[rows, :] = total.astype(bf16)

        row_chunks(output.shape[0], ROWS, rows_of_output)

    def finish_input_grad():
        wait_all(token_loads)
        grad_swap.wait()

        def rows_of_grad(rows):
            values = tokens_here[rows, :].astype(f32)
            inverse = rms_inverse(values)
            scaled = grad_own_here[rows, :].astype(f32) + grad_other_here[rows, :].astype(f32)
            input_grad[rows, :] = grad_resid_here[rows, :] + norm_back(
                scaled * gain_here[...], values * inverse, inverse
            )

        row_chunks(input_grad.shape[0], ROWS, rows_of_grad)

    grad_swap.start()
    for early in range(DEPTH - 1):
        feed(early, steps, 0, core_copy, own_copy)
        feed(early, late_steps, 1, b_core_copy, b_own_copy)

    start_all(param_loads(0) + param_loads(1) + b_param_loads(1) + b_param_loads(2) + token_loads)
    branch_load(0)
    pl.when(narrow == 0)(lambda: resid_load(resid_low).start())
    pl.when(narrow != 0)(lambda: resid_load(resid_high).start())

    def active(step, count):
        return (step >= 0) & (step < count)

    far = jnp.maximum(z, line - 1 - z)

    def hops(step_up, step_down, count, sums, depth, ups, downs, up, down, channel):
        @pl.when(active(step_up, count) & has_upper)
        def _():
            take(channel, step_up, hop_depth)
            slot = lax.rem(step_up, hop_depth)
            place = lax.rem(step_up, depth)

            def one(target, _):
                @pl.when(has_lower)
                def _():
                    up(step_up, target).wait_recv()
                    sums[place, target] += ups[slot, target]

                up(step_up, target).start()
                return 0

            lax.fori_loop(z + 1, line, one, 0)

        @pl.when(active(step_down, count) & has_lower)
        def _():
            take(channel + 1, step_down, hop_depth)
            slot = lax.rem(step_down, hop_depth)
            place = lax.rem(step_down, depth)

            def one(target, _):
                @pl.when(has_upper)
                def _():
                    down(step_down, target).wait_recv()
                    sums[place, target] += downs[slot, target]

                down(step_down, target).start()
                return 0

            lax.fori_loop(0, z, one, 0)

    def gather_hops(step, count, sums, depth, ups, downs, up, down, channel, total):
        slot = lax.rem(step, hop_depth)
        total[...] = sums[lax.rem(step, depth), z].astype(f32)

        @pl.when(has_lower)
        def _():
            up(step, z).wait_recv()
            total[...] += ups[slot, z].astype(f32)

            @pl.when(step < count - hop_depth)
            def _():
                give(channel, lower)

        @pl.when(has_upper)
        def _():
            down(step, z).wait_recv()
            total[...] += downs[slot, z].astype(f32)

            @pl.when(step < count - hop_depth)
            def _():
                give(channel + 1, upper)

    def retire(step, count, up, down):
        @pl.when(active(step, count))
        def _():
            def sent_up(target, _):
                up(step, target).wait_send()
                return 0

            def sent_down(target, _):
                down(step, target).wait_send()
                return 0

            lax.fori_loop(z + 1, line, sent_up, 0)
            lax.fori_loop(0, z, sent_down, 0)

    def iteration(step, _):
        feed(step + DEPTH - 1, steps, 0, core_copy, own_copy)
        feed(step + DEPTH - 1, late_steps, 1, b_core_copy, b_own_copy)

        retire(step - CROSS_LAG - HOP_LAG * far - 1, steps, up_copy, down_copy)
        retire(step - HOP_LAG * far - 1, late_steps, b_up_copy, b_down_copy)

        @pl.when(step < steps)
        def _():
            slot = lax.rem(step, DEPTH)
            place = lax.rem(step, sum_depth)
            core_copy(step).wait()
            own_copy(step).wait()

            @pl.when(step >= DEPTH)
            def _():
                cross_copy(step - DEPTH).wait_send()

            for target in range(line):
                a_send[slot, target] = a_own[slot, target, 1 - x] + a_in[slot, target, 1 - x]
            take(2, step, DEPTH)
            cross_copy(step).start()
            for target in range(line):
                a_sum[place, target] = a_own[slot, target, x] + a_in[slot, target, x]

            @pl.when(step < steps - DEPTH)
            def _():
                give(0, core_peer)

        @pl.when(step < late_steps)
        def _():
            slot = lax.rem(step, DEPTH)
            b_core_copy(step).wait()
            b_own_copy(step).wait()
            b_sum[lax.rem(step, b_sum_depth)] = b_own[slot] + b_in[slot]

            @pl.when(step < late_steps - DEPTH)
            def _():
                give(1, core_peer)

        crossed = step - CROSS_LAG

        @pl.when(active(crossed, steps))
        def _():
            slot = lax.rem(crossed, DEPTH)
            place = lax.rem(crossed, sum_depth)
            cross_copy(crossed).wait_recv()
            for target in range(line):
                a_sum[place, target] += a_cross[slot, target]

            @pl.when(crossed < steps - DEPTH)
            def _():
                give(2, cross_peer)

        hops(
            step - HOP_LAG * z, step - HOP_LAG * (line - 1 - z), late_steps, b_sum, b_sum_depth, b_up, b_down,
            b_up_copy, b_down_copy, 6,
        )
        hops(
            crossed - HOP_LAG * z, crossed - HOP_LAG * (line - 1 - z), steps, a_sum, sum_depth, a_up, a_down,
            up_copy, down_copy, 4,
        )

        last = crossed - HOP_LAG * far

        @pl.when(active(last, steps))
        def _():
            gather_hops(last, steps, a_sum, sum_depth, a_up, a_down, up_copy, down_copy, 4, a_keep)
            out[pl.ds(last * EARLY, EARLY)] = a_keep[...].astype(bf16)
            slot = lax.rem(last, 2)
            for copy in param_loads(last):
                copy.wait()
            soap_blocks(
                [a_keep[index] for index in range(EARLY)],
                *[[a_params.at[slot, kind, index] for index in range(EARLY)] for kind in range(5)],
                *[
                    [target.at[last * EARLY + index] for index in range(EARLY)]
                    for target in (new_masters, new_first, new_second)
                ],
            )

            @pl.when(last + 2 < steps)
            def _():
                start_all(param_loads(last + 2))

        arrived = step - HOP_LAG * far

        @pl.when(active(arrived, late_steps))
        def _():
            slot = lax.rem(arrived, DEPTH)

            @pl.when(arrived >= DEPTH)
            def _():
                b_cross_copy(arrived - DEPTH).wait_send()

            gather_hops(
                arrived, late_steps, b_sum, b_sum_depth, b_up, b_down, b_up_copy, b_down_copy, 6, b_keep.at[slot]
            )
            b_send[slot] = b_keep[slot, 1 - x].astype(bf16)
            take(3, arrived, DEPTH)
            b_cross_copy(arrived).start()

        paired = arrived - CROSS_LAG

        @pl.when(active(paired, late_steps))
        def _():
            slot = lax.rem(paired, DEPTH)
            b_cross_copy(paired).wait_recv()
            place = slots - 1 - paired
            total = b_keep[slot, x] + b_cross[slot].astype(f32)
            out[place] = total.astype(bf16)

            @pl.when(paired < late_steps - DEPTH)
            def _():
                give(3, cross_peer)

            @pl.when(paired == 0)
            def _():
                small_own[...] = total[: small_own.shape[0]]
                small_swap.start()

            @pl.when(paired > 0)
            def _():
                slot = lax.rem(paired, 2)
                for copy in b_param_loads(paired):
                    copy.wait()
                soap_blocks(
                    [total], *[[b_params.at[slot, kind]] for kind in range(5)],
                    [new_masters.at[place]], [new_first.at[place]], [new_second.at[place]],
                )

                @pl.when(paired + 2 < late_steps)
                def _():
                    start_all(b_param_loads(paired + 2))

        @pl.when((step >= 1) & (step < 2 * TILES + 1))
        def _():
            branch_step(step - 1)

        pl.when(step == 2 * TILES + 1)(finish_output)
        pl.when(step == 4)(finish_input_grad)
        return 0

    lag = HOP_LAG * (line - 1) + CROSS_LAG
    lax.fori_loop(0, max(max(steps, late_steps) + lag, 2 * TILES) + 2, iteration, 0)
    for step in range(max(steps - DEPTH, 0), steps):
        cross_copy(step).wait_send()
    for step in range(max(late_steps - DEPTH, 0), late_steps):
        b_cross_copy(step).wait_send()
    small_swap.wait()


def run_sum_for_owners(grads, wide_count, blocks, token_arrays):
    line = wide_count // 4
    slots, block = grads.shape[0] // wide_count, grads.shape[1:]
    steps = (slots - 1) // (EARLY + 1)
    late_steps = slots - EARLY * steps
    sum_depth = CROSS_LAG + HOP_LAG * (line - 1) + 2
    b_sum_depth = HOP_LAG * (line - 1) + 2
    hop_depth = 2 * HOP_LAG + 2
    dma = pltpu.SemaphoreType.DMA

    def vmem(*shape):
        return pltpu.VMEM(shape + block, bf16)

    def wide_vmem(*shape):
        return pltpu.VMEM(shape + block, f32)

    return pl.pallas_call(
        functools.partial(sum_for_owners, line, steps, late_steps),
        out_shape=[pltpu.VMEM((slots,) + block, bf16)]
        + [pltpu.VMEM(blocks[0].shape, f32)] * 3
        + [pltpu.VMEM(token_arrays[0].shape, f32), pltpu.VMEM(token_arrays[0].shape, bf16)]
        + [pltpu.VMEM((SMALL_ROWS, block[-1]), f32)] * 2,
        in_specs=[ANY_SPEC] * (1 + len(blocks) + len(token_arrays)),
        out_specs=[VMEM_SPEC] * 8,
        scratch_shapes=[
            vmem(DEPTH, line, 2, EARLY),
            vmem(DEPTH, line, 2, EARLY),
            vmem(sum_depth, line, EARLY),
            wide_vmem(EARLY),
            vmem(DEPTH, line, EARLY),
            vmem(DEPTH, line, EARLY),
            vmem(hop_depth, line, EARLY),
            vmem(hop_depth, line, EARLY),
            vmem(DEPTH, line, 2),
            vmem(DEPTH, line, 2),
            vmem(b_sum_depth, line, 2),
            wide_vmem(DEPTH, 2),
            vmem(DEPTH),
            vmem(DEPTH),
            vmem(hop_depth, line, 2),
            vmem(hop_depth, line, 2),
            wide_vmem(2, len(blocks), EARLY),
            wide_vmem(2, len(blocks)),
        ]
        + [pltpu.VMEM(array.shape, array.dtype) for array in token_arrays[:6]]
        + [
            pltpu.VMEM(token_arrays[7].shape[1:], bf16),
            pltpu.VMEM(token_arrays[9].shape[1:], bf16),
            pltpu.VMEM(token_arrays[0].shape, f32),
            pltpu.VMEM(token_arrays[0].shape, bf16),
            pltpu.VMEM(token_arrays[0].shape, bf16),
        ]
        + ([dma((DEPTH,))] * 5 + [dma((hop_depth, line))] * 4) * 2
        + [dma((2, len(blocks)))] * 2
        + [dma((5,)), dma((2,)), dma((3,)), dma((3,)), pltpu.SemaphoreType.REGULAR((8,))],
        compiler_params=params(SUM_VMEM, collective_id=0, has_side_effects=True),
        cost_estimate=pl.CostEstimate(flops=0, bytes_accessed=2 * grads.size * 8, transcendentals=0),
        name="sum_for_owners",
    )(grads.reshape((line, 2, 2, slots) + block), *blocks, *token_arrays)


def write_results(
    reduced, masters, first_moment, second_moment, input_grad, output, small_own, small_other,
    block_grad_out, masters_out, first_out, second_out, input_grad_out, output_out, small_out,
    stage, stage_sems, sems,
):
    copies = [
        pltpu.make_async_copy(source, target, sems.at[index])
        for index, (source, target) in enumerate((
            (masters, masters_out), (first_moment, first_out), (second_moment, second_out),
            (input_grad, input_grad_out), (output, output_out),
        ))
    ]
    start_all(copies)
    small_out[0] = small_own[...]
    small_out[1] = small_other[...]
    group = stage.shape[1]
    steps = masters.shape[0] // group

    def store(step):
        slot = lax.rem(step, 2)
        return pltpu.make_async_copy(
            stage.at[slot], block_grad_out.at[pl.ds(step * group, group)], stage_sems.at[slot]
        )

    @pl.loop(0, steps)
    def _(step):
        @pl.when(step >= 2)
        def _():
            store(step - 2).wait()

        stage[lax.rem(step, 2)] = reduced[pl.ds(step * group, group)].astype(f32)
        store(step).start()

    for step in range(max(steps - 2, 0), steps):
        store(step).wait()
    for copy in copies:
        copy.wait()


def run_write_results(*arrays):
    arrays = [pltpu.with_memory_space_constraint(array, pltpu.VMEM) for array in arrays]
    blocks, rows, small = arrays[1].shape, arrays[4].shape, arrays[-1].shape
    group = largest_group(blocks[0])
    shape = jax.ShapeDtypeStruct
    return pl.pallas_call(
        write_results,
        out_shape=[shape(blocks, f32)] * 4 + [shape(rows, f32), shape(rows, bf16), shape((2,) + small, f32)],
        in_specs=[VMEM_SPEC] * len(arrays),
        out_specs=[ANY_SPEC] * 6 + [VMEM_SPEC],
        scratch_shapes=[
            pltpu.VMEM((2, group) + blocks[1:], f32),
            pltpu.SemaphoreType.DMA((2,)),
            pltpu.SemaphoreType.DMA((5,)),
        ],
        compiler_params=params(WRITE_VMEM),
        name="write_results",
    )(*arrays)


def rope_tables(segment_row):
    token_index = jnp.arange(segment_row.shape[0], dtype=jnp.int32)
    changed = jnp.concatenate([jnp.ones((1,), dtype=bool), segment_row[1:] != segment_row[:-1]])
    begins = lax.cummax(jnp.where(changed, token_index, jnp.zeros_like(token_index)), axis=0)
    places = (token_index - begins).astype(f32)
    frequency = rope_base ** (-(jnp.arange(HEAD_DIM // 2, dtype=f32) * 2.0) / HEAD_DIM)
    angles = places[:, None] * frequency[None, :]
    cosine = jnp.concatenate([jnp.cos(angles), jnp.cos(angles)], axis=-1)
    sine_signed = jnp.concatenate([-jnp.sin(angles), jnp.sin(angles)], axis=-1)
    return (cosine, sine_signed)


def rms_parts(values):
    inverse = rms_inverse(values)
    return (inverse, values * inverse)


def norm_back(grad_scaled, normed, inverse):
    return inverse * (grad_scaled - normed * jnp.mean(grad_scaled * normed, axis=-1, keepdims=True))


def adam_small(param_now, gradient, first_now, second_now, rate_here):
    first_new = beta_first * first_now + (1.0 - beta_first) * gradient
    second_new = beta_second * second_now + (1.0 - beta_second) * gradient * gradient
    param_new = param_now - rate_here * (first_new / first_fix) / (
        jnp.sqrt(second_new / second_fix) + adam_eps
    )
    return (param_new, first_new, second_new)


def swap_halves(values):
    return lax.ppermute(values, "narrow", [(0, 1), (1, 0)])


def in_vmem(array):
    return pltpu.with_memory_space_constraint(array, pltpu.VMEM)


def body(
    tokens,
    cotangent,
    segments,
    owner_list,
    masters,
    first_moment,
    second_moment,
    left_basis,
    right_basis,
    gains,
    gain_first,
    gain_second,
    biases,
    bias_first,
    bias_second,
):
    half = lax.axis_index("narrow")
    wide_index = lax.axis_index("wide")
    wide_count = lax.axis_size("wide")
    tokens_here = tokens.shape[0]
    slots_here = masters.shape[0]
    slots_half = owner_list.shape[0]
    gains_here = gains.shape[0]
    biases_here = biases.shape[1]

    def join_halves(own, other, axis=0):
        return jnp.where(
            half == 0, jnp.concatenate([own, other], axis=axis), jnp.concatenate([other, own], axis=axis)
        )

    masters_low, gains, biases = lax.optimization_barrier((run_cast(masters), gains, biases))
    weights = lax.all_gather(masters_low, "wide", axis=0, tiled=True)
    gain_full = lax.all_gather(gains, ("wide", "narrow"), axis=0, tiled=True).reshape(2, D)
    bias_full = lax.all_gather(biases.reshape(-1).astype(bf16), "wide", axis=0, tiled=True)
    bias_full = bias_full.astype(f32).reshape(1, QKV_WIDTH)
    pair_gains = 2 * gains_here

    position = jnp.arange(slots_half, dtype=jnp.int32)
    empty = owner_list == BLOCK_TOTAL
    number = jnp.where(empty, BLOCK_TOTAL - 1 + jnp.cumsum(empty.astype(jnp.int32)), owner_list)
    weight_rows = jnp.zeros((slots_half,), jnp.int32).at[number].set(position, unique_indices=True)
    rows = weight_rows + weight_rows // slots_here
    half_index = half.astype(jnp.int32).reshape(1)

    segment_row = lax.dynamic_index_in_dim(segments, wide_index, 0, keepdims=False)
    cosine, sine = rope_tables(segment_row)
    token_index = jnp.arange(segment_row.shape[0], dtype=jnp.int32)
    allowed_turned = (
        (segment_row[None, :] == segment_row[:, None]) & (token_index[None, :] >= token_index[:, None])
    ).astype(f32)
    tokens_row = join_halves(tokens, swap_halves(tokens))
    cotangent_row = join_halves(cotangent, swap_halves(cotangent))
    weights, tokens_row, cotangent_row, rows, gain_full, gain_one, gain_two = lax.optimization_barrier(
        (weights, tokens_row, cotangent_row, rows, gain_full, gain_full[0:1], gain_full[1:2])
    )

    low_part, high_part, normed_one_turned, qkv, mixed_turned, log_total = run_attention_forward(
        weight_rows, tokens_row, gain_one, bias_full, cosine, sine, allowed_turned, weights
    )
    low_other = swap_halves(low_part)
    active_grad, down_tiles = run_active_grads(weight_rows, cotangent_row, weights)
    high_sent, low_other = lax.optimization_barrier((high_part, low_other))
    high_other = swap_halves(high_sent)
    grad_low, resid_low, turned_low, *hidden_low = run_hidden_grads(
        0, weight_rows, tokens_row, low_part, low_other, gain_two, active_grad, weights
    )
    grad_low_other = swap_halves(grad_low)
    grad_high, resid_high, turned_high, *hidden_high = run_hidden_grads(
        tokens_here, weight_rows, tokens_row, high_part, high_other, gain_two, active_grad, weights
    )
    grad_high_other = swap_halves(grad_high)
    pair_low, active_low, active_turned_low = hidden_low
    pair_high, active_high, active_turned_high = hidden_high
    grads = run_hidden_weight_grads(
        rows, cotangent_row, [(turned_low, pair_low, active_turned_low), (turned_high, pair_high, active_turned_high)],
        wide_count * (slots_here + 1),
    )
    grad_resid, grad_one_own, grad_one_sent, grads = run_attention_backward(
        weight_rows, rows, half_index, tokens_row, (resid_low, grad_low, grad_low_other),
        (resid_high, grad_high, grad_high_other), cotangent_row, gain_full, cosine, sine, allowed_turned,
        normed_one_turned, qkv, mixed_turned, log_total, weights, grads, wide_count,
    )
    blocks = [masters, first_moment, second_moment, left_basis, right_basis]
    if wide_count == 16:
        token_arrays = [
            grad_resid, grad_one_own, grad_one_sent, tokens, gain_one, resid_low, resid_high, active_low,
            active_high, down_tiles,
        ]
        block_grad, new_masters, new_first, new_second, input_grad, output, small_sums = run_write_results(
            *run_sum_for_owners(grads, wide_count, blocks, token_arrays)
        )
        gain_parts = small_sums[0, :2] + small_sums[1, :2]
        bias_row = small_sums[0, 2]
    else:
        reduced = lax.psum_scatter(grads, "wide", scatter_dimension=0, tiled=True)
        block_grad, new_masters, new_first, new_second, small_sums = run_soap(reduced, *blocks)
        gain_parts = small_sums[:2] + swap_halves(small_sums[:2])
        bias_row = small_sums[2]
        branch_low, branch_high = [
            jnp.einsum("tik,tkd->id", active, down_tiles, preferred_element_type=f32)
            for active in (active_low, active_high)
        ]
        resid_own = jnp.where(half == 0, resid_low, resid_high)
        branch_own = jnp.where(half == 0, branch_low, branch_high)
        branch_sent = jnp.where(half == 0, branch_high, branch_low).astype(bf16)
        output = (resid_own + branch_own + swap_halves(branch_sent).astype(f32)).astype(bf16)
        inverse_one, normed_one = rms_parts(tokens.astype(f32))
        grad_one = grad_one_own.astype(f32) + swap_halves(grad_one_sent).astype(f32)
        input_grad = grad_resid + norm_back(grad_one * gain_full[0:1], normed_one, inverse_one)

    gain_first_index = wide_index * pair_gains
    gain_offset = gain_first_index - jnp.minimum(gain_first_index // BLK, 2 * D // BLK - 2) * BLK
    bias_offset = lax.rem(wide_index * biases_here, BLK)
    gain_grad = lax.dynamic_slice_in_dim(gain_parts.reshape(-1), gain_offset + half * gains_here, gains_here, 0)
    bias_grad = lax.dynamic_slice_in_dim(bias_row, bias_offset, biases_here, 0).reshape(biases.shape)
    new_gains, new_gain_first, new_gain_second = adam_small(gains, gain_grad, gain_first, gain_second, rate_gains)
    new_biases, new_bias_first, new_bias_second = adam_small(biases, bias_grad, bias_first, bias_second, rate_small)

    return (
        output,
        input_grad,
        block_grad,
        new_masters,
        new_first,
        new_second,
        gain_grad,
        new_gains,
        new_gain_first,
        new_gain_second,
        bias_grad,
        new_biases,
        new_bias_first,
        new_bias_second,
    )


def solution(mesh):
    tokens_spec = P(("wide", "narrow"), None)
    blocks_spec = P(("wide", "narrow"), None, None)
    gains_spec = P(("wide", "narrow"))
    bias_spec = P("narrow", "wide")
    in_specs = (
        (tokens_spec, tokens_spec, P(), P()) + (blocks_spec,) * 5 + (gains_spec,) * 3 + (bias_spec,) * 3
    )
    out_specs = (tokens_spec, tokens_spec) + (blocks_spec,) * 4 + (gains_spec,) * 4 + (bias_spec,) * 4
    return jax.shard_map(body, mesh=mesh, in_specs=in_specs, out_specs=out_specs, check_vma=False)
```

```python
import functools

import jax
import jax.numpy as jnp
from jax import lax
from jax.experimental import pallas as pl
from jax.experimental.pallas import tpu as pltpu
from jax.sharding import PartitionSpec as P

D = 1536
FF = 8960
HEADS = 12
KV_HEADS = 2
HEAD_DIM = 128
BLK = 128
STEP_COUNT = 5


beta_first = 0.95
beta_second = 0.95
adam_eps = 1e-08
rate_blocks = 0.03
rate_small = 0.4
rate_gains = 0.6
norm_eps = 1e-06
rope_base = 10000.0
masked_score = -1e30
first_fix = 1.0 - beta_first**STEP_COUNT
second_fix = 1.0 - beta_second**STEP_COUNT
scaling = HEAD_DIM ** (-0.5)

bf16 = jnp.bfloat16
f32 = jnp.float32

NARROW = 2
ROW_BLOCKS = D // BLK
QUERY_COLS = HEADS * HEAD_DIM // NARROW // BLK
PAIR_COLS = KV_HEADS * HEAD_DIM // NARROW // BLK
HIDDEN_COLS = FF // NARROW // BLK
QKV_COLS = QUERY_COLS + 2 * PAIR_COLS
QUERY_WIDTH = QUERY_COLS * BLK
QKV_WIDTH = QKV_COLS * BLK
KEY_BASE = ROW_BLOCKS * QUERY_COLS
VALUE_BASE = KEY_BASE + ROW_BLOCKS * PAIR_COLS
OUT_BASE = VALUE_BASE + ROW_BLOCKS * PAIR_COLS
GATE_BASE = OUT_BASE + QUERY_COLS * ROW_BLOCKS
UP_BASE = GATE_BASE + ROW_BLOCKS * HIDDEN_COLS
DOWN_BASE = UP_BASE + ROW_BLOCKS * HIDDEN_COLS
BLOCK_TOTAL = DOWN_BASE + HIDDEN_COLS * ROW_BLOCKS

TILE_BLOCKS = 6
TILES = -(-HIDDEN_COLS // TILE_BLOCKS)
LAST_BLOCKS = HIDDEN_COLS - (TILES - 1) * TILE_BLOCKS
TILE = TILE_BLOCKS * BLK
COLS = 256
ROWS = 128
SMALL_ROWS = 16
VMEM_LIMIT = 60 * 2**20
SUM_VMEM = 39 * 2**20
WRITE_VMEM = 6 * 2**20

EARLY = 4
DEPTH = 3
CROSS_LAG = 2
HOP_LAG = 1

VMEM_SPEC = pl.BlockSpec(memory_space=pltpu.VMEM)
SMEM_SPEC = pl.BlockSpec(memory_space=pltpu.SMEM)
ANY_SPEC = pl.BlockSpec(memory_space=pl.ANY)


def spans(total, step):
    return [(begin, min(step, total - begin)) for begin in range(0, total, step)]


def dot_nn(left, right):
    return jnp.dot(left, right, preferred_element_type=f32)


def dot_nt(left, right):
    return lax.dot_general(left, right, (((1,), (1,)), ((), ())), preferred_element_type=f32)


def block_ref(ref, row_block, col_block):
    return ref.at[pl.ds(row_block * BLK, BLK), pl.ds(col_block * BLK, BLK)]


def fetch_piece(rows_ref, weights, target, base, pitch, row_blocks, col_blocks, first_col, sem):
    @pl.loop(0, row_blocks)
    def _(i):
        for j in range(col_blocks):
            pltpu.make_async_copy(
                weights.at[rows_ref[base + i * pitch + j]],
                block_ref(target, i, first_col + j),
                sem,
            ).start()


def store_piece(rows_ref, source, grads, base, pitch, row_blocks, col_blocks, first_col, sem):
    @pl.loop(0, row_blocks)
    def _(i):
        for j in range(col_blocks):
            pltpu.make_async_copy(
                block_ref(source, i, first_col + j),
                grads.at[rows_ref[base + i * pitch + j]],
                sem,
            ).start()


def wait_bytes(ref, sem):
    pltpu.make_async_copy(ref, ref, sem).wait()


def copies_between(sources, targets, sems):
    return [
        pltpu.make_async_copy(source, target, sems.at[index])
        for index, (source, target) in enumerate(zip(sources, targets, strict=True))
    ]


def wait_all(copies):
    for copy in copies:
        copy.wait()


def fetch_qkv(rows_ref, weights, w_qkv, sem):
    fetch_piece(rows_ref, weights, w_qkv, 0, QUERY_COLS, ROW_BLOCKS, QUERY_COLS, 0, sem)
    fetch_piece(rows_ref, weights, w_qkv, KEY_BASE, PAIR_COLS, ROW_BLOCKS, PAIR_COLS, QUERY_COLS, sem)
    fetch_piece(
        rows_ref, weights, w_qkv, VALUE_BASE, PAIR_COLS, ROW_BLOCKS, PAIR_COLS, QUERY_COLS + PAIR_COLS, sem
    )


def fetch_out(rows_ref, weights, w_out, sem):
    fetch_piece(rows_ref, weights, w_out, OUT_BASE, ROW_BLOCKS, QUERY_COLS, ROW_BLOCKS, 0, sem)


def rms_inverse(values):
    return lax.rsqrt(jnp.mean(values * values, axis=-1, keepdims=True) + norm_eps)


def row_chunks(total, step, run):
    @pl.loop(0, total // step)
    def _(chunk):
        run(pl.ds(pl.multiple_of(chunk * step, step), step))


def small_places(owner, wide_count):
    gain_row = min(owner * (2 * D // wide_count) // BLK, 2 * D // BLK - 2)
    return (gain_row, owner * (QKV_WIDTH // wide_count) // BLK)


def scores_turned(keys, queries, allowed):
    return jnp.where(allowed, dot_nt(keys, queries) * scaling, masked_score)


def attention_forward(
    rows_ref,
    gain_ref,
    bias_ref,
    x_hbm,
    cos_hbm,
    sin_hbm,
    allowed_hbm,
    weights,
    part_low_ref,
    part_high_ref,
    log_ref,
    normed_turned_out,
    qkv_out,
    mixed_turned_out,
    x_ref,
    cos_ref,
    sin_ref,
    allowed_ref,
    normed_turned,
    qkv,
    mixed_turned,
    w_qkv,
    w_out,
    normed,
    mixed,
    sems,
    load_sems,
    store_sems,
):
    loads = copies_between(
        (x_hbm, cos_hbm, sin_hbm, allowed_hbm), (x_ref, cos_ref, sin_ref, allowed_ref), load_sems
    )
    stores = copies_between(
        (normed_turned, qkv, mixed_turned), (normed_turned_out, qkv_out, mixed_turned_out), store_sems
    )
    start_all(loads)
    fetch_qkv(rows_ref, weights, w_qkv, sems.at[0])
    fetch_out(rows_ref, weights, w_out, sems.at[1])
    length = x_ref.shape[0]
    part = length // NARROW

    def norm_rows(rows):
        values = x_ref[rows, :].astype(f32)
        normed[rows, :] = (values * rms_inverse(values) * gain_ref[...]).astype(bf16)

    loads[0].wait()
    row_chunks(length, ROWS, norm_rows)
    wait_all(loads[1:])
    wait_bytes(w_qkv, sems.at[0])
    for begin, size in spans(QKV_WIDTH, COLS):
        products = dot_nn(normed[...], w_qkv[:, pl.ds(begin, size)]) + bias_ref[:, pl.ds(begin, size)]
        for offset, width in spans(size, HEAD_DIM):
            head = products[:, offset : offset + width]
            if begin + offset < QUERY_WIDTH + PAIR_COLS * BLK:
                head = head * cos_ref[...] + pltpu.roll(head, HEAD_DIM // 2, 1) * sin_ref[...]
            qkv[:, pl.ds(begin + offset, width)] = head.astype(bf16)
    for begin, size in spans(D, COLS):
        normed_turned[pl.ds(begin, size), :] = normed[:, pl.ds(begin, size)].T
    start_all(stores[:2])
    values_turned = qkv[:, pl.ds(QUERY_WIDTH + HEAD_DIM, HEAD_DIM)].T
    for head in range(QUERY_COLS):
        columns = pl.ds(head * HEAD_DIM, HEAD_DIM)
        for first in range(0, length, part):
            tokens, seen = pl.ds(first, part), first + part
            scores = scores_turned(
                qkv[:seen, pl.ds(QUERY_WIDTH, HEAD_DIM)], qkv[tokens, columns], allowed_ref[:seen, tokens] > 0
            )
            peak = jnp.max(scores, axis=0, keepdims=True)
            expo = jnp.exp(scores - peak)
            total = jnp.sum(expo, axis=0, keepdims=True)
            log_ref[pl.ds(head, 1), tokens] = peak + jnp.log(total)
            probs = (expo / total).astype(bf16)
            mixed_head = dot_nn(values_turned[:, :seen], probs).astype(bf16)
            mixed_turned[columns, tokens] = mixed_head
            mixed[tokens, columns] = mixed_head.T
    stores[2].start()
    wait_bytes(w_out, sems.at[1])
    for part_ref, first in ((part_low_ref, 0), (part_high_ref, part)):
        for begin, size in spans(D, COLS):
            part_ref[:, pl.ds(begin, size)] = dot_nn(
                mixed[pl.ds(first, part), :], w_out[:, pl.ds(begin, size)]
            ).astype(bf16)
    wait_all(stores)


def pair_copies(rows_ref, blocks_hbm, pair, sem, column, place, outward=False):
    return [
        block_copy(blocks_hbm.at[rows_ref[base + i * HIDDEN_COLS + column]], block_ref(pair, i, which), sem, outward)
        for i in range(ROW_BLOCKS)
        for base, which in ((GATE_BASE, 2 * place), (UP_BASE, 2 * place + 1))
    ]


def down_copies(rows_ref, blocks_hbm, down, sem, column, place, outward=False):
    return [
        block_copy(blocks_hbm.at[rows_ref[DOWN_BASE + column * ROW_BLOCKS + i]], block_ref(down, place, i), sem, outward)
        for i in range(ROW_BLOCKS)
    ]


def block_copy(in_hbm, in_vmem, sem, outward):
    return pltpu.make_async_copy(*((in_vmem, in_hbm) if outward else (in_hbm, in_vmem)), sem)


def start_all(copies):
    for copy in copies:
        copy.start()


def half_rows(half_ref, length):
    begin = pl.multiple_of(half_ref[0] * length, length)
    return (pl.ds(begin, length), pl.ds(pl.multiple_of(length - begin, length), length))


def hidden_column(tile, place):
    return jnp.minimum(tile * TILE_BLOCKS + place, HIDDEN_COLS - 1)


def hidden_tiles(run):
    @pl.loop(0, TILES - 1)
    def _(tile):
        run(tile, lax.rem(tile, 2), TILE_BLOCKS, True)

    run(TILES - 1, (TILES - 1) % 2, LAST_BLOCKS, False)


def active_grads(rows_ref, cot_ref, weights, out, down_out, w_down, stage, load_sems, store_sems, down_sems):
    ring = w_down.shape[0]

    def fetch(tile):
        slot = lax.rem(tile, ring)
        for place in range(TILE_BLOCKS):
            start_all(
                down_copies(rows_ref, weights, w_down.at[slot], load_sems.at[slot], hidden_column(tile, place), place)
            )

    def store(tile):
        return pltpu.make_async_copy(stage.at[lax.rem(tile, 2)], out.at[tile], store_sems.at[lax.rem(tile, 2)])

    def store_down(tile):
        slot = lax.rem(tile, ring)
        return pltpu.make_async_copy(w_down.at[slot], down_out.at[tile], down_sems.at[slot])

    fetch(0)

    def run(tile, slot, blocks, more):
        here = lax.rem(tile, ring)

        @pl.when(tile >= ring - 1)
        def _():
            store_down(tile - ring + 1).wait()

        if more:
            fetch(tile + 1)
        wait_bytes(w_down.at[here], load_sems.at[here])
        if blocks < TILE_BLOCKS:
            w_down[here, pl.ds(blocks * BLK, (TILE_BLOCKS - blocks) * BLK), :] = jnp.zeros(
                ((TILE_BLOCKS - blocks) * BLK, D), bf16
            )
        store_down(tile).start()

        @pl.when(tile >= 2)
        def _():
            store(tile - 2).wait()

        for begin, size in spans(blocks * BLK, COLS):
            stage[slot, :, pl.ds(begin, size)] = dot_nt(cot_ref[...], w_down[here, pl.ds(begin, size), :])
        store(tile).start()

    hidden_tiles(run)
    for tile in range(max(TILES - 2, 0), TILES):
        store(tile).wait()
    for tile in range(max(TILES - ring + 1, 0), TILES):
        store_down(tile).wait()


def hidden_grads(
    first_row,
    rows_ref,
    gain_ref,
    other_ref,
    x_hbm,
    own_hbm,
    active_grad,
    weights,
    grad_ref,
    resid_out,
    normed_turned_out,
    pair_grads,
    active,
    active_turned,
    x_ref,
    own_ref,
    resid_ref,
    normed_turned_ref,
    w_pair,
    grad_active,
    straight,
    turned,
    grads,
    normed,
    grad_sum,
    load_sems,
    store_sems,
    token_sems,
):
    length = own_ref.shape[0]
    token_loads = copies_between(
        (x_hbm.at[pl.ds(first_row, length)], own_hbm), (x_ref, own_ref), token_sems
    )
    store_resid = pltpu.make_async_copy(resid_ref, resid_out, token_sems.at[3])
    store_turned = pltpu.make_async_copy(normed_turned_ref, normed_turned_out, token_sems.at[4])
    start_all(token_loads)

    def fetch(tile, slot, place):
        start_all(
            pair_copies(rows_ref, weights, w_pair.at[slot], load_sems.at[slot, 0], hidden_column(tile, place), place)
        )

    def load_grad(tile, slot):
        return pltpu.make_async_copy(active_grad.at[tile, pl.ds(first_row, length)], grad_active.at[slot], load_sems.at[slot, 1])

    def stores(tile, slot):
        return (
            pltpu.make_async_copy(turned.at[slot], active_turned.at[tile], store_sems.at[slot, 0]),
            pltpu.make_async_copy(grads.at[slot], pair_grads.at[tile], store_sems.at[slot, 1]),
            pltpu.make_async_copy(straight.at[slot], active.at[tile], store_sems.at[slot, 2]),
        )

    for place in range(TILE_BLOCKS):
        fetch(0, 0, place)
    load_grad(0, 0).start()

    def norm_rows(rows):
        values = x_ref[rows, :].astype(f32) + own_ref[rows, :].astype(f32) + other_ref[rows, :].astype(f32)
        resid_ref[rows, :] = values
        normed[rows, :] = (values * rms_inverse(values) * gain_ref[...]).astype(bf16)

    wait_all(token_loads)
    row_chunks(length, ROWS, norm_rows)
    store_resid.start()
    grad_sum[...] = jnp.zeros_like(grad_sum)

    def run(tile, slot, blocks, more):
        wait_bytes(w_pair.at[slot], load_sems.at[slot, 0])
        load_grad(tile, slot).wait()
        if more:
            load_grad(tile + 1, 1 - slot).start()

        @pl.when(tile >= 2)
        def _():
            for copy in stores(tile - 2, slot):
                copy.wait()

        for place in range(blocks):
            columns = pl.ds(place * BLK, BLK)
            pair = dot_nn(normed[...], w_pair[slot, :, pl.ds(2 * place * BLK, 2 * BLK)])
            gate = pair[:, :BLK]
            upper = pair[:, BLK:]
            grad = grad_active[slot, :, columns]
            sigmoid = jax.nn.sigmoid(gate)
            silu = gate * sigmoid
            active_here = (silu * upper).astype(bf16)
            straight[slot, :, columns] = active_here
            turned[slot, columns, :] = active_here.T
            grads[slot, :, pl.ds(2 * place * BLK, BLK)] = (
                grad * upper * sigmoid * (1.0 + gate * (1.0 - sigmoid))
            ).astype(bf16)
            grads[slot, :, pl.ds((2 * place + 1) * BLK, BLK)] = (grad * silu).astype(bf16)
            if more:
                fetch(tile + 1, 1 - slot, place)
        if more:
            for place in range(blocks, TILE_BLOCKS):
                fetch(tile + 1, 1 - slot, place)
        turn = pl.ds(pl.multiple_of(tile * COLS, COLS), COLS)
        normed_turned_ref[turn, :] = normed[:, turn].T
        width = 2 * blocks * BLK
        for begin, size in spans(D, COLS):
            columns = pl.ds(begin, size)
            grad_sum[:, columns] += dot_nt(grads[slot, :, :width], w_pair[slot, columns, :width])
        start_all(stores(tile, slot))

    hidden_tiles(run)
    store_turned.start()
    grad_ref[...] = grad_sum[...].astype(bf16)
    for tile in range(max(TILES - 2, 0), TILES):
        wait_all(stores(tile, tile % 2))
    store_resid.wait()
    store_turned.wait()


def hidden_weight_grads(rows_ref, cot_ref, *refs):
    parts, grads, scratch = refs[: 3 * NARROW], refs[3 * NARROW], refs[3 * NARROW + 1 :]
    normed_turned, pair, turned, pair_stage, down_stage, load_sems, store_sems, sems = scratch
    length = cot_ref.shape[0] // NARROW

    def loads(tile, slot):
        copies = []
        for part in range(NARROW):
            pair_grads, active_turned = parts[part * 3 + 1 : part * 3 + 3]
            tokens = pl.ds(part * length, length)
            copies += [
                pltpu.make_async_copy(pair_grads.at[tile], pair.at[slot, tokens], load_sems.at[slot, part * 2]),
                pltpu.make_async_copy(
                    active_turned.at[tile], turned.at[slot, :, tokens], load_sems.at[slot, part * 2 + 1]
                ),
            ]
        return copies

    def drain(slot, blocks):
        wait_bytes(pair_stage.at[slot, :, pl.ds(0, 2 * blocks * BLK)], store_sems.at[slot, 0])
        wait_bytes(down_stage.at[slot, pl.ds(0, blocks * BLK)], store_sems.at[slot, 1])

    turned_loads = [
        pltpu.make_async_copy(parts[part * 3], normed_turned.at[:, pl.ds(part * length, length)], sems.at[part])
        for part in range(NARROW)
    ]
    start_all(loads(0, 0) + turned_loads)
    wait_all(turned_loads)

    def run(tile, slot, blocks, more):
        wait_all(loads(tile, slot))
        if more:
            start_all(loads(tile + 1, 1 - slot))

        @pl.when(tile >= 2)
        def _():
            drain(slot, TILE_BLOCKS)

        width = blocks * BLK
        down = turned[slot, pl.ds(0, width), :]
        for begin, size in spans(D, COLS):
            columns = pl.ds(begin, size)
            down_stage[slot, pl.ds(0, width), columns] = dot_nn(down, cot_ref[:, columns]).astype(bf16)
        for place in range(blocks):
            column = tile * TILE_BLOCKS + place
            start_all(
                down_copies(rows_ref, grads, down_stage.at[slot], store_sems.at[slot, 1], column, place, outward=True)
            )
            columns = pl.ds(2 * place * BLK, 2 * BLK)
            for begin, size in spans(D, 512):
                pair_stage[slot, pl.ds(begin, size), columns] = dot_nn(
                    normed_turned[pl.ds(begin, size), :], pair[slot, :, columns]
                ).astype(bf16)
            start_all(
                pair_copies(rows_ref, grads, pair_stage.at[slot], store_sems.at[slot, 0], column, place, outward=True)
            )

    hidden_tiles(run)
    if TILES > 1:
        drain((TILES - 2) % 2, TILE_BLOCKS)
    drain((TILES - 1) % 2, LAST_BLOCKS)


def attention_backward(
    weight_rows_ref,
    rows_ref,
    half_ref,
    gain_ref,
    log_ref,
    other_low_ref,
    other_high_ref,
    resid_low_hbm,
    own_low_hbm,
    resid_high_hbm,
    own_high_hbm,
    cot_hbm,
    qkv_hbm,
    cos_hbm,
    sin_hbm,
    allowed_hbm,
    mixed_turned_hbm,
    normed_turned_hbm,
    x_hbm,
    weights,
    grads_in,
    grad_resid_ref,
    grad_own_ref,
    grad_other_ref,
    grads,
    resid_low_ref,
    own_low_ref,
    resid_high_ref,
    own_high_ref,
    cot_ref,
    qkv_ref,
    cos_ref,
    sin_ref,
    allowed_ref,
    mixed_turned_ref,
    normed_turned_ref,
    x_ref,
    w_qkv,
    w_out,
    grad_resid,
    grad_attention,
    grad_mixed,
    grad_qkv,
    grad_sum,
    grad_keys,
    grad_values,
    gain_part,
    gain_two_part,
    bias_part,
    qkv_stage,
    out_stage,
    small_stage,
    blank,
    load_sems,
    store_sems,
    token_sems,
):
    del grads_in
    loads = copies_between(
        (
            cot_hbm, resid_low_hbm, own_low_hbm, resid_high_hbm, own_high_hbm, qkv_hbm, cos_hbm, sin_hbm, allowed_hbm, mixed_turned_hbm, normed_turned_hbm, x_hbm,
        ),
        (
            cot_ref, resid_low_ref, own_low_ref, resid_high_ref, own_high_ref, qkv_ref, cos_ref, sin_ref, allowed_ref, mixed_turned_ref, normed_turned_ref, x_ref,
        ),
        token_sems,
    )
    start_all(loads[:5])
    wide_count = small_stage.shape[0]
    owner_rows = grads.shape[0] // wide_count
    small_stage[...] = jnp.zeros_like(small_stage)
    fetch_out(weight_rows_ref, weights, w_out, load_sems.at[1])
    start_all(loads[5:])
    fetch_qkv(weight_rows_ref, weights, w_qkv, load_sems.at[0])
    length = x_ref.shape[0]
    empty_count = rows_ref.shape[0] - BLOCK_TOTAL
    blank[...] = jnp.zeros_like(blank)
    for index in range(empty_count):
        pltpu.make_async_copy(blank.at[index], grads.at[rows_ref[BLOCK_TOTAL + index]], store_sems.at[2]).start()

    gain_two_part[...] = jnp.zeros_like(gain_two_part)
    part = length // NARROW
    own_rows, other_rows = half_rows(half_ref, part)
    for first, resid_ref, own_ref, other_ref, needed in (
        (0, resid_low_ref, own_low_ref, other_low_ref, loads[:3]),
        (part, resid_high_ref, own_high_ref, other_high_ref, loads[3:5]),
    ):
        wait_all(needed)

        def resid_rows(rows, first=first, resid_ref=resid_ref, own_ref=own_ref, other_ref=other_ref):
            values = resid_ref[rows, :]
            inverse = rms_inverse(values)
            normed = values * inverse
            grad_normed = own_ref[rows, :].astype(f32) + other_ref[rows, :].astype(f32)
            gain_two_part[...] += jnp.sum(grad_normed * normed, axis=0, keepdims=True) / NARROW
            scaled = grad_normed * gain_ref[1:2, :]
            place = pl.ds(rows.start + first, rows.size)
            total = cot_ref[place, :].astype(f32) + inverse * (
                scaled - normed * jnp.mean(scaled * normed, axis=-1, keepdims=True)
            )
            grad_resid[place, :] = total
            grad_attention[place, :] = total.astype(bf16)

        row_chunks(part, ROWS, resid_rows)
    grad_resid_ref[...] = grad_resid[own_rows, :]
    wait_bytes(w_out, load_sems.at[1])
    for begin, size in spans(QUERY_WIDTH, COLS):
        grad_mixed[:, pl.ds(begin, size)] = dot_nt(grad_attention[...], w_out[pl.ds(begin, size), :]).astype(bf16)
    wait_all(loads[5:9])
    keys_turned = qkv_ref[:, pl.ds(QUERY_WIDTH, HEAD_DIM)].T

    def rope_back(vector):
        return vector * cos_ref[...] - pltpu.roll(vector, HEAD_DIM // 2, 1) * sin_ref[...]

    grad_keys[...] = jnp.zeros_like(grad_keys)
    grad_values[...] = jnp.zeros_like(grad_values)
    for head in range(QUERY_COLS):
        columns = pl.ds(head * HEAD_DIM, HEAD_DIM)
        grad_queries = []
        for first in range(0, length, part):
            tokens, seen = pl.ds(first, part), first + part
            queries = qkv_ref[tokens, columns]
            grad_mixed_here = grad_mixed[tokens, columns]
            scores = scores_turned(
                qkv_ref[:seen, pl.ds(QUERY_WIDTH, HEAD_DIM)], queries, allowed_ref[:seen, tokens] > 0
            )
            probs = jnp.exp(scores - log_ref[pl.ds(head, 1), tokens])
            grad_values[:seen, :] += dot_nn(probs.astype(bf16), grad_mixed_here)
            grad_probs = dot_nt(qkv_ref[:seen, pl.ds(QUERY_WIDTH + HEAD_DIM, HEAD_DIM)], grad_mixed_here)
            row_dot = jnp.sum(probs * grad_probs, axis=0, keepdims=True)
            grad_scores = (probs * (grad_probs - row_dot)).astype(bf16)
            grad_keys[:seen, :] += dot_nn(grad_scores, queries)
            grad_queries.append(dot_nn(keys_turned[:, :seen], grad_scores).T * scaling)
        grad_qkv[:, columns] = rope_back(jnp.concatenate(grad_queries, axis=0)).astype(bf16)
    grad_qkv[:, pl.ds(QUERY_WIDTH, HEAD_DIM)] = rope_back(grad_keys[...] * scaling).astype(bf16)
    grad_qkv[:, pl.ds(QUERY_WIDTH + HEAD_DIM, HEAD_DIM)] = grad_values[...].astype(bf16)
    wait_all(loads[9:])

    for begin, size in spans(D, COLS):
        out_stage[:, pl.ds(begin, size)] = dot_nn(
            mixed_turned_ref[...], grad_attention[:, pl.ds(begin, size)]
        ).astype(bf16)
    store_piece(rows_ref, out_stage, grads, OUT_BASE, ROW_BLOCKS, QUERY_COLS, ROW_BLOCKS, 0, store_sems.at[1])
    for begin, size in spans(QKV_WIDTH, COLS):
        qkv_stage[:, pl.ds(begin, size)] = dot_nn(
            normed_turned_ref[...], grad_qkv[:, pl.ds(begin, size)]
        ).astype(bf16)
    store_piece(rows_ref, qkv_stage, grads, 0, QUERY_COLS, ROW_BLOCKS, QUERY_COLS, 0, store_sems.at[0])
    store_piece(rows_ref, qkv_stage, grads, KEY_BASE, PAIR_COLS, ROW_BLOCKS, PAIR_COLS, QUERY_COLS, store_sems.at[0])
    store_piece(
        rows_ref, qkv_stage, grads, VALUE_BASE, PAIR_COLS, ROW_BLOCKS, PAIR_COLS, QUERY_COLS + PAIR_COLS, store_sems.at[0]
    )
    wait_bytes(w_qkv, load_sems.at[0])
    for begin, size in spans(D, COLS):
        grad_sum[:, pl.ds(begin, size)] = dot_nt(grad_qkv[...], w_qkv[pl.ds(begin, size), :])
    grad_own_ref[...] = grad_sum[own_rows, :].astype(bf16)
    grad_other_ref[...] = grad_sum[other_rows, :].astype(bf16)
    gain_part[...] = jnp.zeros_like(gain_part)
    bias_part[...] = dot_nn(jnp.ones((SMALL_ROWS, length), bf16), grad_qkv[...])[:1]

    def gain_rows(rows):
        tokens = x_ref[rows, :].astype(f32)
        gain_part[...] += jnp.sum(grad_sum[rows, :] * tokens * rms_inverse(tokens), axis=0, keepdims=True)

    row_chunks(length, ROWS, gain_rows)
    for owner in range(wide_count):
        gain_row, bias_row = small_places(owner, wide_count)
        small_rows = []
        for row in (gain_row, gain_row + 1):
            columns = pl.ds(row % (D // BLK) * BLK, BLK)
            if row < D // BLK:
                small_rows.append(gain_part[:, columns])
            else:
                small_rows.append(gain_two_part[:, columns])
        small_rows.append(bias_part[:, pl.ds(bias_row * BLK, BLK)])
        small_rows.append(jnp.zeros((SMALL_ROWS - len(small_rows), BLK), f32))
        small_stage[owner, pl.ds(0, SMALL_ROWS), :] = jnp.concatenate(small_rows, axis=0).astype(bf16)
        pltpu.make_async_copy(
            small_stage.at[owner], grads.at[owner * owner_rows + owner_rows - 1], store_sems.at[3]
        ).start()
    wait_bytes(small_stage, store_sems.at[3])
    wait_bytes(qkv_stage, store_sems.at[0])
    wait_bytes(out_stage, store_sems.at[1])
    if empty_count > 0:
        wait_bytes(blank.at[pl.ds(0, empty_count)], store_sems.at[2])


def soap_update(
    grad_in,
    masters_ref,
    first_ref,
    second_ref,
    left_ref,
    right_ref,
    grad_out,
    masters_out,
    first_out,
    second_out,
    small_ref,
    grad_stage,
    masters_stage,
    first_stage,
    second_stage,
    sems,
):
    group = grad_stage.shape[1]
    outputs = (
        (grad_stage, grad_out), (masters_stage, masters_out), (first_stage, first_out), (second_stage, second_out)
    )
    steps = masters_ref.shape[0] // group
    small_ref[...] = grad_in[masters_ref.shape[0], :SMALL_ROWS].astype(f32)

    def stores(step):
        slot = lax.rem(step, 2)
        places = pl.ds(step * group, group)
        return [
            pltpu.make_async_copy(stage.at[slot], out.at[places], sems.at[slot, index])
            for index, (stage, out) in enumerate(outputs)
        ]

    @pl.loop(0, steps)
    def _(step):
        @pl.when(step >= 2)
        def _():
            for copy in stores(step - 2):
                copy.wait()

        soap_group(
            step * group, lax.rem(step, 2), grad_in, masters_ref, first_ref, second_ref, left_ref, right_ref,
            *[stage for stage, _ in outputs],
        )
        start_all(stores(step))

    for step in range(max(steps - 2, 0), steps):
        for copy in stores(step):
            copy.wait()


def soap_group(
    first_block, slot, grad_in, masters_ref, first_ref, second_ref, left_ref, right_ref,
    grad_stage, masters_stage, first_stage, second_stage,
):
    places = range(grad_stage.shape[1])
    blocks = [first_block + place for place in places]
    for place, block in enumerate(blocks):
        grad_stage[slot, place] = grad_in[block].astype(f32)
    soap_blocks(
        [grad_in[block] for block in blocks],
        *[[ref.at[block] for block in blocks] for ref in (masters_ref, first_ref, second_ref, left_ref, right_ref)],
        *[[stage.at[slot, place] for place in places] for stage in (masters_stage, first_stage, second_stage)],
    )


def soap_blocks(grads, masters, firsts, seconds, lefts, rights, masters_out, firsts_out, seconds_out):
    count = range(len(grads))
    rights = [right[...].astype(bf16) for right in rights]
    products = [dot_nn(grads[index].astype(bf16), rights[index]).astype(bf16) for index in count]
    lefts = [left[...].astype(bf16) for left in lefts]
    rotated_blocks = [dot_nn(lefts[index].T, products[index]) for index in count]
    normalized = []
    for index in count:
        rotated = rotated_blocks[index]
        new_first = beta_first * firsts[index][...] + (1.0 - beta_first) * rotated
        new_second = beta_second * seconds[index][...] + (1.0 - beta_second) * rotated * rotated
        firsts_out[index][...] = new_first
        seconds_out[index][...] = new_second
        normalized.append(
            (new_first / first_fix / (jnp.sqrt(new_second / second_fix) + adam_eps)).astype(bf16)
        )
    products = [dot_nt(normalized[index], rights[index]).astype(bf16) for index in count]
    for index in count:
        masters_out[index][...] = masters[index][...] - rate_blocks * dot_nn(lefts[index], products[index])


def params(limit=VMEM_LIMIT, **options):
    return pltpu.CompilerParams(vmem_limit_bytes=limit, **options)


def cast_blocks(source, out, wide, low, load_sems, store_sems):
    parts = load_sems.shape[0]
    group = source.shape[0] // parts
    places = [pl.ds(part * group, group) for part in range(parts)]
    loads = copies_between([source.at[place] for place in places], [wide.at[place] for place in places], load_sems)
    stores = copies_between([low.at[place] for place in places], [out.at[place] for place in places], store_sems)
    start_all(loads)
    for place, load, store in zip(places, loads, stores):
        load.wait()
        low[place] = wide[place].astype(bf16)
        store.start()
    wait_all(stores)


def run_cast(blocks):
    parts = blocks.shape[0] // largest_group(blocks.shape[0])
    return pl.pallas_call(
        cast_blocks,
        out_shape=jax.ShapeDtypeStruct(blocks.shape, bf16),
        in_specs=[ANY_SPEC],
        out_specs=ANY_SPEC,
        scratch_shapes=[
            pltpu.VMEM(blocks.shape, f32),
            pltpu.VMEM(blocks.shape, bf16),
            pltpu.SemaphoreType.DMA((parts,)),
            pltpu.SemaphoreType.DMA((parts,)),
        ],
        compiler_params=params(),
        name="cast_blocks",
    )(blocks)


def run_attention_forward(rows, x, gain, bias, cosine, sine, allowed, weights):
    length = x.shape[0]
    shape = jax.ShapeDtypeStruct
    kept = [((D, length), bf16), ((length, QKV_WIDTH), bf16), ((QUERY_WIDTH, length), bf16)]
    low, high, log_total, *kept_arrays = pl.pallas_call(
        attention_forward,
        out_shape=[
            shape((length // NARROW, D), bf16),
            shape((length // NARROW, D), bf16),
            shape((8, length), f32),
        ]
        + [shape(*one) for one in kept],
        in_specs=[SMEM_SPEC] + [VMEM_SPEC] * 2 + [ANY_SPEC] * 5,
        out_specs=[VMEM_SPEC] * 3 + [ANY_SPEC] * 3,
        scratch_shapes=[pltpu.VMEM(array.shape, array.dtype) for array in (x, cosine, sine, allowed)]
        + [pltpu.VMEM(*one) for one in kept]
        + [
            pltpu.VMEM((D, QKV_WIDTH), bf16),
            pltpu.VMEM((QUERY_WIDTH, D), bf16),
            pltpu.VMEM((length, D), bf16),
            pltpu.VMEM((length, QUERY_WIDTH), bf16),
            pltpu.SemaphoreType.DMA((2,)),
            pltpu.SemaphoreType.DMA((4,)),
            pltpu.SemaphoreType.DMA((3,)),
        ],
        compiler_params=params(),
        name="attention_forward",
    )(rows, gain, bias, x, cosine, sine, allowed, weights)
    return (low, high, *kept_arrays, log_total)


def hidden_cost(length, products, bytes_moved):
    return pl.CostEstimate(
        flops=2 * products * length * D * TILE * TILES, bytes_accessed=bytes_moved, transcendentals=0
    )


def run_active_grads(rows, cotangent, weights):
    length = cotangent.shape[0]
    return pl.pallas_call(
        active_grads,
        out_shape=[
            jax.ShapeDtypeStruct((TILES, length, TILE), f32),
            jax.ShapeDtypeStruct((TILES, TILE, D), bf16),
        ],
        in_specs=[SMEM_SPEC, VMEM_SPEC, ANY_SPEC],
        out_specs=[ANY_SPEC] * 2,
        scratch_shapes=[
            pltpu.VMEM((4, TILE, D), bf16),
            pltpu.VMEM((2, length, TILE), f32),
            pltpu.SemaphoreType.DMA((4,)),
            pltpu.SemaphoreType.DMA((2,)),
            pltpu.SemaphoreType.DMA((4,)),
        ],
        compiler_params=params(),
        cost_estimate=hidden_cost(length, 1, TILES * TILE * (2 * D + 4 * length)),
        name="active_grads",
    )(rows, cotangent, weights)


def run_hidden_grads(first_row, rows, x, own, other, gain, active_grad, weights):
    length = own.shape[0]
    shape = jax.ShapeDtypeStruct
    return pl.pallas_call(
        functools.partial(hidden_grads, first_row),
        out_shape=[
            shape((length, D), bf16),
            shape((length, D), f32),
            shape((D, length), bf16),
            shape((TILES, length, 2 * TILE), bf16),
            shape((TILES, length, TILE), bf16),
            shape((TILES, TILE, length), bf16),
        ],
        in_specs=[SMEM_SPEC, VMEM_SPEC, VMEM_SPEC] + [ANY_SPEC] * 4,
        out_specs=[VMEM_SPEC] + [ANY_SPEC] * 5,
        scratch_shapes=[
            pltpu.VMEM((length, D), bf16),
            pltpu.VMEM((length, D), bf16),
            pltpu.VMEM((length, D), f32),
            pltpu.VMEM((D, length), bf16),
            pltpu.VMEM((2, D, 2 * TILE), bf16),
            pltpu.VMEM((2, length, TILE), f32),
            pltpu.VMEM((2, length, TILE), bf16),
            pltpu.VMEM((2, TILE, length), bf16),
            pltpu.VMEM((2, length, 2 * TILE), bf16),
            pltpu.VMEM((length, D), bf16),
            pltpu.VMEM((length, D), f32),
            pltpu.SemaphoreType.DMA((2, 2)),
            pltpu.SemaphoreType.DMA((2, 3)),
            pltpu.SemaphoreType.DMA((5,)),
        ],
        compiler_params=params(),
        cost_estimate=hidden_cost(length, 4, 2 * TILES * TILE * (2 * D + 6 * length)),
        name="hidden_grads",
    )(rows, gain, in_vmem(other), x, own, active_grad, weights)


def run_hidden_weight_grads(rows, cotangent, parts, slots):
    length = cotangent.shape[0]
    return pl.pallas_call(
        hidden_weight_grads,
        out_shape=jax.ShapeDtypeStruct((slots, BLK, BLK), bf16),
        in_specs=[SMEM_SPEC, VMEM_SPEC] + [ANY_SPEC] * (3 * NARROW),
        out_specs=ANY_SPEC,
        scratch_shapes=[
            pltpu.VMEM((D, length), bf16),
            pltpu.VMEM((2, length, 2 * TILE), bf16),
            pltpu.VMEM((2, TILE, length), bf16),
            pltpu.VMEM((2, D, 2 * TILE), bf16),
            pltpu.VMEM((2, TILE, D), bf16),
            pltpu.SemaphoreType.DMA((2, 2 * NARROW)),
            pltpu.SemaphoreType.DMA((2, 2)),
            pltpu.SemaphoreType.DMA((NARROW,)),
        ],
        compiler_params=params(),
        cost_estimate=hidden_cost(length, 3, 2 * TILES * TILE * 3 * (D + length)),
        name="hidden_weight_grads",
    )(rows, cotangent, *[array for part in parts for array in part])


def run_attention_backward(
    weight_rows, rows, half, x, low, high, cotangent, gains, cosine, sine, allowed, normed_turned, qkv, mixed_turned,
    log_total, weights, grads, wide_count,
):
    length = x.shape[0]
    shape = jax.ShapeDtypeStruct
    empty_count = max(rows.shape[0] - BLOCK_TOTAL, 1)
    (resid_low, own_low, other_low), (resid_high, own_high, other_high) = low, high
    loaded = (resid_low, own_low, resid_high, own_high, cotangent, qkv, cosine, sine, allowed, mixed_turned, normed_turned, x)
    operands = (weight_rows, rows, half, gains, log_total, in_vmem(other_low), in_vmem(other_high), *loaded, weights, grads)
    return pl.pallas_call(
        attention_backward,
        out_shape=[
            shape((length // NARROW, D), f32),
            shape((length // NARROW, D), bf16),
            shape((length // NARROW, D), bf16),
            shape(grads.shape, bf16),
        ],
        in_specs=[SMEM_SPEC] * 3 + [VMEM_SPEC] * 4 + [ANY_SPEC] * (len(loaded) + 2),
        out_specs=[VMEM_SPEC] * 3 + [ANY_SPEC],
        input_output_aliases={len(operands) - 1: 3},
        scratch_shapes=[pltpu.VMEM(array.shape, array.dtype) for array in loaded]
        + [
            pltpu.VMEM((D, QKV_WIDTH), bf16),
            pltpu.VMEM((QUERY_WIDTH, D), bf16),
            pltpu.VMEM((length, D), f32),
            pltpu.VMEM((length, D), bf16),
            pltpu.VMEM((length, QUERY_WIDTH), bf16),
            pltpu.VMEM((length, QKV_WIDTH), bf16),
            pltpu.VMEM((length, D), f32),
            pltpu.VMEM((length, HEAD_DIM), f32),
            pltpu.VMEM((length, HEAD_DIM), f32),
            pltpu.VMEM((1, D), f32),
            pltpu.VMEM((1, D), f32),
            pltpu.VMEM((1, QKV_WIDTH), f32),
            pltpu.VMEM((D, QKV_WIDTH), bf16),
            pltpu.VMEM((QUERY_WIDTH, D), bf16),
            pltpu.VMEM((wide_count, BLK, BLK), bf16),
            pltpu.VMEM((empty_count, BLK, BLK), bf16),
            pltpu.SemaphoreType.DMA((2,)),
            pltpu.SemaphoreType.DMA((4,)),
            pltpu.SemaphoreType.DMA((len(loaded),)),
        ],
        compiler_params=params(),
        name="attention_backward",
    )(*operands)


def largest_group(count):
    return max(size for size in range(1, 11) if count % size == 0)


def run_soap(reduced, masters, first_moment, second_moment, left_basis, right_basis):
    slots = masters.shape[0]
    group = largest_group(slots)
    shape = jax.ShapeDtypeStruct(masters.shape, f32)
    return pl.pallas_call(
        soap_update,
        out_shape=[shape] * 4 + [jax.ShapeDtypeStruct((SMALL_ROWS, BLK), f32)],
        in_specs=[VMEM_SPEC] * 6,
        out_specs=[ANY_SPEC] * 4 + [VMEM_SPEC],
        scratch_shapes=[pltpu.VMEM((2, group, BLK, BLK), f32)] * 4 + [pltpu.SemaphoreType.DMA((2, 4))],
        compiler_params=params(),
        name="soap_update",
    )(reduced, masters, first_moment, second_moment, left_basis, right_basis)


def sum_for_owners(
    line, steps, late_steps,
    grads, masters, first_moment, second_moment, left_basis, right_basis,
    grad_resid, grad_own, grad_sent, tokens, gain, resid_low, resid_high, active_low, active_high, down,
    out, new_masters, new_first, new_second, input_grad, output, small_own, small_other,
    a_in, a_own, a_sum, a_keep, a_send, a_cross, a_up, a_down,
    b_in, b_own, b_sum, b_keep, b_send, b_cross, b_up, b_down,
    a_params, b_params, grad_resid_here, grad_own_here, grad_other_here, tokens_here, gain_here, resid_here,
    active_here, down_here, branch_sum, branch_sent, branch_other,
    core_send, core_recv, own_sems, cross_send, cross_recv, up_send, up_recv, down_send, down_recv,
    b_core_send, b_core_recv, b_own_sems, b_cross_send, b_cross_recv, b_up_send, b_up_recv, b_down_send, b_down_recv,
    a_param_sems, b_param_sems, token_sems, branch_sems, swap_send, swap_recv, credits,
):
    wide = lax.axis_index("wide")
    narrow = lax.axis_index("narrow")
    z = wide // 4
    x = lax.rem(wide // 2, 2)
    core = lax.rem(wide, 2)
    mesh_id = pl.DeviceIdType.MESH
    core_peer = (wide + 1 - 2 * core, narrow)
    cross_peer = (wide + 2 - 4 * x, narrow)
    upper = (lax.rem(wide + 4, 4 * line), narrow)
    lower = (lax.rem(wide + 4 * line - 4, 4 * line), narrow)
    swap_peer = (wide, 1 - narrow)
    slots = out.shape[0]
    has_upper = z < line - 1
    has_lower = z > 0
    sum_depth = a_sum.shape[0]
    hop_depth = a_up.shape[0]
    b_sum_depth = b_sum.shape[0]

    barrier = pltpu.get_barrier_semaphore()
    pl.semaphore_signal(barrier, inc=1, device_id=core_peer, device_id_type=mesh_id)
    pl.semaphore_signal(barrier, inc=1, device_id=cross_peer, device_id_type=mesh_id)
    pl.semaphore_signal(barrier, inc=1, device_id=swap_peer, device_id_type=mesh_id)

    @pl.when(has_upper)
    def _():
        pl.semaphore_signal(barrier, inc=1, device_id=upper, device_id_type=mesh_id)

    @pl.when(has_lower)
    def _():
        pl.semaphore_signal(barrier, inc=1, device_id=lower, device_id_type=mesh_id)

    pl.semaphore_wait(barrier, 3 + has_upper.astype(jnp.int32) + has_lower.astype(jnp.int32))

    def remote(source, target, send_sem, recv_sem, peer):
        return pltpu.make_async_remote_copy(
            src_ref=source, dst_ref=target, send_sem=send_sem, recv_sem=recv_sem, device_id=peer, device_id_type=mesh_id
        )

    def core_copy(step):
        slot = lax.rem(step, DEPTH)
        source = grads.at[:, :, 1 - core, pl.ds(step * EARLY, EARLY)]
        return remote(source, a_in.at[slot], core_send.at[slot], core_recv.at[slot], core_peer)

    def own_copy(step):
        slot = lax.rem(step, DEPTH)
        return pltpu.make_async_copy(
            grads.at[:, :, core, pl.ds(step * EARLY, EARLY)], a_own.at[slot], own_sems.at[slot]
        )

    def b_core_copy(step):
        slot = lax.rem(step, DEPTH)
        source = grads.at[:, :, 1 - core, slots - 1 - step]
        return remote(source, b_in.at[slot], b_core_send.at[slot], b_core_recv.at[slot], core_peer)

    def b_own_copy(step):
        slot = lax.rem(step, DEPTH)
        return pltpu.make_async_copy(
            grads.at[:, :, core, slots - 1 - step], b_own.at[slot], b_own_sems.at[slot]
        )

    def cross_copy(step):
        slot = lax.rem(step, DEPTH)
        return remote(a_send.at[slot], a_cross.at[slot], cross_send.at[slot], cross_recv.at[slot], cross_peer)

    def b_cross_copy(step):
        slot = lax.rem(step, DEPTH)
        return remote(b_send.at[slot], b_cross.at[slot], b_cross_send.at[slot], b_cross_recv.at[slot], cross_peer)

    def up_copy(step, target):
        slot = lax.rem(step, hop_depth)
        return remote(
            a_sum.at[lax.rem(step, sum_depth), target], a_up.at[slot, target],
            up_send.at[slot, target], up_recv.at[slot, target], upper,
        )

    def down_copy(step, target):
        slot = lax.rem(step, hop_depth)
        return remote(
            a_sum.at[lax.rem(step, sum_depth), target], a_down.at[slot, target],
            down_send.at[slot, target], down_recv.at[slot, target], lower,
        )

    def b_up_copy(step, target):
        slot = lax.rem(step, hop_depth)
        return remote(
            b_sum.at[lax.rem(step, b_sum_depth), target], b_up.at[slot, target],
            b_up_send.at[slot, target], b_up_recv.at[slot, target], upper,
        )

    def b_down_copy(step, target):
        slot = lax.rem(step, hop_depth)
        return remote(
            b_sum.at[lax.rem(step, b_sum_depth), target], b_down.at[slot, target],
            b_down_send.at[slot, target], b_down_recv.at[slot, target], lower,
        )

    def give(channel, peer):
        pl.semaphore_signal(credits.at[channel], inc=1, device_id=peer, device_id_type=mesh_id)

    def take(channel, step, depth):
        @pl.when(step >= depth)
        def _():
            pl.semaphore_wait(credits.at[channel], 1)

    def feed(step, count, channel, remote_copy, local_copy):
        @pl.when(step < count)
        def _():
            take(channel, step, DEPTH)
            remote_copy(step).start()
            local_copy(step).start()

    sources = (masters, first_moment, second_moment, left_basis, right_basis)

    def param_loads(step):
        slot = lax.rem(step, 2)
        places = pl.ds(step * EARLY, EARLY)
        return [
            pltpu.make_async_copy(source.at[places], a_params.at[slot, index], a_param_sems.at[slot, index])
            for index, source in enumerate(sources)
        ]

    def b_param_loads(step):
        slot = lax.rem(step, 2)
        return [
            pltpu.make_async_copy(
                source.at[slots - 1 - step], b_params.at[slot, index], b_param_sems.at[slot, index]
            )
            for index, source in enumerate(sources)
        ]

    token_loads = [
        pltpu.make_async_copy(source, target, token_sems.at[1 + index])
        for index, (source, target) in enumerate((
            (grad_resid, grad_resid_here), (grad_own, grad_own_here), (tokens, tokens_here), (gain, gain_here),
        ))
    ]
    grad_swap = remote(grad_sent, grad_other_here, swap_send.at[0], swap_recv.at[0], swap_peer)
    small_swap = remote(small_own, small_other, swap_send.at[1], swap_recv.at[1], swap_peer)

    branch_swap = remote(branch_sent, branch_other, swap_send.at[2], swap_recv.at[2], swap_peer)

    def branch_load(index):
        tile = lax.rem(index, TILES)
        takes_low = narrow == jnp.where(index < TILES, 1, 0)

        @pl.when(takes_low)
        def _():
            pltpu.make_async_copy(active_low.at[tile], active_here, branch_sems.at[0]).start()

        @pl.when(jnp.logical_not(takes_low))
        def _():
            pltpu.make_async_copy(active_high.at[tile], active_here, branch_sems.at[0]).start()

        pltpu.make_async_copy(down.at[tile], down_here, branch_sems.at[1]).start()

    def branch_step(index):
        pltpu.make_async_copy(active_low.at[0], active_here, branch_sems.at[0]).wait()
        pltpu.make_async_copy(down.at[0], down_here, branch_sems.at[1]).wait()

        @pl.when(lax.rem(index, TILES) == 0)
        def _():
            branch_sum[...] = jnp.zeros_like(branch_sum)

        for begin, size in spans(D, COLS):
            columns = pl.ds(begin, size)
            branch_sum[:, columns] += dot_nn(active_here[...], down_here[:, columns])

        @pl.when(index < 2 * TILES - 1)
        def _():
            branch_load(index + 1)

        @pl.when(index == TILES - 1)
        def _():
            branch_sent[...] = branch_sum[...].astype(bf16)
            branch_swap.start()

    def resid_load(source):
        return pltpu.make_async_copy(source, resid_here, token_sems.at[0])

    def finish_output():
        resid_load(resid_low).wait()
        branch_swap.wait()

        def rows_of_output(rows):
            total = resid_here[rows, :] + branch_sum[rows, :] + branch_other[rows, :].astype(f32)
            output[rows, :] = total.astype(bf16)

        row_chunks(output.shape[0], ROWS, rows_of_output)

    def finish_input_grad():
        wait_all(token_loads)
        grad_swap.wait()

        def rows_of_grad(rows):
            values = tokens_here[rows, :].astype(f32)
            inverse = rms_inverse(values)
            scaled = grad_own_here[rows, :].astype(f32) + grad_other_here[rows, :].astype(f32)
            input_grad[rows, :] = grad_resid_here[rows, :] + norm_back(
                scaled * gain_here[...], values * inverse, inverse
            )

        row_chunks(input_grad.shape[0], ROWS, rows_of_grad)

    grad_swap.start()
    for early in range(DEPTH - 1):
        feed(early, steps, 0, core_copy, own_copy)
        feed(early, late_steps, 1, b_core_copy, b_own_copy)

    start_all(param_loads(0) + param_loads(1) + b_param_loads(1) + b_param_loads(2) + token_loads)
    branch_load(0)
    pl.when(narrow == 0)(lambda: resid_load(resid_low).start())
    pl.when(narrow != 0)(lambda: resid_load(resid_high).start())

    def active(step, count):
        return (step >= 0) & (step < count)

    far = jnp.maximum(z, line - 1 - z)

    def hops(step_up, step_down, count, sums, depth, ups, downs, up, down, channel):
        @pl.when(active(step_up, count) & has_upper)
        def _():
            take(channel, step_up, hop_depth)
            slot = lax.rem(step_up, hop_depth)
            place = lax.rem(step_up, depth)

            def one(target, _):
                @pl.when(has_lower)
                def _():
                    up(step_up, target).wait_recv()
                    sums[place, target] += ups[slot, target]

                up(step_up, target).start()
                return 0

            lax.fori_loop(z + 1, line, one, 0)

        @pl.when(active(step_down, count) & has_lower)
        def _():
            take(channel + 1, step_down, hop_depth)
            slot = lax.rem(step_down, hop_depth)
            place = lax.rem(step_down, depth)

            def one(target, _):
                @pl.when(has_upper)
                def _():
                    down(step_down, target).wait_recv()
                    sums[place, target] += downs[slot, target]

                down(step_down, target).start()
                return 0

            lax.fori_loop(0, z, one, 0)

    def gather_hops(step, count, sums, depth, ups, downs, up, down, channel, total):
        slot = lax.rem(step, hop_depth)
        total[...] = sums[lax.rem(step, depth), z].astype(f32)

        @pl.when(has_lower)
        def _():
            up(step, z).wait_recv()
            total[...] += ups[slot, z].astype(f32)

            @pl.when(step < count - hop_depth)
            def _():
                give(channel, lower)

        @pl.when(has_upper)
        def _():
            down(step, z).wait_recv()
            total[...] += downs[slot, z].astype(f32)

            @pl.when(step < count - hop_depth)
            def _():
                give(channel + 1, upper)

    def retire(step, count, up, down):
        @pl.when(active(step, count))
        def _():
            def sent_up(target, _):
                up(step, target).wait_send()
                return 0

            def sent_down(target, _):
                down(step, target).wait_send()
                return 0

            lax.fori_loop(z + 1, line, sent_up, 0)
            lax.fori_loop(0, z, sent_down, 0)

    def iteration(step, _):
        feed(step + DEPTH - 1, steps, 0, core_copy, own_copy)
        feed(step + DEPTH - 1, late_steps, 1, b_core_copy, b_own_copy)

        retire(step - CROSS_LAG - HOP_LAG * far - 1, steps, up_copy, down_copy)
        retire(step - HOP_LAG * far - 1, late_steps, b_up_copy, b_down_copy)

        @pl.when(step < steps)
        def _():
            slot = lax.rem(step, DEPTH)
            place = lax.rem(step, sum_depth)
            core_copy(step).wait()
            own_copy(step).wait()

            @pl.when(step >= DEPTH)
            def _():
                cross_copy(step - DEPTH).wait_send()

            for target in range(line):
                a_send[slot, target] = a_own[slot, target, 1 - x] + a_in[slot, target, 1 - x]
            take(2, step, DEPTH)
            cross_copy(step).start()
            for target in range(line):
                a_sum[place, target] = a_own[slot, target, x] + a_in[slot, target, x]

            @pl.when(step < steps - DEPTH)
            def _():
                give(0, core_peer)

        @pl.when(step < late_steps)
        def _():
            slot = lax.rem(step, DEPTH)
            b_core_copy(step).wait()
            b_own_copy(step).wait()
            b_sum[lax.rem(step, b_sum_depth)] = b_own[slot] + b_in[slot]

            @pl.when(step < late_steps - DEPTH)
            def _():
                give(1, core_peer)

        crossed = step - CROSS_LAG

        @pl.when(active(crossed, steps))
        def _():
            slot = lax.rem(crossed, DEPTH)
            place = lax.rem(crossed, sum_depth)
            cross_copy(crossed).wait_recv()
            for target in range(line):
                a_sum[place, target] += a_cross[slot, target]

            @pl.when(crossed < steps - DEPTH)
            def _():
                give(2, cross_peer)

        hops(
            step - HOP_LAG * z, step - HOP_LAG * (line - 1 - z), late_steps, b_sum, b_sum_depth, b_up, b_down,
            b_up_copy, b_down_copy, 6,
        )
        hops(
            crossed - HOP_LAG * z, crossed - HOP_LAG * (line - 1 - z), steps, a_sum, sum_depth, a_up, a_down,
            up_copy, down_copy, 4,
        )

        last = crossed - HOP_LAG * far

        @pl.when(active(last, steps))
        def _():
            gather_hops(last, steps, a_sum, sum_depth, a_up, a_down, up_copy, down_copy, 4, a_keep)
            out[pl.ds(last * EARLY, EARLY)] = a_keep[...].astype(bf16)
            slot = lax.rem(last, 2)
            for copy in param_loads(last):
                copy.wait()
            soap_blocks(
                [a_keep[index] for index in range(EARLY)],
                *[[a_params.at[slot, kind, index] for index in range(EARLY)] for kind in range(5)],
                *[
                    [target.at[last * EARLY + index] for index in range(EARLY)]
                    for target in (new_masters, new_first, new_second)
                ],
            )

            @pl.when(last + 2 < steps)
            def _():
                start_all(param_loads(last + 2))

        arrived = step - HOP_LAG * far

        @pl.when(active(arrived, late_steps))
        def _():
            slot = lax.rem(arrived, DEPTH)

            @pl.when(arrived >= DEPTH)
            def _():
                b_cross_copy(arrived - DEPTH).wait_send()

            gather_hops(
                arrived, late_steps, b_sum, b_sum_depth, b_up, b_down, b_up_copy, b_down_copy, 6, b_keep.at[slot]
            )
            b_send[slot] = b_keep[slot, 1 - x].astype(bf16)
            take(3, arrived, DEPTH)
            b_cross_copy(arrived).start()

        paired = arrived - CROSS_LAG

        @pl.when(active(paired, late_steps))
        def _():
            slot = lax.rem(paired, DEPTH)
            b_cross_copy(paired).wait_recv()
            place = slots - 1 - paired
            total = b_keep[slot, x] + b_cross[slot].astype(f32)
            out[place] = total.astype(bf16)

            @pl.when(paired < late_steps - DEPTH)
            def _():
                give(3, cross_peer)

            @pl.when(paired == 0)
            def _():
                small_own[...] = total[: small_own.shape[0]]
                small_swap.start()

            @pl.when(paired > 0)
            def _():
                slot = lax.rem(paired, 2)
                for copy in b_param_loads(paired):
                    copy.wait()
                soap_blocks(
                    [total], *[[b_params.at[slot, kind]] for kind in range(5)],
                    [new_masters.at[place]], [new_first.at[place]], [new_second.at[place]],
                )

                @pl.when(paired + 2 < late_steps)
                def _():
                    start_all(b_param_loads(paired + 2))

        @pl.when((step >= 1) & (step < 2 * TILES + 1))
        def _():
            branch_step(step - 1)

        pl.when(step == 2 * TILES + 1)(finish_output)
        pl.when(step == 4)(finish_input_grad)
        return 0

    lag = HOP_LAG * (line - 1) + CROSS_LAG
    lax.fori_loop(0, max(max(steps, late_steps) + lag, 2 * TILES) + 2, iteration, 0)
    for step in range(max(steps - DEPTH, 0), steps):
        cross_copy(step).wait_send()
    for step in range(max(late_steps - DEPTH, 0), late_steps):
        b_cross_copy(step).wait_send()
    small_swap.wait()


def run_sum_for_owners(grads, wide_count, blocks, token_arrays):
    line = wide_count // 4
    slots, block = grads.shape[0] // wide_count, grads.shape[1:]
    steps = (slots - 1) // (EARLY + 1)
    late_steps = slots - EARLY * steps
    sum_depth = CROSS_LAG + HOP_LAG * (line - 1) + 2
    b_sum_depth = HOP_LAG * (line - 1) + 2
    hop_depth = 2 * HOP_LAG + 2
    dma = pltpu.SemaphoreType.DMA

    def vmem(*shape):
        return pltpu.VMEM(shape + block, bf16)

    def wide_vmem(*shape):
        return pltpu.VMEM(shape + block, f32)

    return pl.pallas_call(
        functools.partial(sum_for_owners, line, steps, late_steps),
        out_shape=[pltpu.VMEM((slots,) + block, bf16)]
        + [pltpu.VMEM(blocks[0].shape, f32)] * 3
        + [pltpu.VMEM(token_arrays[0].shape, f32), pltpu.VMEM(token_arrays[0].shape, bf16)]
        + [pltpu.VMEM((SMALL_ROWS, block[-1]), f32)] * 2,
        in_specs=[ANY_SPEC] * (1 + len(blocks) + len(token_arrays)),
        out_specs=[VMEM_SPEC] * 8,
        scratch_shapes=[
            vmem(DEPTH, line, 2, EARLY),
            vmem(DEPTH, line, 2, EARLY),
            vmem(sum_depth, line, EARLY),
            wide_vmem(EARLY),
            vmem(DEPTH, line, EARLY),
            vmem(DEPTH, line, EARLY),
            vmem(hop_depth, line, EARLY),
            vmem(hop_depth, line, EARLY),
            vmem(DEPTH, line, 2),
            vmem(DEPTH, line, 2),
            vmem(b_sum_depth, line, 2),
            wide_vmem(DEPTH, 2),
            vmem(DEPTH),
            vmem(DEPTH),
            vmem(hop_depth, line, 2),
            vmem(hop_depth, line, 2),
            wide_vmem(2, len(blocks), EARLY),
            wide_vmem(2, len(blocks)),
        ]
        + [pltpu.VMEM(array.shape, array.dtype) for array in token_arrays[:6]]
        + [
            pltpu.VMEM(token_arrays[7].shape[1:], bf16),
            pltpu.VMEM(token_arrays[9].shape[1:], bf16),
            pltpu.VMEM(token_arrays[0].shape, f32),
            pltpu.VMEM(token_arrays[0].shape, bf16),
            pltpu.VMEM(token_arrays[0].shape, bf16),
        ]
        + ([dma((DEPTH,))] * 5 + [dma((hop_depth, line))] * 4) * 2
        + [dma((2, len(blocks)))] * 2
        + [dma((5,)), dma((2,)), dma((3,)), dma((3,)), pltpu.SemaphoreType.REGULAR((8,))],
        compiler_params=params(SUM_VMEM, collective_id=0, has_side_effects=True),
        cost_estimate=pl.CostEstimate(flops=0, bytes_accessed=2 * grads.size * 8, transcendentals=0),
        name="sum_for_owners",
    )(grads.reshape((line, 2, 2, slots) + block), *blocks, *token_arrays)


def write_results(
    reduced, masters, first_moment, second_moment, input_grad, output, small_own, small_other,
    block_grad_out, masters_out, first_out, second_out, input_grad_out, output_out, small_out,
    stage, stage_sems, sems,
):
    copies = [
        pltpu.make_async_copy(source, target, sems.at[index])
        for index, (source, target) in enumerate((
            (masters, masters_out), (first_moment, first_out), (second_moment, second_out),
            (input_grad, input_grad_out), (output, output_out),
        ))
    ]
    start_all(copies)
    small_out[0] = small_own[...]
    small_out[1] = small_other[...]
    group = stage.shape[1]
    steps = masters.shape[0] // group

    def store(step):
        slot = lax.rem(step, 2)
        return pltpu.make_async_copy(
            stage.at[slot], block_grad_out.at[pl.ds(step * group, group)], stage_sems.at[slot]
        )

    @pl.loop(0, steps)
    def _(step):
        @pl.when(step >= 2)
        def _():
            store(step - 2).wait()

        stage[lax.rem(step, 2)] = reduced[pl.ds(step * group, group)].astype(f32)
        store(step).start()

    for step in range(max(steps - 2, 0), steps):
        store(step).wait()
    for copy in copies:
        copy.wait()


def run_write_results(*arrays):
    arrays = [pltpu.with_memory_space_constraint(array, pltpu.VMEM) for array in arrays]
    blocks, rows, small = arrays[1].shape, arrays[4].shape, arrays[-1].shape
    group = largest_group(blocks[0])
    shape = jax.ShapeDtypeStruct
    return pl.pallas_call(
        write_results,
        out_shape=[shape(blocks, f32)] * 4 + [shape(rows, f32), shape(rows, bf16), shape((2,) + small, f32)],
        in_specs=[VMEM_SPEC] * len(arrays),
        out_specs=[ANY_SPEC] * 6 + [VMEM_SPEC],
        scratch_shapes=[
            pltpu.VMEM((2, group) + blocks[1:], f32),
            pltpu.SemaphoreType.DMA((2,)),
            pltpu.SemaphoreType.DMA((5,)),
        ],
        compiler_params=params(WRITE_VMEM),
        name="write_results",
    )(*arrays)


def rope_tables(segment_row):
    token_index = jnp.arange(segment_row.shape[0], dtype=jnp.int32)
    changed = jnp.concatenate([jnp.ones((1,), dtype=bool), segment_row[1:] != segment_row[:-1]])
    begins = lax.cummax(jnp.where(changed, token_index, jnp.zeros_like(token_index)), axis=0)
    places = (token_index - begins).astype(f32)
    frequency = rope_base ** (-(jnp.arange(HEAD_DIM // 2, dtype=f32) * 2.0) / HEAD_DIM)
    angles = places[:, None] * frequency[None, :]
    cosine = jnp.concatenate([jnp.cos(angles), jnp.cos(angles)], axis=-1)
    sine_signed = jnp.concatenate([-jnp.sin(angles), jnp.sin(angles)], axis=-1)
    return (cosine, sine_signed)


def rms_parts(values):
    inverse = rms_inverse(values)
    return (inverse, values * inverse)


def norm_back(grad_scaled, normed, inverse):
    return inverse * (grad_scaled - normed * jnp.mean(grad_scaled * normed, axis=-1, keepdims=True))


def adam_small(param_now, gradient, first_now, second_now, rate_here):
    first_new = beta_first * first_now + (1.0 - beta_first) * gradient
    second_new = beta_second * second_now + (1.0 - beta_second) * gradient * gradient
    param_new = param_now - rate_here * (first_new / first_fix) / (
        jnp.sqrt(second_new / second_fix) + adam_eps
    )
    return (param_new, first_new, second_new)


def swap_halves(values):
    return lax.ppermute(values, "narrow", [(0, 1), (1, 0)])


def in_vmem(array):
    return pltpu.with_memory_space_constraint(array, pltpu.VMEM)


def body(
    tokens,
    cotangent,
    segments,
    owner_list,
    masters,
    first_moment,
    second_moment,
    left_basis,
    right_basis,
    gains,
    gain_first,
    gain_second,
    biases,
    bias_first,
    bias_second,
):
    half = lax.axis_index("narrow")
    wide_index = lax.axis_index("wide")
    wide_count = lax.axis_size("wide")
    tokens_here = tokens.shape[0]
    slots_here = masters.shape[0]
    slots_half = owner_list.shape[0]
    gains_here = gains.shape[0]
    biases_here = biases.shape[1]

    def join_halves(own, other, axis=0):
        return jnp.where(
            half == 0, jnp.concatenate([own, other], axis=axis), jnp.concatenate([other, own], axis=axis)
        )

    masters_low, gains, biases = lax.optimization_barrier((run_cast(masters), gains, biases))
    weights = lax.all_gather(masters_low, "wide", axis=0, tiled=True)
    gain_full = lax.all_gather(gains, ("wide", "narrow"), axis=0, tiled=True).reshape(2, D)
    bias_full = lax.all_gather(biases.reshape(-1).astype(bf16), "wide", axis=0, tiled=True)
    bias_full = bias_full.astype(f32).reshape(1, QKV_WIDTH)
    pair_gains = 2 * gains_here

    position = jnp.arange(slots_half, dtype=jnp.int32)
    empty = owner_list == BLOCK_TOTAL
    number = jnp.where(empty, BLOCK_TOTAL - 1 + jnp.cumsum(empty.astype(jnp.int32)), owner_list)
    weight_rows = jnp.zeros((slots_half,), jnp.int32).at[number].set(position, unique_indices=True)
    rows = weight_rows + weight_rows // slots_here
    half_index = half.astype(jnp.int32).reshape(1)

    segment_row = lax.dynamic_index_in_dim(segments, wide_index, 0, keepdims=False)
    cosine, sine = rope_tables(segment_row)
    token_index = jnp.arange(segment_row.shape[0], dtype=jnp.int32)
    allowed_turned = (
        (segment_row[None, :] == segment_row[:, None]) & (token_index[None, :] >= token_index[:, None])
    ).astype(f32)
    tokens_row = join_halves(tokens, swap_halves(tokens))
    cotangent_row = join_halves(cotangent, swap_halves(cotangent))
    weights, tokens_row, cotangent_row, rows, gain_full, gain_one, gain_two = lax.optimization_barrier(
        (weights, tokens_row, cotangent_row, rows, gain_full, gain_full[0:1], gain_full[1:2])
    )

    low_part, high_part, normed_one_turned, qkv, mixed_turned, log_total = run_attention_forward(
        weight_rows, tokens_row, gain_one, bias_full, cosine, sine, allowed_turned, weights
    )
    low_other = swap_halves(low_part)
    active_grad, down_tiles = run_active_grads(weight_rows, cotangent_row, weights)
    high_sent, low_other = lax.optimization_barrier((high_part, low_other))
    high_other = swap_halves(high_sent)
    grad_low, resid_low, turned_low, *hidden_low = run_hidden_grads(
        0, weight_rows, tokens_row, low_part, low_other, gain_two, active_grad, weights
    )
    grad_low_other = swap_halves(grad_low)
    grad_high, resid_high, turned_high, *hidden_high = run_hidden_grads(
        tokens_here, weight_rows, tokens_row, high_part, high_other, gain_two, active_grad, weights
    )
    grad_high_other = swap_halves(grad_high)
    pair_low, active_low, active_turned_low = hidden_low
    pair_high, active_high, active_turned_high = hidden_high
    grads = run_hidden_weight_grads(
        rows, cotangent_row, [(turned_low, pair_low, active_turned_low), (turned_high, pair_high, active_turned_high)],
        wide_count * (slots_here + 1),
    )
    grad_resid, grad_one_own, grad_one_sent, grads = run_attention_backward(
        weight_rows, rows, half_index, tokens_row, (resid_low, grad_low, grad_low_other),
        (resid_high, grad_high, grad_high_other), cotangent_row, gain_full, cosine, sine, allowed_turned,
        normed_one_turned, qkv, mixed_turned, log_total, weights, grads, wide_count,
    )
    blocks = [masters, first_moment, second_moment, left_basis, right_basis]
    if wide_count == 16:
        token_arrays = [
            grad_resid, grad_one_own, grad_one_sent, tokens, gain_one, resid_low, resid_high, active_low,
            active_high, down_tiles,
        ]
        block_grad, new_masters, new_first, new_second, input_grad, output, small_sums = run_write_results(
            *run_sum_for_owners(grads, wide_count, blocks, token_arrays)
        )
        gain_parts = small_sums[0, :2] + small_sums[1, :2]
        bias_row = small_sums[0, 2]
    else:
        reduced = lax.psum_scatter(grads, "wide", scatter_dimension=0, tiled=True)
        block_grad, new_masters, new_first, new_second, small_sums = run_soap(reduced, *blocks)
        gain_parts = small_sums[:2] + swap_halves(small_sums[:2])
        bias_row = small_sums[2]
        branch_low, branch_high = [
            jnp.einsum("tik,tkd->id", active, down_tiles, preferred_element_type=f32)
            for active in (active_low, active_high)
        ]
        resid_own = jnp.where(half == 0, resid_low, resid_high)
        branch_own = jnp.where(half == 0, branch_low, branch_high)
        branch_sent = jnp.where(half == 0, branch_high, branch_low).astype(bf16)
        output = (resid_own + branch_own + swap_halves(branch_sent).astype(f32)).astype(bf16)
        inverse_one, normed_one = rms_parts(tokens.astype(f32))
        grad_one = grad_one_own.astype(f32) + swap_halves(grad_one_sent).astype(f32)
        input_grad = grad_resid + norm_back(grad_one * gain_full[0:1], normed_one, inverse_one)

    gain_first_index = wide_index * pair_gains
    gain_offset = gain_first_index - jnp.minimum(gain_first_index // BLK, 2 * D // BLK - 2) * BLK
    bias_offset = lax.rem(wide_index * biases_here, BLK)
    gain_grad = lax.dynamic_slice_in_dim(gain_parts.reshape(-1), gain_offset + half * gains_here, gains_here, 0)
    bias_grad = lax.dynamic_slice_in_dim(bias_row, bias_offset, biases_here, 0).reshape(biases.shape)
    new_gains, new_gain_first, new_gain_second = adam_small(gains, gain_grad, gain_first, gain_second, rate_gains)
    new_biases, new_bias_first, new_bias_second = adam_small(biases, bias_grad, bias_first, bias_second, rate_small)

    return (
        output,
        input_grad,
        block_grad,
        new_masters,
        new_first,
        new_second,
        gain_grad,
        new_gains,
        new_gain_first,
        new_gain_second,
        bias_grad,
        new_biases,
        new_bias_first,
        new_bias_second,
    )


def solution(mesh):
    tokens_spec = P(("wide", "narrow"), None)
    blocks_spec = P(("wide", "narrow"), None, None)
    gains_spec = P(("wide", "narrow"))
    bias_spec = P("narrow", "wide")
    in_specs = (
        (tokens_spec, tokens_spec, P(), P()) + (blocks_spec,) * 5 + (gains_spec,) * 3 + (bias_spec,) * 3
    )
    out_specs = (tokens_spec, tokens_spec) + (blocks_spec,) * 4 + (gains_spec,) * 4 + (bias_spec,) * 4
    return jax.shard_map(body, mesh=mesh, in_specs=in_specs, out_specs=out_specs, check_vma=False)
```
